32 devices in a mesh: seq: 2 (over x), tok: 16 (over z, y, core).
Axes of the slice: x: 2, y: 2, z: 4, core: 2. Of those that a mesh axis runs over, the one named last changes fastest.
Arguments:
- tokens: bfloat16 [6, 4096, 768], P('seq', 'tok'), may hold values from -6 to 6
- skip_features: bfloat16 [6, 4096, 8, 128], P('seq', 'tok'), may hold values from -6 to 6
- crop_sides: int32 [6, 45], P('seq'), may hold values from 0 to 6, as said below
- ln1_gain: float32 [768], replicated, may hold values from 0.5 to 1.5
- ln1_bias: float32 [768], replicated, may hold values from -1.25 to 1.25
- qkv_weight: bfloat16 [768, 2304], replicated, may hold values from -0.21875 to 0.21875
- qv_bias: float32 [2, 768], replicated, may hold values from -1.25 to 1.25
- out_weight: bfloat16 [768, 768], replicated, may hold values from -2 to 2
- out_bias: float32 [768], replicated, may hold values from -1.25 to 1.25
- ln2_gain: float32 [768], replicated, may hold values from 0.5 to 1.5
- ln2_bias: float32 [768], replicated, may hold values from -1.25 to 1.25
- fc1_weight: bfloat16 [768, 3072], replicated, may hold values from -0.21875 to 0.21875
- fc1_bias: float32 [3072], replicated, may hold values from -1.25 to 1.25
- fc2_weight: bfloat16 [3072, 768], replicated, may hold values from -0.109375 to 0.109375
- fc2_bias: float32 [768], replicated, may hold values from -1.25 to 1.25
- deconv_weight: bfloat16 [768, 1024], replicated, may hold values from -0.21875 to 0.21875
- conv1_weight: bfloat16 [27, 256, 128], replicated, may hold values from -0.078125 to 0.078125
- conv2_weight: bfloat16 [27, 128, 128], replicated, may hold values from -0.109375 to 0.109375
- conv3_weight: bfloat16 [256, 128], replicated, may hold values from -0.375 to 0.375
- cotangent: bfloat16 [6, 4096, 8, 128], P('seq', 'tok'), may hold values from -6 to 6
Outputs:
- section_out: bfloat16 [6, 4096, 8, 128], P('seq', 'tok')
- token_grad: float32 [6, 4096, 768], P('seq', 'tok')
- skip_grad: float32 [6, 4096, 8, 128], P('seq', 'tok')
- ln1_gain_grad: float32 [768], P('tok')
- ln1_bias_grad: float32 [768], P('tok')
- qkv_grad: float32 [768, 2304], P('tok')
- qv_bias_grad: float32 [2, 768], P(None, 'tok')
- out_grad: float32 [768, 768], P('tok')
- out_bias_grad: float32 [768], P('tok')
- ln2_gain_grad: float32 [768], P('tok')
- ln2_bias_grad: float32 [768], P('tok')
- fc1_grad: float32 [768, 3072], P('tok')
- fc1_bias_grad: float32 [3072], P('tok')
- fc2_grad: float32 [3072, 768], P('tok')
- fc2_bias_grad: float32 [768], P('tok')
- deconv_grad: float32 [768, 1024], P('tok')
- conv1_grad: float32 [27, 256, 128], P(None, None, 'tok')
- conv2_grad: float32 [27, 128, 128], P(None, None, 'tok')
- conv3_grad: float32 [256, 128], P(None, 'tok')
The draws below stay inside these ranges and needn't reach their ends.
Inputs may be any that keep to these rules, and one draw needn't show every extreme that they name: `crop_sides`: row by row, the sides in patches of the crops packed in order into one sequence: 4 or 6, then zeros; the crops' sizes side * side * side add up to exactly 4096, and a row holds a positive multiple of 8 crops of side 6.
All inputs are finite; a program needn't handle non-finite values.
Results may differ from the reference program's by a relative error of at most 0.028.
Values may be sent and summed in bfloat16 or wider, within the bound.
A program may use at most 640 MiB of HBM per device.

```python
import math
from functools import partial
import jax
import jax.numpy as jnp
import numpy as np
from jax import lax

D = 768
HEADS = 12
HEAD_DIM = 64
FF = 3072
C = 128
LEN = 4096
SEQS = 6
CROPS = 45


def draw_crop_sides(key, part):
    key = jax.random.fold_in(key, 11)
    kind_key, order_key = jax.random.split(key)
    big_count = 8 * jax.random.randint(kind_key, (SEQS, 1), 1, LEN // 1728 + 1)
    crop_count = big_count + (LEN - 216 * big_count) // 64
    slot_index = jnp.arange(CROPS, dtype=jnp.int32)[None, :]
    scores = jax.random.randint(order_key, (SEQS, CROPS), 0, 1 << 20) * CROPS + slot_index
    scores = jnp.where(slot_index < crop_count, scores, (1 << 30) + slot_index)
    ordering = jnp.argsort(scores, axis=1)
    ranking = jnp.argsort(ordering, axis=1)
    return jnp.where(ranking < big_count, 6, jnp.where(ranking < crop_count, 4, 0)).astype(jnp.int32)


def strengthened(result, own_key, source, target, shards_of, factor):
    owner, partner = [(jnp.arange(result.shape[dim]) // (result.shape[dim] // shards_of)).reshape([-1 if axis == dim else 1 for axis in range(result.ndim)]) for dim in (source, target)]
    chosen = jax.random.permutation(own_key, shards_of)[partner]
    strong = (owner == chosen) | (owner == (partner + shards_of // 2) % shards_of)
    return jnp.where(strong, factor * result, result)


def block_scale(key, shape, shards, smallest, top_value):
    factor_of = 1.0
    for dim, blocks in shards:
        draws = jax.random.uniform(jax.random.fold_in(jax.random.fold_in(key, 6), dim), (blocks,), jnp.float32, smallest / len(shards), top_value / len(shards))
        factor_of = factor_of * jnp.repeat(jnp.exp(draws), shape[dim] // blocks).reshape((-1,) + (1,) * (len(shape) - 1 - dim))
    return factor_of


def centred(stream_key, shape, deviation, bound, shards=(), kind=jnp.bfloat16):
    entries = jax.random.normal(stream_key, shape, jnp.float32) * deviation
    if len(shards) > 0:
        entries = block_scale(stream_key, shape, shards, -0.22, 0.18) * entries
    return jnp.clip(entries, min=-bound, max=bound).astype(kind)


def gaussian_with(rng, dims, deviation, limit, pieces, heavy, kind=jnp.bfloat16):
    entries = deviation * jax.random.normal(rng, dims, jnp.float32)
    if pieces:
        entries = entries * block_scale(rng, dims, pieces, -0.22, 0.18)
    return jnp.clip(strengthened(entries, jax.random.fold_in(rng, 3), *heavy), -limit, limit).astype(kind)


def setup_inputs(seed: int = 0) -> dict:
    arg_keys = jax.random.split(jax.random.key(seed), 21)
    return {
        "tokens": centred(arg_keys[0], (SEQS, LEN, D), 1.0, 6.0, ((0, 2), (1, 16))),
        "skip_features": centred(arg_keys[1], (SEQS, LEN, 8, C), 1.0, 6.0, ((0, 2), (1, 16))),
        "crop_sides": draw_crop_sides(jax.random.fold_in(arg_keys[20], 71), 0),
        "ln1_gain": jnp.clip(1.0 + 0.1 * jax.random.normal(arg_keys[3], (D,), jnp.float32), 0.5, 1.5),
        "ln1_bias": centred(arg_keys[4], (D,), 0.2, 1.25, (), jnp.float32),
        "qkv_weight": centred(arg_keys[5], (D, 3 * D), D ** -0.5, 0.21875),
        "qv_bias": centred(arg_keys[6], (2, D), 0.2, 1.25, (), jnp.float32),
        "out_weight": centred(arg_keys[7], (D, D), (max(D // 96, 4)) ** -0.5, 2.0),
        "out_bias": centred(arg_keys[8], (D,), 0.2, 1.25, (), jnp.float32),
        "ln2_gain": jnp.clip(1.0 + 0.1 * jax.random.normal(arg_keys[9], (D,), jnp.float32), 0.5, 1.5),
        "ln2_bias": centred(arg_keys[10], (D,), 0.2, 1.25, (), jnp.float32),
        "fc1_weight": centred(arg_keys[11], (D, FF), D ** -0.5, 0.21875),
        "fc1_bias": centred(arg_keys[12], (FF,), 0.2, 1.25, (), jnp.float32),
        "fc2_weight": centred(arg_keys[13], (FF, D), FF ** -0.5, 0.109375),
        "fc2_bias": centred(arg_keys[14], (D,), 0.2, 1.25, (), jnp.float32),
        "deconv_weight": centred(arg_keys[15], (D, 8 * C), D ** -0.5, 0.21875),
        "conv1_weight": centred(arg_keys[16], (27, 2 * C, C), (54 * C) ** -0.5, 0.078125),
        "conv2_weight": centred(arg_keys[17], (27, C, C), (27 * C) ** -0.5, 0.109375),
        "conv3_weight": centred(arg_keys[18], (2 * C, C), (2 * C) ** -0.5, 0.375),
        "cotangent": gaussian_with(arg_keys[19], (SEQS, LEN, 8, C), 1.0, 6.0, ((0, 2), (1, 16)), (1, 3, 16, 2.0)),
    }


@jax.custom_vjp
def low(v):
    return lax.optimization_barrier(v.astype(jnp.bfloat16)).astype(jnp.float32)

@jax.custom_vjp
def low_back(v):
    return v

def low_keep(v):
    return (low(v), None)

def low_pass(kept, grad):
    return (grad,)

def back_keep(v):
    return (v, None)

def back_low(kept, grad):
    return (low(grad),)
low.defvjp(low_keep, low_pass)
low_back.defvjp(back_keep, back_low)
side_small = 4
side_big = 6
halo_rows = 43
norm_eps = 1e-05
far_below = -1e+30
key_margin = 256
query_block = 512
highest = lax.Precision.HIGHEST
in_part = {-1: (1, 2), 0: (0, 2), 1: (0, 1)}
out_part = {-1: (0, 1), 0: (0, 2), 1: (1, 2)}

def all_offsets():
    step_values = (-1, 0, 1)
    return [(step_x, step_y, step_z) for step_x in step_values for step_y in step_values for step_z in step_values]

def index_tuples(table_shape):
    tuples_out = [()]
    for extent in table_shape:
        tuples_out = [prefix + (position,) for prefix in tuples_out for position in range(extent)]
    return tuples_out

def tap_table(offset):
    in_lists = [list(range(in_part[offset_entry][0], in_part[offset_entry][1])) for offset_entry in offset]
    out_lists = [list(range(out_part[offset_entry][0], out_part[offset_entry][1])) for offset_entry in offset]
    table_shape = tuple((len(members) for members in in_lists)) + tuple((len(members) for members in out_lists))
    tap_index = np.zeros(table_shape, dtype=np.int32)
    for entry_index in index_tuples(table_shape):
        flat_tap = 0
        for axis_id in range(3):
            source_sub = in_lists[axis_id][entry_index[axis_id]]
            target_sub = out_lists[axis_id][entry_index[3 + axis_id]]
            flat_tap = flat_tap * 3 + 2 * offset[axis_id] + source_sub - target_sub + 1
        tap_index[entry_index] = flat_tap
    return tap_index

def sub_cut(array_in, parts, offset):
    begins = [parts[offset_entry][0] for offset_entry in offset]
    finish = [parts[offset_entry][1] for offset_entry in offset]
    return array_in[:, :, begins[0]:finish[0], begins[1]:finish[1], begins[2]:finish[2]]

def sub_pad(array_in, parts, offset):
    widths = [(0, 0), (0, 0)] + [(parts[offset_entry][0], 2 - parts[offset_entry][1]) for offset_entry in offset] + [(0, 0)]
    return jnp.pad(array_in, widths)

def crop_bounds(sides):
    volumes = sides * sides * sides
    ends_at = jnp.cumsum(volumes, axis=-1, dtype=jnp.int32)
    return (ends_at - volumes, ends_at)

def locate(sides, places):
    starts, ends_at = crop_bounds(sides)
    inside = (places[:, :, None] >= starts[:, None, :]) & (places[:, :, None] < ends_at[:, None, :])
    numbers = jnp.arange(sides.shape[-1], dtype=jnp.int32)
    found = jnp.any(inside, axis=-1)
    segment = lax.optimization_barrier(jnp.sum(jnp.where(inside, numbers, 0), axis=-1, dtype=jnp.int32))
    segment = jnp.where(found, segment, -1)
    side_of = lax.optimization_barrier(jnp.sum(jnp.where(inside, sides[:, None, :], 0), axis=-1, dtype=jnp.int32))
    first_of = lax.optimization_barrier(jnp.sum(jnp.where(inside, starts[:, None, :], 0), axis=-1, dtype=jnp.int32))
    return (inside, segment, side_of, first_of)

def geometry(side_of, first_of, places):
    local_pos = places - first_of
    safe_side = jnp.maximum(side_of, 1)
    return (local_pos // (safe_side * safe_side), local_pos // safe_side % safe_side, local_pos % safe_side, side_of, side_of == side_big)

def step_sizes(offset):
    near_step = offset[0] * side_small * side_small + offset[1] * side_small + offset[2]
    far_step = offset[0] * side_big * side_big + offset[1] * side_big + offset[2]
    return (near_step, far_step)

def in_crop(shape_info, offset):
    row_pos, column, depth_pos, side_of, is_big = shape_info
    inside_crop = (row_pos + offset[0] >= 0) & (row_pos + offset[0] < side_of)
    inside_crop = inside_crop & (column + offset[1] >= 0) & (column + offset[1] < side_of)
    return inside_crop & (depth_pos + offset[2] >= 0) & (depth_pos + offset[2] < side_of)

def shifted(padded, offset, shape_info, length):
    near_step, far_step = step_sizes(offset)
    small_view = lax.slice_in_dim(padded, halo_rows + near_step, halo_rows + near_step + length, axis=1)
    big_view = lax.slice_in_dim(padded, halo_rows + far_step, halo_rows + far_step + length, axis=1)
    is_big = shape_info[4][:, :, None, None, None, None]
    inside_crop = in_crop(shape_info, offset)[:, :, None, None, None, None]
    picked = jnp.where(is_big, big_view, small_view)
    return jnp.where(inside_crop, picked, jnp.zeros((), padded.dtype))

def offset_term(padded, kernel, shape_info, offset):
    length = padded.shape[1] - 2 * halo_rows
    source = sub_cut(shifted(padded, offset, shape_info, length), in_part, offset)
    kernel_block = kernel[tap_table(offset)]
    term_part = jnp.einsum('stxyzc,xyzXYZcd->stXYZd', source, kernel_block, precision=highest)
    return sub_pad(term_part, out_part, offset)

def conv_field(padded, kernel, shape_info):
    result_sum = 0.0
    for offset in all_offsets():
        term_fn = jax.checkpoint(partial(offset_term, offset=offset))
        result_sum = result_sum + term_fn(padded, kernel, shape_info)
    return result_sum

def pad_rows(field):
    return jnp.pad(field, ((0, 0), (halo_rows, halo_rows), (0, 0), (0, 0), (0, 0), (0, 0)))

def layer_norm(values_in, gain, shift):
    centered = values_in - lax.optimization_barrier(jnp.mean(values_in, axis=-1, keepdims=True))
    variance = lax.optimization_barrier(jnp.mean(centered * centered, axis=-1, keepdims=True))
    return centered * lax.rsqrt(variance + norm_eps) * gain + shift

def crop_totals(inside_float, field):
    return jnp.einsum('stk,stc->skc', inside_float, lax.optimization_barrier(jnp.sum(field, axis=(2, 3, 4))), precision=highest)

def spread(inside_float, crop_values):
    return jnp.einsum('stk,skc->stc', inside_float, crop_values, precision=highest)[:, :, None, None, None, :]

def instance_norm(field, inside_float, counts):
    means = crop_totals(inside_float, field) / counts[:, :, None]
    squares = crop_totals(inside_float, field * field) / counts[:, :, None]
    scales = lax.rsqrt(squares - means * means + norm_eps)
    return (field - spread(inside_float, means)) * spread(inside_float, scales)

def attention(query_heads, key_heads, value_heads, segment):
    length = query_heads.shape[0]
    margin_pad = ((key_margin, key_margin), (0, 0), (0, 0))
    key_padded = jnp.pad(key_heads, margin_pad)
    value_padded = jnp.pad(value_heads, margin_pad)
    segment_padded = jnp.pad(segment, (key_margin, key_margin), constant_values=-1)
    scale_factor = 1.0 / math.sqrt(HEAD_DIM)
    key_span = query_block + 2 * key_margin

    def per_block(block_index):
        begin_row = block_index * query_block
        query_part = lax.dynamic_slice_in_dim(query_heads, begin_row, query_block, 0)
        key_part = lax.dynamic_slice_in_dim(key_padded, begin_row, key_span, 0)
        value_part = lax.dynamic_slice_in_dim(value_padded, begin_row, key_span, 0)
        query_crop = lax.dynamic_slice_in_dim(segment, begin_row, query_block, 0)
        key_crop = lax.dynamic_slice_in_dim(segment_padded, begin_row, key_span, 0)
        scores = low_back(jnp.einsum('qhd,khd->hqk', query_part, key_part, precision=highest) * scale_factor)
        same_crop = (query_crop[:, None] == key_crop[None, :])[None, :, :]
        scores = jnp.where(same_crop, scores, far_below)
        row_max = lax.optimization_barrier(jnp.max(scores, axis=-1, keepdims=True))
        weights = jnp.exp(scores - row_max)
        attn_probs = weights / lax.optimization_barrier(jnp.sum(weights, axis=-1, keepdims=True))
        return jnp.einsum('hqk,khd->qhd', low(attn_probs), value_part, precision=highest)
    outputs = lax.map(jax.checkpoint(per_block), jnp.arange(length // query_block, dtype=jnp.int32))
    return outputs.reshape(length, -1)

def sequence_forward(values_in, skip_in, sides, params):
    ln1_gain, ln1_bias, qkv_weight, qv_bias, out_weight, out_bias, ln2_gain, ln2_bias, fc1_weight, fc1_bias, fc2_weight, fc2_bias, deconv_weight, conv1_weight, conv2_weight, conv3_weight = params
    length, model_width = values_in.shape
    channels = conv2_weight.shape[2]
    places = jnp.arange(length, dtype=jnp.int32)[None, :]
    sides_row = sides[None, :]
    inside, segment, side_of, first_of = locate(sides_row, places)
    normed_one = low(layer_norm(values_in, ln1_gain, ln1_bias))
    qkv_bias = jnp.concatenate([qv_bias[0], jnp.zeros_like(qv_bias[0]), qv_bias[1]])
    projected = low(low_back(jnp.dot(normed_one, qkv_weight, precision=highest) + qkv_bias))
    query_heads = projected[:, :model_width].reshape(length, HEADS, HEAD_DIM)
    key_heads = projected[:, model_width:2 * model_width].reshape(length, HEADS, HEAD_DIM)
    value_heads = projected[:, 2 * model_width:].reshape(length, HEADS, HEAD_DIM)
    attended = low(low_back(attention(query_heads, key_heads, value_heads, segment[0])))
    resid_one = values_in + low_back(jnp.dot(attended, out_weight, precision=highest) + out_bias)
    normed_two = low(layer_norm(resid_one, ln2_gain, ln2_bias))
    pre_act = low_back(jnp.dot(normed_two, fc1_weight, precision=highest) + fc1_bias)
    activated = low(jax.nn.gelu(pre_act, approximate=False))
    resid_two = resid_one + low_back(jnp.dot(activated, fc2_weight, precision=highest) + fc2_bias)
    upsampled = low(low_back(jnp.dot(low(resid_two), deconv_weight, precision=highest)))
    upsampled = upsampled.reshape(1, length, 2, 2, 2, channels)
    joined = jnp.concatenate([upsampled, skip_in.reshape(1, length, 2, 2, 2, channels)], axis=-1)
    shape_info = geometry(side_of, first_of, places)
    inside_float = inside.astype(jnp.float32)
    counts = jnp.maximum(8.0 * (sides_row * sides_row * sides_row).astype(jnp.float32), 1.0)
    first_conv = low_back(conv_field(pad_rows(joined), conv1_weight, shape_info))
    side_conv = low_back(jnp.einsum('stxyzc,cd->stxyzd', joined, conv3_weight, precision=highest))
    hidden = low(jax.nn.silu(instance_norm(first_conv, inside_float, counts)))
    second_conv = low_back(conv_field(pad_rows(hidden), conv2_weight, shape_info))
    summed = instance_norm(second_conv, inside_float, counts) + instance_norm(side_conv, inside_float, counts)
    return jax.nn.silu(summed).reshape(length, 8, channels)

def reference(tokens, skip_features, crop_sides, ln1_gain, ln1_bias, qkv_weight, qv_bias, out_weight, out_bias, ln2_gain, ln2_bias, fc1_weight, fc1_bias, fc2_weight, fc2_bias, deconv_weight, conv1_weight, conv2_weight, conv3_weight, cotangent):
    params = (ln1_gain, ln1_bias, qkv_weight.astype(jnp.float32), qv_bias, out_weight.astype(jnp.float32), out_bias, ln2_gain, ln2_bias, fc1_weight.astype(jnp.float32), fc1_bias, fc2_weight.astype(jnp.float32), fc2_bias, deconv_weight.astype(jnp.float32), conv1_weight.astype(jnp.float32), conv2_weight.astype(jnp.float32), conv3_weight.astype(jnp.float32))

    def forward(inputs, skips, weights_all):

        def per_sequence(members):
            return sequence_forward(members[0], members[1], members[2], weights_all)
        return lax.map(jax.checkpoint(per_sequence), (inputs, skips, crop_sides))
    outputs, pull = jax.vjp(forward, tokens.astype(jnp.float32), skip_features.astype(jnp.float32), params)
    token_grad, skip_grad, grads = pull(cotangent.astype(jnp.float32))
    return (outputs.astype(jnp.bfloat16), token_grad, skip_grad, grads[0], grads[1], grads[2], grads[3], grads[4], grads[5], grads[6], grads[7], grads[8], grads[9], grads[10], grads[11], grads[12], grads[13], grads[14], grads[15])
```

```python
from functools import partial
import math

import jax
import jax.numpy as jnp
import numpy as np
from jax import lax
from jax.experimental import pallas as pl
from jax.experimental.pallas import tpu as pltpu
from jax.sharding import PartitionSpec as P

HEADS = 12
HEAD_DIM = 64


side_small = 4
side_big = 6
halo_rows = 43
key_reach = 215
norm_eps = 1e-05
far_below = -1e30
highest = lax.Precision.HIGHEST
in_part = {-1: (1, 2), 0: (0, 2), 1: (0, 1)}
out_part = {-1: (0, 1), 0: (0, 2), 1: (1, 2)}


def passed_along(block, axis, distance):
    devices = range(lax.axis_size(axis))
    route = [(i - distance, i) for i in devices if i - distance in devices]
    return lax.ppermute(block, axis, route)


def all_offsets():
    step_values = (-1, 0, 1)
    return [
        (step_x, step_y, step_z)
        for step_x in step_values
        for step_y in step_values
        for step_z in step_values
    ]


def crop_bounds(sides):
    volumes = sides * sides * sides
    ends_at = jnp.cumsum(volumes, axis=-1, dtype=jnp.int32)
    return (ends_at - volumes, ends_at)


def locate(sides, places):
    starts, ends_at = crop_bounds(sides)
    inside = (places[:, :, None] >= starts[:, None, :]) & (places[:, :, None] < ends_at[:, None, :])
    numbers = jnp.arange(sides.shape[-1], dtype=jnp.int32)
    found = jnp.any(inside, axis=-1)
    segment = jnp.sum(jnp.where(inside, numbers, 0), axis=-1, dtype=jnp.int32)
    segment = jnp.where(found, segment, -1)
    side_of = jnp.sum(jnp.where(inside, sides[:, None, :], 0), axis=-1, dtype=jnp.int32)
    first_of = jnp.sum(jnp.where(inside, starts[:, None, :], 0), axis=-1, dtype=jnp.int32)
    return (inside, segment, side_of, first_of)


def geometry(side_of, first_of, places):
    local_pos = places - first_of
    safe_side = jnp.maximum(side_of, 1)
    return (
        local_pos // (safe_side * safe_side),
        local_pos // safe_side % safe_side,
        local_pos % safe_side,
        side_of,
        side_of == side_big,
    )


def step_sizes(offset):
    near_step = offset[0] * side_small * side_small + offset[1] * side_small + offset[2]
    far_step = offset[0] * side_big * side_big + offset[1] * side_big + offset[2]
    return (near_step, far_step)


def in_crop(shape_info, offset):
    row_pos, column, depth_pos, side_of, is_big = shape_info
    inside_crop = (row_pos + offset[0] >= 0) & (row_pos + offset[0] < side_of)
    inside_crop = inside_crop & (column + offset[1] >= 0) & (column + offset[1] < side_of)
    return inside_crop & (depth_pos + offset[2] >= 0) & (depth_pos + offset[2] < side_of)


def layer_norm(values_in, gain, shift):
    centered = values_in - jnp.mean(values_in, axis=-1, keepdims=True)
    variance = jnp.mean(centered * centered, axis=-1, keepdims=True)
    return centered * lax.rsqrt(variance + norm_eps) * gain + shift


def crop_scores(query_heads, key_heads, same_crop):
    raw_scores = jnp.einsum(
        "sqhd,skhd->shqk", query_heads, key_heads, preferred_element_type=jnp.float32
    )
    return jnp.where(same_crop, raw_scores * (1.0 / math.sqrt(HEAD_DIM)), far_below)


EDGE = 48
WINDOW = 256
TILE = 128
CROP_ROWS = 48
SUBS = 8
VMEM_LIMIT = 60 * 1024 * 1024
lowest_step = {-1: -43, 0: -7, 1: 11}
low_type = jnp.bfloat16
wide = jnp.float32


def dot(left, right):
    return jnp.dot(left, right, preferred_element_type=wide)


def three_terms(field):
    first = field.astype(low_type)
    rest = field - first.astype(wide)
    second = rest.astype(low_type)
    third = (rest - second.astype(wide)).astype(low_type)
    return (first, second, third)


def exact_dot(chosen, field):
    first, second, third = three_terms(field)
    return dot(chosen, first) + dot(chosen, second) + dot(chosen, third)


def sub_lanes(number, width):
    return slice(number * width, (number + 1) * width)


def banded(taps):
    begin = jnp.pad(taps, ((0, 0), (0, 0), (0, 1), (0, 0), (0, 0)))
    later = jnp.pad(taps, ((0, 0), (0, 0), (1, 0), (0, 0), (0, 0)))
    both = jnp.concatenate([begin, later], axis=-1)
    return both.reshape(3, 12 * taps.shape[3], 2 * taps.shape[4])


def forward_band(weight):
    return banded(weight.reshape((3, 3, 3) + weight.shape[1:]))


def backward_band(weight):
    taps = weight.reshape((3, 3, 3) + weight.shape[1:])
    return banded(taps[::-1, ::-1, ::-1].swapaxes(3, 4))


def window_positions(step):
    return {-1: ((0, 1),), 0: ((1, 0), (2, 1)), 1: ((3, 0),)}[step]


def fill_windows(x_ref, place_ref, p_ref, rows, width):
    tile = min(rows, TILE)
    for base in range(0, rows, tile):
        own = slice(base, base + tile)
        for number, (step_x, step_y, step_z) in enumerate(all_offsets()):
            low = (EDGE + base + lowest_step[step_x]) // 16 * 16
            centre = (step_x, step_y, step_z) == (0, 0, 0)
            if not centre:
                lane = lax.broadcasted_iota(jnp.int32, (tile, WINDOW), 1) + low
                chosen = jnp.where(lane == place_ref[0, own, number : number + 1], 1.0, 0.0)
                chosen = chosen.astype(low_type)
            for x_to, x_from in window_positions(step_x):
                for y_to, y_from in window_positions(step_y):
                    z_to, z_from = window_positions(step_z)[0]
                    count = (2 if step_z == 0 else 1) * width
                    to = ((x_to * 4 + y_to) * 4 + z_to) * width
                    source = (x_from * 4 + y_from * 2 + z_from) * width
                    if centre:
                        got = x_ref[EDGE + base : EDGE + base + tile, source : source + count]
                    else:
                        got = dot(chosen, x_ref[low : low + WINDOW, source : source + count])
                    p_ref[own, to : to + count] = got.astype(low_type)


def window_conv(p_ref, band_ref, pair, width):
    first, second = pair
    total = None
    for tap in range(3):
        begin = ((first + tap) * 4 + second) * 4 * width
        term = dot(p_ref[:, begin : begin + 12 * width], band_ref[tap])
        total = term if total is None else total + term
    return total


def all_pairs():
    return [(first, second) for first in range(2) for second in range(2)]


def add_grads(left_ref, p_ref, total_ref, width, channels):
    for tap_x in range(3):
        for tap_y in range(3):
            term = None
            for number, (first, second) in enumerate(all_pairs()):
                begin = ((first + tap_x) * 4 + second + tap_y) * 4 * channels
                left = left_ref[number * 2 * width : (number + 1) * 2 * width, :]
                part = dot(left, p_ref[:, begin : begin + 4 * channels])
                term = part if term is None else term + part
            total_ref[tap_x * 3 + tap_y] += term


def fold_grads(total_ref, grad_ref, width, channels):
    for tap_x in range(3):
        for tap_y in range(3):
            for tap_z in range(3):
                number = tap_x * 3 + tap_y
                here = total_ref[number, :width, sub_lanes(tap_z, channels)]
                there = total_ref[number, width:, sub_lanes(tap_z + 1, channels)]
                grad_ref[26 - (number * 3 + tap_z)] = here + there


def kernel_call(body, seqs, inputs, shared, outputs, summed, scratch, flops):
    def row_spec(shape):
        return pl.BlockSpec((1,) + tuple(shape[1:]), lambda i: (i,) + (0,) * (len(shape) - 1))

    def whole_spec(shape):
        return pl.BlockSpec(tuple(shape), lambda i: (0,) * len(shape))

    moved = sum(math.prod(a.shape) * a.dtype.itemsize for a in list(inputs) + list(shared))
    moved += sum(math.prod(s) * jnp.dtype(t).itemsize for s, t in list(outputs) + list(summed))
    return pl.pallas_call(
        body,
        grid=(seqs,),
        in_specs=[row_spec(a.shape) for a in inputs] + [whole_spec(a.shape) for a in shared],
        out_specs=[row_spec(s) for s, _ in outputs] + [whole_spec(s) for s, _ in summed],
        out_shape=[jax.ShapeDtypeStruct(s, t) for s, t in list(outputs) + list(summed)],
        scratch_shapes=scratch,
        compiler_params=pltpu.CompilerParams(vmem_limit_bytes=VMEM_LIMIT),
        cost_estimate=pl.CostEstimate(flops=flops, bytes_accessed=moved, transcendentals=0),
    )(*inputs, *shared)


def conv_scratch(rows, width):
    return [
        pltpu.VMEM((rows + 192, SUBS * width), low_type),
        pltpu.VMEM((rows, 64 * width), low_type),
    ]


def conv_flops(seqs, rows, inner, outer):
    return 2 * seqs * rows * (36 * 4 * inner * 2 * outer + 56 * WINDOW * inner)


def put_edges(low_pay, high_pay, number, field, channels, rows):
    lanes = sub_lanes(number, channels)
    low_pay[0, :, lanes] = field[:EDGE].astype(low_type)
    high_pay[0, :, lanes] = field[rows - EDGE :].astype(low_type)


def put_sums(sums_ref, low_pay, high_pay, number, value, channels):
    lanes = sub_lanes(number, channels)
    sums_ref[0, :, lanes] = value
    pay_lanes = sub_lanes(SUBS + number, channels)
    low_pay[0, :, pay_lanes] = value.astype(low_type)
    high_pay[0, :, pay_lanes] = value.astype(low_type)


def taken_sums(sums_ref, left_pay, right_pay, number, channels):
    lanes = sub_lanes(number, channels)
    pay_lanes = sub_lanes(SUBS + number, channels)
    total = sums_ref[0, :, lanes] + left_pay[0, :, pay_lanes].astype(wide)
    return total + right_pay[0, :, pay_lanes].astype(wide)


def mean_and_scale(total, square, inverse):
    mean = total * inverse
    variance = jnp.maximum(square * inverse - mean * mean, 0.0)
    return (mean, lax.rsqrt(variance + norm_eps))


def silu_parts(value):
    gate = 1.0 / (1.0 + jnp.exp(-value))
    return (value * gate, gate * (1.0 + value * (1.0 - gate)))


def first_conv_kernel(rows, channels):
    width = 2 * channels

    def body(
        up, up_left, up_right, skip, skip_left, skip_right, place, crop_t, band, side,
        first_out, side_out, sums, low_pay, high_pay, x_ref, p_ref,
    ):
        for number in range(SUBS):
            for half, (own, left, right) in enumerate(
                ((up, up_left, up_right), (skip, skip_left, skip_right))
            ):
                to = sub_lanes(2 * number + half, channels)
                lanes = sub_lanes(number, channels)
                x_ref[:EDGE, to] = left[0, :, lanes]
                x_ref[EDGE : EDGE + rows, to] = own[0, :, lanes]
                x_ref[EDGE + rows : 2 * EDGE + rows, to] = right[0, :, lanes]
        x_ref[2 * EDGE + rows :, :] = jnp.zeros((96, SUBS * width), low_type)
        fill_windows(x_ref, place, p_ref, rows, width)
        total = [jnp.zeros((rows, channels), wide) for _ in range(4)]
        for index, pair in enumerate(all_pairs()):
            result = window_conv(p_ref, band, pair, width)
            first_out[0, :, sub_lanes(index, width)] = result
            for half in range(2):
                number = 2 * index + half
                value = result[:, sub_lanes(half, channels)]
                put_edges(low_pay, high_pay, number, value, channels, rows)
                flat = dot(x_ref[EDGE : EDGE + rows, sub_lanes(number, width)], side[...])
                side_out[0, :, sub_lanes(number, channels)] = flat
                terms = (value, value * value, flat, flat * flat)
                total = [have + term for have, term in zip(total, terms)]
        for number in range(4):
            value = exact_dot(crop_t[0], total[number])
            put_sums(sums, low_pay, high_pay, number, value, channels)

    return body


def second_conv_kernel(rows, channels):
    def body(
        first, left_pay, right_pay, own_sums, inverse, owner, place, crop_t, band,
        second_out, stats, sums, low_pay, high_pay, x_ref, p_ref,
    ):
        taken = [taken_sums(own_sums, left_pay, right_pay, n, channels) for n in range(4)]
        mean, scale = mean_and_scale(taken[0], taken[1], inverse[0])
        side_mean, side_scale = mean_and_scale(taken[2], taken[3], inverse[0])
        for number, value in enumerate((mean, scale, side_mean, side_scale)):
            stats[0, :, sub_lanes(number, channels)] = value
        mean_rows = exact_dot(owner[0], mean)
        scale_rows = exact_dot(owner[0], scale)
        parts = (
            (left_pay, slice(0, EDGE)),
            (first, slice(EDGE, EDGE + rows)),
            (right_pay, slice(EDGE + rows, 2 * EDGE + rows)),
        )
        for number in range(SUBS):
            lanes = sub_lanes(number, channels)
            for field, place_rows in parts:
                normed = field[0, :, lanes].astype(wide) - mean_rows[place_rows]
                normed = normed * scale_rows[place_rows]
                x_ref[place_rows, lanes] = silu_parts(normed)[0].astype(low_type)
        x_ref[2 * EDGE + rows :, :] = jnp.zeros((96, SUBS * channels), low_type)
        fill_windows(x_ref, place, p_ref, rows, channels)
        total = [jnp.zeros((rows, channels), wide) for _ in range(2)]
        for index, pair in enumerate(all_pairs()):
            result = window_conv(p_ref, band, pair, channels)
            second_out[0, :, sub_lanes(index, 2 * channels)] = result
            for half in range(2):
                value = result[:, sub_lanes(half, channels)]
                put_edges(low_pay, high_pay, 2 * index + half, value, channels, rows)
                total = [total[0] + value, total[1] + value * value]
        for number in range(2):
            value = exact_dot(crop_t[0], total[number])
            put_sums(sums, low_pay, high_pay, number, value, channels)

    return body


def output_kernel(rows, channels):
    def body(
        second, side_field, cotangent, stats, left_pay, right_pay, own_sums, inverse, owner, crop_t,
        section, grad_out, second_stats, sums, low_pay, high_pay,
    ):
        taken = [taken_sums(own_sums, left_pay, right_pay, n, channels) for n in range(2)]
        mean, scale = mean_and_scale(taken[0], taken[1], inverse[0])
        second_stats[0, :, sub_lanes(0, channels)] = mean
        second_stats[0, :, sub_lanes(1, channels)] = scale
        own = owner[0, EDGE : EDGE + rows, :]
        mean_rows = exact_dot(own, mean)
        scale_rows = exact_dot(own, scale)
        side_mean = exact_dot(own, stats[0, :, sub_lanes(2, channels)])
        side_scale = exact_dot(own, stats[0, :, sub_lanes(3, channels)])
        total = [jnp.zeros((rows, channels), wide) for _ in range(3)]
        for number in range(SUBS):
            lanes = sub_lanes(number, channels)
            normed = (second[0, :, lanes] - mean_rows) * scale_rows
            side = (side_field[0, :, lanes] - side_mean) * side_scale
            value, slope = silu_parts(normed + side)
            section[0, :, lanes] = value.astype(low_type)
            grad = cotangent[0, :, lanes].astype(wide) * slope
            grad_out[0, :, lanes] = grad
            put_edges(low_pay, high_pay, number, grad, channels, rows)
            terms = (grad, grad * normed, grad * side)
            total = [have + term for have, term in zip(total, terms)]
        for number in range(3):
            value = exact_dot(crop_t[0], total[number])
            put_sums(sums, low_pay, high_pay, number, value, channels)

    return body


def second_back_kernel(rows, channels, seqs):
    def body(
        grad, grad_left, grad_right, own_sums, second, second_left, second_right, side_field, first,
        stats, second_stats, inverse, owner, place, crop_t, band,
        first_grad, side_grad, sums, low_pay, high_pay, weight_grad,
        x_ref, p_ref, left_ref, total_ref,
    ):
        means = [
            taken_sums(own_sums, grad_left, grad_right, n, channels) * inverse[0] for n in range(3)
        ]
        mean_rows = exact_dot(owner[0], second_stats[0, :, sub_lanes(0, channels)])
        scale_rows = exact_dot(owner[0], second_stats[0, :, sub_lanes(1, channels)])
        lead_rows = exact_dot(owner[0], means[0])
        slope_rows = exact_dot(owner[0], means[1])
        parts = (
            (grad_left, second_left, slice(0, EDGE)),
            (grad, second, slice(EDGE, EDGE + rows)),
            (grad_right, second_right, slice(EDGE + rows, 2 * EDGE + rows)),
        )
        own = slice(EDGE, EDGE + rows)
        side_mean = exact_dot(owner[0, own, :], stats[0, :, sub_lanes(2, channels)])
        side_scale = exact_dot(owner[0, own, :], stats[0, :, sub_lanes(3, channels)])
        side_slope = exact_dot(owner[0, own, :], means[2])
        first_mean = exact_dot(owner[0, own, :], stats[0, :, sub_lanes(0, channels)])
        first_scale = exact_dot(owner[0, own, :], stats[0, :, sub_lanes(1, channels)])
        for number in range(SUBS):
            lanes = sub_lanes(number, channels)
            for grad_from, field, at in parts:
                normed = (field[0, :, lanes].astype(wide) - mean_rows[at]) * scale_rows[at]
                pulled = grad_from[0, :, lanes].astype(wide) - lead_rows[at]
                pulled = scale_rows[at] * (pulled - normed * slope_rows[at])
                x_ref[at, lanes] = pulled.astype(low_type)
            side = (side_field[0, :, lanes] - side_mean) * side_scale
            pulled = side_scale * (grad[0, :, lanes] - lead_rows[own] - side * side_slope)
            side_grad[0, :, lanes] = pulled.astype(low_type)
            normed = (first[0, :, lanes] - first_mean) * first_scale
            hidden = silu_parts(normed)[0]
            left_ref[lanes, :] = jnp.transpose(hidden).astype(low_type)
        x_ref[2 * EDGE + rows :, :] = jnp.zeros((96, SUBS * channels), low_type)
        fill_windows(x_ref, place, p_ref, rows, channels)
        total = [jnp.zeros((rows, channels), wide) for _ in range(2)]
        for index, pair in enumerate(all_pairs()):
            result = window_conv(p_ref, band, pair, channels)
            for half in range(2):
                number = 2 * index + half
                lanes = sub_lanes(number, channels)
                normed = (first[0, :, lanes] - first_mean) * first_scale
                value = result[:, sub_lanes(half, channels)] * silu_parts(normed)[1]
                first_grad[0, :, lanes] = value
                put_edges(low_pay, high_pay, number, value, channels, rows)
                total = [total[0] + value, total[1] + value * normed]
        for number in range(2):
            value = exact_dot(crop_t[0], total[number])
            put_sums(sums, low_pay, high_pay, number, value, channels)

        @pl.when(pl.program_id(0) == 0)
        def _():
            total_ref[...] = jnp.zeros_like(total_ref)

        add_grads(left_ref, p_ref, total_ref, channels, channels)

        @pl.when(pl.program_id(0) == seqs - 1)
        def _():
            fold_grads(total_ref, weight_grad, channels, channels)

    return body


def first_back_kernel(rows, channels, seqs):
    width = 2 * channels

    def body(
        grad, grad_left, grad_right, own_sums, first, first_left, first_right, stats, inverse, owner,
        place, side_grad, up, skip, band, side_weight,
        up_grad, skip_grad, weight_grad, side_weight_grad,
        x_ref, p_ref, left_ref, total_ref,
    ):
        means = [
            taken_sums(own_sums, grad_left, grad_right, n, channels) * inverse[0] for n in range(2)
        ]
        mean_rows = exact_dot(owner[0], stats[0, :, sub_lanes(0, channels)])
        scale_rows = exact_dot(owner[0], stats[0, :, sub_lanes(1, channels)])
        lead_rows = exact_dot(owner[0], means[0])
        slope_rows = exact_dot(owner[0], means[1])
        parts = (
            (grad_left, first_left, slice(0, EDGE)),
            (grad, first, slice(EDGE, EDGE + rows)),
            (grad_right, first_right, slice(EDGE + rows, 2 * EDGE + rows)),
        )
        for number in range(SUBS):
            lanes = sub_lanes(number, channels)
            for grad_from, field, at in parts:
                normed = (field[0, :, lanes].astype(wide) - mean_rows[at]) * scale_rows[at]
                pulled = grad_from[0, :, lanes].astype(wide) - lead_rows[at]
                pulled = scale_rows[at] * (pulled - normed * slope_rows[at])
                x_ref[at, lanes] = pulled.astype(low_type)
            for half, field in enumerate((up, skip)):
                turned = jnp.transpose(field[0, :, lanes].astype(wide)).astype(low_type)
                left_ref[sub_lanes(2 * number + half, channels), :] = turned
        x_ref[2 * EDGE + rows :, :] = jnp.zeros((96, SUBS * channels), low_type)
        fill_windows(x_ref, place, p_ref, rows, channels)
        for index, pair in enumerate(all_pairs()):
            result = window_conv(p_ref, band, pair, channels)
            for half in range(2):
                number = 2 * index + half
                lanes = sub_lanes(number, channels)
                value = result[:, sub_lanes(half, width)]
                value = value + dot(side_grad[0, :, lanes], side_weight[...])
                up_grad[0, :, lanes] = value[:, :channels].astype(low_type)
                skip_grad[0, :, lanes] = value[:, channels:]

        @pl.when(pl.program_id(0) == 0)
        def _():
            total_ref[...] = jnp.zeros_like(total_ref)
            side_weight_grad[...] = jnp.zeros_like(side_weight_grad)

        for number in range(SUBS):
            side_weight_grad[...] += dot(
                left_ref[sub_lanes(number, width), :], side_grad[0, :, sub_lanes(number, channels)]
            )
        add_grads(left_ref, p_ref, total_ref, width, channels)

        @pl.when(pl.program_id(0) == seqs - 1)
        def _():
            fold_grads(total_ref, weight_grad, width, channels)

    return body


def exchanged(low_pay, high_pay):
    return (passed_along(high_pay, "tok", 1), passed_along(low_pay, "tok", -1))


def with_far(sums, reaches):
    total = sums
    for distance in range(2, reaches + 1):
        for shift_by in (distance, -distance):
            total = total + passed_along(sums.astype(low_type), "tok", shift_by).astype(wide)
    return total


def conv_section(upsampled, skip, cotangent, weights, geometry_in, reaches):
    conv1_weight, conv2_weight, conv3_weight = weights
    seqs, rows, lanes = upsampled.shape
    channels = lanes // SUBS
    width = 2 * channels
    place, owner, crop_t, inverse = geometry_in
    field = ((seqs, rows, lanes), wide)
    low_field = ((seqs, rows, lanes), low_type)

    def pay(count):
        return ((seqs, EDGE, (SUBS + count) * channels), low_type)

    def table(count):
        return ((seqs, CROP_ROWS, count * channels), wide)

    skip_left, skip_right = exchanged(skip[:, :EDGE], skip[:, rows - EDGE :])
    up_left, up_right = exchanged(upsampled[:, :EDGE], upsampled[:, rows - EDGE :])
    first, side_field, sums, low_pay, high_pay = kernel_call(
        first_conv_kernel(rows, channels),
        seqs,
        (upsampled, up_left, up_right, skip, skip_left, skip_right, place, crop_t),
        (forward_band(conv1_weight), conv3_weight),
        (field, field, table(4), pay(4), pay(4)),
        (),
        conv_scratch(rows, width),
        conv_flops(seqs, rows, width, channels),
    )
    first_left, first_right = exchanged(low_pay, high_pay)
    second, stats, sums, low_pay, high_pay = kernel_call(
        second_conv_kernel(rows, channels),
        seqs,
        (first, first_left, first_right, with_far(sums, reaches), inverse, owner, place, crop_t),
        (forward_band(conv2_weight),),
        (field, table(4), table(2), pay(2), pay(2)),
        (),
        conv_scratch(rows, channels),
        conv_flops(seqs, rows, channels, channels),
    )
    second_left, second_right = exchanged(low_pay, high_pay)
    section_out, grad, second_stats, sums, low_pay, high_pay = kernel_call(
        output_kernel(rows, channels),
        seqs,
        (
            second, side_field, cotangent, stats, second_left, second_right,
            with_far(sums, reaches), inverse, owner, crop_t,
        ),
        (),
        (low_field, field, table(2), table(3), pay(3), pay(3)),
        (),
        [],
        seqs * rows * lanes * 20,
    )
    grad_left, grad_right = exchanged(low_pay, high_pay)
    first_grad, side_grad, sums, low_pay, high_pay, conv2_grad = kernel_call(
        second_back_kernel(rows, channels, seqs),
        seqs,
        (
            grad, grad_left, grad_right, with_far(sums, reaches), second, second_left, second_right,
            side_field, first, stats, second_stats, inverse, owner, place, crop_t,
        ),
        (backward_band(conv2_weight),),
        (field, low_field, table(2), pay(2), pay(2)),
        (((27, channels, channels), wide),),
        conv_scratch(rows, channels)
        + [
            pltpu.VMEM((SUBS * channels, rows), low_type),
            pltpu.VMEM((9, 2 * channels, 4 * channels), wide),
        ],
        2 * conv_flops(seqs, rows, channels, channels),
    )
    back_left, back_right = exchanged(low_pay, high_pay)
    up_grad, skip_grad, conv1_grad, conv3_grad = kernel_call(
        first_back_kernel(rows, channels, seqs),
        seqs,
        (
            first_grad, back_left, back_right, with_far(sums, reaches), first, first_left,
            first_right, stats, inverse, owner, place, side_grad, upsampled, skip,
        ),
        (backward_band(conv1_weight), conv3_weight.T),
        (low_field, field),
        (((27, width, channels), wide), ((width, channels), wide)),
        conv_scratch(rows, channels)
        + [
            pltpu.VMEM((SUBS * width, rows), low_type),
            pltpu.VMEM((9, 2 * width, 4 * channels), wide),
        ],
        2 * conv_flops(seqs, rows, channels, width),
    )
    return (section_out, up_grad, skip_grad, conv1_grad, conv2_grad, conv3_grad)


def crop_tables(crop_sides, inside, shape_info, first_row, row_count):
    seqs, crops = crop_sides.shape
    spare = CROP_ROWS - crops
    own = jnp.arange(row_count, dtype=jnp.int32)[None, :] + EDGE
    columns = []
    for offset in all_offsets():
        near_step, far_step = step_sizes(offset)
        step = jnp.where(shape_info[4], far_step, near_step)
        columns.append(jnp.where(in_crop(shape_info, offset), own + step, -1))
    place = jnp.stack(columns, axis=-1).astype(jnp.int32)
    wide_places = first_row - EDGE + jnp.arange(row_count + 2 * EDGE, dtype=jnp.int32)
    wide_places = jnp.broadcast_to(wide_places, (seqs, row_count + 2 * EDGE))
    owner = jnp.pad(locate(crop_sides, wide_places)[0], ((0, 0), (0, 0), (0, spare)))
    crop_t = jnp.pad(inside.swapaxes(1, 2), ((0, 0), (0, spare), (0, 0)))
    counts = jnp.maximum(8.0 * (crop_sides * crop_sides * crop_sides).astype(wide), 1.0)
    inverse = jnp.pad(1.0 / counts, ((0, 0), (0, spare)), constant_values=1.0)
    inverse = jnp.broadcast_to(inverse[:, :, None], (seqs, CROP_ROWS, 128))
    return (place, owner.astype(low_type), crop_t.astype(low_type), inverse)


def local(
    tokens,
    skip_features,
    crop_sides,
    ln1_gain,
    ln1_bias,
    qkv_weight,
    qv_bias,
    out_weight,
    out_bias,
    ln2_gain,
    ln2_bias,
    fc1_weight,
    fc1_bias,
    fc2_weight,
    fc2_bias,
    deconv_weight,
    conv1_weight,
    conv2_weight,
    conv3_weight,
    cotangent,
):
    seq_count, row_count, model_width = tokens.shape
    channels = conv2_weight.shape[2]
    score_scale = 1.0 / math.sqrt(HEAD_DIM)
    first_row = lax.axis_index("tok") * row_count
    places = jnp.broadcast_to(
        first_row + jnp.arange(row_count, dtype=jnp.int32), (seq_count, row_count)
    )
    inside, segment, side_of, first_of = locate(crop_sides, places)
    shape_info = geometry(side_of, first_of, places)
    reaches = (key_reach + row_count - 1) // row_count
    token_values = tokens.astype(jnp.float32)
    normed_low = layer_norm(token_values, ln1_gain, ln1_bias).astype(jnp.bfloat16)
    qkv_bias = jnp.concatenate([qv_bias[0], jnp.zeros_like(qv_bias[0]), qv_bias[1]])
    projected = (
        jnp.einsum("std,de->ste", normed_low, qkv_weight, preferred_element_type=jnp.float32)
        + qkv_bias
    ).astype(jnp.bfloat16)
    queries = projected[:, :, :model_width]
    keys = projected[:, :, model_width : 2 * model_width]
    values = projected[:, :, 2 * model_width :]
    key_parts = [keys]
    value_parts = [values]
    place_parts = [places]
    moves = []
    for distance in range(1, reaches + 1):
        row_take = row_count
        for shift_by in (distance, -distance):
            if shift_by > 0:
                key_send = keys
                value_send = values
                got_first = first_row - (distance - 1) * row_count - row_take
            else:
                key_send = keys
                value_send = values
                got_first = first_row + distance * row_count
            got_keys, got_values = passed_along((key_send, value_send), "tok", shift_by)
            key_parts.append(got_keys)
            value_parts.append(got_values)
            place_parts.append(
                jnp.broadcast_to(
                    got_first + jnp.arange(row_take, dtype=jnp.int32), (seq_count, row_take)
                )
            )
            moves.append((shift_by, row_take))
    window_keys = jnp.concatenate(key_parts, axis=1).reshape(seq_count, -1, HEADS, HEAD_DIM)
    window_values = jnp.concatenate(value_parts, axis=1).reshape(seq_count, -1, HEADS, HEAD_DIM)
    key_crop = locate(crop_sides, jnp.concatenate(place_parts, axis=1))[1]
    same_crop = segment[:, None, :, None] == key_crop[:, None, None, :]
    query_heads = queries.reshape(seq_count, row_count, HEADS, HEAD_DIM)
    scores = crop_scores(query_heads, window_keys, same_crop)
    row_max = jnp.max(scores, axis=-1, keepdims=True)
    weights = jnp.exp(scores - row_max)
    totals = jnp.sum(weights, axis=-1, keepdims=True)
    log_total = row_max + jnp.log(totals)
    probs_low = (weights / totals).astype(jnp.bfloat16)
    attended = jnp.einsum(
        "shqk,skhd->sqhd", probs_low, window_values, preferred_element_type=jnp.float32
    )
    attended = attended.astype(jnp.bfloat16).reshape(seq_count, row_count, model_width)
    resid_one = (
        token_values
        + jnp.einsum("std,de->ste", attended, out_weight, preferred_element_type=jnp.float32)
        + out_bias
    )
    normed_two = layer_norm(resid_one, ln2_gain, ln2_bias).astype(jnp.bfloat16)
    pre_act = (
        jnp.einsum("std,df->stf", normed_two, fc1_weight, preferred_element_type=jnp.float32)
        + fc1_bias
    )
    act_low = jax.nn.gelu(pre_act, approximate=False).astype(jnp.bfloat16)
    resid_two = (
        resid_one
        + jnp.einsum("stf,fd->std", act_low, fc2_weight, preferred_element_type=jnp.float32)
        + fc2_bias
    )
    resid_low = resid_two.astype(jnp.bfloat16)
    upsampled = jnp.einsum(
        "std,de->ste", resid_low, deconv_weight, preferred_element_type=jnp.float32
    )
    upsampled = upsampled.astype(jnp.bfloat16)
    geometry_in = crop_tables(crop_sides, inside, shape_info, first_row, row_count)
    section_out, up_grad, skip_grad, conv1_grad, conv2_grad, conv3_grad = conv_section(
        upsampled,
        skip_features.reshape(seq_count, row_count, 8 * channels),
        cotangent.reshape(seq_count, row_count, 8 * channels),
        (conv1_weight, conv2_weight, conv3_weight),
        geometry_in,
        reaches,
    )
    section_out = section_out.reshape(seq_count, row_count, 8, channels)
    skip_grad = skip_grad.reshape(seq_count, row_count, 8, channels)
    deconv_grad = jnp.einsum("std,ste->de", resid_low, up_grad, preferred_element_type=jnp.float32)
    resid_two_grad = jnp.einsum(
        "ste,de->std", up_grad, deconv_weight, preferred_element_type=jnp.float32
    )
    branch_low = resid_two_grad.astype(jnp.bfloat16)
    fc2_bias_grad = jnp.sum(branch_low.astype(jnp.float32), axis=(0, 1))
    fc2_grad = jnp.einsum("stf,std->fd", act_low, branch_low, preferred_element_type=jnp.float32)
    act_grad = jnp.einsum("std,fd->stf", branch_low, fc2_weight, preferred_element_type=jnp.float32)
    gelu_pull = jax.vjp(partial(jax.nn.gelu, approximate=False), pre_act)[1]
    pre_low = gelu_pull(act_grad)[0].astype(jnp.bfloat16)
    fc1_bias_grad = jnp.sum(pre_low.astype(jnp.float32), axis=(0, 1))
    fc1_grad = jnp.einsum("std,stf->df", normed_two, pre_low, preferred_element_type=jnp.float32)
    normed_two_grad = jnp.einsum(
        "stf,df->std", pre_low, fc1_weight, preferred_element_type=jnp.float32
    )
    second_ln_pull = jax.vjp(layer_norm, resid_one, ln2_gain, ln2_bias)[1]
    resid_part, ln2_gain_grad, ln2_bias_grad = second_ln_pull(normed_two_grad)
    resid_one_grad = resid_two_grad + resid_part
    mixed_low = resid_one_grad.astype(jnp.bfloat16)
    out_bias_grad = jnp.sum(mixed_low.astype(jnp.float32), axis=(0, 1))
    out_grad = jnp.einsum("std,ste->de", attended, mixed_low, preferred_element_type=jnp.float32)
    attended_grad = jnp.einsum(
        "ste,de->std", mixed_low, out_weight, preferred_element_type=jnp.float32
    )
    attended_grad = attended_grad.astype(jnp.bfloat16).reshape(
        seq_count, row_count, HEADS, HEAD_DIM
    )
    scores_again = crop_scores(query_heads, window_keys, same_crop)
    attn_probs = jnp.exp(scores_again - log_total)
    probs_again = attn_probs.astype(jnp.bfloat16)
    probs_grad = jnp.einsum(
        "sqhd,skhd->shqk", attended_grad, window_values, preferred_element_type=jnp.float32
    )
    row_inner = jnp.sum(attn_probs * probs_grad, axis=-1, keepdims=True)
    score_low = (attn_probs * (probs_grad - row_inner)).astype(jnp.bfloat16)
    query_grad = (
        jnp.einsum("shqk,skhd->sqhd", score_low, window_keys, preferred_element_type=jnp.float32)
        * score_scale
    )
    key_grad = (
        jnp.einsum("shqk,sqhd->skhd", score_low, query_heads, preferred_element_type=jnp.float32)
        * score_scale
    )
    value_grad = jnp.einsum(
        "shqk,sqhd->skhd", probs_again, attended_grad, preferred_element_type=jnp.float32
    )
    key_grad = key_grad.reshape(seq_count, -1, model_width)
    value_grad = value_grad.reshape(seq_count, -1, model_width)
    key_own = key_grad[:, :row_count]
    value_own = value_grad[:, :row_count]
    cursor = row_count
    for shift_by, row_take in moves:
        key_piece = key_grad[:, cursor : cursor + row_take]
        value_piece = value_grad[:, cursor : cursor + row_take]
        cursor = cursor + row_take
        back_keys, back_values = (
            passed_along(key_piece.astype(jnp.bfloat16), "tok", -shift_by).astype(key_piece.dtype),
            passed_along(value_piece.astype(jnp.bfloat16), "tok", -shift_by).astype(
                value_piece.dtype
            ),
        )
        if shift_by > 0:
            key_own = key_own.at[:, row_count - row_take :].add(back_keys)
            value_own = value_own.at[:, row_count - row_take :].add(back_values)
        else:
            key_own = key_own.at[:, :row_take].add(back_keys)
            value_own = value_own.at[:, :row_take].add(back_values)
    qkv_grad_low = jnp.concatenate(
        [query_grad.reshape(seq_count, row_count, model_width), key_own, value_own], axis=-1
    ).astype(jnp.bfloat16)
    qkv_grad = jnp.einsum(
        "std,ste->de", normed_low, qkv_grad_low, preferred_element_type=jnp.float32
    )
    column_sums = jnp.sum(qkv_grad_low.astype(jnp.float32), axis=(0, 1))
    qv_bias_grad = jnp.stack([column_sums[:model_width], column_sums[2 * model_width :]])
    normed_one_grad = jnp.einsum(
        "ste,de->std", qkv_grad_low, qkv_weight, preferred_element_type=jnp.float32
    )
    first_ln_pull = jax.vjp(layer_norm, token_values, ln1_gain, ln1_bias)[1]
    token_part, ln1_gain_grad, ln1_bias_grad = first_ln_pull(normed_one_grad)
    token_grad = resid_one_grad + token_part
    weight_shares = (
        lax.psum_scatter(
            ln1_gain_grad.astype(jnp.bfloat16), "tok", scatter_dimension=0, tiled=True
        ).astype(jnp.float32),
        lax.psum_scatter(
            ln1_bias_grad.astype(jnp.bfloat16), "tok", scatter_dimension=0, tiled=True
        ).astype(jnp.float32),
        lax.psum_scatter(
            qkv_grad.astype(jnp.bfloat16), "tok", scatter_dimension=0, tiled=True
        ).astype(jnp.float32),
        lax.psum_scatter(
            qv_bias_grad.astype(jnp.bfloat16), "tok", scatter_dimension=1, tiled=True
        ).astype(jnp.float32),
        lax.psum_scatter(
            out_grad.astype(jnp.bfloat16), "tok", scatter_dimension=0, tiled=True
        ).astype(jnp.float32),
        lax.psum_scatter(
            out_bias_grad.astype(jnp.bfloat16), "tok", scatter_dimension=0, tiled=True
        ).astype(jnp.float32),
        lax.psum_scatter(
            ln2_gain_grad.astype(jnp.bfloat16), "tok", scatter_dimension=0, tiled=True
        ).astype(jnp.float32),
        lax.psum_scatter(
            ln2_bias_grad.astype(jnp.bfloat16), "tok", scatter_dimension=0, tiled=True
        ).astype(jnp.float32),
        lax.psum_scatter(
            fc1_grad.astype(jnp.bfloat16), "tok", scatter_dimension=0, tiled=True
        ).astype(jnp.float32),
        lax.psum_scatter(
            fc1_bias_grad.astype(jnp.bfloat16), "tok", scatter_dimension=0, tiled=True
        ).astype(jnp.float32),
        lax.psum_scatter(
            fc2_grad.astype(jnp.bfloat16), "tok", scatter_dimension=0, tiled=True
        ).astype(jnp.float32),
        lax.psum_scatter(
            fc2_bias_grad.astype(jnp.bfloat16), "tok", scatter_dimension=0, tiled=True
        ).astype(jnp.float32),
        lax.psum_scatter(
            deconv_grad.astype(jnp.bfloat16), "tok", scatter_dimension=0, tiled=True
        ).astype(jnp.float32),
        lax.psum_scatter(
            conv1_grad.astype(jnp.bfloat16), "tok", scatter_dimension=2, tiled=True
        ).astype(jnp.float32),
        lax.psum_scatter(
            conv2_grad.astype(jnp.bfloat16), "tok", scatter_dimension=2, tiled=True
        ).astype(jnp.float32),
        lax.psum_scatter(
            conv3_grad.astype(jnp.bfloat16), "tok", scatter_dimension=1, tiled=True
        ).astype(jnp.float32),
    )
    finished = (
        lax.psum(weight_shares[0].astype(jnp.bfloat16), "seq").astype(jnp.float32),
        lax.psum(weight_shares[1].astype(jnp.bfloat16), "seq").astype(jnp.float32),
        lax.psum(weight_shares[2].astype(jnp.bfloat16), "seq").astype(jnp.float32),
        lax.psum(weight_shares[3].astype(jnp.bfloat16), "seq").astype(jnp.float32),
        lax.psum(weight_shares[4].astype(jnp.bfloat16), "seq").astype(jnp.float32),
        lax.psum(weight_shares[5].astype(jnp.bfloat16), "seq").astype(jnp.float32),
        lax.psum(weight_shares[6].astype(jnp.bfloat16), "seq").astype(jnp.float32),
        lax.psum(weight_shares[7].astype(jnp.bfloat16), "seq").astype(jnp.float32),
        lax.psum(weight_shares[8].astype(jnp.bfloat16), "seq").astype(jnp.float32),
        lax.psum(weight_shares[9].astype(jnp.bfloat16), "seq").astype(jnp.float32),
        lax.psum(weight_shares[10].astype(jnp.bfloat16), "seq").astype(jnp.float32),
        lax.psum(weight_shares[11].astype(jnp.bfloat16), "seq").astype(jnp.float32),
        lax.psum(weight_shares[12].astype(jnp.bfloat16), "seq").astype(jnp.float32),
        lax.psum(weight_shares[13].astype(jnp.bfloat16), "seq").astype(jnp.float32),
        lax.psum(weight_shares[14].astype(jnp.bfloat16), "seq").astype(jnp.float32),
        lax.psum(weight_shares[15].astype(jnp.bfloat16), "seq").astype(jnp.float32),
    )
    return (
        section_out,
        token_grad,
        skip_grad,
        finished[0],
        finished[1],
        finished[2],
        finished[3],
        finished[4],
        finished[5],
        finished[6],
        finished[7],
        finished[8],
        finished[9],
        finished[10],
        finished[11],
        finished[12],
        finished[13],
        finished[14],
        finished[15],
    )


def solution(mesh):
    in_specs = (
        P("seq", "tok", None),
        P("seq", "tok", None, None),
        P("seq", None),
        P(),
        P(),
        P(),
        P(),
        P(),
        P(),
        P(),
        P(),
        P(),
        P(),
        P(),
        P(),
        P(),
        P(),
        P(),
        P(),
        P("seq", "tok", None, None),
    )
    out_specs = (
        P("seq", "tok", None, None),
        P("seq", "tok", None),
        P("seq", "tok", None, None),
        P("tok"),
        P("tok"),
        P("tok", None),
        P(None, "tok"),
        P("tok", None),
        P("tok"),
        P("tok"),
        P("tok"),
        P("tok", None),
        P("tok"),
        P("tok", None),
        P("tok"),
        P("tok", None),
        P(None, None, "tok"),
        P(None, None, "tok"),
        P(None, "tok"),
    )
    return jax.shard_map(local, mesh=mesh, in_specs=in_specs, out_specs=out_specs, check_vma=False)
```

```python
from functools import partial
import math

import jax
import jax.numpy as jnp
import numpy as np
from jax import lax
from jax.experimental import pallas as pl
from jax.experimental.pallas import tpu as pltpu
from jax.sharding import PartitionSpec as P

HEADS = 12
HEAD_DIM = 64


side_small = 4
side_big = 6
halo_rows = 43
key_reach = 215
norm_eps = 1e-05
far_below = -1e30
highest = lax.Precision.HIGHEST
in_part = {-1: (1, 2), 0: (0, 2), 1: (0, 1)}
out_part = {-1: (0, 1), 0: (0, 2), 1: (1, 2)}


def passed_along(block, axis, distance):
    devices = range(lax.axis_size(axis))
    route = [(i - distance, i) for i in devices if i - distance in devices]
    return lax.ppermute(block, axis, route)


def all_offsets():
    step_values = (-1, 0, 1)
    return [
        (step_x, step_y, step_z)
        for step_x in step_values
        for step_y in step_values
        for step_z in step_values
    ]


def crop_bounds(sides):
    volumes = sides * sides * sides
    ends_at = jnp.cumsum(volumes, axis=-1, dtype=jnp.int32)
    return (ends_at - volumes, ends_at)


def locate(sides, places):
    starts, ends_at = crop_bounds(sides)
    inside = (places[:, :, None] >= starts[:, None, :]) & (places[:, :, None] < ends_at[:, None, :])
    numbers = jnp.arange(sides.shape[-1], dtype=jnp.int32)
    found = jnp.any(inside, axis=-1)
    segment = jnp.sum(jnp.where(inside, numbers, 0), axis=-1, dtype=jnp.int32)
    segment = jnp.where(found, segment, -1)
    side_of = jnp.sum(jnp.where(inside, sides[:, None, :], 0), axis=-1, dtype=jnp.int32)
    first_of = jnp.sum(jnp.where(inside, starts[:, None, :], 0), axis=-1, dtype=jnp.int32)
    return (inside, segment, side_of, first_of)


def geometry(side_of, first_of, places):
    local_pos = places - first_of
    safe_side = jnp.maximum(side_of, 1)
    return (
        local_pos // (safe_side * safe_side),
        local_pos // safe_side % safe_side,
        local_pos % safe_side,
        side_of,
        side_of == side_big,
    )


def step_sizes(offset):
    near_step = offset[0] * side_small * side_small + offset[1] * side_small + offset[2]
    far_step = offset[0] * side_big * side_big + offset[1] * side_big + offset[2]
    return (near_step, far_step)


def in_crop(shape_info, offset):
    row_pos, column, depth_pos, side_of, is_big = shape_info
    inside_crop = (row_pos + offset[0] >= 0) & (row_pos + offset[0] < side_of)
    inside_crop = inside_crop & (column + offset[1] >= 0) & (column + offset[1] < side_of)
    return inside_crop & (depth_pos + offset[2] >= 0) & (depth_pos + offset[2] < side_of)


def layer_norm(values_in, gain, shift):
    centered = values_in - jnp.mean(values_in, axis=-1, keepdims=True)
    variance = jnp.mean(centered * centered, axis=-1, keepdims=True)
    return centered * lax.rsqrt(variance + norm_eps) * gain + shift


def crop_scores(query_heads, key_heads, same_crop):
    raw_scores = jnp.einsum(
        "sqhd,skhd->shqk", query_heads, key_heads, preferred_element_type=jnp.float32
    )
    return jnp.where(same_crop, raw_scores * (1.0 / math.sqrt(HEAD_DIM)), far_below)


EDGE = 48
WINDOW = 256
TILE = 128
CROP_ROWS = 48
SUBS = 8
VMEM_LIMIT = 60 * 1024 * 1024
lowest_step = {-1: -43, 0: -7, 1: 11}
low_type = jnp.bfloat16
wide = jnp.float32


def dot(left, right):
    return jnp.dot(left, right, preferred_element_type=wide)


def three_terms(field):
    first = field.astype(low_type)
    rest = field - first.astype(wide)
    second = rest.astype(low_type)
    third = (rest - second.astype(wide)).astype(low_type)
    return (first, second, third)


def exact_dot(chosen, field):
    first, second, third = three_terms(field)
    return dot(chosen, first) + dot(chosen, second) + dot(chosen, third)


def sub_lanes(number, width):
    return slice(number * width, (number + 1) * width)


def banded(taps):
    begin = jnp.pad(taps, ((0, 0), (0, 0), (0, 1), (0, 0), (0, 0)))
    later = jnp.pad(taps, ((0, 0), (0, 0), (1, 0), (0, 0), (0, 0)))
    both = jnp.concatenate([begin, later], axis=-1)
    return both.reshape(3, 12 * taps.shape[3], 2 * taps.shape[4])


def forward_band(weight):
    return banded(weight.reshape((3, 3, 3) + weight.shape[1:]))


def backward_band(weight):
    taps = weight.reshape((3, 3, 3) + weight.shape[1:])
    return banded(taps[::-1, ::-1, ::-1].swapaxes(3, 4))


def window_positions(step):
    return {-1: ((0, 1),), 0: ((1, 0), (2, 1)), 1: ((3, 0),)}[step]


def fill_windows(x_ref, place_ref, p_ref, rows, width):
    tile = min(rows, TILE)
    for base in range(0, rows, tile):
        own = slice(base, base + tile)
        for number, (step_x, step_y, step_z) in enumerate(all_offsets()):
            low = (EDGE + base + lowest_step[step_x]) // 16 * 16
            centre = (step_x, step_y, step_z) == (0, 0, 0)
            if not centre:
                lane = lax.broadcasted_iota(jnp.int32, (tile, WINDOW), 1) + low
                chosen = jnp.where(lane == place_ref[0, own, number : number + 1], 1.0, 0.0)
                chosen = chosen.astype(low_type)
            for x_to, x_from in window_positions(step_x):
                for y_to, y_from in window_positions(step_y):
                    z_to, z_from = window_positions(step_z)[0]
                    count = (2 if step_z == 0 else 1) * width
                    to = ((x_to * 4 + y_to) * 4 + z_to) * width
                    source = (x_from * 4 + y_from * 2 + z_from) * width
                    if centre:
                        got = x_ref[EDGE + base : EDGE + base + tile, source : source + count]
                    else:
                        got = dot(chosen, x_ref[low : low + WINDOW, source : source + count])
                    p_ref[own, to : to + count] = got.astype(low_type)


def window_conv(p_ref, band_ref, pair, width):
    first, second = pair
    total = None
    for tap in range(3):
        begin = ((first + tap) * 4 + second) * 4 * width
        term = dot(p_ref[:, begin : begin + 12 * width], band_ref[tap])
        total = term if total is None else total + term
    return total


def all_pairs():
    return [(first, second) for first in range(2) for second in range(2)]


def add_grads(left_ref, p_ref, total_ref, width, channels):
    for tap_x in range(3):
        for tap_y in range(3):
            term = None
            for number, (first, second) in enumerate(all_pairs()):
                begin = ((first + tap_x) * 4 + second + tap_y) * 4 * channels
                left = left_ref[number * 2 * width : (number + 1) * 2 * width, :]
                part = dot(left, p_ref[:, begin : begin + 4 * channels])
                term = part if term is None else term + part
            total_ref[tap_x * 3 + tap_y] += term


def fold_grads(total_ref, grad_ref, width, channels):
    for tap_x in range(3):
        for tap_y in range(3):
            for tap_z in range(3):
                number = tap_x * 3 + tap_y
                here = total_ref[number, :width, sub_lanes(tap_z, channels)]
                there = total_ref[number, width:, sub_lanes(tap_z + 1, channels)]
                tap = 26 - (number * 3 + tap_z)
                for half in range(width // channels):
                    rows = slice(half * channels, (half + 1) * channels)
                    grad_ref[tap, half] = jnp.transpose(here[rows] + there[rows])


def kernel_call(body, seqs, inputs, shared, outputs, summed, scratch, flops):
    def row_spec(shape):
        return pl.BlockSpec((1,) + tuple(shape[1:]), lambda i: (i,) + (0,) * (len(shape) - 1))

    def whole_spec(shape):
        return pl.BlockSpec(tuple(shape), lambda i: (0,) * len(shape))

    moved = sum(math.prod(a.shape) * a.dtype.itemsize for a in list(inputs) + list(shared))
    moved += sum(math.prod(s) * jnp.dtype(t).itemsize for s, t in list(outputs) + list(summed))
    return pl.pallas_call(
        body,
        grid=(seqs,),
        in_specs=[row_spec(a.shape) for a in inputs] + [whole_spec(a.shape) for a in shared],
        out_specs=[row_spec(s) for s, _ in outputs] + [whole_spec(s) for s, _ in summed],
        out_shape=[jax.ShapeDtypeStruct(s, t) for s, t in list(outputs) + list(summed)],
        scratch_shapes=scratch,
        compiler_params=pltpu.CompilerParams(vmem_limit_bytes=VMEM_LIMIT),
        cost_estimate=pl.CostEstimate(flops=flops, bytes_accessed=moved, transcendentals=0),
    )(*inputs, *shared)


def conv_scratch(rows, width):
    return [
        pltpu.VMEM((rows + 192, SUBS * width), low_type),
        pltpu.VMEM((rows, 64 * width), low_type),
    ]


def conv_flops(seqs, rows, inner, outer):
    return 2 * seqs * rows * (36 * 4 * inner * 2 * outer + 56 * WINDOW * inner)


def put_edges(low_pay, high_pay, number, field, channels, rows):
    lanes = sub_lanes(number, channels)
    low_pay[0, :, lanes] = field[:EDGE].astype(low_type)
    high_pay[0, :, lanes] = field[rows - EDGE :].astype(low_type)


def put_sums(sums_ref, low_pay, high_pay, number, value, channels):
    lanes = sub_lanes(number, channels)
    sums_ref[0, :, lanes] = value
    pay_lanes = sub_lanes(SUBS + number, channels)
    low_pay[0, :, pay_lanes] = value.astype(low_type)
    high_pay[0, :, pay_lanes] = value.astype(low_type)


def taken_sums(sums_ref, left_pay, right_pay, number, channels):
    lanes = sub_lanes(number, channels)
    pay_lanes = sub_lanes(SUBS + number, channels)
    total = sums_ref[0, :, lanes] + left_pay[0, :, pay_lanes].astype(wide)
    return total + right_pay[0, :, pay_lanes].astype(wide)


def mean_and_scale(total, square, inverse):
    mean = total * inverse
    variance = jnp.maximum(square * inverse - mean * mean, 0.0)
    return (mean, lax.rsqrt(variance + norm_eps))


def silu_parts(value):
    gate = 1.0 / (1.0 + jnp.exp(-value))
    return (value * gate, gate * (1.0 + value * (1.0 - gate)))


def first_conv_kernel(rows, channels):
    width = 2 * channels

    def body(
        up, up_left, up_right, skip, skip_left, skip_right, place, crop_t, band, side,
        first_out, side_out, sums, low_pay, high_pay, x_ref, p_ref,
    ):
        for number in range(SUBS):
            for half, (own, left, right) in enumerate(
                ((up, up_left, up_right), (skip, skip_left, skip_right))
            ):
                to = sub_lanes(2 * number + half, channels)
                lanes = sub_lanes(number, channels)
                x_ref[:EDGE, to] = left[0, :, lanes]
                x_ref[EDGE : EDGE + rows, to] = own[0, :, lanes]
                x_ref[EDGE + rows : 2 * EDGE + rows, to] = right[0, :, lanes]
        x_ref[2 * EDGE + rows :, :] = jnp.zeros((96, SUBS * width), low_type)
        fill_windows(x_ref, place, p_ref, rows, width)
        total = [jnp.zeros((rows, channels), wide) for _ in range(4)]
        for index, pair in enumerate(all_pairs()):
            result = window_conv(p_ref, band, pair, width)
            first_out[0, :, sub_lanes(index, width)] = result
            for half in range(2):
                number = 2 * index + half
                value = result[:, sub_lanes(half, channels)]
                put_edges(low_pay, high_pay, number, value, channels, rows)
                flat = dot(x_ref[EDGE : EDGE + rows, sub_lanes(number, width)], side[...])
                side_out[0, :, sub_lanes(number, channels)] = flat
                terms = (value, value * value, flat, flat * flat)
                total = [have + term for have, term in zip(total, terms)]
        for number in range(4):
            value = exact_dot(crop_t[0], total[number])
            put_sums(sums, low_pay, high_pay, number, value, channels)

    return body


def second_conv_kernel(rows, channels):
    def body(
        first, left_pay, right_pay, own_sums, inverse, owner, place, crop_t, band,
        second_out, stats, sums, low_pay, high_pay, x_ref, p_ref,
    ):
        taken = [taken_sums(own_sums, left_pay, right_pay, n, channels) for n in range(4)]
        mean, scale = mean_and_scale(taken[0], taken[1], inverse[0])
        side_mean, side_scale = mean_and_scale(taken[2], taken[3], inverse[0])
        for number, value in enumerate((mean, scale, side_mean, side_scale)):
            stats[0, :, sub_lanes(number, channels)] = value
        mean_rows = exact_dot(owner[0], mean)
        scale_rows = exact_dot(owner[0], scale)
        parts = (
            (left_pay, slice(0, EDGE)),
            (first, slice(EDGE, EDGE + rows)),
            (right_pay, slice(EDGE + rows, 2 * EDGE + rows)),
        )
        for number in range(SUBS):
            lanes = sub_lanes(number, channels)
            for field, place_rows in parts:
                normed = field[0, :, lanes].astype(wide) - mean_rows[place_rows]
                normed = normed * scale_rows[place_rows]
                x_ref[place_rows, lanes] = silu_parts(normed)[0].astype(low_type)
        x_ref[2 * EDGE + rows :, :] = jnp.zeros((96, SUBS * channels), low_type)
        fill_windows(x_ref, place, p_ref, rows, channels)
        total = [jnp.zeros((rows, channels), wide) for _ in range(2)]
        for index, pair in enumerate(all_pairs()):
            result = window_conv(p_ref, band, pair, channels)
            second_out[0, :, sub_lanes(index, 2 * channels)] = result
            for half in range(2):
                value = result[:, sub_lanes(half, channels)]
                put_edges(low_pay, high_pay, 2 * index + half, value, channels, rows)
                total = [total[0] + value, total[1] + value * value]
        for number in range(2):
            value = exact_dot(crop_t[0], total[number])
            put_sums(sums, low_pay, high_pay, number, value, channels)

    return body


def output_kernel(rows, channels):
    def body(
        second, side_field, cotangent, stats, left_pay, right_pay, own_sums, inverse, owner, crop_t,
        section, grad_out, second_stats, sums, low_pay, high_pay,
    ):
        taken = [taken_sums(own_sums, left_pay, right_pay, n, channels) for n in range(2)]
        mean, scale = mean_and_scale(taken[0], taken[1], inverse[0])
        second_stats[0, :, sub_lanes(0, channels)] = mean
        second_stats[0, :, sub_lanes(1, channels)] = scale
        own = owner[0, EDGE : EDGE + rows, :]
        mean_rows = exact_dot(own, mean)
        scale_rows = exact_dot(own, scale)
        side_mean = exact_dot(own, stats[0, :, sub_lanes(2, channels)])
        side_scale = exact_dot(own, stats[0, :, sub_lanes(3, channels)])
        total = [jnp.zeros((rows, channels), wide) for _ in range(3)]
        for number in range(SUBS):
            lanes = sub_lanes(number, channels)
            normed = (second[0, :, lanes] - mean_rows) * scale_rows
            side = (side_field[0, :, lanes] - side_mean) * side_scale
            value, slope = silu_parts(normed + side)
            section[0, :, lanes] = value.astype(low_type)
            grad = cotangent[0, :, lanes].astype(wide) * slope
            grad_out[0, :, lanes] = grad
            put_edges(low_pay, high_pay, number, grad, channels, rows)
            terms = (grad, grad * normed, grad * side)
            total = [have + term for have, term in zip(total, terms)]
        for number in range(3):
            value = exact_dot(crop_t[0], total[number])
            put_sums(sums, low_pay, high_pay, number, value, channels)

    return body


def second_back_kernel(rows, channels, seqs):
    def body(
        grad, grad_left, grad_right, own_sums, second, second_left, second_right, side_field, first,
        stats, second_stats, inverse, owner, place, crop_t, band,
        first_grad, side_grad, sums, low_pay, high_pay, weight_grad,
        x_ref, p_ref, left_ref, total_ref,
    ):
        means = [
            taken_sums(own_sums, grad_left, grad_right, n, channels) * inverse[0] for n in range(3)
        ]
        mean_rows = exact_dot(owner[0], second_stats[0, :, sub_lanes(0, channels)])
        scale_rows = exact_dot(owner[0], second_stats[0, :, sub_lanes(1, channels)])
        lead_rows = exact_dot(owner[0], means[0])
        slope_rows = exact_dot(owner[0], means[1])
        parts = (
            (grad_left, second_left, slice(0, EDGE)),
            (grad, second, slice(EDGE, EDGE + rows)),
            (grad_right, second_right, slice(EDGE + rows, 2 * EDGE + rows)),
        )
        own = slice(EDGE, EDGE + rows)
        side_mean = exact_dot(owner[0, own, :], stats[0, :, sub_lanes(2, channels)])
        side_scale = exact_dot(owner[0, own, :], stats[0, :, sub_lanes(3, channels)])
        side_slope = exact_dot(owner[0, own, :], means[2])
        first_mean = exact_dot(owner[0, own, :], stats[0, :, sub_lanes(0, channels)])
        first_scale = exact_dot(owner[0, own, :], stats[0, :, sub_lanes(1, channels)])
        for number in range(SUBS):
            lanes = sub_lanes(number, channels)
            for grad_from, field, at in parts:
                normed = (field[0, :, lanes].astype(wide) - mean_rows[at]) * scale_rows[at]
                pulled = grad_from[0, :, lanes].astype(wide) - lead_rows[at]
                pulled = scale_rows[at] * (pulled - normed * slope_rows[at])
                x_ref[at, lanes] = pulled.astype(low_type)
            side = (side_field[0, :, lanes] - side_mean) * side_scale
            pulled = side_scale * (grad[0, :, lanes] - lead_rows[own] - side * side_slope)
            side_grad[0, :, lanes] = pulled.astype(low_type)
            normed = (first[0, :, lanes] - first_mean) * first_scale
            hidden = silu_parts(normed)[0]
            left_ref[lanes, :] = jnp.transpose(hidden).astype(low_type)
        x_ref[2 * EDGE + rows :, :] = jnp.zeros((96, SUBS * channels), low_type)
        fill_windows(x_ref, place, p_ref, rows, channels)
        total = [jnp.zeros((rows, channels), wide) for _ in range(2)]
        for index, pair in enumerate(all_pairs()):
            result = window_conv(p_ref, band, pair, channels)
            for half in range(2):
                number = 2 * index + half
                lanes = sub_lanes(number, channels)
                normed = (first[0, :, lanes] - first_mean) * first_scale
                value = result[:, sub_lanes(half, channels)] * silu_parts(normed)[1]
                first_grad[0, :, lanes] = value
                put_edges(low_pay, high_pay, number, value, channels, rows)
                total = [total[0] + value, total[1] + value * normed]
        for number in range(2):
            value = exact_dot(crop_t[0], total[number])
            put_sums(sums, low_pay, high_pay, number, value, channels)

        @pl.when(pl.program_id(0) == 0)
        def _():
            total_ref[...] = jnp.zeros_like(total_ref)

        add_grads(left_ref, p_ref, total_ref, channels, channels)

        @pl.when(pl.program_id(0) == seqs - 1)
        def _():
            fold_grads(total_ref, weight_grad, channels, channels)

    return body


def first_back_kernel(rows, channels, seqs):
    width = 2 * channels

    def body(
        grad, grad_left, grad_right, own_sums, first, first_left, first_right, stats, inverse, owner,
        place, side_grad, up, skip, band, side_weight,
        up_grad, skip_grad, weight_grad, side_weight_grad,
        x_ref, p_ref, left_ref, total_ref,
    ):
        means = [
            taken_sums(own_sums, grad_left, grad_right, n, channels) * inverse[0] for n in range(2)
        ]
        mean_rows = exact_dot(owner[0], stats[0, :, sub_lanes(0, channels)])
        scale_rows = exact_dot(owner[0], stats[0, :, sub_lanes(1, channels)])
        lead_rows = exact_dot(owner[0], means[0])
        slope_rows = exact_dot(owner[0], means[1])
        parts = (
            (grad_left, first_left, slice(0, EDGE)),
            (grad, first, slice(EDGE, EDGE + rows)),
            (grad_right, first_right, slice(EDGE + rows, 2 * EDGE + rows)),
        )
        for number in range(SUBS):
            lanes = sub_lanes(number, channels)
            for grad_from, field, at in parts:
                normed = (field[0, :, lanes].astype(wide) - mean_rows[at]) * scale_rows[at]
                pulled = grad_from[0, :, lanes].astype(wide) - lead_rows[at]
                pulled = scale_rows[at] * (pulled - normed * slope_rows[at])
                x_ref[at, lanes] = pulled.astype(low_type)
            for half, field in enumerate((up, skip)):
                turned = jnp.transpose(field[0, :, lanes].astype(wide)).astype(low_type)
                left_ref[sub_lanes(2 * number + half, channels), :] = turned
        x_ref[2 * EDGE + rows :, :] = jnp.zeros((96, SUBS * channels), low_type)
        fill_windows(x_ref, place, p_ref, rows, channels)
        for index, pair in enumerate(all_pairs()):
            result = window_conv(p_ref, band, pair, channels)
            for half in range(2):
                number = 2 * index + half
                lanes = sub_lanes(number, channels)
                value = result[:, sub_lanes(half, width)]
                value = value + dot(side_grad[0, :, lanes], side_weight[...])
                up_grad[0, :, lanes] = value[:, :channels].astype(low_type)
                skip_grad[0, :, lanes] = value[:, channels:]

        @pl.when(pl.program_id(0) == 0)
        def _():
            total_ref[...] = jnp.zeros_like(total_ref)
            side_weight_grad[...] = jnp.zeros_like(side_weight_grad)

        for number in range(SUBS):
            side_weight_grad[...] += dot(
                left_ref[sub_lanes(number, width), :], side_grad[0, :, sub_lanes(number, channels)]
            )
        add_grads(left_ref, p_ref, total_ref, width, channels)

        @pl.when(pl.program_id(0) == seqs - 1)
        def _():
            fold_grads(total_ref, weight_grad, width, channels)

    return body


def exchanged(low_pay, high_pay):
    return (passed_along(high_pay, "tok", 1), passed_along(low_pay, "tok", -1))


def with_far(sums, reaches):
    total = sums
    for distance in range(2, reaches + 1):
        for shift_by in (distance, -distance):
            total = total + passed_along(sums.astype(low_type), "tok", shift_by).astype(wide)
    return total


def conv_section(upsampled, skip, cotangent, weights, geometry_in, reaches):
    conv1_weight, conv2_weight, conv3_weight = weights
    seqs, rows, lanes = upsampled.shape
    channels = lanes // SUBS
    width = 2 * channels
    place, owner, crop_t, inverse = geometry_in
    field = ((seqs, rows, lanes), wide)
    low_field = ((seqs, rows, lanes), low_type)

    def pay(count):
        return ((seqs, EDGE, (SUBS + count) * channels), low_type)

    def table(count):
        return ((seqs, CROP_ROWS, count * channels), wide)

    skip_left, skip_right = exchanged(skip[:, :EDGE], skip[:, rows - EDGE :])
    up_left, up_right = exchanged(upsampled[:, :EDGE], upsampled[:, rows - EDGE :])
    first, side_field, sums, low_pay, high_pay = kernel_call(
        first_conv_kernel(rows, channels),
        seqs,
        (upsampled, up_left, up_right, skip, skip_left, skip_right, place, crop_t),
        (forward_band(conv1_weight), conv3_weight),
        (field, field, table(4), pay(4), pay(4)),
        (),
        conv_scratch(rows, width),
        conv_flops(seqs, rows, width, channels),
    )
    first_left, first_right = exchanged(low_pay, high_pay)
    second, stats, sums, low_pay, high_pay = kernel_call(
        second_conv_kernel(rows, channels),
        seqs,
        (first, first_left, first_right, with_far(sums, reaches), inverse, owner, place, crop_t),
        (forward_band(conv2_weight),),
        (field, table(4), table(2), pay(2), pay(2)),
        (),
        conv_scratch(rows, channels),
        conv_flops(seqs, rows, channels, channels),
    )
    second_left, second_right = exchanged(low_pay, high_pay)
    section_out, grad, second_stats, sums, low_pay, high_pay = kernel_call(
        output_kernel(rows, channels),
        seqs,
        (
            second, side_field, cotangent, stats, second_left, second_right,
            with_far(sums, reaches), inverse, owner, crop_t,
        ),
        (),
        (low_field, field, table(2), table(3), pay(3), pay(3)),
        (),
        [],
        seqs * rows * lanes * 20,
    )
    grad_left, grad_right = exchanged(low_pay, high_pay)
    first_grad, side_grad, sums, low_pay, high_pay, conv2_grad = kernel_call(
        second_back_kernel(rows, channels, seqs),
        seqs,
        (
            grad, grad_left, grad_right, with_far(sums, reaches), second, second_left, second_right,
            side_field, first, stats, second_stats, inverse, owner, place, crop_t,
        ),
        (backward_band(conv2_weight),),
        (field, low_field, table(2), pay(2), pay(2)),
        (((27, 1, channels, channels), wide),),
        conv_scratch(rows, channels)
        + [
            pltpu.VMEM((SUBS * channels, rows), low_type),
            pltpu.VMEM((9, 2 * channels, 4 * channels), wide),
        ],
        2 * conv_flops(seqs, rows, channels, channels),
    )
    back_left, back_right = exchanged(low_pay, high_pay)
    up_grad, skip_grad, conv1_grad, conv3_grad = kernel_call(
        first_back_kernel(rows, channels, seqs),
        seqs,
        (
            first_grad, back_left, back_right, with_far(sums, reaches), first, first_left,
            first_right, stats, inverse, owner, place, side_grad, upsampled, skip,
        ),
        (backward_band(conv1_weight), conv3_weight.T),
        (low_field, field),
        (((27, 2, channels, channels), wide), ((width, channels), wide)),
        conv_scratch(rows, channels)
        + [
            pltpu.VMEM((SUBS * width, rows), low_type),
            pltpu.VMEM((9, 2 * width, 4 * channels), wide),
        ],
        2 * conv_flops(seqs, rows, channels, width),
    )
    return (section_out, up_grad, skip_grad, conv1_grad, conv2_grad, conv3_grad)


PIECE_BYTES = 2400 * 1024


def bit_count(size):
    return size.bit_length() - 1


def pieces_of(shapes):
    pieces = []
    for index, (shards, rows, lanes) in enumerate(shapes):
        parts = max(1, round(shards * rows * lanes * 2 / PIECE_BYTES))
        while rows % (16 * parts) != 0 and parts > 1:
            parts -= 1
        take = rows // parts
        pieces.extend((index, part * take, take, lanes) for part in range(parts))
    return pieces


def all_of(count):
    return (slice(None),) * count


def reduce_kernel(pieces, arrays, tok_bits, seq_bits):
    phases = tok_bits + seq_bits
    mesh_id = pl.DeviceIdType.MESH

    def body(*refs):
        given = refs[:arrays]
        results = refs[arrays : 2 * arrays]
        count = len(pieces)
        rest = refs[2 * arrays :]
        kept = rest[:count]
        landed = [rest[count + i * phases : count + (i + 1) * phases] for i in range(count)]
        local_sem, send_sem, recv_sem = rest[count + count * phases :]
        tok = lax.axis_index("tok")
        seq = lax.axis_index("seq")

        def bit_of(phase):
            if phase < tok_bits:
                return (tok // (1 << phase)) % 2
            return (seq // (1 << (phase - tok_bits))) % 2

        def partner(phase):
            bit = bit_of(phase)
            if phase < tok_bits:
                return (seq, tok + (1 << phase) * (1 - 2 * bit))
            return (seq + (1 << (phase - tok_bits)) * (1 - 2 * bit), tok)

        barrier = pltpu.get_barrier_semaphore()
        for phase in range(phases):
            pl.semaphore_signal(barrier, inc=1, device_id=partner(phase), device_id_type=mesh_id)
        pl.semaphore_wait(barrier, phases)

        def local_copy(piece):
            index, begin, take, _ = pieces[piece]
            view = given[index].at[all_of(tok_bits - 1) + (bit_of(0), pl.ds(begin, take))]
            return pltpu.make_async_copy(view, kept[piece], local_sem.at[piece])

        def remote_copy(piece, phase):
            index, begin, take, _ = pieces[piece]
            if phase == 0:
                view = given[index].at[all_of(tok_bits - 1) + (1 - bit_of(0), pl.ds(begin, take))]
            elif phase < tok_bits:
                view = landed[piece][phase - 1].at[all_of(tok_bits - 1 - phase) + (1 - bit_of(phase),)]
            else:
                view = landed[piece][phase - 1]
            return pltpu.make_async_remote_copy(
                src_ref=view,
                dst_ref=landed[piece][phase],
                send_sem=send_sem.at[piece, phase],
                recv_sem=recv_sem.at[piece, phase],
                device_id=partner(phase),
                device_id_type=mesh_id,
            )

        def begin(piece):
            remote_copy(piece, 0).start()
            local_copy(piece).start()

        def finish(piece, phase):
            index, first, take, _ = pieces[piece]
            remote_copy(piece, phase).wait_recv()
            got = landed[piece][phase]
            if phase == 0:
                local_copy(piece).wait()

            if phase < tok_bits:
                kept_bits = tok_bits - 1 - phase

                def step(block, carry):
                    at = tuple((block // (1 << bit)) % 2 for bit in reversed(range(kept_bits)))
                    if phase == 0:
                        mine = kept[piece][at]
                    else:
                        mine = landed[piece][phase - 1][at + (bit_of(phase),)]
                    got[at] = got[at] + mine
                    return carry

                lax.fori_loop(0, 1 << kept_bits, step, 0)
            elif phase + 1 < phases:
                got[...] = got[...] + landed[piece][phase - 1][...]
            if phase + 1 < phases:
                remote_copy(piece, phase + 1).start()
            else:
                total = got[...].astype(wide) + landed[piece][phase - 1][...].astype(wide)
                results[index][pl.ds(first, take), :] = total

        begin(0)
        for step in range(count + phases - 1):
            if step + 1 < count:
                begin(step + 1)
            for phase in range(phases):
                if 0 <= step - phase < count:
                    finish(step - phase, phase)
        for piece in range(count):
            for phase in range(phases):
                remote_copy(piece, phase).wait_send()

    return body


def reduced(grads):
    shards = lax.axis_size("tok")
    tok_bits = bit_count(shards)
    seq_bits = bit_count(lax.axis_size("seq"))
    shapes = [g.shape for g in grads]
    pieces = pieces_of(shapes)
    scratch = [
        pltpu.VMEM((2,) * (tok_bits - 1) + (take, lanes), low_type) for _, _, take, lanes in pieces
    ]
    for _, _, take, lanes in pieces:
        for phase in range(tok_bits - 1):
            bits = tok_bits - 1 - phase
            scratch.append(pltpu.VMEM((2,) * bits + (take, lanes), low_type))
        scratch += [pltpu.VMEM((take, lanes), low_type) for _ in range(1 + seq_bits)]
    count, phases = len(pieces), tok_bits + seq_bits
    scratch += [
        pltpu.SemaphoreType.DMA((count,)),
        pltpu.SemaphoreType.DMA((count, phases)),
        pltpu.SemaphoreType.DMA((count, phases)),
    ]
    total = sum(math.prod(s) for s in shapes)
    return pl.pallas_call(
        reduce_kernel(pieces, len(grads), tok_bits, seq_bits),
        in_specs=[pl.BlockSpec(memory_space=pl.ANY)] * len(grads),
        out_specs=[pl.BlockSpec(memory_space=pltpu.VMEM)] * len(grads),
        out_shape=[jax.ShapeDtypeStruct(s[1:], wide) for s in shapes],
        scratch_shapes=scratch,
        compiler_params=pltpu.CompilerParams(
            vmem_limit_bytes=VMEM_LIMIT, collective_id=0, has_side_effects=True
        ),
        cost_estimate=pl.CostEstimate(flops=total, bytes_accessed=4 * total, transcendentals=0),
    )(*[g.reshape((2,) * tok_bits + g.shape[1:]) for g in grads])


def sharded_rows(grad):
    shards = lax.axis_size("tok")
    rows = grad.shape[0] // shards
    grad = grad.astype(low_type)
    if rows % 16 == 0:
        return grad.reshape(shards, rows, grad.shape[1])
    return grad.reshape(shards, rows * grad.shape[1] // 128, 128)


def conv_rows(turned):
    shards = lax.axis_size("tok")
    taps, halves, channels, lanes = turned.shape
    split = turned.reshape(taps, halves, shards, channels // shards, lanes)
    return jnp.moveaxis(split, 2, 0).reshape(shards, -1, lanes)


def conv_share(rows, taps, halves):
    split = rows.reshape(taps, halves, -1, rows.shape[-1])
    return jnp.moveaxis(split, 2, 3).reshape(taps, halves * rows.shape[-1], -1)


def reduced_all(conv_grads, matrices, vectors):
    shards = lax.axis_size("tok")
    parts = [conv_rows(g) for g in conv_grads]
    flat = jnp.concatenate([v.reshape(shards, -1) for v in vectors], axis=1)
    used = flat.shape[1]
    taken = sum(p.shape[1] for p in parts)
    rows = -(-used // 128)
    rows += -(rows + taken) % 16
    flat = jnp.pad(flat, ((0, 0), (0, rows * 128 - used))).reshape(shards, rows, 128)
    packed = jnp.concatenate([p.astype(low_type) for p in parts] + [flat.astype(low_type)], axis=1)
    results = reduced([packed] + [sharded_rows(m) for m in matrices])
    shares = []
    cursor = 0
    for part, grad in zip(parts, conv_grads):
        rows_here = results[0][cursor : cursor + part.shape[1]]
        shares.append(conv_share(rows_here, grad.shape[0], grad.shape[1]))
        cursor += part.shape[1]
    flat = results[0][cursor:].reshape(-1)
    cursor = 0
    pieces = []
    for vector in vectors:
        size = vector.size // shards
        pieces.append(flat[cursor : cursor + size])
        cursor += size
    whole = [r.reshape(-1, m.shape[1]) for r, m in zip(results[1:], matrices)]
    return (shares, whole, pieces)


def crop_tables(crop_sides, inside, shape_info, first_row, row_count):
    seqs, crops = crop_sides.shape
    spare = CROP_ROWS - crops
    own = jnp.arange(row_count, dtype=jnp.int32)[None, :] + EDGE
    columns = []
    for offset in all_offsets():
        near_step, far_step = step_sizes(offset)
        step = jnp.where(shape_info[4], far_step, near_step)
        columns.append(jnp.where(in_crop(shape_info, offset), own + step, -1))
    place = jnp.stack(columns, axis=-1).astype(jnp.int32)
    wide_places = first_row - EDGE + jnp.arange(row_count + 2 * EDGE, dtype=jnp.int32)
    wide_places = jnp.broadcast_to(wide_places, (seqs, row_count + 2 * EDGE))
    owner = jnp.pad(locate(crop_sides, wide_places)[0], ((0, 0), (0, 0), (0, spare)))
    crop_t = jnp.pad(inside.swapaxes(1, 2), ((0, 0), (0, spare), (0, 0)))
    counts = jnp.maximum(8.0 * (crop_sides * crop_sides * crop_sides).astype(wide), 1.0)
    inverse = jnp.pad(1.0 / counts, ((0, 0), (0, spare)), constant_values=1.0)
    inverse = jnp.broadcast_to(inverse[:, :, None], (seqs, CROP_ROWS, 128))
    return (place, owner.astype(low_type), crop_t.astype(low_type), inverse)


def local(
    tokens,
    skip_features,
    crop_sides,
    ln1_gain,
    ln1_bias,
    qkv_weight,
    qv_bias,
    out_weight,
    out_bias,
    ln2_gain,
    ln2_bias,
    fc1_weight,
    fc1_bias,
    fc2_weight,
    fc2_bias,
    deconv_weight,
    conv1_weight,
    conv2_weight,
    conv3_weight,
    cotangent,
):
    seq_count, row_count, model_width = tokens.shape
    channels = conv2_weight.shape[2]
    score_scale = 1.0 / math.sqrt(HEAD_DIM)
    first_row = lax.axis_index("tok") * row_count
    places = jnp.broadcast_to(
        first_row + jnp.arange(row_count, dtype=jnp.int32), (seq_count, row_count)
    )
    inside, segment, side_of, first_of = locate(crop_sides, places)
    shape_info = geometry(side_of, first_of, places)
    reaches = (key_reach + row_count - 1) // row_count
    token_values = tokens.astype(jnp.float32)
    normed_low = layer_norm(token_values, ln1_gain, ln1_bias).astype(jnp.bfloat16)
    qkv_bias = jnp.concatenate([qv_bias[0], jnp.zeros_like(qv_bias[0]), qv_bias[1]])
    projected = (
        jnp.einsum("std,de->ste", normed_low, qkv_weight, preferred_element_type=jnp.float32)
        + qkv_bias
    ).astype(jnp.bfloat16)
    queries = projected[:, :, :model_width]
    keys = projected[:, :, model_width : 2 * model_width]
    values = projected[:, :, 2 * model_width :]
    key_parts = [keys]
    value_parts = [values]
    place_parts = [places]
    moves = []
    for distance in range(1, reaches + 1):
        row_take = row_count
        for shift_by in (distance, -distance):
            if shift_by > 0:
                key_send = keys
                value_send = values
                got_first = first_row - (distance - 1) * row_count - row_take
            else:
                key_send = keys
                value_send = values
                got_first = first_row + distance * row_count
            got_keys, got_values = passed_along((key_send, value_send), "tok", shift_by)
            key_parts.append(got_keys)
            value_parts.append(got_values)
            place_parts.append(
                jnp.broadcast_to(
                    got_first + jnp.arange(row_take, dtype=jnp.int32), (seq_count, row_take)
                )
            )
            moves.append((shift_by, row_take))
    window_keys = jnp.concatenate(key_parts, axis=1).reshape(seq_count, -1, HEADS, HEAD_DIM)
    window_values = jnp.concatenate(value_parts, axis=1).reshape(seq_count, -1, HEADS, HEAD_DIM)
    key_crop = locate(crop_sides, jnp.concatenate(place_parts, axis=1))[1]
    same_crop = segment[:, None, :, None] == key_crop[:, None, None, :]
    query_heads = queries.reshape(seq_count, row_count, HEADS, HEAD_DIM)
    scores = crop_scores(query_heads, window_keys, same_crop)
    row_max = jnp.max(scores, axis=-1, keepdims=True)
    weights = jnp.exp(scores - row_max)
    totals = jnp.sum(weights, axis=-1, keepdims=True)
    log_total = row_max + jnp.log(totals)
    probs_low = (weights / totals).astype(jnp.bfloat16)
    attended = jnp.einsum(
        "shqk,skhd->sqhd", probs_low, window_values, preferred_element_type=jnp.float32
    )
    attended = attended.astype(jnp.bfloat16).reshape(seq_count, row_count, model_width)
    resid_one = (
        token_values
        + jnp.einsum("std,de->ste", attended, out_weight, preferred_element_type=jnp.float32)
        + out_bias
    )
    normed_two = layer_norm(resid_one, ln2_gain, ln2_bias).astype(jnp.bfloat16)
    pre_act = (
        jnp.einsum("std,df->stf", normed_two, fc1_weight, preferred_element_type=jnp.float32)
        + fc1_bias
    )
    act_low = jax.nn.gelu(pre_act, approximate=False).astype(jnp.bfloat16)
    resid_two = (
        resid_one
        + jnp.einsum("stf,fd->std", act_low, fc2_weight, preferred_element_type=jnp.float32)
        + fc2_bias
    )
    resid_low = resid_two.astype(jnp.bfloat16)
    upsampled = jnp.einsum(
        "std,de->ste", resid_low, deconv_weight, preferred_element_type=jnp.float32
    )
    upsampled = upsampled.astype(jnp.bfloat16)
    geometry_in = crop_tables(crop_sides, inside, shape_info, first_row, row_count)
    section_out, up_grad, skip_grad, conv1_grad, conv2_grad, conv3_grad = conv_section(
        upsampled,
        skip_features.reshape(seq_count, row_count, 8 * channels),
        cotangent.reshape(seq_count, row_count, 8 * channels),
        (conv1_weight, conv2_weight, conv3_weight),
        geometry_in,
        reaches,
    )
    section_out = section_out.reshape(seq_count, row_count, 8, channels)
    skip_grad = skip_grad.reshape(seq_count, row_count, 8, channels)
    deconv_grad = jnp.einsum("std,ste->de", resid_low, up_grad, preferred_element_type=jnp.float32)
    resid_two_grad = jnp.einsum(
        "ste,de->std", up_grad, deconv_weight, preferred_element_type=jnp.float32
    )
    branch_low = resid_two_grad.astype(jnp.bfloat16)
    fc2_bias_grad = jnp.sum(branch_low.astype(jnp.float32), axis=(0, 1))
    fc2_grad = jnp.einsum("stf,std->fd", act_low, branch_low, preferred_element_type=jnp.float32)
    act_grad = jnp.einsum("std,fd->stf", branch_low, fc2_weight, preferred_element_type=jnp.float32)
    gelu_pull = jax.vjp(partial(jax.nn.gelu, approximate=False), pre_act)[1]
    pre_low = gelu_pull(act_grad)[0].astype(jnp.bfloat16)
    fc1_bias_grad = jnp.sum(pre_low.astype(jnp.float32), axis=(0, 1))
    fc1_grad = jnp.einsum("std,stf->df", normed_two, pre_low, preferred_element_type=jnp.float32)
    normed_two_grad = jnp.einsum(
        "stf,df->std", pre_low, fc1_weight, preferred_element_type=jnp.float32
    )
    second_ln_pull = jax.vjp(layer_norm, resid_one, ln2_gain, ln2_bias)[1]
    resid_part, ln2_gain_grad, ln2_bias_grad = second_ln_pull(normed_two_grad)
    resid_one_grad = resid_two_grad + resid_part
    mixed_low = resid_one_grad.astype(jnp.bfloat16)
    out_bias_grad = jnp.sum(mixed_low.astype(jnp.float32), axis=(0, 1))
    out_grad = jnp.einsum("std,ste->de", attended, mixed_low, preferred_element_type=jnp.float32)
    attended_grad = jnp.einsum(
        "ste,de->std", mixed_low, out_weight, preferred_element_type=jnp.float32
    )
    attended_grad = attended_grad.astype(jnp.bfloat16).reshape(
        seq_count, row_count, HEADS, HEAD_DIM
    )
    scores_again = crop_scores(query_heads, window_keys, same_crop)
    attn_probs = jnp.exp(scores_again - log_total)
    probs_again = attn_probs.astype(jnp.bfloat16)
    probs_grad = jnp.einsum(
        "sqhd,skhd->shqk", attended_grad, window_values, preferred_element_type=jnp.float32
    )
    row_inner = jnp.sum(attn_probs * probs_grad, axis=-1, keepdims=True)
    score_low = (attn_probs * (probs_grad - row_inner)).astype(jnp.bfloat16)
    query_grad = (
        jnp.einsum("shqk,skhd->sqhd", score_low, window_keys, preferred_element_type=jnp.float32)
        * score_scale
    )
    key_grad = (
        jnp.einsum("shqk,sqhd->skhd", score_low, query_heads, preferred_element_type=jnp.float32)
        * score_scale
    )
    value_grad = jnp.einsum(
        "shqk,sqhd->skhd", probs_again, attended_grad, preferred_element_type=jnp.float32
    )
    key_grad = key_grad.reshape(seq_count, -1, model_width)
    value_grad = value_grad.reshape(seq_count, -1, model_width)
    key_own = key_grad[:, :row_count]
    value_own = value_grad[:, :row_count]
    cursor = row_count
    for shift_by, row_take in moves:
        key_piece = key_grad[:, cursor : cursor + row_take]
        value_piece = value_grad[:, cursor : cursor + row_take]
        cursor = cursor + row_take
        back_keys, back_values = (
            passed_along(key_piece.astype(jnp.bfloat16), "tok", -shift_by).astype(key_piece.dtype),
            passed_along(value_piece.astype(jnp.bfloat16), "tok", -shift_by).astype(
                value_piece.dtype
            ),
        )
        if shift_by > 0:
            key_own = key_own.at[:, row_count - row_take :].add(back_keys)
            value_own = value_own.at[:, row_count - row_take :].add(back_values)
        else:
            key_own = key_own.at[:, :row_take].add(back_keys)
            value_own = value_own.at[:, :row_take].add(back_values)
    qkv_grad_low = jnp.concatenate(
        [query_grad.reshape(seq_count, row_count, model_width), key_own, value_own], axis=-1
    ).astype(jnp.bfloat16)
    qkv_grad = jnp.einsum(
        "std,ste->de", normed_low, qkv_grad_low, preferred_element_type=jnp.float32
    )
    column_sums = jnp.sum(qkv_grad_low.astype(jnp.float32), axis=(0, 1))
    qv_bias_grad = jnp.stack([column_sums[:model_width], column_sums[2 * model_width :]])
    normed_one_grad = jnp.einsum(
        "ste,de->std", qkv_grad_low, qkv_weight, preferred_element_type=jnp.float32
    )
    first_ln_pull = jax.vjp(layer_norm, token_values, ln1_gain, ln1_bias)[1]
    token_part, ln1_gain_grad, ln1_bias_grad = first_ln_pull(normed_one_grad)
    token_grad = resid_one_grad + token_part
    conv3_turned = jnp.moveaxis(conv3_grad.reshape(1, 2, channels, channels), 2, 3)
    conv_shares, shares, vectors = reduced_all(
        (conv1_grad, conv2_grad, conv3_turned),
        (deconv_grad, fc2_grad, fc1_grad, out_grad, qkv_grad),
        (
            ln1_gain_grad, ln1_bias_grad, qv_bias_grad[0], qv_bias_grad[1], out_bias_grad,
            ln2_gain_grad, ln2_bias_grad, fc1_bias_grad, fc2_bias_grad,
        ),
    )
    return (
        section_out,
        token_grad,
        skip_grad,
        vectors[0],
        vectors[1],
        shares[4],
        jnp.stack([vectors[2], vectors[3]]),
        shares[3],
        vectors[4],
        vectors[5],
        vectors[6],
        shares[2],
        vectors[7],
        shares[1],
        vectors[8],
        shares[0],
        conv_shares[0],
        conv_shares[1],
        conv_shares[2][0],
    )


def solution(mesh):
    in_specs = (
        P("seq", "tok", None),
        P("seq", "tok", None, None),
        P("seq", None),
        P(),
        P(),
        P(),
        P(),
        P(),
        P(),
        P(),
        P(),
        P(),
        P(),
        P(),
        P(),
        P(),
        P(),
        P(),
        P(),
        P("seq", "tok", None, None),
    )
    out_specs = (
        P("seq", "tok", None, None),
        P("seq", "tok", None),
        P("seq", "tok", None, None),
        P("tok"),
        P("tok"),
        P("tok", None),
        P(None, "tok"),
        P("tok", None),
        P("tok"),
        P("tok"),
        P("tok"),
        P("tok", None),
        P("tok"),
        P("tok", None),
        P("tok"),
        P("tok", None),
        P(None, None, "tok"),
        P(None, None, "tok"),
        P(None, "tok"),
    )
    return jax.shard_map(local, mesh=mesh, in_specs=in_specs, out_specs=out_specs, check_vma=False)
```

```python
from functools import partial
import math

import jax
import jax.numpy as jnp
import numpy as np
from jax import lax
from jax.experimental import pallas as pl
from jax.experimental.pallas import tpu as pltpu
from jax.sharding import PartitionSpec as P

HEADS = 12
HEAD_DIM = 64


side_small = 4
side_big = 6
halo_rows = 43
key_reach = 215
norm_eps = 1e-05
far_below = -1e30
highest = lax.Precision.HIGHEST
in_part = {-1: (1, 2), 0: (0, 2), 1: (0, 1)}
out_part = {-1: (0, 1), 0: (0, 2), 1: (1, 2)}


def passed_along(block, axis, distance):
    devices = range(lax.axis_size(axis))
    route = [(i - distance, i) for i in devices if i - distance in devices]
    return lax.ppermute(block, axis, route)


def all_offsets():
    step_values = (-1, 0, 1)
    return [
        (step_x, step_y, step_z)
        for step_x in step_values
        for step_y in step_values
        for step_z in step_values
    ]


EDGE = 48
WINDOW = 256
TILE = 128
CROP_ROWS = 48
SUBS = 8
VMEM_LIMIT = 60 * 1024 * 1024
lowest_step = {-1: -43, 0: -7, 1: 11}
low_type = jnp.bfloat16
wide = jnp.float32


def dot(left, right):
    return jnp.dot(left, right, preferred_element_type=wide)


def three_terms(field):
    first = field.astype(low_type)
    rest = field - first.astype(wide)
    second = rest.astype(low_type)
    third = (rest - second.astype(wide)).astype(low_type)
    return (first, second, third)


def exact_dot(chosen, field):
    first, second, third = three_terms(field)
    return dot(chosen, first) + dot(chosen, second) + dot(chosen, third)


def sub_lanes(number, width):
    return slice(number * width, (number + 1) * width)


def all_taps():
    return [(x, y, z) for x in range(3) for y in range(3) for z in range(3)]


def forward_band(weight, band_ref):
    inner, outer = weight.shape[1:]
    band_ref[...] = jnp.zeros_like(band_ref)
    for tap_x, tap_y, tap_z in all_taps():
        for side in range(2):
            rows = sub_lanes(tap_y * 4 + tap_z + side, inner)
            lanes = sub_lanes(side, outer)
            band_ref[tap_x, rows, lanes] = weight[tap_x * 9 + tap_y * 3 + tap_z]


def backward_band(weight, band_ref):
    inner, outer = weight.shape[1:]
    band_ref[...] = jnp.zeros_like(band_ref)
    for tap_x, tap_y, tap_z in all_taps():
        for side in range(2):
            rows = sub_lanes(side, inner)
            lanes = sub_lanes(tap_y * 4 + tap_z + side, outer)
            band_ref[tap_x, rows, lanes] = weight[26 - (tap_x * 9 + tap_y * 3 + tap_z)]


def once(fill, *refs):
    @pl.when(pl.program_id(0) == 0)
    def _():
        fill(*refs)


def window_positions(step):
    return {-1: ((0, 1),), 0: ((1, 0), (2, 1)), 1: ((3, 0),)}[step]


def fill_windows(x_ref, place_ref, p_ref, rows, width):
    tile = min(rows, TILE)
    for base in range(0, rows, tile):
        own = slice(base, base + tile)
        for number, (step_x, step_y, step_z) in enumerate(all_offsets()):
            low = (EDGE + base + lowest_step[step_x]) // 16 * 16
            centre = (step_x, step_y, step_z) == (0, 0, 0)
            if not centre:
                lane = lax.broadcasted_iota(jnp.int32, (tile, WINDOW), 1) + low
                chosen = jnp.where(lane == place_ref[0, own, number : number + 1], 1.0, 0.0)
                chosen = chosen.astype(low_type)
            for x_to, x_from in window_positions(step_x):
                for y_to, y_from in window_positions(step_y):
                    z_to, z_from = window_positions(step_z)[0]
                    count = (2 if step_z == 0 else 1) * width
                    to = ((x_to * 4 + y_to) * 4 + z_to) * width
                    source = (x_from * 4 + y_from * 2 + z_from) * width
                    if centre:
                        got = x_ref[EDGE + base : EDGE + base + tile, source : source + count]
                    else:
                        got = dot(chosen, x_ref[low : low + WINDOW, source : source + count])
                    p_ref[own, to : to + count] = got.astype(low_type)


def window_conv(p_ref, band_ref, pair, width, product):
    first, second = pair
    total = None
    for tap in range(3):
        begin = ((first + tap) * 4 + second) * 4 * width
        term = product(p_ref[:, begin : begin + 12 * width], band_ref[tap])
        total = term if total is None else total + term
    return total


def all_pairs():
    return [(first, second) for first in range(2) for second in range(2)]


def add_grads(left_ref, p_ref, total_ref, width, channels):
    for tap_x in range(3):
        for tap_y in range(3):
            term = None
            for number, (first, second) in enumerate(all_pairs()):
                begin = ((first + tap_x) * 4 + second + tap_y) * 4 * channels
                left = left_ref[number * 2 * width : (number + 1) * 2 * width, :]
                part = dot(left, p_ref[:, begin : begin + 4 * channels])
                term = part if term is None else term + part
            total_ref[tap_x * 3 + tap_y] += term


def fold_grads(total_ref, grad_ref, width, channels):
    for tap_x in range(3):
        for tap_y in range(3):
            for tap_z in range(3):
                number = tap_x * 3 + tap_y
                here = total_ref[number, :width, sub_lanes(tap_z, channels)]
                there = total_ref[number, width:, sub_lanes(tap_z + 1, channels)]
                tap = 26 - (number * 3 + tap_z)
                for half in range(width // channels):
                    rows = slice(half * channels, (half + 1) * channels)
                    grad_ref[tap, half] = jnp.transpose(here[rows] + there[rows])


def kernel_call(body, seqs, inputs, shared, outputs, summed, scratch, flops):
    def row_spec(shape):
        return pl.BlockSpec((1,) + tuple(shape[1:]), lambda i: (i,) + (0,) * (len(shape) - 1))

    def whole_spec(shape):
        return pl.BlockSpec(
            tuple(shape), lambda i: (0,) * len(shape), pipeline_mode=pl.Buffered(1)
        )

    moved = sum(math.prod(a.shape) * a.dtype.itemsize for a in list(inputs) + list(shared))
    moved += sum(math.prod(s) * jnp.dtype(t).itemsize for s, t in list(outputs) + list(summed))
    return pl.pallas_call(
        body,
        grid=(seqs,),
        in_specs=[row_spec(a.shape) for a in inputs] + [whole_spec(a.shape) for a in shared],
        out_specs=[row_spec(s) for s, _ in outputs] + [whole_spec(s) for s, _ in summed],
        out_shape=[jax.ShapeDtypeStruct(s, t) for s, t in list(outputs) + list(summed)],
        scratch_shapes=scratch,
        compiler_params=pltpu.CompilerParams(vmem_limit_bytes=VMEM_LIMIT),
        cost_estimate=pl.CostEstimate(flops=flops, bytes_accessed=moved, transcendentals=0),
    )(*inputs, *shared)


def conv_scratch(rows, width, band_shape):
    return [
        pltpu.VMEM((rows + 192, SUBS * width), low_type),
        pltpu.VMEM((rows, 64 * width), low_type),
        pltpu.VMEM((3,) + band_shape, low_type),
    ]


def conv_flops(seqs, rows, inner, outer):
    return 2 * seqs * rows * (36 * 4 * inner * 2 * outer + 56 * WINDOW * inner)


def put_edges(low_pay, high_pay, number, field, channels, rows):
    lanes = sub_lanes(number, channels)
    low_pay[0, :, lanes] = field[:EDGE].astype(low_type)
    high_pay[0, :, lanes] = field[rows - EDGE :].astype(low_type)


def put_sums(sums_ref, low_pay, high_pay, number, value, channels):
    lanes = sub_lanes(number, channels)
    sums_ref[0, :, lanes] = value
    pay_lanes = sub_lanes(SUBS + number, channels)
    low_pay[0, :, pay_lanes] = value.astype(low_type)
    high_pay[0, :, pay_lanes] = value.astype(low_type)


def taken_sums(sums_ref, left_pay, right_pay, number, channels):
    lanes = sub_lanes(number, channels)
    pay_lanes = sub_lanes(SUBS + number, channels)
    total = sums_ref[0, :, lanes] + left_pay[0, :, pay_lanes].astype(wide)
    return total + right_pay[0, :, pay_lanes].astype(wide)


def mean_and_scale(total, square, inverse):
    mean = total * inverse
    variance = jnp.maximum(square * inverse - mean * mean, 0.0)
    return (mean, lax.rsqrt(variance + norm_eps))


def silu_parts(value):
    gate = 1.0 / (1.0 + jnp.exp(-value))
    return (value * gate, gate * (1.0 + value * (1.0 - gate)))


def first_conv_kernel(rows, channels):
    width = 2 * channels

    def body(
        up, up_left, up_right, skip, skip_left, skip_right, place, crop_t, weight, side,
        first_out, side_out, sums, low_pay, high_pay, x_ref, p_ref, band_ref,
    ):
        once(forward_band, weight, band_ref)
        for number in range(SUBS):
            for half, (own, left, right) in enumerate(
                ((up, up_left, up_right), (skip, skip_left, skip_right))
            ):
                to = sub_lanes(2 * number + half, channels)
                lanes = sub_lanes(number, channels)
                x_ref[:EDGE, to] = left[0, :, lanes]
                x_ref[EDGE : EDGE + rows, to] = own[0, :, lanes]
                x_ref[EDGE + rows : 2 * EDGE + rows, to] = right[0, :, lanes]
        x_ref[2 * EDGE + rows :, :] = jnp.zeros((96, SUBS * width), low_type)
        fill_windows(x_ref, place, p_ref, rows, width)
        total = [jnp.zeros((rows, channels), wide) for _ in range(4)]
        for index, pair in enumerate(all_pairs()):
            result = window_conv(p_ref, band_ref, pair, width, dot)
            first_out[0, :, sub_lanes(index, width)] = result
            for half in range(2):
                number = 2 * index + half
                value = result[:, sub_lanes(half, channels)]
                put_edges(low_pay, high_pay, number, value, channels, rows)
                flat = dot(x_ref[EDGE : EDGE + rows, sub_lanes(number, width)], side[...])
                side_out[0, :, sub_lanes(number, channels)] = flat
                terms = (value, value * value, flat, flat * flat)
                total = [have + term for have, term in zip(total, terms)]
        for number in range(4):
            value = exact_dot(crop_t[0], total[number])
            put_sums(sums, low_pay, high_pay, number, value, channels)

    return body


def second_conv_kernel(rows, channels):
    def body(
        first, left_pay, right_pay, own_sums, inverse, owner, place, crop_t, weight,
        second_out, stats, sums, low_pay, high_pay, x_ref, p_ref, band_ref,
    ):
        once(forward_band, weight, band_ref)
        taken = [taken_sums(own_sums, left_pay, right_pay, n, channels) for n in range(4)]
        mean, scale = mean_and_scale(taken[0], taken[1], inverse[0])
        side_mean, side_scale = mean_and_scale(taken[2], taken[3], inverse[0])
        for number, value in enumerate((mean, scale, side_mean, side_scale)):
            stats[0, :, sub_lanes(number, channels)] = value
        mean_rows = exact_dot(owner[0], mean)
        scale_rows = exact_dot(owner[0], scale)
        parts = (
            (left_pay, slice(0, EDGE)),
            (first, slice(EDGE, EDGE + rows)),
            (right_pay, slice(EDGE + rows, 2 * EDGE + rows)),
        )
        for number in range(SUBS):
            lanes = sub_lanes(number, channels)
            for field, place_rows in parts:
                normed = field[0, :, lanes].astype(wide) - mean_rows[place_rows]
                normed = normed * scale_rows[place_rows]
                x_ref[place_rows, lanes] = silu_parts(normed)[0].astype(low_type)
        x_ref[2 * EDGE + rows :, :] = jnp.zeros((96, SUBS * channels), low_type)
        fill_windows(x_ref, place, p_ref, rows, channels)
        total = [jnp.zeros((rows, channels), wide) for _ in range(2)]
        for index, pair in enumerate(all_pairs()):
            result = window_conv(p_ref, band_ref, pair, channels, dot)
            second_out[0, :, sub_lanes(index, 2 * channels)] = result
            for half in range(2):
                value = result[:, sub_lanes(half, channels)]
                put_edges(low_pay, high_pay, 2 * index + half, value, channels, rows)
                total = [total[0] + value, total[1] + value * value]
        for number in range(2):
            value = exact_dot(crop_t[0], total[number])
            put_sums(sums, low_pay, high_pay, number, value, channels)

    return body


def output_kernel(rows, channels):
    def body(
        second, side_field, cotangent, stats, left_pay, right_pay, own_sums, inverse, owner, crop_t,
        section, grad_out, second_stats, sums, low_pay, high_pay,
    ):
        taken = [taken_sums(own_sums, left_pay, right_pay, n, channels) for n in range(2)]
        mean, scale = mean_and_scale(taken[0], taken[1], inverse[0])
        second_stats[0, :, sub_lanes(0, channels)] = mean
        second_stats[0, :, sub_lanes(1, channels)] = scale
        own = owner[0, EDGE : EDGE + rows, :]
        mean_rows = exact_dot(own, mean)
        scale_rows = exact_dot(own, scale)
        side_mean = exact_dot(own, stats[0, :, sub_lanes(2, channels)])
        side_scale = exact_dot(own, stats[0, :, sub_lanes(3, channels)])
        total = [jnp.zeros((rows, channels), wide) for _ in range(3)]
        for number in range(SUBS):
            lanes = sub_lanes(number, channels)
            normed = (second[0, :, lanes] - mean_rows) * scale_rows
            side = (side_field[0, :, lanes] - side_mean) * side_scale
            value, slope = silu_parts(normed + side)
            section[0, :, lanes] = value.astype(low_type)
            grad = cotangent[0, :, lanes].astype(wide) * slope
            grad_out[0, :, lanes] = grad
            put_edges(low_pay, high_pay, number, grad, channels, rows)
            terms = (grad, grad * normed, grad * side)
            total = [have + term for have, term in zip(total, terms)]
        for number in range(3):
            value = exact_dot(crop_t[0], total[number])
            put_sums(sums, low_pay, high_pay, number, value, channels)

    return body


def second_back_kernel(rows, channels, seqs):
    def body(
        grad, grad_left, grad_right, own_sums, second, second_left, second_right, side_field, first,
        stats, second_stats, inverse, owner, place, crop_t, weight,
        first_grad, side_grad, sums, low_pay, high_pay, weight_grad,
        x_ref, p_ref, band_ref, left_ref, total_ref,
    ):
        once(backward_band, weight, band_ref)
        means = [
            taken_sums(own_sums, grad_left, grad_right, n, channels) * inverse[0] for n in range(3)
        ]
        mean_rows = exact_dot(owner[0], second_stats[0, :, sub_lanes(0, channels)])
        scale_rows = exact_dot(owner[0], second_stats[0, :, sub_lanes(1, channels)])
        lead_rows = exact_dot(owner[0], means[0])
        slope_rows = exact_dot(owner[0], means[1])
        parts = (
            (grad_left, second_left, slice(0, EDGE)),
            (grad, second, slice(EDGE, EDGE + rows)),
            (grad_right, second_right, slice(EDGE + rows, 2 * EDGE + rows)),
        )
        own = slice(EDGE, EDGE + rows)
        side_mean = exact_dot(owner[0, own, :], stats[0, :, sub_lanes(2, channels)])
        side_scale = exact_dot(owner[0, own, :], stats[0, :, sub_lanes(3, channels)])
        side_slope = exact_dot(owner[0, own, :], means[2])
        first_mean = exact_dot(owner[0, own, :], stats[0, :, sub_lanes(0, channels)])
        first_scale = exact_dot(owner[0, own, :], stats[0, :, sub_lanes(1, channels)])
        for number in range(SUBS):
            lanes = sub_lanes(number, channels)
            for grad_from, field, at in parts:
                normed = (field[0, :, lanes].astype(wide) - mean_rows[at]) * scale_rows[at]
                pulled = grad_from[0, :, lanes].astype(wide) - lead_rows[at]
                pulled = scale_rows[at] * (pulled - normed * slope_rows[at])
                x_ref[at, lanes] = pulled.astype(low_type)
            side = (side_field[0, :, lanes] - side_mean) * side_scale
            pulled = side_scale * (grad[0, :, lanes] - lead_rows[own] - side * side_slope)
            side_grad[0, :, lanes] = pulled.astype(low_type)
            normed = (first[0, :, lanes] - first_mean) * first_scale
            hidden = silu_parts(normed)[0]
            left_ref[lanes, :] = jnp.transpose(hidden).astype(low_type)
        x_ref[2 * EDGE + rows :, :] = jnp.zeros((96, SUBS * channels), low_type)
        fill_windows(x_ref, place, p_ref, rows, channels)
        total = [jnp.zeros((rows, channels), wide) for _ in range(2)]
        for index, pair in enumerate(all_pairs()):
            result = window_conv(p_ref, band_ref, pair, channels, dot_t)
            for half in range(2):
                number = 2 * index + half
                lanes = sub_lanes(number, channels)
                normed = (first[0, :, lanes] - first_mean) * first_scale
                value = result[:, sub_lanes(half, channels)] * silu_parts(normed)[1]
                first_grad[0, :, lanes] = value
                put_edges(low_pay, high_pay, number, value, channels, rows)
                total = [total[0] + value, total[1] + value * normed]
        for number in range(2):
            value = exact_dot(crop_t[0], total[number])
            put_sums(sums, low_pay, high_pay, number, value, channels)

        @pl.when(pl.program_id(0) == 0)
        def _():
            total_ref[...] = jnp.zeros_like(total_ref)

        add_grads(left_ref, p_ref, total_ref, channels, channels)

        @pl.when(pl.program_id(0) == seqs - 1)
        def _():
            fold_grads(total_ref, weight_grad, channels, channels)

    return body


def first_back_kernel(rows, channels, seqs):
    width = 2 * channels

    def body(
        grad, grad_left, grad_right, own_sums, first, first_left, first_right, stats, inverse, owner,
        place, side_grad, up, skip, weight, side_weight,
        up_grad, skip_grad, weight_grad, side_weight_grad,
        x_ref, p_ref, band_ref, left_ref, total_ref,
    ):
        once(backward_band, weight, band_ref)
        means = [
            taken_sums(own_sums, grad_left, grad_right, n, channels) * inverse[0] for n in range(2)
        ]
        mean_rows = exact_dot(owner[0], stats[0, :, sub_lanes(0, channels)])
        scale_rows = exact_dot(owner[0], stats[0, :, sub_lanes(1, channels)])
        lead_rows = exact_dot(owner[0], means[0])
        slope_rows = exact_dot(owner[0], means[1])
        parts = (
            (grad_left, first_left, slice(0, EDGE)),
            (grad, first, slice(EDGE, EDGE + rows)),
            (grad_right, first_right, slice(EDGE + rows, 2 * EDGE + rows)),
        )
        for number in range(SUBS):
            lanes = sub_lanes(number, channels)
            for grad_from, field, at in parts:
                normed = (field[0, :, lanes].astype(wide) - mean_rows[at]) * scale_rows[at]
                pulled = grad_from[0, :, lanes].astype(wide) - lead_rows[at]
                pulled = scale_rows[at] * (pulled - normed * slope_rows[at])
                x_ref[at, lanes] = pulled.astype(low_type)
            for half, field in enumerate((up, skip)):
                turned = jnp.transpose(field[0, :, lanes].astype(wide)).astype(low_type)
                left_ref[sub_lanes(2 * number + half, channels), :] = turned
        x_ref[2 * EDGE + rows :, :] = jnp.zeros((96, SUBS * channels), low_type)
        fill_windows(x_ref, place, p_ref, rows, channels)
        for index, pair in enumerate(all_pairs()):
            result = window_conv(p_ref, band_ref, pair, channels, dot_t)
            for half in range(2):
                number = 2 * index + half
                lanes = sub_lanes(number, channels)
                value = result[:, sub_lanes(half, width)]
                value = value + dot_t(side_grad[0, :, lanes], side_weight[...])
                up_grad[0, :, lanes] = value[:, :channels].astype(low_type)
                skip_grad[0, :, lanes] = value[:, channels:]

        @pl.when(pl.program_id(0) == 0)
        def _():
            total_ref[...] = jnp.zeros_like(total_ref)
            side_weight_grad[...] = jnp.zeros_like(side_weight_grad)

        for number in range(SUBS):
            side_weight_grad[...] += dot(
                left_ref[sub_lanes(number, width), :], side_grad[0, :, sub_lanes(number, channels)]
            )
        add_grads(left_ref, p_ref, total_ref, width, channels)

        @pl.when(pl.program_id(0) == seqs - 1)
        def _():
            fold_grads(total_ref, weight_grad, width, channels)

    return body


def exchanged(low_pay, high_pay):
    return (passed_along(high_pay, "tok", 1), passed_along(low_pay, "tok", -1))


def with_far(sums, reaches):
    total = sums
    for distance in range(2, reaches + 1):
        for shift_by in (distance, -distance):
            total = total + passed_along(sums.astype(low_type), "tok", shift_by).astype(wide)
    return total


def conv_section(upsampled, skip, cotangent, weights, geometry_in, reaches):
    conv1_weight, conv2_weight, conv3_weight = weights
    seqs, rows, lanes = upsampled.shape
    channels = lanes // SUBS
    width = 2 * channels
    place, owner, crop_t, inverse = geometry_in
    field = ((seqs, rows, lanes), wide)
    low_field = ((seqs, rows, lanes), low_type)

    def pay(count):
        return ((seqs, EDGE, (SUBS + count) * channels), low_type)

    def table(count):
        return ((seqs, CROP_ROWS, count * channels), wide)

    skip_left, skip_right = exchanged(skip[:, :EDGE], skip[:, rows - EDGE :])
    up_left, up_right = exchanged(upsampled[:, :EDGE], upsampled[:, rows - EDGE :])
    first, side_field, sums, low_pay, high_pay = kernel_call(
        first_conv_kernel(rows, channels),
        seqs,
        (upsampled, up_left, up_right, skip, skip_left, skip_right, place, crop_t),
        (conv1_weight, conv3_weight),
        (field, field, table(4), pay(4), pay(4)),
        (),
        conv_scratch(rows, width, (12 * width, 2 * channels)),
        conv_flops(seqs, rows, width, channels),
    )
    first_left, first_right = exchanged(low_pay, high_pay)
    second, stats, sums, low_pay, high_pay = kernel_call(
        second_conv_kernel(rows, channels),
        seqs,
        (first, first_left, first_right, with_far(sums, reaches), inverse, owner, place, crop_t),
        (conv2_weight,),
        (field, table(4), table(2), pay(2), pay(2)),
        (),
        conv_scratch(rows, channels, (12 * channels, 2 * channels)),
        conv_flops(seqs, rows, channels, channels),
    )
    second_left, second_right = exchanged(low_pay, high_pay)
    section_out, grad, second_stats, sums, low_pay, high_pay = kernel_call(
        output_kernel(rows, channels),
        seqs,
        (
            second, side_field, cotangent, stats, second_left, second_right,
            with_far(sums, reaches), inverse, owner, crop_t,
        ),
        (),
        (low_field, field, table(2), table(3), pay(3), pay(3)),
        (),
        [],
        seqs * rows * lanes * 20,
    )
    grad_left, grad_right = exchanged(low_pay, high_pay)
    first_grad, side_grad, sums, low_pay, high_pay, conv2_grad = kernel_call(
        second_back_kernel(rows, channels, seqs),
        seqs,
        (
            grad, grad_left, grad_right, with_far(sums, reaches), second, second_left, second_right,
            side_field, first, stats, second_stats, inverse, owner, place, crop_t,
        ),
        (conv2_weight,),
        (field, low_field, table(2), pay(2), pay(2)),
        (((27, 1, channels, channels), wide),),
        conv_scratch(rows, channels, (2 * channels, 12 * channels))
        + [
            pltpu.VMEM((SUBS * channels, rows), low_type),
            pltpu.VMEM((9, 2 * channels, 4 * channels), wide),
        ],
        2 * conv_flops(seqs, rows, channels, channels),
    )
    back_left, back_right = exchanged(low_pay, high_pay)
    up_grad, skip_grad, conv1_grad, conv3_grad = kernel_call(
        first_back_kernel(rows, channels, seqs),
        seqs,
        (
            first_grad, back_left, back_right, with_far(sums, reaches), first, first_left,
            first_right, stats, inverse, owner, place, side_grad, upsampled, skip,
        ),
        (conv1_weight, conv3_weight),
        (low_field, field),
        (((27, 2, channels, channels), wide), ((width, channels), wide)),
        conv_scratch(rows, channels, (2 * width, 12 * channels))
        + [
            pltpu.VMEM((SUBS * width, rows), low_type),
            pltpu.VMEM((9, 2 * width, 4 * channels), wide),
        ],
        2 * conv_flops(seqs, rows, channels, width),
    )
    return (section_out, up_grad, skip_grad, conv1_grad, conv2_grad, conv3_grad)


PIECE_BYTES = 2400 * 1024


def bit_count(size):
    return size.bit_length() - 1


def pieces_of(shapes):
    pieces = []
    for index, (shards, rows, lanes) in enumerate(shapes):
        parts = max(1, round(shards * rows * lanes * 2 / PIECE_BYTES))
        while rows % (16 * parts) != 0 and parts > 1:
            parts -= 1
        take = rows // parts
        pieces.extend((index, part * take, take, lanes) for part in range(parts))
    return pieces


def all_of(count):
    return (slice(None),) * count


def reduce_kernel(pieces, arrays, tok_bits, seq_bits):
    phases = tok_bits + seq_bits
    mesh_id = pl.DeviceIdType.MESH

    def body(*refs):
        given = refs[:arrays]
        results = refs[arrays : 2 * arrays]
        count = len(pieces)
        rest = refs[2 * arrays :]
        kept = rest[:count]
        landed = [rest[count + i * phases : count + (i + 1) * phases] for i in range(count)]
        local_sem, send_sem, recv_sem = rest[count + count * phases :]
        tok = lax.axis_index("tok")
        seq = lax.axis_index("seq")

        def bit_of(phase):
            if phase < tok_bits:
                return (tok // (1 << phase)) % 2
            return (seq // (1 << (phase - tok_bits))) % 2

        def partner(phase):
            bit = bit_of(phase)
            if phase < tok_bits:
                return (seq, tok + (1 << phase) * (1 - 2 * bit))
            return (seq + (1 << (phase - tok_bits)) * (1 - 2 * bit), tok)

        barrier = pltpu.get_barrier_semaphore()
        for phase in range(phases):
            pl.semaphore_signal(barrier, inc=1, device_id=partner(phase), device_id_type=mesh_id)
        pl.semaphore_wait(barrier, phases)

        def local_copy(piece):
            index, begin, take, _ = pieces[piece]
            view = given[index].at[all_of(tok_bits - 1) + (bit_of(0), pl.ds(begin, take))]
            return pltpu.make_async_copy(view, kept[piece], local_sem.at[piece])

        def remote_copy(piece, phase):
            index, begin, take, _ = pieces[piece]
            if phase == 0:
                view = given[index].at[all_of(tok_bits - 1) + (1 - bit_of(0), pl.ds(begin, take))]
            elif phase < tok_bits:
                view = landed[piece][phase - 1].at[all_of(tok_bits - 1 - phase) + (1 - bit_of(phase),)]
            else:
                view = landed[piece][phase - 1]
            return pltpu.make_async_remote_copy(
                src_ref=view,
                dst_ref=landed[piece][phase],
                send_sem=send_sem.at[piece, phase],
                recv_sem=recv_sem.at[piece, phase],
                device_id=partner(phase),
                device_id_type=mesh_id,
            )

        def begin(piece):
            remote_copy(piece, 0).start()
            local_copy(piece).start()

        def finish(piece, phase):
            index, first, take, _ = pieces[piece]
            remote_copy(piece, phase).wait_recv()
            got = landed[piece][phase]
            if phase == 0:
                local_copy(piece).wait()

            if phase < tok_bits:
                kept_bits = tok_bits - 1 - phase

                def step(block, carry):
                    at = tuple((block // (1 << bit)) % 2 for bit in reversed(range(kept_bits)))
                    if phase == 0:
                        mine = kept[piece][at]
                    else:
                        mine = landed[piece][phase - 1][at + (bit_of(phase),)]
                    got[at] = got[at] + mine
                    return carry

                lax.fori_loop(0, 1 << kept_bits, step, 0)
            elif phase + 1 < phases:
                got[...] = got[...] + landed[piece][phase - 1][...]
            if phase + 1 < phases:
                remote_copy(piece, phase + 1).start()
            else:
                total = got[...].astype(wide) + landed[piece][phase - 1][...].astype(wide)
                results[index][pl.ds(first, take), :] = total

        begin(0)
        for step in range(count + phases - 1):
            if step + 1 < count:
                begin(step + 1)
            for phase in range(phases):
                if 0 <= step - phase < count:
                    finish(step - phase, phase)
        for piece in range(count):
            for phase in range(phases):
                remote_copy(piece, phase).wait_send()

    return body


def reduced(grads):
    shards = lax.axis_size("tok")
    tok_bits = bit_count(shards)
    seq_bits = bit_count(lax.axis_size("seq"))
    shapes = [g.shape for g in grads]
    pieces = pieces_of(shapes)
    scratch = [
        pltpu.VMEM((2,) * (tok_bits - 1) + (take, lanes), low_type) for _, _, take, lanes in pieces
    ]
    for _, _, take, lanes in pieces:
        for phase in range(tok_bits - 1):
            bits = tok_bits - 1 - phase
            scratch.append(pltpu.VMEM((2,) * bits + (take, lanes), low_type))
        scratch += [pltpu.VMEM((take, lanes), low_type) for _ in range(1 + seq_bits)]
    count, phases = len(pieces), tok_bits + seq_bits
    scratch += [
        pltpu.SemaphoreType.DMA((count,)),
        pltpu.SemaphoreType.DMA((count, phases)),
        pltpu.SemaphoreType.DMA((count, phases)),
    ]
    total = sum(math.prod(s) for s in shapes)
    return pl.pallas_call(
        reduce_kernel(pieces, len(grads), tok_bits, seq_bits),
        in_specs=[pl.BlockSpec(memory_space=pl.ANY)] * len(grads),
        out_specs=[pl.BlockSpec(memory_space=pltpu.VMEM)] * len(grads),
        out_shape=[jax.ShapeDtypeStruct(s[1:], wide) for s in shapes],
        scratch_shapes=scratch,
        compiler_params=pltpu.CompilerParams(
            vmem_limit_bytes=VMEM_LIMIT, collective_id=0, has_side_effects=True
        ),
        cost_estimate=pl.CostEstimate(flops=total, bytes_accessed=4 * total, transcendentals=0),
    )(*[g.reshape((2,) * tok_bits + g.shape[1:]) for g in grads])


def sharded_rows(grad):
    shards = lax.axis_size("tok")
    rows = grad.shape[0] // shards
    grad = grad.astype(low_type)
    if rows % 16 == 0:
        return grad.reshape(shards, rows, grad.shape[1])
    return grad.reshape(shards, rows * grad.shape[1] // 128, 128)


def conv_rows(turned):
    shards = lax.axis_size("tok")
    taps, halves, channels, lanes = turned.shape
    split = turned.reshape(taps, halves, shards, channels // shards, lanes)
    return jnp.moveaxis(split, 2, 0).reshape(shards, -1, lanes)


def conv_share(rows, taps, halves):
    split = rows.reshape(taps, halves, -1, rows.shape[-1])
    return jnp.moveaxis(split, 2, 3).reshape(taps, halves * rows.shape[-1], -1)


def reduced_all(conv_grads, matrices, vectors):
    shards = lax.axis_size("tok")
    parts = [conv_rows(g) for g in conv_grads]
    flat = jnp.concatenate([v.reshape(shards, -1) for v in vectors], axis=1)
    used = flat.shape[1]
    taken = sum(p.shape[1] for p in parts)
    rows = -(-used // 128)
    rows += -(rows + taken) % 16
    flat = jnp.pad(flat, ((0, 0), (0, rows * 128 - used))).reshape(shards, rows, 128)
    packed = jnp.concatenate([p.astype(low_type) for p in parts] + [flat.astype(low_type)], axis=1)
    results = reduced([packed] + [sharded_rows(m) for m in matrices])
    shares = []
    cursor = 0
    for part, grad in zip(parts, conv_grads):
        rows_here = results[0][cursor : cursor + part.shape[1]]
        shares.append(conv_share(rows_here, grad.shape[0], grad.shape[1]))
        cursor += part.shape[1]
    flat = results[0][cursor:].reshape(-1)
    cursor = 0
    pieces = []
    for vector in vectors:
        size = vector.size // shards
        pieces.append(flat[cursor : cursor + size])
        cursor += size
    whole = [r.reshape(-1, m.shape[1]) for r, m in zip(results[1:], matrices)]
    return (shares, whole, pieces)


REACH = 224
QUERY_TILE = 128


def dot_t(left, right):
    return lax.dot_general(
        left, right, (((1,), (1,)), ((), ())), preferred_element_type=wide
    )


def counted(shape, axis):
    return lax.broadcasted_iota(jnp.int32, shape, axis).astype(wide)


def geometry_kernel(rows, crops):
    reach_rows = rows + 2 * REACH
    tile = min(rows, QUERY_TILE)
    window = tile + 2 * REACH

    def body(side_row, side_column, place, owner, crop_t, inverse, bias):
        first_row = (lax.axis_index("tok") * rows).astype(wide)
        sides_r = side_row[0].astype(wide)
        sides_c = side_column[0].astype(wide)
        volume_r = sides_r * sides_r * sides_r
        volume_c = sides_c * sides_c * sides_c
        shape = (crops, crops)
        start_r = jnp.sum(
            jnp.where(counted(shape, 0) < counted(shape, 1), volume_c, 0.0), axis=0, keepdims=True
        )
        start_c = jnp.sum(
            jnp.where(counted(shape, 1) < counted(shape, 0), volume_r, 0.0), axis=1, keepdims=True
        )

        def inside_of(length, begin):
            at = counted((length, crops), 0) + begin
            return ((at >= start_r) & (at < start_r + volume_r), at)

        wide_inside, _ = inside_of(rows + 2 * EDGE, first_row - EDGE)
        owner[0] = jnp.where(wide_inside, 1.0, 0.0).astype(low_type)
        inside, _ = inside_of(rows, first_row)
        side = jnp.sum(jnp.where(inside, sides_r, 0.0), axis=1, keepdims=True)
        first = jnp.sum(jnp.where(inside, start_r, 0.0), axis=1, keepdims=True)
        own = counted((rows, 1), 0)
        offset = own + first_row - first
        safe = jnp.maximum(side, 1.0)
        row_pos = jnp.floor((offset + 0.5) / (safe * safe))
        offset = offset - row_pos * safe * safe
        column = jnp.floor((offset + 0.5) / safe)
        depth_pos = offset - column * safe
        lane = counted((1, 32), 1)
        step_x = jnp.floor((lane + 0.5) / 9.0)
        step_y = jnp.floor((lane - 9.0 * step_x + 0.5) / 3.0)
        step_z = lane - 9.0 * step_x - 3.0 * step_y - 1.0
        step_x, step_y = (step_x - 1.0, step_y - 1.0)
        valid = None
        for at, step in ((row_pos, step_x), (column, step_y), (depth_pos, step_z)):
            moved = at + step
            here = (moved >= 0.0) & (moved < side)
            valid = here if valid is None else valid & here
        target = own + EDGE + (step_x * safe + step_y) * safe + step_z
        place[0] = jnp.where(valid, target, -1.0).astype(jnp.int32)
        at = counted((crops, rows), 1) + first_row
        inside_t = (at >= start_c) & (at < start_c + volume_c)
        crop_t[0] = jnp.where(inside_t, 1.0, 0.0).astype(low_type)
        inverse[0] = jnp.broadcast_to(1.0 / jnp.maximum(8.0 * volume_c, 1.0), (crops, 128))
        key_inside, _ = inside_of(reach_rows, first_row - REACH)
        key_first = jnp.sum(jnp.where(key_inside, start_r + 1.0, 0.0), axis=1, keepdims=True)
        query_first = jnp.sum(jnp.where(inside_t, start_c + 1.0, 0.0), axis=0, keepdims=True)
        for number in range(rows // tile):
            base = number * tile
            same = key_first[base : base + window] == query_first[:, base : base + tile]
            bias[0, number] = jnp.where(same, 0.0, far_below)

    return body


def geometry_tables(crop_sides, rows):
    seqs, crops = crop_sides.shape
    sides = jnp.pad(crop_sides, ((0, 0), (0, CROP_ROWS - crops)))
    tile = min(rows, QUERY_TILE)
    return kernel_call(
        geometry_kernel(rows, CROP_ROWS),
        seqs,
        (sides[:, None, :], sides[:, :, None]),
        (),
        (
            ((seqs, rows, 32), jnp.int32),
            ((seqs, rows + 2 * EDGE, CROP_ROWS), low_type),
            ((seqs, CROP_ROWS, rows), low_type),
            ((seqs, CROP_ROWS, 128), wide),
            ((seqs, rows // tile, tile + 2 * REACH, tile), wide),
        ),
        (),
        [],
        0,
    )


def normed_rows(values):
    centered = values - jnp.mean(values, axis=-1, keepdims=True)
    variance = jnp.mean(centered * centered, axis=-1, keepdims=True)
    scale = lax.rsqrt(variance + norm_eps)
    return (centered * scale, scale)


def norm_pull(grad, normed, scale, gain):
    inner = grad * gain
    first = jnp.mean(inner, axis=-1, keepdims=True)
    second = jnp.mean(inner * normed, axis=-1, keepdims=True)
    return scale * (inner - first - normed * second)


def error_function(value):
    bounded = jnp.clip(value, -3.832506856900711, 3.832506856900711)
    square = bounded * bounded
    top = 0.00022905065861350646
    for term in (0.0034082910107109506, 0.050955695062380861, 0.18520832239976145, 1.128379143519084):
        top = top * square + term
    bottom = -1.1791602954361697e-7
    for term in (
        0.000023547966471313185, 0.0010179625278914885, 0.014070470171167667,
        0.11098505178285362, 0.49746925110067538, 1.0,
    ):
        bottom = bottom * square + term
    return bounded * top / bottom


def gelu_parts(value):
    cumulative = 0.5 + 0.5 * error_function(value * math.sqrt(0.5))
    density = jnp.exp(-0.5 * value * value) * (1.0 / math.sqrt(2.0 * math.pi))
    return (value * cumulative, cumulative + value * density)


def head_lanes(block, half):
    lane = lax.broadcasted_iota(jnp.int32, block.shape, 1)
    chosen = lane < HEAD_DIM if half == 0 else lane >= HEAD_DIM
    return jnp.where(chosen, block, jnp.zeros_like(block))


def turned(block):
    return jnp.transpose(block.astype(wide))


def forward_kernel(rows, model_width, hidden):
    tile = min(rows, QUERY_TILE)
    window = tile + 2 * REACH
    chunk = 768
    scale = 1.0 / math.sqrt(HEAD_DIM)

    def body(
        tokens, left, right, bias, ln1_gain, ln1_bias, qkv_weight, qkv_bias, out_weight, out_bias,
        ln2_gain, ln2_bias, fc1_weight, fc1_bias, fc2_weight, fc2_bias, deconv_weight,
        normed_out, queries, keys, values, attended, log_totals, resid_out, second_out,
        act_out, slope_out, resid_low, upsampled, near_ref, turned_ref,
    ):
        begin = 0
        for field in (left, tokens, right):
            length = field.shape[1]
            normed = normed_rows(field[0].astype(wide))[0] * ln1_gain[...] + ln1_bias[...]
            near_ref[begin : begin + length, :] = normed.astype(low_type)
            begin += length
        own = near_ref[REACH : REACH + rows, :]
        normed_out[0] = own
        part = slice(0, model_width)
        queries[0] = (dot(own, qkv_weight[:, part]) + qkv_bias[:, part]).astype(low_type)
        part = slice(model_width, 2 * model_width)
        keys[0] = (dot(near_ref[...], qkv_weight[:, part]) + qkv_bias[:, part]).astype(low_type)
        part = slice(2 * model_width, 3 * model_width)
        found = dot(near_ref[...], qkv_weight[:, part]) + qkv_bias[:, part]
        values[0] = found.astype(low_type)
        for pair in range(model_width // 128):
            lanes = sub_lanes(pair, 128)
            turned_ref[lanes, :] = turned(values[0, :, lanes]).astype(low_type)
        for number in range(rows // tile):
            base = number * tile
            at = slice(base, base + tile)
            near = slice(base, base + window)
            for pair in range(model_width // 128):
                lanes = sub_lanes(pair, 128)
                query = queries[0, at, lanes] * scale
                key = keys[0, near, lanes]
                halves = []
                for half in range(2):
                    head = 2 * pair + half
                    scores = dot_t(key, head_lanes(query, half)) + bias[0, number]
                    top = jnp.max(scores, axis=0, keepdims=True)
                    weights = jnp.exp(scores - top)
                    total = jnp.sum(weights, axis=0, keepdims=True)
                    log_totals[0, head : head + 1, at] = top + jnp.log(total)
                    probs = (weights * (1.0 / total)).astype(low_type)
                    value = turned_ref[head * HEAD_DIM : (head + 1) * HEAD_DIM, near]
                    halves.append(dot(value, probs))
                both = jnp.concatenate(halves, axis=0)
                attended[0, at, lanes] = jnp.transpose(both).astype(low_type)
        resid = tokens[0].astype(wide) + dot(attended[0], out_weight[...]) + out_bias[...]
        resid_out[0] = resid
        second = normed_rows(resid)[0] * ln2_gain[...] + ln2_bias[...]
        second_out[0] = second.astype(low_type)
        total = resid + fc2_bias[...]
        for number in range(hidden // chunk):
            lanes = sub_lanes(number, chunk)
            pre = dot(second_out[0], fc1_weight[:, lanes]) + fc1_bias[:, lanes]
            act, slope = gelu_parts(pre)
            act_out[0, :, lanes] = act.astype(low_type)
            slope_out[0, :, lanes] = slope.astype(low_type)
            total = total + dot(act_out[0, :, lanes], fc2_weight[lanes, :])
        resid_low[0] = total.astype(low_type)
        upsampled[0] = dot(resid_low[0], deconv_weight[...]).astype(low_type)

    return body


def backward_kernel(rows, model_width, hidden):
    tile = min(rows, QUERY_TILE)
    window = tile + 2 * REACH
    chunk = 768
    scale = 1.0 / math.sqrt(HEAD_DIM)

    def body(
        up_grad, slope, resid, queries, keys, values, log_totals, bias,
        deconv_weight, fc2_weight, fc1_weight, out_weight, ln2_gain,
        branch_out, pre_out, resid_grad, mixed_out, query_grad, key_own, value_own, low_pay, high_pay,
        fc2_sum, fc1_sum, out_sum, gain_sum, shift_sum,
        near_key, near_value, turned_ref, pulled_ref,
    ):
        @pl.when(pl.program_id(0) == 0)
        def _():
            for ref in (fc2_sum, fc1_sum, out_sum, gain_sum, shift_sum):
                ref[...] = jnp.zeros_like(ref)

        def column_sum(field):
            return jnp.sum(field, axis=0, keepdims=True)

        incoming = dot_t(up_grad[0], deconv_weight[...])
        branch = incoming.astype(low_type)
        branch_out[0] = branch
        fc2_sum[...] += column_sum(branch.astype(wide))
        total = None
        for number in range(hidden // chunk):
            lanes = sub_lanes(number, chunk)
            act_grad = dot_t(branch_out[0], fc2_weight[lanes, :])
            pre = (act_grad * slope[0, :, lanes].astype(wide)).astype(low_type)
            pre_out[0, :, lanes] = pre
            fc1_sum[:, lanes] += column_sum(pre.astype(wide))
            term = dot_t(pre_out[0, :, lanes], fc1_weight[:, lanes])
            total = term if total is None else total + term
        normed, norm_scale = normed_rows(resid[0])
        gain_sum[...] += column_sum(total * normed)
        shift_sum[...] += column_sum(total)
        mixed = incoming + norm_pull(total, normed, norm_scale, ln2_gain[...])
        resid_grad[0] = mixed
        mixed = mixed.astype(low_type)
        mixed_out[0] = mixed
        out_sum[...] += column_sum(mixed.astype(wide))
        pulled_ref[...] = dot_t(mixed_out[0], out_weight[...]).astype(low_type)
        for pair in range(model_width // 128):
            lanes = sub_lanes(pair, 128)
            turned_ref[lanes, :] = turned(keys[0, :, lanes]).astype(low_type)
        near_key[...] = jnp.zeros_like(near_key)
        near_value[...] = jnp.zeros_like(near_value)
        for number in range(rows // tile):
            base = number * tile
            at = slice(base, base + tile)
            near = slice(base, base + window)
            for pair in range(model_width // 128):
                lanes = sub_lanes(pair, 128)
                query = queries[0, at, lanes] * scale
                pulled = pulled_ref[at, lanes]
                key = keys[0, near, lanes]
                value = values[0, near, lanes]
                halves = []
                key_term = None
                value_term = None
                for half in range(2):
                    head = 2 * pair + half
                    one_query = head_lanes(query, half)
                    one_pull = head_lanes(pulled, half)
                    scores = dot_t(key, one_query) + bias[0, number]
                    probs = jnp.exp(scores - log_totals[0, head : head + 1, at])
                    probs_grad = dot_t(value, one_pull)
                    inner = jnp.sum(probs * probs_grad, axis=0, keepdims=True)
                    score_grad = (probs * (probs_grad - inner)).astype(low_type)
                    here = dot(score_grad, one_query)
                    key_term = here if key_term is None else key_term + here
                    here = dot(probs.astype(low_type), one_pull)
                    value_term = here if value_term is None else value_term + here
                    key_turned = turned_ref[head * HEAD_DIM : (head + 1) * HEAD_DIM, near]
                    halves.append(dot(key_turned, score_grad) * scale)
                near_key[near, lanes] += key_term
                near_value[near, lanes] += value_term
                both = jnp.concatenate(halves, axis=0)
                query_grad[0, at, lanes] = jnp.transpose(both).astype(low_type)
        for field, own_out, begin in (
            (near_key, key_own, 0),
            (near_value, value_own, model_width),
        ):
            lanes = slice(begin, begin + model_width)
            own_out[0] = field[REACH : REACH + rows, :]
            low_pay[0, :, lanes] = field[:REACH, :].astype(low_type)
            high_pay[0, :, lanes] = field[REACH + rows :, :].astype(low_type)

    return body


def token_kernel(rows, model_width, joined):
    def body(*refs):
        tokens, resid_grad, query_grad, key_own, value_own = refs[:5]
        rest = refs[5:]
        if joined:
            from_left, from_right = rest[:2]
            rest = rest[2:]
        (qkv_weight, ln1_gain, grad_out, token_grad, bias_sum, gain_sum, shift_sum) = rest[:7]

        @pl.when(pl.program_id(0) == 0)
        def _():
            for ref in (bias_sum, gain_sum, shift_sum):
                ref[...] = jnp.zeros_like(ref)

        grad_out[0, :, :model_width] = query_grad[0]
        for number, own in enumerate((key_own, value_own)):
            lanes = sub_lanes(number, model_width)
            to = sub_lanes(number + 1, model_width)
            value = own[0]
            if joined:
                spare = jnp.zeros((rows - REACH, model_width), wide)
                value = value + jnp.concatenate([from_left[0, :, lanes].astype(wide), spare], axis=0)
                value = value + jnp.concatenate([spare, from_right[0, :, lanes].astype(wide)], axis=0)
            grad_out[0, :, to] = value.astype(low_type)
        bias_sum[...] += jnp.sum(grad_out[0].astype(wide), axis=0, keepdims=True)
        total = dot_t(grad_out[0], qkv_weight[...])
        normed, norm_scale = normed_rows(tokens[0].astype(wide))
        gain_sum[...] += jnp.sum(total * normed, axis=0, keepdims=True)
        shift_sum[...] += jnp.sum(total, axis=0, keepdims=True)
        token_grad[0] = resid_grad[0] + norm_pull(total, normed, norm_scale, ln1_gain[...])

    return body


def near_rows(field):
    rows = field.shape[1]
    lefts, rights = ([], [])
    distance, missing = (1, REACH)
    while missing > 0:
        take = min(rows, missing)
        lefts.insert(0, passed_along(field[:, rows - take :], "tok", distance))
        rights.append(passed_along(field[:, :take], "tok", -distance))
        distance, missing = (distance + 1, missing - take)
    if len(lefts) == 1:
        return (lefts[0], rights[0])
    return (jnp.concatenate(lefts, axis=1), jnp.concatenate(rights, axis=1))


def returned_rows(own, low_pay, high_pay):
    rows = own.shape[1]
    distance, missing = (1, REACH)
    while missing > 0:
        take = min(rows, missing)
        low_piece = low_pay[:, missing - take : missing]
        begin = REACH - missing
        high_piece = high_pay[:, begin : begin + take]
        own = own.at[:, rows - take :].add(passed_along(low_piece, "tok", -distance).astype(wide))
        own = own.at[:, :take].add(passed_along(high_piece, "tok", distance).astype(wide))
        distance, missing = (distance + 1, missing - take)
    return own


def local(
    tokens,
    skip_features,
    crop_sides,
    ln1_gain,
    ln1_bias,
    qkv_weight,
    qv_bias,
    out_weight,
    out_bias,
    ln2_gain,
    ln2_bias,
    fc1_weight,
    fc1_bias,
    fc2_weight,
    fc2_bias,
    deconv_weight,
    conv1_weight,
    conv2_weight,
    conv3_weight,
    cotangent,
):
    seq_count, row_count, model_width = tokens.shape
    channels = conv2_weight.shape[2]
    hidden = fc1_weight.shape[1]
    reaches = (key_reach + row_count - 1) // row_count
    reach_rows = row_count + 2 * REACH
    near_left, near_right = near_rows(tokens)
    place, owner, crop_t, inverse, bias = geometry_tables(crop_sides, row_count)

    def flat(vector):
        return vector.reshape(1, -1)

    def block(lanes, kind, rows=row_count):
        return ((seq_count, rows, lanes), kind)

    qkv_bias = jnp.concatenate([qv_bias[0], jnp.zeros_like(qv_bias[0]), qv_bias[1]])
    matrix_flops = 2 * seq_count * row_count * model_width
    (
        normed_low, queries, keys, values, attended, log_totals, resid_one, normed_two,
        act_low, slope_low, resid_low, upsampled,
    ) = kernel_call(
        forward_kernel(row_count, model_width, hidden),
        seq_count,
        (tokens, near_left, near_right, bias),
        (
            flat(ln1_gain), flat(ln1_bias), qkv_weight, flat(qkv_bias), out_weight, flat(out_bias),
            flat(ln2_gain), flat(ln2_bias), fc1_weight, flat(fc1_bias), fc2_weight, flat(fc2_bias),
            deconv_weight,
        ),
        (
            block(model_width, low_type),
            block(model_width, low_type),
            block(model_width, low_type, reach_rows),
            block(model_width, low_type, reach_rows),
            block(model_width, low_type),
            block(row_count, wide, 16),
            block(model_width, wide),
            block(model_width, low_type),
            block(hidden, low_type),
            block(hidden, low_type),
            block(model_width, low_type),
            block(8 * channels, low_type),
        ),
        (),
        [
            pltpu.VMEM((reach_rows, model_width), low_type),
            pltpu.VMEM((model_width, reach_rows), low_type),
        ],
        matrix_flops * (8 * model_width + 2 * hidden + 8 * channels),
    )
    section_out, up_grad, skip_grad, conv1_grad, conv2_grad, conv3_grad = conv_section(
        upsampled,
        skip_features.reshape(seq_count, row_count, 8 * channels),
        cotangent.reshape(seq_count, row_count, 8 * channels),
        (conv1_weight, conv2_weight, conv3_weight),
        (place, owner, crop_t, inverse),
        reaches,
    )
    section_out = section_out.reshape(seq_count, row_count, 8, channels)
    skip_grad = skip_grad.reshape(seq_count, row_count, 8, channels)
    (
        branch_low, pre_low, resid_grad, mixed_low, query_grad, key_own, value_own, low_pay, high_pay,
        fc2_bias_grad, fc1_bias_grad, out_bias_grad, ln2_gain_grad, ln2_bias_grad,
    ) = kernel_call(
        backward_kernel(row_count, model_width, hidden),
        seq_count,
        (up_grad, slope_low, resid_one, queries, keys, values, log_totals, bias),
        (deconv_weight, fc2_weight, fc1_weight, out_weight, flat(ln2_gain)),
        (
            block(model_width, low_type),
            block(hidden, low_type),
            block(model_width, wide),
            block(model_width, low_type),
            block(model_width, low_type),
            block(model_width, wide),
            block(model_width, wide),
            block(2 * model_width, low_type, REACH),
            block(2 * model_width, low_type, REACH),
        ),
        (
            ((1, model_width), wide),
            ((1, hidden), wide),
            ((1, model_width), wide),
            ((1, model_width), wide),
            ((1, model_width), wide),
        ),
        [
            pltpu.VMEM((reach_rows, model_width), wide),
            pltpu.VMEM((reach_rows, model_width), wide),
            pltpu.VMEM((model_width, reach_rows), low_type),
            pltpu.VMEM((row_count, model_width), low_type),
        ],
        matrix_flops * (12 * model_width + 2 * hidden + 8 * channels),
    )
    joined = row_count >= REACH
    returned = ()
    if joined:
        returned = exchanged(low_pay, high_pay)
    else:
        both = jnp.concatenate([key_own, value_own], axis=-1)
        both = returned_rows(both, low_pay, high_pay)
        key_own, value_own = (both[:, :, :model_width], both[:, :, model_width:])
    qkv_grad_low, token_grad, column_sums, ln1_gain_grad, ln1_bias_grad = kernel_call(
        token_kernel(row_count, model_width, joined),
        seq_count,
        (tokens, resid_grad, query_grad, key_own, value_own) + tuple(returned),
        (qkv_weight, flat(ln1_gain)),
        (block(3 * model_width, low_type), block(model_width, wide)),
        (
            ((1, 3 * model_width), wide),
            ((1, model_width), wide),
            ((1, model_width), wide),
        ),
        [],
        matrix_flops * 3 * model_width,
    )

    def weight_product(left, right):
        return jnp.einsum(
            "rd,re->de",
            left.reshape(-1, left.shape[-1]),
            right.reshape(-1, right.shape[-1]),
            preferred_element_type=wide,
        )

    deconv_grad = weight_product(resid_low, up_grad)
    fc2_grad = weight_product(act_low, branch_low)
    fc1_grad = weight_product(normed_two, pre_low)
    out_grad = weight_product(attended, mixed_low)
    qkv_grad = weight_product(normed_low, qkv_grad_low)
    query_sums = column_sums[:, :model_width]
    value_sums = column_sums[:, 2 * model_width :]
    conv3_turned = jnp.moveaxis(conv3_grad.reshape(1, 2, channels, channels), 2, 3)
    conv_shares, shares, vectors = reduced_all(
        (conv1_grad, conv2_grad, conv3_turned),
        (deconv_grad, fc2_grad, fc1_grad, out_grad, qkv_grad),
        (
            ln1_gain_grad, ln1_bias_grad, query_sums, value_sums, out_bias_grad,
            ln2_gain_grad, ln2_bias_grad, fc1_bias_grad, fc2_bias_grad,
        ),
    )
    return (
        section_out,
        token_grad,
        skip_grad,
        vectors[0],
        vectors[1],
        shares[4],
        jnp.stack([vectors[2], vectors[3]]),
        shares[3],
        vectors[4],
        vectors[5],
        vectors[6],
        shares[2],
        vectors[7],
        shares[1],
        vectors[8],
        shares[0],
        conv_shares[0],
        conv_shares[1],
        conv_shares[2][0],
    )


def solution(mesh):
    in_specs = (
        P("seq", "tok", None),
        P("seq", "tok", None, None),
        P("seq", None),
        P(),
        P(),
        P(),
        P(),
        P(),
        P(),
        P(),
        P(),
        P(),
        P(),
        P(),
        P(),
        P(),
        P(),
        P(),
        P(),
        P("seq", "tok", None, None),
    )
    out_specs = (
        P("seq", "tok", None, None),
        P("seq", "tok", None),
        P("seq", "tok", None, None),
        P("tok"),
        P("tok"),
        P("tok", None),
        P(None, "tok"),
        P("tok", None),
        P("tok"),
        P("tok"),
        P("tok"),
        P("tok", None),
        P("tok"),
        P("tok", None),
        P("tok"),
        P("tok", None),
        P(None, None, "tok"),
        P(None, None, "tok"),
        P(None, "tok"),
    )
    return jax.shard_map(local, mesh=mesh, in_specs=in_specs, out_specs=out_specs, check_vma=False)
```

```python
from functools import partial
import math

import jax
import jax.numpy as jnp
import numpy as np
from jax import lax
from jax.experimental import pallas as pl
from jax.experimental.pallas import tpu as pltpu
from jax.sharding import PartitionSpec as P

HEADS = 12
HEAD_DIM = 64


side_small = 4
side_big = 6
halo_rows = 43
key_reach = 215
norm_eps = 1e-05
far_below = -1e30
highest = lax.Precision.HIGHEST
in_part = {-1: (1, 2), 0: (0, 2), 1: (0, 1)}
out_part = {-1: (0, 1), 0: (0, 2), 1: (1, 2)}


def passed_along(block, axis, distance):
    devices = range(lax.axis_size(axis))
    route = [(i - distance, i) for i in devices if i - distance in devices]
    return lax.ppermute(block, axis, route)


def all_offsets():
    step_values = (-1, 0, 1)
    return [
        (step_x, step_y, step_z)
        for step_x in step_values
        for step_y in step_values
        for step_z in step_values
    ]


EDGE = 48
WINDOW = 256
TILE = 128
CROP_ROWS = 48
SUBS = 8
VMEM_LIMIT = 60 * 1024 * 1024
lowest_step = {-1: -43, 0: -7, 1: 11}
low_type = jnp.bfloat16
wide = jnp.float32


def dot(left, right):
    return jnp.dot(left, right, preferred_element_type=wide)


def three_terms(field):
    first = field.astype(low_type)
    rest = field - first.astype(wide)
    second = rest.astype(low_type)
    third = (rest - second.astype(wide)).astype(low_type)
    return (first, second, third)


def exact_dot(chosen, field):
    first, second, third = three_terms(field)
    return dot(chosen, first) + dot(chosen, second) + dot(chosen, third)


def sub_lanes(number, width):
    return slice(number * width, (number + 1) * width)


def all_taps():
    return [(x, y, z) for x in range(3) for y in range(3) for z in range(3)]


def forward_band(weight, band_ref):
    inner, outer = weight.shape[1:]
    band_ref[...] = jnp.zeros_like(band_ref)
    for tap_x, tap_y, tap_z in all_taps():
        for side in range(2):
            rows = sub_lanes(tap_y * 4 + tap_z + side, inner)
            lanes = sub_lanes(side, outer)
            band_ref[tap_x, rows, lanes] = weight[tap_x * 9 + tap_y * 3 + tap_z]


def backward_band(weight, band_ref):
    inner, outer = weight.shape[1:]
    band_ref[...] = jnp.zeros_like(band_ref)
    for tap_x, tap_y, tap_z in all_taps():
        for side in range(2):
            rows = sub_lanes(side, inner)
            lanes = sub_lanes(tap_y * 4 + tap_z + side, outer)
            band_ref[tap_x, rows, lanes] = weight[26 - (tap_x * 9 + tap_y * 3 + tap_z)]


def once(fill, *refs):
    @pl.when(pl.program_id(0) == 0)
    def _():
        fill(*refs)


def window_positions(step):
    return {-1: ((0, 1),), 0: ((1, 0), (2, 1)), 1: ((3, 0),)}[step]


def fill_windows(x_ref, place_ref, p_ref, rows, width):
    tile = min(rows, TILE)
    for base in range(0, rows, tile):
        own = slice(base, base + tile)
        for number, (step_x, step_y, step_z) in enumerate(all_offsets()):
            low = (EDGE + base + lowest_step[step_x]) // 16 * 16
            centre = (step_x, step_y, step_z) == (0, 0, 0)
            if not centre:
                lane = lax.broadcasted_iota(jnp.int32, (tile, WINDOW), 1) + low
                chosen = jnp.where(lane == place_ref[0, own, number : number + 1], 1.0, 0.0)
                chosen = chosen.astype(low_type)
            for x_to, x_from in window_positions(step_x):
                for y_to, y_from in window_positions(step_y):
                    z_to, z_from = window_positions(step_z)[0]
                    count = (2 if step_z == 0 else 1) * width
                    to = ((x_to * 4 + y_to) * 4 + z_to) * width
                    source = (x_from * 4 + y_from * 2 + z_from) * width
                    if centre:
                        got = x_ref[EDGE + base : EDGE + base + tile, source : source + count]
                    else:
                        got = dot(chosen, x_ref[low : low + WINDOW, source : source + count])
                    p_ref[own, to : to + count] = got.astype(low_type)


def window_conv(p_ref, band_ref, pair, width, product):
    first, second = pair
    total = None
    for tap in range(3):
        begin = ((first + tap) * 4 + second) * 4 * width
        term = product(p_ref[:, begin : begin + 12 * width], band_ref[tap])
        total = term if total is None else total + term
    return total


def all_pairs():
    return [(first, second) for first in range(2) for second in range(2)]


def add_grads(left_ref, p_ref, total_ref, width, channels):
    for tap_x in range(3):
        for tap_y in range(3):
            term = None
            for number, (first, second) in enumerate(all_pairs()):
                begin = ((first + tap_x) * 4 + second + tap_y) * 4 * channels
                left = left_ref[number * 2 * width : (number + 1) * 2 * width, :]
                part = dot(left, p_ref[:, begin : begin + 4 * channels])
                term = part if term is None else term + part
            total_ref[tap_x * 3 + tap_y] += term


def fold_grads(total_ref, grad_ref, width, channels):
    for tap_x in range(3):
        for tap_y in range(3):
            for tap_z in range(3):
                number = tap_x * 3 + tap_y
                here = total_ref[number, :width, sub_lanes(tap_z, channels)]
                there = total_ref[number, width:, sub_lanes(tap_z + 1, channels)]
                tap = 26 - (number * 3 + tap_z)
                for half in range(width // channels):
                    rows = slice(half * channels, (half + 1) * channels)
                    grad_ref[tap, half] = jnp.transpose(here[rows] + there[rows])


def kernel_call(body, seqs, inputs, shared, outputs, summed, scratch, flops):
    def row_spec(shape):
        return pl.BlockSpec((1,) + tuple(shape[1:]), lambda i: (i,) + (0,) * (len(shape) - 1))

    def whole_spec(shape):
        return pl.BlockSpec(
            tuple(shape), lambda i: (0,) * len(shape), pipeline_mode=pl.Buffered(1)
        )

    moved = sum(math.prod(a.shape) * a.dtype.itemsize for a in list(inputs) + list(shared))
    moved += sum(math.prod(s) * jnp.dtype(t).itemsize for s, t in list(outputs) + list(summed))
    return pl.pallas_call(
        body,
        grid=(seqs,),
        in_specs=[row_spec(a.shape) for a in inputs] + [whole_spec(a.shape) for a in shared],
        out_specs=[row_spec(s) for s, _ in outputs] + [whole_spec(s) for s, _ in summed],
        out_shape=[jax.ShapeDtypeStruct(s, t) for s, t in list(outputs) + list(summed)],
        scratch_shapes=scratch,
        compiler_params=pltpu.CompilerParams(vmem_limit_bytes=VMEM_LIMIT),
        cost_estimate=pl.CostEstimate(flops=flops, bytes_accessed=moved, transcendentals=0),
    )(*inputs, *shared)


def conv_scratch(rows, width, band_shape):
    return [
        pltpu.VMEM((rows + 192, SUBS * width), low_type),
        pltpu.VMEM((rows, 64 * width), low_type),
        pltpu.VMEM((3,) + band_shape, low_type),
    ]


def conv_flops(seqs, rows, inner, outer):
    return 2 * seqs * rows * (36 * 4 * inner * 2 * outer + 56 * WINDOW * inner)


def put_edges(low_pay, high_pay, number, field, channels, rows):
    lanes = sub_lanes(number, channels)
    low_pay[0, :, lanes] = field[:EDGE].astype(low_type)
    high_pay[0, :, lanes] = field[rows - EDGE :].astype(low_type)


def put_sums(sums_ref, low_pay, high_pay, number, value, channels):
    lanes = sub_lanes(number, channels)
    sums_ref[0, :, lanes] = value
    pay_lanes = sub_lanes(SUBS + number, channels)
    low_pay[0, :, pay_lanes] = value.astype(low_type)
    high_pay[0, :, pay_lanes] = value.astype(low_type)


def taken_sums(sums_ref, left_pay, right_pay, number, channels):
    lanes = sub_lanes(number, channels)
    pay_lanes = sub_lanes(SUBS + number, channels)
    total = sums_ref[0, :, lanes] + left_pay[0, :, pay_lanes].astype(wide)
    return total + right_pay[0, :, pay_lanes].astype(wide)


def mean_and_scale(total, square, inverse):
    mean = total * inverse
    variance = jnp.maximum(square * inverse - mean * mean, 0.0)
    return (mean, lax.rsqrt(variance + norm_eps))


def silu_parts(value):
    gate = 1.0 / (1.0 + jnp.exp(-value))
    return (value * gate, gate * (1.0 + value * (1.0 - gate)))


def first_conv_kernel(rows, channels):
    width = 2 * channels

    def body(
        up, up_left, up_right, skip, skip_left, skip_right, place, crop_t, weight, side,
        first_out, side_out, sums, low_pay, high_pay, x_ref, p_ref, band_ref,
    ):
        once(forward_band, weight, band_ref)
        for number in range(SUBS):
            for half, (own, left, right) in enumerate(
                ((up, up_left, up_right), (skip, skip_left, skip_right))
            ):
                to = sub_lanes(2 * number + half, channels)
                lanes = sub_lanes(number, channels)
                x_ref[:EDGE, to] = left[0, :, lanes]
                x_ref[EDGE : EDGE + rows, to] = own[0, :, lanes]
                x_ref[EDGE + rows : 2 * EDGE + rows, to] = right[0, :, lanes]
        x_ref[2 * EDGE + rows :, :] = jnp.zeros((96, SUBS * width), low_type)
        fill_windows(x_ref, place, p_ref, rows, width)
        total = [jnp.zeros((rows, channels), wide) for _ in range(4)]
        for index, pair in enumerate(all_pairs()):
            result = window_conv(p_ref, band_ref, pair, width, dot)
            first_out[0, :, sub_lanes(index, width)] = result
            for half in range(2):
                number = 2 * index + half
                value = result[:, sub_lanes(half, channels)]
                put_edges(low_pay, high_pay, number, value, channels, rows)
                flat = dot(x_ref[EDGE : EDGE + rows, sub_lanes(number, width)], side[...])
                side_out[0, :, sub_lanes(number, channels)] = flat
                terms = (value, value * value, flat, flat * flat)
                total = [have + term for have, term in zip(total, terms)]
        for number in range(4):
            value = exact_dot(crop_t[0], total[number])
            put_sums(sums, low_pay, high_pay, number, value, channels)

    return body


def second_conv_kernel(rows, channels):
    def body(
        first, left_pay, right_pay, own_sums, inverse, owner, place, crop_t, weight,
        second_out, stats, sums, low_pay, high_pay, x_ref, p_ref, band_ref,
    ):
        once(forward_band, weight, band_ref)
        taken = [taken_sums(own_sums, left_pay, right_pay, n, channels) for n in range(4)]
        mean, scale = mean_and_scale(taken[0], taken[1], inverse[0])
        side_mean, side_scale = mean_and_scale(taken[2], taken[3], inverse[0])
        for number, value in enumerate((mean, scale, side_mean, side_scale)):
            stats[0, :, sub_lanes(number, channels)] = value
        mean_rows = exact_dot(owner[0], mean)
        scale_rows = exact_dot(owner[0], scale)
        parts = (
            (left_pay, slice(0, EDGE)),
            (first, slice(EDGE, EDGE + rows)),
            (right_pay, slice(EDGE + rows, 2 * EDGE + rows)),
        )
        for number in range(SUBS):
            lanes = sub_lanes(number, channels)
            for field, place_rows in parts:
                normed = field[0, :, lanes].astype(wide) - mean_rows[place_rows]
                normed = normed * scale_rows[place_rows]
                x_ref[place_rows, lanes] = silu_parts(normed)[0].astype(low_type)
        x_ref[2 * EDGE + rows :, :] = jnp.zeros((96, SUBS * channels), low_type)
        fill_windows(x_ref, place, p_ref, rows, channels)
        total = [jnp.zeros((rows, channels), wide) for _ in range(2)]
        for index, pair in enumerate(all_pairs()):
            result = window_conv(p_ref, band_ref, pair, channels, dot)
            second_out[0, :, sub_lanes(index, 2 * channels)] = result
            for half in range(2):
                value = result[:, sub_lanes(half, channels)]
                put_edges(low_pay, high_pay, 2 * index + half, value, channels, rows)
                total = [total[0] + value, total[1] + value * value]
        for number in range(2):
            value = exact_dot(crop_t[0], total[number])
            put_sums(sums, low_pay, high_pay, number, value, channels)

    return body


def output_kernel(rows, channels):
    def body(
        second, side_field, cotangent, stats, left_pay, right_pay, own_sums, inverse, owner, crop_t,
        section, grad_out, second_stats, sums, low_pay, high_pay,
    ):
        taken = [taken_sums(own_sums, left_pay, right_pay, n, channels) for n in range(2)]
        mean, scale = mean_and_scale(taken[0], taken[1], inverse[0])
        second_stats[0, :, sub_lanes(0, channels)] = mean
        second_stats[0, :, sub_lanes(1, channels)] = scale
        own = owner[0, EDGE : EDGE + rows, :]
        mean_rows = exact_dot(own, mean)
        scale_rows = exact_dot(own, scale)
        side_mean = exact_dot(own, stats[0, :, sub_lanes(2, channels)])
        side_scale = exact_dot(own, stats[0, :, sub_lanes(3, channels)])
        total = [jnp.zeros((rows, channels), wide) for _ in range(3)]
        for number in range(SUBS):
            lanes = sub_lanes(number, channels)
            normed = (second[0, :, lanes] - mean_rows) * scale_rows
            side = (side_field[0, :, lanes] - side_mean) * side_scale
            value, slope = silu_parts(normed + side)
            section[0, :, lanes] = value.astype(low_type)
            grad = cotangent[0, :, lanes].astype(wide) * slope
            grad_out[0, :, lanes] = grad
            put_edges(low_pay, high_pay, number, grad, channels, rows)
            terms = (grad, grad * normed, grad * side)
            total = [have + term for have, term in zip(total, terms)]
        for number in range(3):
            value = exact_dot(crop_t[0], total[number])
            put_sums(sums, low_pay, high_pay, number, value, channels)

    return body


def second_back_kernel(rows, channels, seqs):
    def body(
        grad, grad_left, grad_right, own_sums, second, second_left, second_right, side_field, first,
        stats, second_stats, inverse, owner, place, crop_t, weight,
        first_grad, side_grad, sums, low_pay, high_pay, weight_grad,
        x_ref, p_ref, band_ref, left_ref, total_ref,
    ):
        once(backward_band, weight, band_ref)
        means = [
            taken_sums(own_sums, grad_left, grad_right, n, channels) * inverse[0] for n in range(3)
        ]
        mean_rows = exact_dot(owner[0], second_stats[0, :, sub_lanes(0, channels)])
        scale_rows = exact_dot(owner[0], second_stats[0, :, sub_lanes(1, channels)])
        lead_rows = exact_dot(owner[0], means[0])
        slope_rows = exact_dot(owner[0], means[1])
        parts = (
            (grad_left, second_left, slice(0, EDGE)),
            (grad, second, slice(EDGE, EDGE + rows)),
            (grad_right, second_right, slice(EDGE + rows, 2 * EDGE + rows)),
        )
        own = slice(EDGE, EDGE + rows)
        side_mean = exact_dot(owner[0, own, :], stats[0, :, sub_lanes(2, channels)])
        side_scale = exact_dot(owner[0, own, :], stats[0, :, sub_lanes(3, channels)])
        side_slope = exact_dot(owner[0, own, :], means[2])
        first_mean = exact_dot(owner[0, own, :], stats[0, :, sub_lanes(0, channels)])
        first_scale = exact_dot(owner[0, own, :], stats[0, :, sub_lanes(1, channels)])
        for number in range(SUBS):
            lanes = sub_lanes(number, channels)
            for grad_from, field, at in parts:
                normed = (field[0, :, lanes].astype(wide) - mean_rows[at]) * scale_rows[at]
                pulled = grad_from[0, :, lanes].astype(wide) - lead_rows[at]
                pulled = scale_rows[at] * (pulled - normed * slope_rows[at])
                x_ref[at, lanes] = pulled.astype(low_type)
            side = (side_field[0, :, lanes] - side_mean) * side_scale
            pulled = side_scale * (grad[0, :, lanes] - lead_rows[own] - side * side_slope)
            side_grad[0, :, lanes] = pulled.astype(low_type)
            normed = (first[0, :, lanes] - first_mean) * first_scale
            hidden = silu_parts(normed)[0]
            left_ref[lanes, :] = jnp.transpose(hidden).astype(low_type)
        x_ref[2 * EDGE + rows :, :] = jnp.zeros((96, SUBS * channels), low_type)
        fill_windows(x_ref, place, p_ref, rows, channels)
        total = [jnp.zeros((rows, channels), wide) for _ in range(2)]
        for index, pair in enumerate(all_pairs()):
            result = window_conv(p_ref, band_ref, pair, channels, dot_t)
            for half in range(2):
                number = 2 * index + half
                lanes = sub_lanes(number, channels)
                normed = (first[0, :, lanes] - first_mean) * first_scale
                value = result[:, sub_lanes(half, channels)] * silu_parts(normed)[1]
                first_grad[0, :, lanes] = value
                put_edges(low_pay, high_pay, number, value, channels, rows)
                total = [total[0] + value, total[1] + value * normed]
        for number in range(2):
            value = exact_dot(crop_t[0], total[number])
            put_sums(sums, low_pay, high_pay, number, value, channels)

        @pl.when(pl.program_id(0) == 0)
        def _():
            total_ref[...] = jnp.zeros_like(total_ref)

        add_grads(left_ref, p_ref, total_ref, channels, channels)

        @pl.when(pl.program_id(0) == seqs - 1)
        def _():
            fold_grads(total_ref, weight_grad, channels, channels)

    return body


def first_back_kernel(rows, channels, seqs):
    width = 2 * channels

    def body(
        grad, grad_left, grad_right, own_sums, first, first_left, first_right, stats, inverse, owner,
        place, side_grad, up, skip, weight, side_weight,
        up_grad, skip_grad, weight_grad, side_weight_grad,
        x_ref, p_ref, band_ref, left_ref, total_ref,
    ):
        once(backward_band, weight, band_ref)
        means = [
            taken_sums(own_sums, grad_left, grad_right, n, channels) * inverse[0] for n in range(2)
        ]
        mean_rows = exact_dot(owner[0], stats[0, :, sub_lanes(0, channels)])
        scale_rows = exact_dot(owner[0], stats[0, :, sub_lanes(1, channels)])
        lead_rows = exact_dot(owner[0], means[0])
        slope_rows = exact_dot(owner[0], means[1])
        parts = (
            (grad_left, first_left, slice(0, EDGE)),
            (grad, first, slice(EDGE, EDGE + rows)),
            (grad_right, first_right, slice(EDGE + rows, 2 * EDGE + rows)),
        )
        for number in range(SUBS):
            lanes = sub_lanes(number, channels)
            for grad_from, field, at in parts:
                normed = (field[0, :, lanes].astype(wide) - mean_rows[at]) * scale_rows[at]
                pulled = grad_from[0, :, lanes].astype(wide) - lead_rows[at]
                pulled = scale_rows[at] * (pulled - normed * slope_rows[at])
                x_ref[at, lanes] = pulled.astype(low_type)
            for half, field in enumerate((up, skip)):
                turned = jnp.transpose(field[0, :, lanes].astype(wide)).astype(low_type)
                left_ref[sub_lanes(2 * number + half, channels), :] = turned
        x_ref[2 * EDGE + rows :, :] = jnp.zeros((96, SUBS * channels), low_type)
        fill_windows(x_ref, place, p_ref, rows, channels)
        for index, pair in enumerate(all_pairs()):
            result = window_conv(p_ref, band_ref, pair, channels, dot_t)
            for half in range(2):
                number = 2 * index + half
                lanes = sub_lanes(number, channels)
                value = result[:, sub_lanes(half, width)]
                value = value + dot_t(side_grad[0, :, lanes], side_weight[...])
                up_grad[0, :, lanes] = value[:, :channels].astype(low_type)
                skip_grad[0, :, lanes] = value[:, channels:]

        @pl.when(pl.program_id(0) == 0)
        def _():
            total_ref[...] = jnp.zeros_like(total_ref)
            side_weight_grad[...] = jnp.zeros_like(side_weight_grad)

        for number in range(SUBS):
            side_weight_grad[...] += dot(
                left_ref[sub_lanes(number, width), :], side_grad[0, :, sub_lanes(number, channels)]
            )
        add_grads(left_ref, p_ref, total_ref, width, channels)

        @pl.when(pl.program_id(0) == seqs - 1)
        def _():
            fold_grads(total_ref, weight_grad, width, channels)

    return body


def exchanged(low_pay, high_pay):
    return (passed_along(high_pay, "tok", 1), passed_along(low_pay, "tok", -1))


def with_far(sums, reaches):
    total = sums
    for distance in range(2, reaches + 1):
        for shift_by in (distance, -distance):
            total = total + passed_along(sums.astype(low_type), "tok", shift_by).astype(wide)
    return total


def conv_section(upsampled, skip, cotangent, weights, geometry_in, reaches):
    conv1_weight, conv2_weight, conv3_weight = weights
    seqs, rows, lanes = upsampled.shape
    channels = lanes // SUBS
    width = 2 * channels
    place, owner, crop_t, inverse = geometry_in
    field = ((seqs, rows, lanes), wide)
    low_field = ((seqs, rows, lanes), low_type)

    def pay(count):
        return ((seqs, EDGE, (SUBS + count) * channels), low_type)

    def table(count):
        return ((seqs, CROP_ROWS, count * channels), wide)

    skip_left, skip_right = exchanged(skip[:, :EDGE], skip[:, rows - EDGE :])
    up_left, up_right = exchanged(upsampled[:, :EDGE], upsampled[:, rows - EDGE :])
    first, side_field, sums, low_pay, high_pay = kernel_call(
        first_conv_kernel(rows, channels),
        seqs,
        (upsampled, up_left, up_right, skip, skip_left, skip_right, place, crop_t),
        (conv1_weight, conv3_weight),
        (field, field, table(4), pay(4), pay(4)),
        (),
        conv_scratch(rows, width, (12 * width, 2 * channels)),
        conv_flops(seqs, rows, width, channels),
    )
    first_left, first_right = exchanged(low_pay, high_pay)
    second, stats, sums, low_pay, high_pay = kernel_call(
        second_conv_kernel(rows, channels),
        seqs,
        (first, first_left, first_right, with_far(sums, reaches), inverse, owner, place, crop_t),
        (conv2_weight,),
        (field, table(4), table(2), pay(2), pay(2)),
        (),
        conv_scratch(rows, channels, (12 * channels, 2 * channels)),
        conv_flops(seqs, rows, channels, channels),
    )
    second_left, second_right = exchanged(low_pay, high_pay)
    section_out, grad, second_stats, sums, low_pay, high_pay = kernel_call(
        output_kernel(rows, channels),
        seqs,
        (
            second, side_field, cotangent, stats, second_left, second_right,
            with_far(sums, reaches), inverse, owner, crop_t,
        ),
        (),
        (low_field, field, table(2), table(3), pay(3), pay(3)),
        (),
        [],
        seqs * rows * lanes * 20,
    )
    grad_left, grad_right = exchanged(low_pay, high_pay)
    first_grad, side_grad, sums, low_pay, high_pay, conv2_grad = kernel_call(
        second_back_kernel(rows, channels, seqs),
        seqs,
        (
            grad, grad_left, grad_right, with_far(sums, reaches), second, second_left, second_right,
            side_field, first, stats, second_stats, inverse, owner, place, crop_t,
        ),
        (conv2_weight,),
        (field, low_field, table(2), pay(2), pay(2)),
        (((27, 1, channels, channels), wide),),
        conv_scratch(rows, channels, (2 * channels, 12 * channels))
        + [
            pltpu.VMEM((SUBS * channels, rows), low_type),
            pltpu.VMEM((9, 2 * channels, 4 * channels), wide),
        ],
        2 * conv_flops(seqs, rows, channels, channels),
    )
    back_left, back_right = exchanged(low_pay, high_pay)
    up_grad, skip_grad, conv1_grad, conv3_grad = kernel_call(
        first_back_kernel(rows, channels, seqs),
        seqs,
        (
            first_grad, back_left, back_right, with_far(sums, reaches), first, first_left,
            first_right, stats, inverse, owner, place, side_grad, upsampled, skip,
        ),
        (conv1_weight, conv3_weight),
        (low_field, field),
        (((27, 2, channels, channels), wide), ((width, channels), wide)),
        conv_scratch(rows, channels, (2 * width, 12 * channels))
        + [
            pltpu.VMEM((SUBS * width, rows), low_type),
            pltpu.VMEM((9, 2 * width, 4 * channels), wide),
        ],
        2 * conv_flops(seqs, rows, channels, width),
    )
    return (section_out, up_grad, skip_grad, conv1_grad, conv2_grad, conv3_grad)


PIECE_BYTES = 2400 * 1024


def bit_count(size):
    return size.bit_length() - 1


def pieces_of(shapes):
    pieces = []
    for index, (shards, rows, lanes) in enumerate(shapes):
        parts = max(1, round(shards * rows * lanes * 2 / PIECE_BYTES))
        while rows % (16 * parts) != 0 and parts > 1:
            parts -= 1
        take = rows // parts
        pieces.extend((index, part * take, take, lanes) for part in range(parts))
    return pieces


def all_of(count):
    return (slice(None),) * count


def reduce_kernel(pieces, arrays, tok_bits, seq_bits):
    phases = tok_bits + seq_bits
    mesh_id = pl.DeviceIdType.MESH

    def body(*refs):
        given = refs[:arrays]
        results = refs[arrays : 2 * arrays]
        count = len(pieces)
        rest = refs[2 * arrays :]
        kept = rest[:count]
        landed = [rest[count + i * phases : count + (i + 1) * phases] for i in range(count)]
        local_sem, send_sem, recv_sem = rest[count + count * phases :]
        tok = lax.axis_index("tok")
        seq = lax.axis_index("seq")

        def bit_of(phase):
            if phase < tok_bits:
                return (tok // (1 << phase)) % 2
            return (seq // (1 << (phase - tok_bits))) % 2

        def partner(phase):
            bit = bit_of(phase)
            if phase < tok_bits:
                return (seq, tok + (1 << phase) * (1 - 2 * bit))
            return (seq + (1 << (phase - tok_bits)) * (1 - 2 * bit), tok)

        barrier = pltpu.get_barrier_semaphore()
        for phase in range(phases):
            pl.semaphore_signal(barrier, inc=1, device_id=partner(phase), device_id_type=mesh_id)
        pl.semaphore_wait(barrier, phases)

        def local_copy(piece):
            index, begin, take, _ = pieces[piece]
            view = given[index].at[all_of(tok_bits - 1) + (bit_of(0), pl.ds(begin, take))]
            return pltpu.make_async_copy(view, kept[piece], local_sem.at[piece])

        def remote_copy(piece, phase):
            index, begin, take, _ = pieces[piece]
            if phase == 0:
                view = given[index].at[all_of(tok_bits - 1) + (1 - bit_of(0), pl.ds(begin, take))]
            elif phase < tok_bits:
                view = landed[piece][phase - 1].at[all_of(tok_bits - 1 - phase) + (1 - bit_of(phase),)]
            else:
                view = landed[piece][phase - 1]
            return pltpu.make_async_remote_copy(
                src_ref=view,
                dst_ref=landed[piece][phase],
                send_sem=send_sem.at[piece, phase],
                recv_sem=recv_sem.at[piece, phase],
                device_id=partner(phase),
                device_id_type=mesh_id,
            )

        def begin(piece):
            remote_copy(piece, 0).start()
            local_copy(piece).start()

        def finish(piece, phase):
            index, first, take, _ = pieces[piece]
            remote_copy(piece, phase).wait_recv()
            got = landed[piece][phase]
            if phase == 0:
                local_copy(piece).wait()

            if phase < tok_bits:
                kept_bits = tok_bits - 1 - phase

                def step(block, carry):
                    at = tuple((block // (1 << bit)) % 2 for bit in reversed(range(kept_bits)))
                    if phase == 0:
                        mine = kept[piece][at]
                    else:
                        mine = landed[piece][phase - 1][at + (bit_of(phase),)]
                    got[at] = got[at] + mine
                    return carry

                lax.fori_loop(0, 1 << kept_bits, step, 0)
            elif phase + 1 < phases:
                got[...] = got[...] + landed[piece][phase - 1][...]
            if phase + 1 < phases:
                remote_copy(piece, phase + 1).start()
            else:
                total = got[...].astype(wide) + landed[piece][phase - 1][...].astype(wide)
                results[index][pl.ds(first, take), :] = total

        begin(0)
        for step in range(count + phases - 1):
            if step + 1 < count:
                begin(step + 1)
            for phase in range(phases):
                if 0 <= step - phase < count:
                    finish(step - phase, phase)
        for piece in range(count):
            for phase in range(phases):
                remote_copy(piece, phase).wait_send()

    return body


def reduced(grads):
    shards = lax.axis_size("tok")
    tok_bits = bit_count(shards)
    seq_bits = bit_count(lax.axis_size("seq"))
    shapes = [g.shape for g in grads]
    pieces = pieces_of(shapes)
    scratch = [
        pltpu.VMEM((2,) * (tok_bits - 1) + (take, lanes), low_type) for _, _, take, lanes in pieces
    ]
    for _, _, take, lanes in pieces:
        for phase in range(tok_bits - 1):
            bits = tok_bits - 1 - phase
            scratch.append(pltpu.VMEM((2,) * bits + (take, lanes), low_type))
        scratch += [pltpu.VMEM((take, lanes), low_type) for _ in range(1 + seq_bits)]
    count, phases = len(pieces), tok_bits + seq_bits
    scratch += [
        pltpu.SemaphoreType.DMA((count,)),
        pltpu.SemaphoreType.DMA((count, phases)),
        pltpu.SemaphoreType.DMA((count, phases)),
    ]
    total = sum(math.prod(s) for s in shapes)
    return pl.pallas_call(
        reduce_kernel(pieces, len(grads), tok_bits, seq_bits),
        in_specs=[pl.BlockSpec(memory_space=pl.ANY)] * len(grads),
        out_specs=[pl.BlockSpec(memory_space=pltpu.VMEM)] * len(grads),
        out_shape=[jax.ShapeDtypeStruct(s[1:], wide) for s in shapes],
        scratch_shapes=scratch,
        compiler_params=pltpu.CompilerParams(
            vmem_limit_bytes=VMEM_LIMIT, collective_id=0, has_side_effects=True
        ),
        cost_estimate=pl.CostEstimate(flops=total, bytes_accessed=4 * total, transcendentals=0),
    )(*[g.reshape((2,) * tok_bits + g.shape[1:]) for g in grads])


def sharded_rows(grad):
    shards = lax.axis_size("tok")
    rows = grad.shape[0] // shards
    grad = grad.astype(low_type)
    if rows % 16 == 0:
        return grad.reshape(shards, rows, grad.shape[1])
    return grad.reshape(shards, rows * grad.shape[1] // 128, 128)


def conv_rows(turned):
    shards = lax.axis_size("tok")
    taps, halves, channels, lanes = turned.shape
    split = turned.reshape(taps, halves, shards, channels // shards, lanes)
    return jnp.moveaxis(split, 2, 0).reshape(shards, -1, lanes)


def conv_share(rows, taps, halves):
    split = rows.reshape(taps, halves, -1, rows.shape[-1])
    return jnp.moveaxis(split, 2, 3).reshape(taps, halves * rows.shape[-1], -1)


def reduced_all(conv_grads, matrices, vectors):
    shards = lax.axis_size("tok")
    parts = [conv_rows(g) for g in conv_grads]
    flat = jnp.concatenate([v.reshape(shards, -1) for v in vectors], axis=1)
    used = flat.shape[1]
    taken = sum(p.shape[1] for p in parts)
    rows = -(-used // 128)
    rows += -(rows + taken) % 16
    flat = jnp.pad(flat, ((0, 0), (0, rows * 128 - used))).reshape(shards, rows, 128)
    packed = jnp.concatenate([p.astype(low_type) for p in parts] + [flat.astype(low_type)], axis=1)
    results = reduced([packed] + [sharded_rows(m) for m in matrices])
    shares = []
    cursor = 0
    for part, grad in zip(parts, conv_grads):
        rows_here = results[0][cursor : cursor + part.shape[1]]
        shares.append(conv_share(rows_here, grad.shape[0], grad.shape[1]))
        cursor += part.shape[1]
    flat = results[0][cursor:].reshape(-1)
    cursor = 0
    pieces = []
    for vector in vectors:
        size = vector.size // shards
        pieces.append(flat[cursor : cursor + size])
        cursor += size
    whole = [r.reshape(-1, m.shape[1]) for r, m in zip(results[1:], matrices)]
    return (shares, whole, pieces)


REACH = 224
QUERY_TILE = 128
AHEAD = 3
CLOSING_LIMIT = 63 * 1024 * 1024


def dot_t(left, right):
    return lax.dot_general(
        left, right, (((1,), (1,)), ((), ())), preferred_element_type=wide
    )


def counted(shape, axis):
    return lax.broadcasted_iota(jnp.int32, shape, axis).astype(wide)


def geometry_kernel(rows, crops):
    reach_rows = rows + 2 * REACH
    tile = min(rows, QUERY_TILE)
    window = tile + 2 * REACH

    def body(side_row, side_column, place, owner, crop_t, inverse, bias, edge_bias):
        first_row = (lax.axis_index("tok") * rows).astype(wide)
        sides_r = side_row[0].astype(wide)
        sides_c = side_column[0].astype(wide)
        volume_r = sides_r * sides_r * sides_r
        volume_c = sides_c * sides_c * sides_c
        shape = (crops, crops)
        start_r = jnp.sum(
            jnp.where(counted(shape, 0) < counted(shape, 1), volume_c, 0.0), axis=0, keepdims=True
        )
        start_c = jnp.sum(
            jnp.where(counted(shape, 1) < counted(shape, 0), volume_r, 0.0), axis=1, keepdims=True
        )

        def inside_of(length, begin):
            at = counted((length, crops), 0) + begin
            return ((at >= start_r) & (at < start_r + volume_r), at)

        wide_inside, _ = inside_of(rows + 2 * EDGE, first_row - EDGE)
        owner[0] = jnp.where(wide_inside, 1.0, 0.0).astype(low_type)
        inside, _ = inside_of(rows, first_row)
        side = jnp.sum(jnp.where(inside, sides_r, 0.0), axis=1, keepdims=True)
        first = jnp.sum(jnp.where(inside, start_r, 0.0), axis=1, keepdims=True)
        own = counted((rows, 1), 0)
        offset = own + first_row - first
        safe = jnp.maximum(side, 1.0)
        row_pos = jnp.floor((offset + 0.5) / (safe * safe))
        offset = offset - row_pos * safe * safe
        column = jnp.floor((offset + 0.5) / safe)
        depth_pos = offset - column * safe
        lane = counted((1, 32), 1)
        step_x = jnp.floor((lane + 0.5) / 9.0)
        step_y = jnp.floor((lane - 9.0 * step_x + 0.5) / 3.0)
        step_z = lane - 9.0 * step_x - 3.0 * step_y - 1.0
        step_x, step_y = (step_x - 1.0, step_y - 1.0)
        valid = None
        for at, step in ((row_pos, step_x), (column, step_y), (depth_pos, step_z)):
            moved = at + step
            here = (moved >= 0.0) & (moved < side)
            valid = here if valid is None else valid & here
        target = own + EDGE + (step_x * safe + step_y) * safe + step_z
        place[0] = jnp.where(valid, target, -1.0).astype(jnp.int32)
        at = counted((crops, rows), 1) + first_row
        inside_t = (at >= start_c) & (at < start_c + volume_c)
        crop_t[0] = jnp.where(inside_t, 1.0, 0.0).astype(low_type)
        inverse[0] = jnp.broadcast_to(1.0 / jnp.maximum(8.0 * volume_c, 1.0), (crops, 128))
        key_inside, _ = inside_of(reach_rows, first_row - REACH)
        key_first = jnp.sum(jnp.where(key_inside, start_r + 1.0, 0.0), axis=1, keepdims=True)
        query_first = jnp.sum(jnp.where(inside_t, start_c + 1.0, 0.0), axis=0, keepdims=True)
        for number in range(rows // tile):
            base = number * tile
            same = key_first[base : base + window] == query_first[:, base : base + tile]
            bias[0, number] = jnp.where(same, 0.0, far_below)
        for side in range(2):
            begin_row = 0 if side == 0 else max(rows - REACH, 0)
            begin = first_row - REACH if side == 0 else first_row + rows
            at = counted((crops, REACH), 1) + begin
            inside_t = (at >= start_c) & (at < start_c + volume_c)
            query_first = jnp.sum(jnp.where(inside_t, start_c + 1.0, 0.0), axis=0, keepdims=True)
            same = key_first[REACH + begin_row : 2 * REACH + begin_row] == query_first
            edge_bias[0, side] = jnp.where(same, 0.0, far_below)

    return body


def geometry_tables(crop_sides, rows):
    seqs, crops = crop_sides.shape
    sides = jnp.pad(crop_sides, ((0, 0), (0, CROP_ROWS - crops)))
    tile = min(rows, QUERY_TILE)
    return kernel_call(
        geometry_kernel(rows, CROP_ROWS),
        seqs,
        (sides[:, None, :], sides[:, :, None]),
        (),
        (
            ((seqs, rows, 32), jnp.int32),
            ((seqs, rows + 2 * EDGE, CROP_ROWS), low_type),
            ((seqs, CROP_ROWS, rows), low_type),
            ((seqs, CROP_ROWS, 128), wide),
            ((seqs, rows // tile, tile + 2 * REACH, tile), wide),
            ((seqs, 2, REACH, REACH), wide),
        ),
        (),
        [],
        0,
    )


def normed_rows(values):
    centered = values - jnp.mean(values, axis=-1, keepdims=True)
    variance = jnp.mean(centered * centered, axis=-1, keepdims=True)
    scale = lax.rsqrt(variance + norm_eps)
    return (centered * scale, scale)


def norm_pull(grad, normed, scale, gain):
    inner = grad * gain
    first = jnp.mean(inner, axis=-1, keepdims=True)
    second = jnp.mean(inner * normed, axis=-1, keepdims=True)
    return scale * (inner - first - normed * second)


def error_function(value):
    bounded = jnp.clip(value, -3.832506856900711, 3.832506856900711)
    square = bounded * bounded
    top = 0.00022905065861350646
    for term in (0.0034082910107109506, 0.050955695062380861, 0.18520832239976145, 1.128379143519084):
        top = top * square + term
    bottom = -1.1791602954361697e-7
    for term in (
        0.000023547966471313185, 0.0010179625278914885, 0.014070470171167667,
        0.11098505178285362, 0.49746925110067538, 1.0,
    ):
        bottom = bottom * square + term
    return bounded * top / bottom


def gelu_parts(value):
    cumulative = 0.5 + 0.5 * error_function(value * math.sqrt(0.5))
    density = jnp.exp(-0.5 * value * value) * (1.0 / math.sqrt(2.0 * math.pi))
    return (value * cumulative, cumulative + value * density)


def head_lanes(block, half):
    lane = lax.broadcasted_iota(jnp.int32, block.shape, 1)
    chosen = lane < HEAD_DIM if half == 0 else lane >= HEAD_DIM
    return jnp.where(chosen, block, jnp.zeros_like(block))


def turned(block):
    return jnp.transpose(block.astype(wide))


def forward_kernel(rows, model_width, hidden):
    tile = min(rows, QUERY_TILE)
    window = tile + 2 * REACH
    chunk = 768
    scale = 1.0 / math.sqrt(HEAD_DIM)

    def body(
        tokens, left, right, bias, ln1_gain, ln1_bias, qkv_weight, qkv_bias, out_weight, out_bias,
        ln2_gain, ln2_bias, fc1_weight, fc1_bias, fc2_weight, fc2_bias, deconv_weight,
        normed_out, queries, keys, values, attended, log_totals, resid_out, second_out,
        act_out, slope_out, resid_low, upsampled, near_ref, turned_ref,
    ):
        begin = 0
        for field in (left, tokens, right):
            length = field.shape[1]
            normed = normed_rows(field[0].astype(wide))[0] * ln1_gain[...] + ln1_bias[...]
            near_ref[begin : begin + length, :] = normed.astype(low_type)
            begin += length
        own = near_ref[REACH : REACH + rows, :]
        normed_out[0] = own
        part = slice(0, model_width)
        queries[0] = (dot(near_ref[...], qkv_weight[:, part]) + qkv_bias[:, part]).astype(low_type)
        part = slice(model_width, 2 * model_width)
        keys[0] = (dot(near_ref[...], qkv_weight[:, part]) + qkv_bias[:, part]).astype(low_type)
        part = slice(2 * model_width, 3 * model_width)
        found = dot(near_ref[...], qkv_weight[:, part]) + qkv_bias[:, part]
        values[0] = found.astype(low_type)
        for pair in range(model_width // 128):
            lanes = sub_lanes(pair, 128)
            turned_ref[lanes, :] = turned(values[0, :, lanes]).astype(low_type)
        for number in range(rows // tile):
            base = number * tile
            at = slice(base, base + tile)
            near = slice(base, base + window)
            for pair in range(model_width // 128):
                lanes = sub_lanes(pair, 128)
                query = queries[0, REACH + base : REACH + base + tile, lanes] * scale
                key = keys[0, near, lanes]
                halves = []
                for half in range(2):
                    head = 2 * pair + half
                    scores = dot_t(key, head_lanes(query, half)) + bias[0, number]
                    top = jnp.max(scores, axis=0, keepdims=True)
                    weights = jnp.exp(scores - top)
                    total = jnp.sum(weights, axis=0, keepdims=True)
                    log_totals[0, head : head + 1, at] = top + jnp.log(total)
                    probs = (weights * (1.0 / total)).astype(low_type)
                    value = turned_ref[head * HEAD_DIM : (head + 1) * HEAD_DIM, near]
                    halves.append(dot(value, probs))
                both = jnp.concatenate(halves, axis=0)
                attended[0, at, lanes] = jnp.transpose(both).astype(low_type)
        resid = tokens[0].astype(wide) + dot(attended[0], out_weight[...]) + out_bias[...]
        resid_out[0] = resid
        second = normed_rows(resid)[0] * ln2_gain[...] + ln2_bias[...]
        second_out[0] = second.astype(low_type)
        total = resid + fc2_bias[...]
        for number in range(hidden // chunk):
            lanes = sub_lanes(number, chunk)
            pre = dot(second_out[0], fc1_weight[:, lanes]) + fc1_bias[:, lanes]
            act, slope = gelu_parts(pre)
            act_out[0, :, lanes] = act.astype(low_type)
            slope_out[0, :, lanes] = slope.astype(low_type)
            total = total + dot(act_out[0, :, lanes], fc2_weight[lanes, :])
        resid_low[0] = total.astype(low_type)
        upsampled[0] = dot(resid_low[0], deconv_weight[...]).astype(low_type)

    return body


def hidden_back_kernel(rows, model_width, hidden):
    chunk = 768

    def body(
        up_grad, slope, resid, attended, log_totals,
        deconv_weight, fc2_weight, fc1_weight, out_weight, ln2_gain,
        branch_out, pre_out, resid_grad, mixed_out, pulled_out, stats,
        fc2_sum, fc1_sum, out_sum, gain_sum, shift_sum,
    ):
        @pl.when(pl.program_id(0) == 0)
        def _():
            for ref in (fc2_sum, fc1_sum, out_sum, gain_sum, shift_sum):
                ref[...] = jnp.zeros_like(ref)

        def column_sum(field):
            return jnp.sum(field, axis=0, keepdims=True)

        incoming = dot_t(up_grad[0], deconv_weight[...])
        branch = incoming.astype(low_type)
        branch_out[0] = branch
        fc2_sum[...] += column_sum(branch.astype(wide))
        total = None
        for number in range(hidden // chunk):
            lanes = sub_lanes(number, chunk)
            act_grad = dot_t(branch_out[0], fc2_weight[lanes, :])
            pre = (act_grad * slope[0, :, lanes].astype(wide)).astype(low_type)
            pre_out[0, :, lanes] = pre
            fc1_sum[:, lanes] += column_sum(pre.astype(wide))
            term = dot_t(pre_out[0, :, lanes], fc1_weight[:, lanes])
            total = term if total is None else total + term
        normed, norm_scale = normed_rows(resid[0])
        gain_sum[...] += column_sum(total * normed)
        shift_sum[...] += column_sum(total)
        mixed = incoming + norm_pull(total, normed, norm_scale, ln2_gain[...])
        resid_grad[0] = mixed
        mixed = mixed.astype(low_type)
        mixed_out[0] = mixed
        out_sum[...] += column_sum(mixed.astype(wide))
        pulled = dot_t(mixed_out[0], out_weight[...]).astype(low_type)
        pulled_out[0] = pulled
        product = pulled.astype(wide) * attended[0].astype(wide)
        lane = lax.broadcasted_iota(jnp.int32, (16, model_width), 1)
        begin = lax.broadcasted_iota(jnp.int32, (16, model_width), 0) * HEAD_DIM
        chosen = (lane >= begin) & (lane < begin + HEAD_DIM)
        chosen = jnp.where(chosen, 1.0, 0.0).astype(low_type)
        inner = None
        for term in three_terms(product):
            part = dot_t(chosen, term)
            inner = part if inner is None else inner + part
        for pair in range(model_width // 128):
            heads = slice(2 * pair, 2 * pair + 2)
            unused = jnp.zeros((4, rows), wide)
            stats[0, pair] = jnp.concatenate([log_totals[0, heads], inner[heads], unused], axis=0)

    return body


def attention_back_kernel(rows, model_width):
    tile = min(rows, QUERY_TILE)
    window = tile + 2 * REACH
    scale = 1.0 / math.sqrt(HEAD_DIM)

    def body(
        queries, keys, values, pulls, stats, bias,
        query_grad, key_own, value_own, low_pay, high_pay, near_key, near_value, turned_ref,
    ):
        for pair in range(model_width // 128):
            lanes = sub_lanes(pair, 128)
            turned_ref[lanes, :] = turned(keys[0, :, lanes]).astype(low_type)
        near_key[...] = jnp.zeros_like(near_key)
        near_value[...] = jnp.zeros_like(near_value)
        for number in range(rows // tile):
            base = number * tile
            at = slice(base, base + tile)
            near = slice(base, base + window)
            for pair in range(model_width // 128):
                lanes = sub_lanes(pair, 128)
                query = queries[0, REACH + base : REACH + base + tile, lanes] * scale
                key = keys[0, near, lanes]
                value = values[0, near, lanes]
                halves = []
                for half in range(2):
                    head = 2 * pair + half
                    probs, score_grad, one_query, one_pull = head_unit(
                        key, value, query, pulls[0, at, lanes], bias[0, number],
                        stats[0, pair, half : half + 1, at], stats[0, pair, 2 + half : 3 + half, at],
                        half,
                    )
                    near_key[near, lanes] += dot(score_grad, one_query)
                    near_value[near, lanes] += dot(probs, one_pull)
                    key_turned = turned_ref[head * HEAD_DIM : (head + 1) * HEAD_DIM, near]
                    halves.append(dot(key_turned, score_grad) * scale)
                both = jnp.concatenate(halves, axis=0)
                query_grad[0, at, lanes] = jnp.transpose(both).astype(low_type)
        for field, own_out, begin in (
            (near_key, key_own, 0),
            (near_value, value_own, model_width),
        ):
            lanes = slice(begin, begin + model_width)
            own_out[0] = field[REACH : REACH + rows, :]
            low_pay[0, :, lanes] = field[:REACH, :].astype(low_type)
            high_pay[0, :, lanes] = field[REACH + rows :, :].astype(low_type)

    return body


def token_kernel(rows, model_width):
    def body(
        tokens, resid_grad, query_grad, key_own, value_own, qkv_weight, ln1_gain,
        grad_out, token_grad, bias_sum, gain_sum, shift_sum,
    ):
        @pl.when(pl.program_id(0) == 0)
        def _():
            for ref in (bias_sum, gain_sum, shift_sum):
                ref[...] = jnp.zeros_like(ref)

        grad_out[0, :, :model_width] = query_grad[0]
        for number, own in enumerate((key_own, value_own)):
            to = sub_lanes(number + 1, model_width)
            grad_out[0, :, to] = own[0].astype(low_type)
        bias_sum[...] += jnp.sum(grad_out[0].astype(wide), axis=0, keepdims=True)
        total = dot_t(grad_out[0], qkv_weight[...])
        normed, norm_scale = normed_rows(tokens[0].astype(wide))
        gain_sum[...] += jnp.sum(total * normed, axis=0, keepdims=True)
        shift_sum[...] += jnp.sum(total, axis=0, keepdims=True)
        token_grad[0] = resid_grad[0] + norm_pull(total, normed, norm_scale, ln1_gain[...])

    return body


def near_rows(field):
    rows = field.shape[1]
    lefts, rights = ([], [])
    distance, missing = (1, REACH)
    while missing > 0:
        take = min(rows, missing)
        lefts.insert(0, passed_along(field[:, rows - take :], "tok", distance))
        rights.append(passed_along(field[:, :take], "tok", -distance))
        distance, missing = (distance + 1, missing - take)
    if len(lefts) == 1:
        return (lefts[0], rights[0])
    return (jnp.concatenate(lefts, axis=1), jnp.concatenate(rights, axis=1))


def returned_rows(own, low_pay, high_pay):
    rows = own.shape[1]
    distance, missing = (1, REACH)
    while missing > 0:
        take = min(rows, missing)
        low_piece = low_pay[:, missing - take : missing]
        begin = REACH - missing
        high_piece = high_pay[:, begin : begin + take]
        own = own.at[:, rows - take :].add(passed_along(low_piece, "tok", -distance).astype(wide))
        own = own.at[:, :take].add(passed_along(high_piece, "tok", distance).astype(wide))
        distance, missing = (distance + 1, missing - take)
    return own


def head_unit(key, value, query, pulled, bias, log_total, inner, half):
    one_query = head_lanes(query, half)
    one_pull = head_lanes(pulled, half)
    scores = dot_t(key, one_query) + bias
    probs = jnp.exp(scores - log_total)
    probs_grad = dot_t(value, one_pull)
    score_grad = (probs * (probs_grad - inner)).astype(low_type)
    return (probs.astype(low_type), score_grad, one_query, one_pull)


def piece_list(shapes):
    pieces = []
    for index, (rows, lanes) in enumerate(shapes):
        if lanes % 256 != 0:
            parts = 2 if rows % 64 == 0 else 1
            for part in range(parts):
                pieces.append((index, part * rows // parts, rows // parts, 0, lanes, 0))
            continue
        take = 768 if lanes % 768 == 0 else lanes
        step = 48 if rows % 48 == 0 else rows
        for begin in range(0, rows, step):
            for lane in range(0, lanes, take):
                pieces.append((index, begin, step, lane, take, 1))
    return pieces


def half_slice(piece, half):
    _, _, rows, _, lanes, axis = piece
    if isinstance(half, int) and axis == 0:
        return (slice(half * (rows // 2), (half + 1) * (rows // 2)), slice(None))
    if isinstance(half, int):
        return (slice(None), slice(half * (lanes // 2), (half + 1) * (lanes // 2)))
    if axis == 0:
        return (pl.ds(pl.multiple_of(half * (rows // 2), 16), rows // 2), slice(None))
    return (slice(None), pl.ds(pl.multiple_of(half * (lanes // 2), 128), lanes // 2))


def half_shape(piece):
    _, _, rows, _, lanes, axis = piece
    return (rows // 2, lanes) if axis == 0 else (rows, lanes // 2)


def closing_kernel(rows, model_width, seqs, shapes, bits):
    early = piece_list(shapes[:-1])
    last = len(shapes) - 1
    late = [p for p in piece_list(shapes[last:])]
    late = [(last,) + p[1:] for p in late]
    pieces = early + late
    count = len(pieces)
    mesh_id = pl.DeviceIdType.MESH
    tile = min(rows, QUERY_TILE)
    window = tile + 2 * REACH
    scale = 1.0 / math.sqrt(HEAD_DIM)
    pairs = model_width // 128
    phases = bits + 2
    vector_phases = bits + 1
    slots = AHEAD + 2

    def body(*refs):
        given = refs[: len(shapes) - 1]
        (
            queries, keys, values, pulls, pulls_left, pulls_right, stats, stats_left, stats_right,
            bias, edge_bias, normed_low, tokens, resid_grad, qkv_weight, ln1_gain, early_vectors,
        ) = refs[len(shapes) - 1 : len(shapes) + 16]
        rest = refs[len(shapes) + 16 :]
        results = rest[: len(shapes)]
        token_grad, vector_out = rest[len(shapes) : len(shapes) + 2]
        rest = rest[len(shapes) + 2 :]
        (
            near, key_turned, key_total, value_total, grads, normed_turned, late_grad, kept,
            vectors, vectors_landed, near_sem, local_sem, core_send, core_recv, send_sem, recv_sem,
            vector_send, vector_recv,
        ) = rest[:18]
        landed = [rest[18 + i * phases : 18 + (i + 1) * phases] for i in range(count)]
        tok = lax.axis_index("tok")
        seq = lax.axis_index("seq")
        core = tok % 2

        def tok_bit(bit):
            return (tok // (1 << bit)) % 2

        def tok_step(bit):
            return (1 << bit) * (1 - 2 * tok_bit(bit))

        def kept_bit(phase):
            first = seq if phase == 1 else tok_bit(phase - 1)
            second = tok_bit(phase) if phase < bits else seq
            return (1 - core) * first + core * second

        def partner(phase):
            if phase == 0:
                return (seq, tok + tok_step(0))
            if phase > bits:
                return (1 - seq, tok)
            first = 0 if phase == 1 else tok_step(phase - 1)
            second = tok_step(phase) if phase < bits else 0
            across = 0
            if phase == 1:
                across = 1 - core
            if phase == bits:
                across = core
            return (
                seq + across * (1 - 2 * seq),
                tok + (1 - core) * first + core * second,
            )

        def vector_partner(phase):
            if phase < bits:
                return (seq, tok + tok_step(phase))
            return (1 - seq, tok)

        barrier = pltpu.get_barrier_semaphore()
        for phase in range(vector_phases):
            pl.semaphore_signal(
                barrier, inc=1, device_id=vector_partner(phase), device_id_type=mesh_id
            )
        pl.semaphore_wait(barrier, vector_phases)

        def source(number, core_bit):
            index, begin, take, lane, lanes, _ = pieces[number]
            at = (slice(None),) * (bits - 1) + (core_bit,)
            if index == last:
                return late_grad.at[(number - len(early),) + at]
            return given[index].at[at + (pl.ds(begin, take), pl.ds(lane, lanes))]

        def core_copy(number, half, receiver):
            index, begin, take, lane, lanes, axis = pieces[number]
            at = (slice(None),) * (bits - 1) + (1 - core,)
            if axis == 0:
                part = (pl.ds(begin + half * (take // 2), take // 2), pl.ds(lane, lanes))
            else:
                part = (pl.ds(begin, take), pl.ds(lane + half * (lanes // 2), lanes // 2))
            if index == last:
                view = late_grad.at[
                    (number - len(early),)
                    + at
                    + (slice(None), pl.ds(half * (lanes // 2), lanes // 2))
                ]
            else:
                view = given[index].at[at + part]
            if receiver == 0:
                to = landed[number][0].at[(slice(None),) * (bits - 1) + (half,)]
            else:
                to = landed[number][0].at[half]
            return pltpu.make_async_remote_copy(
                src_ref=view,
                dst_ref=to,
                send_sem=core_send.at[number, half],
                recv_sem=core_recv.at[number, half],
                device_id=partner(0),
                device_id_type=mesh_id,
            )

        def local_copy(number):
            slot = number % slots
            _, _, take, _, lanes, _ = pieces[number]
            to = kept.at[slot] if (take, lanes) == (48, 768) else wide_kept[number]
            return pltpu.make_async_copy(source(number, core), to, local_sem.at[number])

        wide_kept = {}
        extra = iter(rest[18 + count * phases :])
        for number, piece in enumerate(early):
            if (piece[2], piece[4]) != (48, 768):
                wide_kept[number] = next(extra)

        def remote_copy(number, phase):
            if phase > bits:
                view = landed[number][bits]
            else:
                view = landed[number][phase - 1].at[
                    (slice(None),) * (bits - phase) + (1 - kept_bit(phase),)
                ]
            return pltpu.make_async_remote_copy(
                src_ref=view,
                dst_ref=landed[number][phase],
                send_sem=send_sem.at[number, phase - 1],
                recv_sem=recv_sem.at[number, phase - 1],
                device_id=partner(phase),
                device_id_type=mesh_id,
            )

        def begin(number):
            for half in range(2):
                for mine in range(2):

                    @pl.when(core == mine)
                    def _():
                        core_copy(number, half, 1 - mine).start()

            if number < len(early):
                local_copy(number).start()

        def bits_of(flat, length):
            return tuple((flat // (1 << bit)) % 2 for bit in reversed(range(length)))

        def finish(number, phase):
            piece = pieces[number]
            index, first, take, lane, lanes, axis = piece
            if phase == 0:
                for half in range(2):
                    for mine in range(2):

                        @pl.when(core == mine)
                        def _():
                            core_copy(number, half, mine).wait_recv()

                if number < len(early):
                    local_copy(number).wait()
                    _, _, t, _, l, _ = piece
                    own = kept.at[number % slots] if (t, l) == (48, 768) else wide_kept[number]
                blocks = 1 << (bits - 1)

                def step(block, carry):
                    at = bits_of(block, bits - 1)
                    for half in range(2):
                        flat = (1 - core) * (2 * block + half) + core * (blocks * half + block)
                        to = bits_of(flat, bits)
                        part = half_slice(piece, half)
                        if number < len(early):
                            mine = own[at + part]
                        else:
                            mine = late_grad[(number - len(early),) + at + (core,) + part]
                        landed[number][0][to] = landed[number][0][to] + mine
                    return carry

                lax.fori_loop(0, blocks, step, 0)
                remote_copy(number, 1).start()
                return
            remote_copy(number, phase).wait_recv()
            got = landed[number][phase]
            if phase <= bits:
                before = landed[number][phase - 1]

                def step(block, carry):
                    at = bits_of(block, bits - phase)
                    got[at] = got[at] + before[at + (kept_bit(phase),)]
                    return carry

                if phase < bits:
                    lax.fori_loop(0, 1 << (bits - phase), step, 0)
                else:
                    got[...] = got[...] + before[kept_bit(phase)]
                remote_copy(number, phase + 1).start()
                return
            height, span = half_shape(piece)
            for half, value in ((seq, landed[number][bits]), (1 - seq, got)):
                if axis == 0:
                    at = (pl.ds(pl.multiple_of(first + half * height, 8), height), pl.ds(lane, span))
                else:
                    at = (pl.ds(first, take), pl.ds(pl.multiple_of(lane + half * span, 128), span))
                results[index][at] = value[...].astype(wide)

        def near_copies(number):
            slot = number % 2
            return [
                pltpu.make_async_copy(field.at[number], near.at[slot, i], near_sem.at[slot, i])
                for i, field in enumerate((queries, keys, values))
            ]

        def own_segment(number, base):
            slot = number % 2
            own = slice(REACH + base, REACH + base + tile)
            near_rows_at = slice(base, base + window)
            inside = slice(REACH - base, REACH - base + rows)

            def step(pair, carry):
                lanes = pl.ds(pl.multiple_of(pair * 128, 128), 128)
                query = near[slot, 0, own, lanes] * scale
                key = near[slot, 1, near_rows_at, lanes]
                value = near[slot, 2, near_rows_at, lanes]
                pulled = pulls[number, base : base + tile, lanes]
                key_term, value_term, halves = (None, None, [])
                for half in range(2):
                    head = 2 * pair + half
                    log_total = stats[number, pair, half : half + 1, base : base + tile]
                    inner = stats[number, pair, 2 + half : 3 + half, base : base + tile]
                    probs, score_grad, one_query, one_pull = head_unit(
                        key, value, query, pulled, bias[number, base // tile], log_total, inner, half
                    )
                    here = dot(score_grad[inside], one_query)
                    key_term = here if key_term is None else key_term + here
                    here = dot(probs[inside], one_pull)
                    value_term = here if value_term is None else value_term + here
                    feature = pl.ds(pl.multiple_of(head * HEAD_DIM, HEAD_DIM), HEAD_DIM)
                    halves.append(dot(key_turned[feature, near_rows_at], score_grad) * scale)
                if base == 0:
                    key_total[:, lanes] = key_term
                    value_total[:, lanes] = value_term
                else:
                    key_total[:, lanes] += key_term
                    value_total[:, lanes] += value_term
                both = jnp.transpose(jnp.concatenate(halves, axis=0)).astype(low_type)
                grads[number * rows + base : number * rows + base + tile, lanes] = both
                return carry

            lax.fori_loop(0, pairs, step, 0)

        def edge_segment(number, side):
            slot = number % 2
            from_rows = slice(0, REACH) if side == 0 else slice(REACH + rows, 2 * REACH + rows)
            begin_row = 0 if side == 0 else rows - REACH
            at = slice(begin_row, begin_row + REACH)
            key_rows = slice(REACH + begin_row, 2 * REACH + begin_row)
            pull_ref, stat_ref = ((pulls_left, stats_left), (pulls_right, stats_right))[side]

            def step(pair, carry):
                lanes = pl.ds(pl.multiple_of(pair * 128, 128), 128)
                query = near[slot, 0, from_rows, lanes] * scale
                key = near[slot, 1, key_rows, lanes]
                value = near[slot, 2, key_rows, lanes]
                pulled = pull_ref[number, :, lanes]
                key_term, value_term = (None, None)
                for half in range(2):
                    log_total = stat_ref[number, pair, half : half + 1, :]
                    inner = stat_ref[number, pair, 2 + half : 3 + half, :]
                    probs, score_grad, one_query, one_pull = head_unit(
                        key, value, query, pulled, edge_bias[number, side], log_total, inner, half
                    )
                    here = dot(score_grad, one_query)
                    key_term = here if key_term is None else key_term + here
                    here = dot(probs, one_pull)
                    value_term = here if value_term is None else value_term + here
                key_total[at, lanes] += key_term
                value_total[at, lanes] += value_term
                return carry

            lax.fori_loop(0, pairs, step, 0)

        def open_sequence(number):
            for copy in near_copies(number):
                copy.wait()
            if number + 1 < seqs:
                for copy in near_copies(number + 1):
                    copy.start()

            def step(pair, carry):
                lanes = pl.ds(pl.multiple_of(pair * 128, 128), 128)
                block = turned(near[number % 2, 1, :, lanes])
                key_turned[lanes, :] = block.astype(low_type)
                return carry

            lax.fori_loop(0, pairs, step, 0)

        def close_sequence(number):
            at = slice(number * rows, (number + 1) * rows)
            grads[at, model_width : 2 * model_width] = key_total[...].astype(low_type)
            grads[at, 2 * model_width :] = value_total[...].astype(low_type)

        def late_product(part):
            lanes = sub_lanes(part, model_width)
            product = dot(normed_turned[...], grads[:, lanes]).astype(low_type)
            shard_rows = model_width >> bits
            for shard in range(1 << bits):
                at = tuple((shard >> bit) & 1 for bit in reversed(range(bits)))
                late_grad[(part,) + at] = product[shard * shard_rows : (shard + 1) * shard_rows]

        def token_segment(number):
            at = slice(number * rows, (number + 1) * rows)
            total = dot_t(grads[at, :], qkv_weight[...])
            normed, norm_scale = normed_rows(tokens[number].astype(wide))
            vectors[0, 0:1, :] += jnp.sum(total * normed, axis=0, keepdims=True)
            vectors[0, 1:2, :] += jnp.sum(total, axis=0, keepdims=True)
            for row, part in ((2, 0), (3, 2)):
                field = grads[at, sub_lanes(part, model_width)].astype(wide)
                vectors[0, row : row + 1, :] += jnp.sum(field, axis=0, keepdims=True)
            pull = norm_pull(total, normed, norm_scale, ln1_gain[...])
            token_grad[number] = resid_grad[number] + pull

        def vector_copy(phase):
            return pltpu.make_async_remote_copy(
                src_ref=vectors.at[phase],
                dst_ref=vectors_landed.at[phase],
                send_sem=vector_send.at[phase],
                recv_sem=vector_recv.at[phase],
                device_id=vector_partner(phase),
                device_id_type=mesh_id,
            )

        segments = []
        for number in range(seqs):
            parts = [partial(own_segment, number, base) for base in range(0, rows, tile)]
            parts += [partial(edge_segment, number, side) for side in range(2)]

            def opened(first, number=number):
                open_sequence(number)
                first()

            def closed(final, number=number):
                final()
                close_sequence(number)

            parts[0] = partial(opened, parts[0])
            parts[-1] = partial(closed, parts[-1])
            segments += parts

        vectors[0, 0:8, :] = jnp.zeros((8, model_width), wide)
        vectors[0, 8:16, :] = early_vectors[...]
        for copy in near_copies(0):
            copy.start()
        begin_at = {number: max(number - AHEAD, 0) for number in range(len(early))}
        land_at = {number: number + 1 for number in range(len(early))}
        first_segment = 1
        compute_steps = max(len(segments) + first_segment, len(early) - 1)
        for part in range(len(late)):
            begin_at[len(early) + part] = compute_steps + part
            land_at[len(early) + part] = max(compute_steps, len(early)) + part + 1
        lags = [0, 2] + [phase + 1 for phase in range(2, phases)]
        token_step = compute_steps + len(late) - 1
        final_step = max(
            max(land_at.values()) + lags[-1] + 1, token_step + seqs + vector_phases
        )
        for step in range(final_step):
            for number in range(count):
                if begin_at[number] == step:
                    part = number - len(early)
                    if part >= 0:
                        late_product(part)
                    begin(number)
            if step == 0:
                for line in range(seqs):
                    for column in range(pairs):
                        block = turned(normed_low[line, :, sub_lanes(column, 128)])
                        at = (sub_lanes(column, 128), slice(line * rows, (line + 1) * rows))
                        normed_turned[at] = block.astype(low_type)
            for number in reversed(range(count)):
                if step - land_at[number] in lags:
                    finish(number, lags.index(step - land_at[number]))
            if 0 <= step - first_segment < len(segments):
                segments[step - first_segment]()
            after = step - token_step
            if 0 <= after < seqs:
                token_segment(after)
            if after == seqs - 1:
                vector_copy(0).start()
            phase = after - seqs
            if 0 <= phase < vector_phases:
                vector_copy(phase).wait_recv()
                if phase + 1 < vector_phases:
                    vectors[phase + 1] = vectors[phase] + vectors_landed[phase]
                    vector_copy(phase + 1).start()
                else:
                    vector_out[...] = vectors[phase] + vectors_landed[phase]
        for number in range(count):
            for half in range(2):
                core_copy(number, half, 0).wait_send()
            for phase in range(1, phases):
                remote_copy(number, phase).wait_send()
        for phase in range(vector_phases):
            vector_copy(phase).wait_send()

    scratch = [
        pltpu.VMEM((2, 3, rows + 2 * REACH, model_width), low_type),
        pltpu.VMEM((model_width, rows + 2 * REACH), low_type),
        pltpu.VMEM((rows, model_width), wide),
        pltpu.VMEM((rows, model_width), wide),
        pltpu.VMEM((seqs * rows, 3 * model_width), low_type),
        pltpu.VMEM((model_width, seqs * rows), low_type),
        pltpu.VMEM((len(late),) + (2,) * bits + (48, 768), low_type),
        pltpu.VMEM((slots,) + (2,) * (bits - 1) + (48, 768), low_type),
        pltpu.VMEM((vector_phases, 16, model_width), wide),
        pltpu.VMEM((vector_phases, 16, model_width), wide),
        pltpu.SemaphoreType.DMA((2, 3)),
        pltpu.SemaphoreType.DMA((count,)),
        pltpu.SemaphoreType.DMA((count, 2)),
        pltpu.SemaphoreType.DMA((count, 2)),
        pltpu.SemaphoreType.DMA((count, phases - 1)),
        pltpu.SemaphoreType.DMA((count, phases - 1)),
        pltpu.SemaphoreType.DMA((vector_phases,)),
        pltpu.SemaphoreType.DMA((vector_phases,)),
    ]
    for piece in pieces:
        block = half_shape(piece)
        scratch += [pltpu.VMEM((2,) * (bits - phase) + block, low_type) for phase in range(bits + 1)]
        scratch.append(pltpu.VMEM(block, low_type))
    for piece in early:
        if (piece[2], piece[4]) != (48, 768):
            scratch.append(pltpu.VMEM((2,) * (bits - 1) + (piece[2], piece[4]), low_type))
    return (body, scratch)


def closing(grads, fields, qkv_shape):
    shards = lax.axis_size("tok")
    bits = bit_count(shards)
    queries, tokens = (fields[0], fields[12])
    seqs, rows, model_width = tokens.shape
    shapes = [g.shape[1:] for g in grads] + [(qkv_shape[0] // shards, qkv_shape[1])]
    body, scratch = closing_kernel(rows, model_width, seqs, shapes, bits)
    given = [g.reshape((2,) * bits + g.shape[1:]) for g in grads]
    held = pl.BlockSpec(memory_space=pltpu.VMEM)
    away = pl.BlockSpec(memory_space=pl.ANY)
    inputs = given + list(fields)
    in_specs = [away] * (len(given) + 3) + [held] * (len(fields) - 3)
    out_shape = [jax.ShapeDtypeStruct(s, wide) for s in shapes]
    out_shape.append(jax.ShapeDtypeStruct(tokens.shape, wide))
    out_shape.append(jax.ShapeDtypeStruct((16, model_width), wide))
    return pl.pallas_call(
        body,
        in_specs=in_specs,
        out_specs=[held] * len(out_shape),
        out_shape=out_shape,
        scratch_shapes=scratch,
        compiler_params=pltpu.CompilerParams(
            vmem_limit_bytes=CLOSING_LIMIT, collective_id=1, has_side_effects=True
        ),
        cost_estimate=pl.CostEstimate(
            flops=40 * 10**9, bytes_accessed=60 * 10**6, transcendentals=0
        ),
    )(*inputs)


def local(
    tokens,
    skip_features,
    crop_sides,
    ln1_gain,
    ln1_bias,
    qkv_weight,
    qv_bias,
    out_weight,
    out_bias,
    ln2_gain,
    ln2_bias,
    fc1_weight,
    fc1_bias,
    fc2_weight,
    fc2_bias,
    deconv_weight,
    conv1_weight,
    conv2_weight,
    conv3_weight,
    cotangent,
):
    seq_count, row_count, model_width = tokens.shape
    channels = conv2_weight.shape[2]
    hidden = fc1_weight.shape[1]
    reaches = (key_reach + row_count - 1) // row_count
    reach_rows = row_count + 2 * REACH
    near_left, near_right = near_rows(tokens)
    place, owner, crop_t, inverse, bias, edge_bias = geometry_tables(crop_sides, row_count)

    def flat(vector):
        return vector.reshape(1, -1)

    def block(lanes, kind, rows=row_count):
        return ((seq_count, rows, lanes), kind)

    qkv_bias = jnp.concatenate([qv_bias[0], jnp.zeros_like(qv_bias[0]), qv_bias[1]])
    matrix_flops = 2 * seq_count * row_count * model_width
    (
        normed_low, queries, keys, values, attended, log_totals, resid_one, normed_two,
        act_low, slope_low, resid_low, upsampled,
    ) = kernel_call(
        forward_kernel(row_count, model_width, hidden),
        seq_count,
        (tokens, near_left, near_right, bias),
        (
            flat(ln1_gain), flat(ln1_bias), qkv_weight, flat(qkv_bias), out_weight, flat(out_bias),
            flat(ln2_gain), flat(ln2_bias), fc1_weight, flat(fc1_bias), fc2_weight, flat(fc2_bias),
            deconv_weight,
        ),
        (
            block(model_width, low_type),
            block(model_width, low_type, reach_rows),
            block(model_width, low_type, reach_rows),
            block(model_width, low_type, reach_rows),
            block(model_width, low_type),
            block(row_count, wide, 16),
            block(model_width, wide),
            block(model_width, low_type),
            block(hidden, low_type),
            block(hidden, low_type),
            block(model_width, low_type),
            block(8 * channels, low_type),
        ),
        (),
        [
            pltpu.VMEM((reach_rows, model_width), low_type),
            pltpu.VMEM((model_width, reach_rows), low_type),
        ],
        matrix_flops * (8 * model_width + 2 * hidden + 8 * channels),
    )
    section_out, up_grad, skip_grad, conv1_grad, conv2_grad, conv3_grad = conv_section(
        upsampled,
        skip_features.reshape(seq_count, row_count, 8 * channels),
        cotangent.reshape(seq_count, row_count, 8 * channels),
        (conv1_weight, conv2_weight, conv3_weight),
        (place, owner, crop_t, inverse),
        reaches,
    )
    section_out = section_out.reshape(seq_count, row_count, 8, channels)
    skip_grad = skip_grad.reshape(seq_count, row_count, 8, channels)
    (
        branch_low, pre_low, resid_grad, mixed_low, pulled, stats,
        fc2_bias_grad, fc1_bias_grad, out_bias_grad, ln2_gain_grad, ln2_bias_grad,
    ) = kernel_call(
        hidden_back_kernel(row_count, model_width, hidden),
        seq_count,
        (up_grad, slope_low, resid_one, attended, log_totals),
        (deconv_weight, fc2_weight, fc1_weight, out_weight, flat(ln2_gain)),
        (
            block(model_width, low_type),
            block(hidden, low_type),
            block(model_width, wide),
            block(model_width, low_type),
            block(model_width, low_type),
            ((seq_count, model_width // 128, 8, row_count), wide),
        ),
        (
            ((1, model_width), wide),
            ((1, hidden), wide),
            ((1, model_width), wide),
            ((1, model_width), wide),
            ((1, model_width), wide),
        ),
        [],
        matrix_flops * (model_width + 2 * hidden + 8 * channels),
    )

    def weight_product(left, right):
        return jnp.einsum(
            "rd,re->de",
            left.reshape(-1, left.shape[-1]),
            right.reshape(-1, right.shape[-1]),
            preferred_element_type=wide,
        )

    deconv_grad = weight_product(resid_low, up_grad)
    fc2_grad = weight_product(act_low, branch_low)
    fc1_grad = weight_product(normed_two, pre_low)
    out_grad = weight_product(attended, mixed_low)
    conv3_turned = jnp.moveaxis(conv3_grad.reshape(1, 2, channels, channels), 2, 3)
    conv_grads = (conv1_grad, conv2_grad, conv3_turned)
    matrices = (deconv_grad, fc2_grad, fc1_grad, out_grad)
    shards = lax.axis_size("tok")
    if row_count >= REACH and lax.axis_size("seq") == 2 and model_width // shards == 48:
        pulls = exchanged(pulled[:, :REACH], pulled[:, row_count - REACH :])
        near_stats = exchanged(stats[..., :REACH], stats[..., row_count - REACH :])
        early = (
            out_bias_grad, ln2_gain_grad, ln2_bias_grad, fc2_bias_grad,
            fc1_bias_grad.reshape(-1, model_width),
        )
        parts = [conv_rows(g).astype(low_type) for g in conv_grads]
        spare = -sum(p.shape[1] for p in parts) % 64
        packed = jnp.concatenate(parts + [jnp.zeros((shards, spare, 128), low_type)], axis=1)
        results = closing(
            [packed] + [sharded_rows(m) for m in matrices],
            (
                queries, keys, values, pulled, pulls[0], pulls[1], stats, near_stats[0],
                near_stats[1], bias, edge_bias, normed_low, tokens, resid_grad, qkv_weight,
                flat(ln1_gain), jnp.concatenate(early, axis=0),
            ),
            qkv_weight.shape,
        )
        conv_shares = []
        cursor = 0
        for part, grad in zip(parts, conv_grads):
            rows_here = results[0][cursor : cursor + part.shape[1]]
            conv_shares.append(conv_share(rows_here, grad.shape[0], grad.shape[1]))
            cursor += part.shape[1]
        shares = results[1:6]
        token_grad, lines = results[6:8]
        span = model_width // shards
        own = lax.dynamic_slice_in_dim(lines[:12], lax.axis_index("tok") * span, span, 1)
        long_span = hidden // shards
        long_line = lines[12:16].reshape(hidden)
        long_own = lax.dynamic_slice_in_dim(
            long_line, lax.axis_index("tok") * long_span, long_span, 0
        )
        vectors = (own[0], own[1], own[2], own[3], own[8], own[9], own[10], long_own, own[11])
    else:
        query_grad, key_own, value_own, low_pay, high_pay = kernel_call(
            attention_back_kernel(row_count, model_width),
            seq_count,
            (queries, keys, values, pulled, stats, bias),
            (),
            (
                block(model_width, low_type),
                block(model_width, wide),
                block(model_width, wide),
                block(2 * model_width, low_type, REACH),
                block(2 * model_width, low_type, REACH),
            ),
            (),
            [
                pltpu.VMEM((reach_rows, model_width), wide),
                pltpu.VMEM((reach_rows, model_width), wide),
                pltpu.VMEM((model_width, reach_rows), low_type),
            ],
            matrix_flops * 12 * model_width,
        )
        both = jnp.concatenate([key_own, value_own], axis=-1)
        both = returned_rows(both, low_pay, high_pay)
        qkv_grad_low, token_grad, column_sums, ln1_gain_grad, ln1_bias_grad = kernel_call(
            token_kernel(row_count, model_width),
            seq_count,
            (tokens, resid_grad, query_grad, both[:, :, :model_width], both[:, :, model_width:]),
            (qkv_weight, flat(ln1_gain)),
            (block(3 * model_width, low_type), block(model_width, wide)),
            (
                ((1, 3 * model_width), wide),
                ((1, model_width), wide),
                ((1, model_width), wide),
            ),
            [],
            matrix_flops * 3 * model_width,
        )
        qkv_grad = weight_product(normed_low, qkv_grad_low)
        conv_shares, shares, vectors = reduced_all(
            conv_grads,
            matrices + (qkv_grad,),
            (
                ln1_gain_grad, ln1_bias_grad, column_sums[:, :model_width],
                column_sums[:, 2 * model_width :], out_bias_grad, ln2_gain_grad, ln2_bias_grad,
                fc1_bias_grad, fc2_bias_grad,
            ),
        )
    return (
        section_out,
        token_grad,
        skip_grad,
        vectors[0],
        vectors[1],
        shares[4],
        jnp.stack([vectors[2], vectors[3]]),
        shares[3],
        vectors[4],
        vectors[5],
        vectors[6],
        shares[2],
        vectors[7],
        shares[1],
        vectors[8],
        shares[0],
        conv_shares[0],
        conv_shares[1],
        conv_shares[2][0],
    )


def solution(mesh):
    in_specs = (
        P("seq", "tok", None),
        P("seq", "tok", None, None),
        P("seq", None),
        P(),
        P(),
        P(),
        P(),
        P(),
        P(),
        P(),
        P(),
        P(),
        P(),
        P(),
        P(),
        P(),
        P(),
        P(),
        P(),
        P("seq", "tok", None, None),
    )
    out_specs = (
        P("seq", "tok", None, None),
        P("seq", "tok", None),
        P("seq", "tok", None, None),
        P("tok"),
        P("tok"),
        P("tok", None),
        P(None, "tok"),
        P("tok", None),
        P("tok"),
        P("tok"),
        P("tok"),
        P("tok", None),
        P("tok"),
        P("tok", None),
        P("tok"),
        P("tok", None),
        P(None, None, "tok"),
        P(None, None, "tok"),
        P(None, "tok"),
    )
    return jax.shard_map(local, mesh=mesh, in_specs=in_specs, out_specs=out_specs, check_vma=False)
```

```python
from functools import partial
import math

import jax
import jax.numpy as jnp
import numpy as np
from jax import lax
from jax.experimental import pallas as pl
from jax.experimental.pallas import tpu as pltpu
from jax.sharding import PartitionSpec as P

HEADS = 12
HEAD_DIM = 64


side_small = 4
side_big = 6
halo_rows = 43
key_reach = 215
norm_eps = 1e-05
far_below = -1e30
highest = lax.Precision.HIGHEST
in_part = {-1: (1, 2), 0: (0, 2), 1: (0, 1)}
out_part = {-1: (0, 1), 0: (0, 2), 1: (1, 2)}


def passed_along(block, axis, distance):
    devices = range(lax.axis_size(axis))
    route = [(i - distance, i) for i in devices if i - distance in devices]
    return lax.ppermute(block, axis, route)


def all_offsets():
    step_values = (-1, 0, 1)
    return [
        (step_x, step_y, step_z)
        for step_x in step_values
        for step_y in step_values
        for step_z in step_values
    ]


EDGE = 48
WINDOW = 256
TILE = 128
CROP_ROWS = 48
SUBS = 8
VMEM_LIMIT = 60 * 1024 * 1024
lowest_step = {-1: -43, 0: -7, 1: 11}
low_type = jnp.bfloat16
wide = jnp.float32


def dot(left, right):
    return jnp.dot(left, right, preferred_element_type=wide)


def three_terms(field):
    first = field.astype(low_type)
    rest = field - first.astype(wide)
    second = rest.astype(low_type)
    third = (rest - second.astype(wide)).astype(low_type)
    return (first, second, third)


def exact_dot(chosen, field):
    first, second, third = three_terms(field)
    return dot(chosen, first) + dot(chosen, second) + dot(chosen, third)


def sub_lanes(number, width):
    return slice(number * width, (number + 1) * width)


def all_taps():
    return [(x, y, z) for x in range(3) for y in range(3) for z in range(3)]


def forward_band(weight, band_ref):
    inner, outer = weight.shape[1:]
    band_ref[...] = jnp.zeros_like(band_ref)
    for tap_x, tap_y, tap_z in all_taps():
        for side in range(2):
            rows = sub_lanes(tap_y * 4 + tap_z + side, inner)
            lanes = sub_lanes(side, outer)
            band_ref[tap_x, rows, lanes] = weight[tap_x * 9 + tap_y * 3 + tap_z]


def backward_band(weight, band_ref):
    inner, outer = weight.shape[1:]
    band_ref[...] = jnp.zeros_like(band_ref)
    for tap_x, tap_y, tap_z in all_taps():
        for side in range(2):
            rows = sub_lanes(side, inner)
            lanes = sub_lanes(tap_y * 4 + tap_z + side, outer)
            band_ref[tap_x, rows, lanes] = weight[26 - (tap_x * 9 + tap_y * 3 + tap_z)]


def once(fill, *refs):
    @pl.when(pl.program_id(0) == 0)
    def _():
        fill(*refs)


def window_positions(step):
    return {-1: ((0, 1),), 0: ((1, 0), (2, 1)), 1: ((3, 0),)}[step]


def fill_windows(x_ref, place_ref, p_ref, rows, width):
    tile = min(rows, TILE)
    for base in range(0, rows, tile):
        own = slice(base, base + tile)
        for number, (step_x, step_y, step_z) in enumerate(all_offsets()):
            low = (EDGE + base + lowest_step[step_x]) // 16 * 16
            centre = (step_x, step_y, step_z) == (0, 0, 0)
            if not centre:
                lane = lax.broadcasted_iota(jnp.int32, (tile, WINDOW), 1) + low
                chosen = jnp.where(lane == place_ref[0, own, number : number + 1], 1.0, 0.0)
                chosen = chosen.astype(low_type)
            for x_to, x_from in window_positions(step_x):
                for y_to, y_from in window_positions(step_y):
                    z_to, z_from = window_positions(step_z)[0]
                    count = (2 if step_z == 0 else 1) * width
                    to = ((x_to * 4 + y_to) * 4 + z_to) * width
                    source = (x_from * 4 + y_from * 2 + z_from) * width
                    if centre:
                        got = x_ref[EDGE + base : EDGE + base + tile, source : source + count]
                    else:
                        got = dot(chosen, x_ref[low : low + WINDOW, source : source + count])
                    p_ref[own, to : to + count] = got.astype(low_type)


def window_conv(p_ref, band_ref, pair, width, product):
    first, second = pair
    total = None
    for tap in range(3):
        begin = ((first + tap) * 4 + second) * 4 * width
        term = product(p_ref[:, begin : begin + 12 * width], band_ref[tap])
        total = term if total is None else total + term
    return total


def all_pairs():
    return [(first, second) for first in range(2) for second in range(2)]


def add_grads(left_ref, p_ref, total_ref, width, channels):
    for tap_x in range(3):
        for tap_y in range(3):
            term = None
            for number, (first, second) in enumerate(all_pairs()):
                begin = ((first + tap_x) * 4 + second + tap_y) * 4 * channels
                left = left_ref[number * 2 * width : (number + 1) * 2 * width, :]
                part = dot(left, p_ref[:, begin : begin + 4 * channels])
                term = part if term is None else term + part
            total_ref[tap_x * 3 + tap_y] += term


def fold_grads(total_ref, grad_ref, width, channels):
    for tap_x in range(3):
        for tap_y in range(3):
            for tap_z in range(3):
                number = tap_x * 3 + tap_y
                here = total_ref[number, :width, sub_lanes(tap_z, channels)]
                there = total_ref[number, width:, sub_lanes(tap_z + 1, channels)]
                tap = 26 - (number * 3 + tap_z)
                for half in range(width // channels):
                    rows = slice(half * channels, (half + 1) * channels)
                    grad_ref[tap, half] = jnp.transpose(here[rows] + there[rows])


def kernel_call(
    body, seqs, inputs, shared, outputs, summed, scratch, flops, away=(), landing=(), collective=None
):
    def row_spec(shape):
        return pl.BlockSpec((1,) + tuple(shape[1:]), lambda i: (i,) + (0,) * (len(shape) - 1))

    def whole_spec(shape):
        return pl.BlockSpec(
            tuple(shape), lambda i: (0,) * len(shape), pipeline_mode=pl.Buffered(1)
        )

    far_spec = pl.BlockSpec(memory_space=pl.ANY)
    moved = sum(math.prod(a.shape) * a.dtype.itemsize for a in list(inputs) + list(shared))
    moved += sum(math.prod(s) * jnp.dtype(t).itemsize for s, t in list(outputs) + list(summed))
    results = list(outputs) + list(summed) + list(landing)
    return pl.pallas_call(
        body,
        grid=(seqs,),
        in_specs=[row_spec(a.shape) for a in inputs]
        + [whole_spec(a.shape) for a in shared]
        + [far_spec] * len(away),
        out_specs=[row_spec(s) for s, _ in outputs]
        + [whole_spec(s) for s, _ in summed]
        + [far_spec] * len(landing),
        out_shape=[jax.ShapeDtypeStruct(s, t) for s, t in results],
        scratch_shapes=scratch,
        compiler_params=pltpu.CompilerParams(
            vmem_limit_bytes=VMEM_LIMIT,
            collective_id=collective,
            has_side_effects=collective is not None,
        ),
        cost_estimate=pl.CostEstimate(flops=flops, bytes_accessed=moved, transcendentals=0),
    )(*inputs, *shared, *away)


def tok_sides():
    tok, count = (lax.axis_index("tok"), lax.axis_size("tok"))
    return (tok > 0, tok < count - 1)


def greet():
    seq, tok, count = (lax.axis_index("seq"), lax.axis_index("tok"), lax.axis_size("tok"))
    barrier = pltpu.get_barrier_semaphore()
    for there, shift in zip(tok_sides(), (count - 1, 1)):

        @pl.when(there)
        def _():
            pl.semaphore_signal(
                barrier,
                inc=1,
                device_id=(seq, lax.rem(tok + shift, count)),
                device_id_type=pl.DeviceIdType.MESH,
            )


def met():
    tok, count = (lax.axis_index("tok"), lax.axis_size("tok"))
    peers = jnp.minimum(tok, 1) + jnp.minimum(count - 1 - tok, 1)
    pl.semaphore_wait(pltpu.get_barrier_semaphore(), peers)


class Edge:
    def __init__(self, low, high, left, right, send_sem, recv_sem):
        self.sources = (low, high)
        self.targets = (right, left)
        self.send_sem = send_sem
        self.recv_sem = recv_sem

    def copy(self, way):
        seq, tok, count = (lax.axis_index("seq"), lax.axis_index("tok"), lax.axis_size("tok"))
        shift = count - 1 if way == 0 else 1
        return pltpu.make_async_remote_copy(
            src_ref=self.sources[way],
            dst_ref=self.targets[way],
            send_sem=self.send_sem.at[way],
            recv_sem=self.recv_sem.at[way],
            device_id=(seq, lax.rem(tok + shift, count)),
            device_id_type=pl.DeviceIdType.MESH,
        )

    def start(self):
        for way, there in enumerate(tok_sides()):

            @pl.when(there)
            def _():
                self.copy(way).start()

    def land(self):
        for way, there in enumerate(tok_sides()):

            @pl.when(there)
            def _():
                self.copy(1 - way).wait_recv()

    def sent(self):
        for way, there in enumerate(tok_sides()):

            @pl.when(there)
            def _():
                self.copy(way).wait_send()


def edge_scratch(seqs, rows, lanes):
    return [
        pltpu.VMEM((seqs, rows, lanes), low_type),
        pltpu.VMEM((seqs, rows, lanes), low_type),
        pltpu.VMEM((rows, lanes), low_type),
        pltpu.SemaphoreType.DMA((seqs, 2)),
        pltpu.SemaphoreType.DMA((seqs, 2)),
        pltpu.SemaphoreType.DMA((seqs,)),
    ]


class Payload:
    def __init__(self, seqs, left, right, low_pay, high_pay, zero_ref, send_sem, recv_sem, zero_sem):
        self.seqs = seqs
        self.refs = (left, right, low_pay, high_pay, send_sem, recv_sem)
        self.zero_ref = zero_ref
        self.zero_sem = zero_sem
        self.step = pl.program_id(0)
        self.low = low_pay.at[pl.ds(self.step, 1)]
        self.high = high_pay.at[pl.ds(self.step, 1)]

    def edge(self, number):
        left, right, low, high, send_sem, recv_sem = (ref.at[number] for ref in self.refs)
        return Edge(low, high, left, right, send_sem, recv_sem)

    def enter(self):
        @pl.when(self.step == 0)
        def _():
            greet()
            self.zero_ref[...] = jnp.zeros_like(self.zero_ref)
            for field, there in zip(self.refs[:2], tok_sides()):

                @pl.when(jnp.logical_not(there))
                def _():
                    copies = [
                        pltpu.make_async_copy(self.zero_ref, field.at[n], self.zero_sem.at[n])
                        for n in range(self.seqs)
                    ]
                    for copy in copies:
                        copy.start()
                    for copy in copies:
                        copy.wait()

    def send(self, greeted=False):
        if not greeted:

            @pl.when(self.step == 0)
            def _():
                met()

        self.edge(self.step).start()

        @pl.when(self.step == self.seqs - 1)
        def _():
            for number in range(self.seqs):
                self.edge(number).land()
            for number in range(self.seqs):
                self.edge(number).sent()


def conv_scratch(rows, width, band_shape):
    return [
        pltpu.VMEM((rows + 192, SUBS * width), low_type),
        pltpu.VMEM((rows, 64 * width), low_type),
        pltpu.VMEM((3,) + band_shape, low_type),
    ]


def conv_flops(seqs, rows, inner, outer):
    return 2 * seqs * rows * (36 * 4 * inner * 2 * outer + 56 * WINDOW * inner)


def put_edges(low_pay, high_pay, number, field, channels, rows):
    lanes = sub_lanes(number, channels)
    low_pay[0, :, lanes] = field[:EDGE].astype(low_type)
    high_pay[0, :, lanes] = field[rows - EDGE :].astype(low_type)


def put_sums(sums_ref, low_pay, high_pay, number, value, channels):
    lanes = sub_lanes(number, channels)
    sums_ref[0, :, lanes] = value
    pay_lanes = sub_lanes(SUBS + number, channels)
    low_pay[0, :, pay_lanes] = value.astype(low_type)
    high_pay[0, :, pay_lanes] = value.astype(low_type)


def taken_sums(sums_ref, left_pay, right_pay, number, channels):
    lanes = sub_lanes(number, channels)
    pay_lanes = sub_lanes(SUBS + number, channels)
    total = sums_ref[0, :, lanes] + left_pay[0, :, pay_lanes].astype(wide)
    return total + right_pay[0, :, pay_lanes].astype(wide)


def mean_and_scale(total, square, inverse):
    mean = total * inverse
    variance = jnp.maximum(square * inverse - mean * mean, 0.0)
    return (mean, lax.rsqrt(variance + norm_eps))


def silu_parts(value):
    gate = 1.0 / (1.0 + jnp.exp(-value))
    return (value * gate, gate * (1.0 + value * (1.0 - gate)))


def first_conv_kernel(rows, channels, seqs):
    width = 2 * channels

    def body(
        up, up_left, up_right, skip, skip_left, skip_right, place, crop_t, weight, side,
        first_out, side_out, sums, to_left, to_right, x_ref, p_ref, band_ref, *edge_refs,
    ):
        pay = Payload(seqs, to_left, to_right, *edge_refs)
        pay.enter()
        low_pay, high_pay = (pay.low, pay.high)
        once(forward_band, weight, band_ref)
        for number in range(SUBS):
            for half, (own, left, right) in enumerate(
                ((up, up_left, up_right), (skip, skip_left, skip_right))
            ):
                to = sub_lanes(2 * number + half, channels)
                lanes = sub_lanes(number, channels)
                x_ref[:EDGE, to] = left[0, :, lanes]
                x_ref[EDGE : EDGE + rows, to] = own[0, :, lanes]
                x_ref[EDGE + rows : 2 * EDGE + rows, to] = right[0, :, lanes]
        x_ref[2 * EDGE + rows :, :] = jnp.zeros((96, SUBS * width), low_type)
        fill_windows(x_ref, place, p_ref, rows, width)
        total = [jnp.zeros((rows, channels), wide) for _ in range(4)]
        for index, pair in enumerate(all_pairs()):
            result = window_conv(p_ref, band_ref, pair, width, dot)
            first_out[0, :, sub_lanes(index, width)] = result
            for half in range(2):
                number = 2 * index + half
                value = result[:, sub_lanes(half, channels)]
                put_edges(low_pay, high_pay, number, value, channels, rows)
                flat = dot(x_ref[EDGE : EDGE + rows, sub_lanes(number, width)], side[...])
                side_out[0, :, sub_lanes(number, channels)] = flat
                terms = (value, value * value, flat, flat * flat)
                total = [have + term for have, term in zip(total, terms)]
        for number in range(4):
            value = exact_dot(crop_t[0], total[number])
            put_sums(sums, low_pay, high_pay, number, value, channels)
        pay.send()

    return body


def second_conv_kernel(rows, channels, seqs):
    def body(
        first, left_pay, right_pay, own_sums, inverse, owner, place, crop_t, weight,
        second_out, stats, sums, to_left, to_right, x_ref, p_ref, band_ref, *edge_refs,
    ):
        pay = Payload(seqs, to_left, to_right, *edge_refs)
        pay.enter()
        low_pay, high_pay = (pay.low, pay.high)
        once(forward_band, weight, band_ref)
        taken = [taken_sums(own_sums, left_pay, right_pay, n, channels) for n in range(4)]
        mean, scale = mean_and_scale(taken[0], taken[1], inverse[0])
        side_mean, side_scale = mean_and_scale(taken[2], taken[3], inverse[0])
        for number, value in enumerate((mean, scale, side_mean, side_scale)):
            stats[0, :, sub_lanes(number, channels)] = value
        mean_rows = exact_dot(owner[0], mean)
        scale_rows = exact_dot(owner[0], scale)
        parts = (
            (left_pay, slice(0, EDGE)),
            (first, slice(EDGE, EDGE + rows)),
            (right_pay, slice(EDGE + rows, 2 * EDGE + rows)),
        )
        for number in range(SUBS):
            lanes = sub_lanes(number, channels)
            for field, place_rows in parts:
                normed = field[0, :, lanes].astype(wide) - mean_rows[place_rows]
                normed = normed * scale_rows[place_rows]
                x_ref[place_rows, lanes] = silu_parts(normed)[0].astype(low_type)
        x_ref[2 * EDGE + rows :, :] = jnp.zeros((96, SUBS * channels), low_type)
        fill_windows(x_ref, place, p_ref, rows, channels)
        total = [jnp.zeros((rows, channels), wide) for _ in range(2)]
        for index, pair in enumerate(all_pairs()):
            result = window_conv(p_ref, band_ref, pair, channels, dot)
            second_out[0, :, sub_lanes(index, 2 * channels)] = result
            for half in range(2):
                value = result[:, sub_lanes(half, channels)]
                put_edges(low_pay, high_pay, 2 * index + half, value, channels, rows)
                total = [total[0] + value, total[1] + value * value]
        for number in range(2):
            value = exact_dot(crop_t[0], total[number])
            put_sums(sums, low_pay, high_pay, number, value, channels)
        pay.send()

    return body


def output_kernel(rows, channels, seqs):
    def body(
        second, side_field, cotangent, stats, left_pay, right_pay, own_sums, inverse, owner, crop_t,
        section, grad_out, second_stats, sums, to_left, to_right, *edge_refs,
    ):
        pay = Payload(seqs, to_left, to_right, *edge_refs)
        pay.enter()
        low_pay, high_pay = (pay.low, pay.high)
        taken = [taken_sums(own_sums, left_pay, right_pay, n, channels) for n in range(2)]
        mean, scale = mean_and_scale(taken[0], taken[1], inverse[0])
        second_stats[0, :, sub_lanes(0, channels)] = mean
        second_stats[0, :, sub_lanes(1, channels)] = scale
        own = owner[0, EDGE : EDGE + rows, :]
        mean_rows = exact_dot(own, mean)
        scale_rows = exact_dot(own, scale)
        side_mean = exact_dot(own, stats[0, :, sub_lanes(2, channels)])
        side_scale = exact_dot(own, stats[0, :, sub_lanes(3, channels)])
        total = [jnp.zeros((rows, channels), wide) for _ in range(3)]
        for number in range(SUBS):
            lanes = sub_lanes(number, channels)
            normed = (second[0, :, lanes] - mean_rows) * scale_rows
            side = (side_field[0, :, lanes] - side_mean) * side_scale
            value, slope = silu_parts(normed + side)
            section[0, :, lanes] = value.astype(low_type)
            grad = cotangent[0, :, lanes].astype(wide) * slope
            grad_out[0, :, lanes] = grad
            put_edges(low_pay, high_pay, number, grad, channels, rows)
            terms = (grad, grad * normed, grad * side)
            total = [have + term for have, term in zip(total, terms)]
        for number in range(3):
            value = exact_dot(crop_t[0], total[number])
            put_sums(sums, low_pay, high_pay, number, value, channels)
        pay.send()

    return body


def second_back_kernel(rows, channels, seqs):
    def body(
        grad, grad_left, grad_right, own_sums, second, second_left, second_right, side_field, first,
        stats, second_stats, inverse, owner, place, crop_t, weight,
        first_grad, side_grad, sums, weight_grad, to_left, to_right,
        x_ref, p_ref, band_ref, left_ref, total_ref, *edge_refs,
    ):
        pay = Payload(seqs, to_left, to_right, *edge_refs)
        pay.enter()
        low_pay, high_pay = (pay.low, pay.high)
        once(backward_band, weight, band_ref)
        means = [
            taken_sums(own_sums, grad_left, grad_right, n, channels) * inverse[0] for n in range(3)
        ]
        mean_rows = exact_dot(owner[0], second_stats[0, :, sub_lanes(0, channels)])
        scale_rows = exact_dot(owner[0], second_stats[0, :, sub_lanes(1, channels)])
        lead_rows = exact_dot(owner[0], means[0])
        slope_rows = exact_dot(owner[0], means[1])
        parts = (
            (grad_left, second_left, slice(0, EDGE)),
            (grad, second, slice(EDGE, EDGE + rows)),
            (grad_right, second_right, slice(EDGE + rows, 2 * EDGE + rows)),
        )
        own = slice(EDGE, EDGE + rows)
        side_mean = exact_dot(owner[0, own, :], stats[0, :, sub_lanes(2, channels)])
        side_scale = exact_dot(owner[0, own, :], stats[0, :, sub_lanes(3, channels)])
        side_slope = exact_dot(owner[0, own, :], means[2])
        first_mean = exact_dot(owner[0, own, :], stats[0, :, sub_lanes(0, channels)])
        first_scale = exact_dot(owner[0, own, :], stats[0, :, sub_lanes(1, channels)])
        for number in range(SUBS):
            lanes = sub_lanes(number, channels)
            for grad_from, field, at in parts:
                normed = (field[0, :, lanes].astype(wide) - mean_rows[at]) * scale_rows[at]
                pulled = grad_from[0, :, lanes].astype(wide) - lead_rows[at]
                pulled = scale_rows[at] * (pulled - normed * slope_rows[at])
                x_ref[at, lanes] = pulled.astype(low_type)
            side = (side_field[0, :, lanes] - side_mean) * side_scale
            pulled = side_scale * (grad[0, :, lanes] - lead_rows[own] - side * side_slope)
            side_grad[0, :, lanes] = pulled.astype(low_type)
            normed = (first[0, :, lanes] - first_mean) * first_scale
            hidden = silu_parts(normed)[0]
            left_ref[lanes, :] = jnp.transpose(hidden).astype(low_type)
        x_ref[2 * EDGE + rows :, :] = jnp.zeros((96, SUBS * channels), low_type)
        fill_windows(x_ref, place, p_ref, rows, channels)
        total = [jnp.zeros((rows, channels), wide) for _ in range(2)]
        for index, pair in enumerate(all_pairs()):
            result = window_conv(p_ref, band_ref, pair, channels, dot_t)
            for half in range(2):
                number = 2 * index + half
                lanes = sub_lanes(number, channels)
                normed = (first[0, :, lanes] - first_mean) * first_scale
                value = result[:, sub_lanes(half, channels)] * silu_parts(normed)[1]
                first_grad[0, :, lanes] = value
                put_edges(low_pay, high_pay, number, value, channels, rows)
                total = [total[0] + value, total[1] + value * normed]
        for number in range(2):
            value = exact_dot(crop_t[0], total[number])
            put_sums(sums, low_pay, high_pay, number, value, channels)
        pay.send()

        @pl.when(pl.program_id(0) == 0)
        def _():
            total_ref[...] = jnp.zeros_like(total_ref)

        add_grads(left_ref, p_ref, total_ref, channels, channels)

        @pl.when(pl.program_id(0) == seqs - 1)
        def _():
            fold_grads(total_ref, weight_grad, channels, channels)

    return body


def first_back_kernel(rows, channels, seqs):
    width = 2 * channels

    def body(
        grad, grad_left, grad_right, own_sums, first, first_left, first_right, stats, inverse, owner,
        place, side_grad, up, skip, weight, side_weight,
        up_grad, skip_grad, weight_grad, side_weight_grad,
        x_ref, p_ref, band_ref, left_ref, total_ref,
    ):
        once(backward_band, weight, band_ref)
        means = [
            taken_sums(own_sums, grad_left, grad_right, n, channels) * inverse[0] for n in range(2)
        ]
        mean_rows = exact_dot(owner[0], stats[0, :, sub_lanes(0, channels)])
        scale_rows = exact_dot(owner[0], stats[0, :, sub_lanes(1, channels)])
        lead_rows = exact_dot(owner[0], means[0])
        slope_rows = exact_dot(owner[0], means[1])
        parts = (
            (grad_left, first_left, slice(0, EDGE)),
            (grad, first, slice(EDGE, EDGE + rows)),
            (grad_right, first_right, slice(EDGE + rows, 2 * EDGE + rows)),
        )
        for number in range(SUBS):
            lanes = sub_lanes(number, channels)
            for grad_from, field, at in parts:
                normed = (field[0, :, lanes].astype(wide) - mean_rows[at]) * scale_rows[at]
                pulled = grad_from[0, :, lanes].astype(wide) - lead_rows[at]
                pulled = scale_rows[at] * (pulled - normed * slope_rows[at])
                x_ref[at, lanes] = pulled.astype(low_type)
            for half, field in enumerate((up, skip)):
                turned = jnp.transpose(field[0, :, lanes].astype(wide)).astype(low_type)
                left_ref[sub_lanes(2 * number + half, channels), :] = turned
        x_ref[2 * EDGE + rows :, :] = jnp.zeros((96, SUBS * channels), low_type)
        fill_windows(x_ref, place, p_ref, rows, channels)
        for index, pair in enumerate(all_pairs()):
            result = window_conv(p_ref, band_ref, pair, channels, dot_t)
            for half in range(2):
                number = 2 * index + half
                lanes = sub_lanes(number, channels)
                value = result[:, sub_lanes(half, width)]
                value = value + dot_t(side_grad[0, :, lanes], side_weight[...])
                up_grad[0, :, lanes] = value[:, :channels].astype(low_type)
                skip_grad[0, :, lanes] = value[:, channels:]

        @pl.when(pl.program_id(0) == 0)
        def _():
            total_ref[...] = jnp.zeros_like(total_ref)
            side_weight_grad[...] = jnp.zeros_like(side_weight_grad)

        for number in range(SUBS):
            side_weight_grad[...] += dot(
                left_ref[sub_lanes(number, width), :], side_grad[0, :, sub_lanes(number, channels)]
            )
        add_grads(left_ref, p_ref, total_ref, width, channels)

        @pl.when(pl.program_id(0) == seqs - 1)
        def _():
            fold_grads(total_ref, weight_grad, width, channels)

    return body


def exchanged(low_pay, high_pay):
    return (passed_along(high_pay, "tok", 1), passed_along(low_pay, "tok", -1))


def with_far(sums, reaches):
    total = sums
    for distance in range(2, reaches + 1):
        for shift_by in (distance, -distance):
            total = total + passed_along(sums.astype(low_type), "tok", shift_by).astype(wide)
    return total


def conv_section(upsampled, skip, edges, cotangent, weights, geometry_in, reaches):
    conv1_weight, conv2_weight, conv3_weight = weights
    seqs, rows, lanes = upsampled.shape
    channels = lanes // SUBS
    width = 2 * channels
    place, owner, crop_t, inverse = geometry_in
    field = ((seqs, rows, lanes), wide)
    low_field = ((seqs, rows, lanes), low_type)

    def pay(count):
        return ((seqs, EDGE, (SUBS + count) * channels), low_type)

    def pay_scratch(count):
        return edge_scratch(seqs, EDGE, (SUBS + count) * channels)

    def table(count):
        return ((seqs, CROP_ROWS, count * channels), wide)

    up_left, up_right, skip_left, skip_right = edges
    first, side_field, sums, first_left, first_right = kernel_call(
        first_conv_kernel(rows, channels, seqs),
        seqs,
        (upsampled, up_left, up_right, skip, skip_left, skip_right, place, crop_t),
        (conv1_weight, conv3_weight),
        (field, field, table(4)),
        (),
        conv_scratch(rows, width, (12 * width, 2 * channels)) + pay_scratch(4),
        conv_flops(seqs, rows, width, channels),
        landing=(pay(4), pay(4)),
        collective=3,
    )
    second, stats, sums, second_left, second_right = kernel_call(
        second_conv_kernel(rows, channels, seqs),
        seqs,
        (first, first_left, first_right, with_far(sums, reaches), inverse, owner, place, crop_t),
        (conv2_weight,),
        (field, table(4), table(2)),
        (),
        conv_scratch(rows, channels, (12 * channels, 2 * channels)) + pay_scratch(2),
        conv_flops(seqs, rows, channels, channels),
        landing=(pay(2), pay(2)),
        collective=4,
    )
    section_out, grad, second_stats, sums, grad_left, grad_right = kernel_call(
        output_kernel(rows, channels, seqs),
        seqs,
        (
            second, side_field, cotangent, stats, second_left, second_right,
            with_far(sums, reaches), inverse, owner, crop_t,
        ),
        (),
        (low_field, field, table(2), table(3)),
        (),
        pay_scratch(3),
        seqs * rows * lanes * 20,
        landing=(pay(3), pay(3)),
        collective=5,
    )
    first_grad, side_grad, sums, conv2_grad, back_left, back_right = kernel_call(
        second_back_kernel(rows, channels, seqs),
        seqs,
        (
            grad, grad_left, grad_right, with_far(sums, reaches), second, second_left, second_right,
            side_field, first, stats, second_stats, inverse, owner, place, crop_t,
        ),
        (conv2_weight,),
        (field, low_field, table(2)),
        (((27, 1, channels, channels), wide),),
        conv_scratch(rows, channels, (2 * channels, 12 * channels))
        + [
            pltpu.VMEM((SUBS * channels, rows), low_type),
            pltpu.VMEM((9, 2 * channels, 4 * channels), wide),
        ]
        + pay_scratch(2),
        2 * conv_flops(seqs, rows, channels, channels),
        landing=(pay(2), pay(2)),
        collective=6,
    )
    up_grad, skip_grad, conv1_grad, conv3_grad = kernel_call(
        first_back_kernel(rows, channels, seqs),
        seqs,
        (
            first_grad, back_left, back_right, with_far(sums, reaches), first, first_left,
            first_right, stats, inverse, owner, place, side_grad, upsampled, skip,
        ),
        (conv1_weight, conv3_weight),
        (low_field, field),
        (((27, 2, channels, channels), wide), ((width, channels), wide)),
        conv_scratch(rows, channels, (2 * width, 12 * channels))
        + [
            pltpu.VMEM((SUBS * width, rows), low_type),
            pltpu.VMEM((9, 2 * width, 4 * channels), wide),
        ],
        2 * conv_flops(seqs, rows, channels, width),
    )
    return (section_out, up_grad, skip_grad, conv1_grad, conv2_grad, conv3_grad)


PIECE_BYTES = 2400 * 1024


def bit_count(size):
    return size.bit_length() - 1


def pieces_of(shapes):
    pieces = []
    for index, (shards, rows, lanes) in enumerate(shapes):
        parts = max(1, round(shards * rows * lanes * 2 / PIECE_BYTES))
        while rows % (16 * parts) != 0 and parts > 1:
            parts -= 1
        take = rows // parts
        pieces.extend((index, part * take, take, lanes) for part in range(parts))
    return pieces


def all_of(count):
    return (slice(None),) * count


def reduce_kernel(pieces, arrays, tok_bits, seq_bits):
    phases = tok_bits + seq_bits
    mesh_id = pl.DeviceIdType.MESH

    def body(*refs):
        given = refs[:arrays]
        results = refs[arrays : 2 * arrays]
        count = len(pieces)
        rest = refs[2 * arrays :]
        kept = rest[:count]
        landed = [rest[count + i * phases : count + (i + 1) * phases] for i in range(count)]
        local_sem, send_sem, recv_sem = rest[count + count * phases :]
        tok = lax.axis_index("tok")
        seq = lax.axis_index("seq")

        def bit_of(phase):
            if phase < tok_bits:
                return (tok // (1 << phase)) % 2
            return (seq // (1 << (phase - tok_bits))) % 2

        def partner(phase):
            bit = bit_of(phase)
            if phase < tok_bits:
                return (seq, tok + (1 << phase) * (1 - 2 * bit))
            return (seq + (1 << (phase - tok_bits)) * (1 - 2 * bit), tok)

        barrier = pltpu.get_barrier_semaphore()
        for phase in range(phases):
            pl.semaphore_signal(barrier, inc=1, device_id=partner(phase), device_id_type=mesh_id)
        pl.semaphore_wait(barrier, phases)

        def local_copy(piece):
            index, begin, take, _ = pieces[piece]
            view = given[index].at[all_of(tok_bits - 1) + (bit_of(0), pl.ds(begin, take))]
            return pltpu.make_async_copy(view, kept[piece], local_sem.at[piece])

        def remote_copy(piece, phase):
            index, begin, take, _ = pieces[piece]
            if phase == 0:
                view = given[index].at[all_of(tok_bits - 1) + (1 - bit_of(0), pl.ds(begin, take))]
            elif phase < tok_bits:
                view = landed[piece][phase - 1].at[all_of(tok_bits - 1 - phase) + (1 - bit_of(phase),)]
            else:
                view = landed[piece][phase - 1]
            return pltpu.make_async_remote_copy(
                src_ref=view,
                dst_ref=landed[piece][phase],
                send_sem=send_sem.at[piece, phase],
                recv_sem=recv_sem.at[piece, phase],
                device_id=partner(phase),
                device_id_type=mesh_id,
            )

        def begin(piece):
            remote_copy(piece, 0).start()
            local_copy(piece).start()

        def finish(piece, phase):
            index, first, take, _ = pieces[piece]
            remote_copy(piece, phase).wait_recv()
            got = landed[piece][phase]
            if phase == 0:
                local_copy(piece).wait()

            if phase < tok_bits:
                kept_bits = tok_bits - 1 - phase

                def step(block, carry):
                    at = tuple((block // (1 << bit)) % 2 for bit in reversed(range(kept_bits)))
                    if phase == 0:
                        mine = kept[piece][at]
                    else:
                        mine = landed[piece][phase - 1][at + (bit_of(phase),)]
                    got[at] = got[at] + mine
                    return carry

                lax.fori_loop(0, 1 << kept_bits, step, 0)
            elif phase + 1 < phases:
                got[...] = got[...] + landed[piece][phase - 1][...]
            if phase + 1 < phases:
                remote_copy(piece, phase + 1).start()
            else:
                total = got[...].astype(wide) + landed[piece][phase - 1][...].astype(wide)
                results[index][pl.ds(first, take), :] = total

        begin(0)
        for step in range(count + phases - 1):
            if step + 1 < count:
                begin(step + 1)
            for phase in range(phases):
                if 0 <= step - phase < count:
                    finish(step - phase, phase)
        for piece in range(count):
            for phase in range(phases):
                remote_copy(piece, phase).wait_send()

    return body


def reduced(grads):
    shards = lax.axis_size("tok")
    tok_bits = bit_count(shards)
    seq_bits = bit_count(lax.axis_size("seq"))
    shapes = [g.shape for g in grads]
    pieces = pieces_of(shapes)
    scratch = [
        pltpu.VMEM((2,) * (tok_bits - 1) + (take, lanes), low_type) for _, _, take, lanes in pieces
    ]
    for _, _, take, lanes in pieces:
        for phase in range(tok_bits - 1):
            bits = tok_bits - 1 - phase
            scratch.append(pltpu.VMEM((2,) * bits + (take, lanes), low_type))
        scratch += [pltpu.VMEM((take, lanes), low_type) for _ in range(1 + seq_bits)]
    count, phases = len(pieces), tok_bits + seq_bits
    scratch += [
        pltpu.SemaphoreType.DMA((count,)),
        pltpu.SemaphoreType.DMA((count, phases)),
        pltpu.SemaphoreType.DMA((count, phases)),
    ]
    total = sum(math.prod(s) for s in shapes)
    return pl.pallas_call(
        reduce_kernel(pieces, len(grads), tok_bits, seq_bits),
        in_specs=[pl.BlockSpec(memory_space=pl.ANY)] * len(grads),
        out_specs=[pl.BlockSpec(memory_space=pltpu.VMEM)] * len(grads),
        out_shape=[jax.ShapeDtypeStruct(s[1:], wide) for s in shapes],
        scratch_shapes=scratch,
        compiler_params=pltpu.CompilerParams(
            vmem_limit_bytes=VMEM_LIMIT, collective_id=0, has_side_effects=True
        ),
        cost_estimate=pl.CostEstimate(flops=total, bytes_accessed=4 * total, transcendentals=0),
    )(*[g.reshape((2,) * tok_bits + g.shape[1:]) for g in grads])


def sharded_rows(grad):
    shards = lax.axis_size("tok")
    rows = grad.shape[0] // shards
    grad = grad.astype(low_type)
    if rows % 16 == 0:
        return grad.reshape(shards, rows, grad.shape[1])
    return grad.reshape(shards, rows * grad.shape[1] // 128, 128)


def conv_rows(turned):
    shards = lax.axis_size("tok")
    taps, halves, channels, lanes = turned.shape
    split = turned.reshape(taps, halves, shards, channels // shards, lanes)
    return jnp.moveaxis(split, 2, 0).reshape(shards, -1, lanes)


def conv_share(rows, taps, halves):
    split = rows.reshape(taps, halves, -1, rows.shape[-1])
    return jnp.moveaxis(split, 2, 3).reshape(taps, halves * rows.shape[-1], -1)


def reduced_all(conv_grads, matrices, vectors):
    shards = lax.axis_size("tok")
    parts = [conv_rows(g) for g in conv_grads]
    flat = jnp.concatenate([v.reshape(shards, -1) for v in vectors], axis=1)
    used = flat.shape[1]
    taken = sum(p.shape[1] for p in parts)
    rows = -(-used // 128)
    rows += -(rows + taken) % 16
    flat = jnp.pad(flat, ((0, 0), (0, rows * 128 - used))).reshape(shards, rows, 128)
    packed = jnp.concatenate([p.astype(low_type) for p in parts] + [flat.astype(low_type)], axis=1)
    results = reduced([packed] + [sharded_rows(m) for m in matrices])
    shares = []
    cursor = 0
    for part, grad in zip(parts, conv_grads):
        rows_here = results[0][cursor : cursor + part.shape[1]]
        shares.append(conv_share(rows_here, grad.shape[0], grad.shape[1]))
        cursor += part.shape[1]
    flat = results[0][cursor:].reshape(-1)
    cursor = 0
    pieces = []
    for vector in vectors:
        size = vector.size // shards
        pieces.append(flat[cursor : cursor + size])
        cursor += size
    whole = [r.reshape(-1, m.shape[1]) for r, m in zip(results[1:], matrices)]
    return (shares, whole, pieces)


REACH = 224
QUERY_TILE = 128
AHEAD = 3
CLOSING_LIMIT = 63 * 1024 * 1024


def dot_t(left, right):
    return lax.dot_general(
        left, right, (((1,), (1,)), ((), ())), preferred_element_type=wide
    )


def counted(shape, axis):
    return lax.broadcasted_iota(jnp.int32, shape, axis).astype(wide)


def geometry_kernel(rows, crops):
    reach_rows = rows + 2 * REACH
    tile = min(rows, QUERY_TILE)
    window = tile + 2 * REACH

    def body(side_row, side_column, place, owner, crop_t, inverse, bias, edge_bias):
        first_row = (lax.axis_index("tok") * rows).astype(wide)
        sides_r = side_row[0].astype(wide)
        sides_c = side_column[0].astype(wide)
        volume_r = sides_r * sides_r * sides_r
        volume_c = sides_c * sides_c * sides_c
        shape = (crops, crops)
        start_r = jnp.sum(
            jnp.where(counted(shape, 0) < counted(shape, 1), volume_c, 0.0), axis=0, keepdims=True
        )
        start_c = jnp.sum(
            jnp.where(counted(shape, 1) < counted(shape, 0), volume_r, 0.0), axis=1, keepdims=True
        )

        def inside_of(length, begin):
            at = counted((length, crops), 0) + begin
            return ((at >= start_r) & (at < start_r + volume_r), at)

        wide_inside, _ = inside_of(rows + 2 * EDGE, first_row - EDGE)
        owner[0] = jnp.where(wide_inside, 1.0, 0.0).astype(low_type)
        inside, _ = inside_of(rows, first_row)
        side = jnp.sum(jnp.where(inside, sides_r, 0.0), axis=1, keepdims=True)
        first = jnp.sum(jnp.where(inside, start_r, 0.0), axis=1, keepdims=True)
        own = counted((rows, 1), 0)
        offset = own + first_row - first
        safe = jnp.maximum(side, 1.0)
        row_pos = jnp.floor((offset + 0.5) / (safe * safe))
        offset = offset - row_pos * safe * safe
        column = jnp.floor((offset + 0.5) / safe)
        depth_pos = offset - column * safe
        lane = counted((1, 32), 1)
        step_x = jnp.floor((lane + 0.5) / 9.0)
        step_y = jnp.floor((lane - 9.0 * step_x + 0.5) / 3.0)
        step_z = lane - 9.0 * step_x - 3.0 * step_y - 1.0
        step_x, step_y = (step_x - 1.0, step_y - 1.0)
        valid = None
        for at, step in ((row_pos, step_x), (column, step_y), (depth_pos, step_z)):
            moved = at + step
            here = (moved >= 0.0) & (moved < side)
            valid = here if valid is None else valid & here
        target = own + EDGE + (step_x * safe + step_y) * safe + step_z
        place[0] = jnp.where(valid, target, -1.0).astype(jnp.int32)
        at = counted((crops, rows), 1) + first_row
        inside_t = (at >= start_c) & (at < start_c + volume_c)
        crop_t[0] = jnp.where(inside_t, 1.0, 0.0).astype(low_type)
        inverse[0] = jnp.broadcast_to(1.0 / jnp.maximum(8.0 * volume_c, 1.0), (crops, 128))
        key_inside, _ = inside_of(reach_rows, first_row - REACH)
        key_first = jnp.sum(jnp.where(key_inside, start_r + 1.0, 0.0), axis=1, keepdims=True)
        query_first = jnp.sum(jnp.where(inside_t, start_c + 1.0, 0.0), axis=0, keepdims=True)
        for number in range(rows // tile):
            base = number * tile
            same = key_first[base : base + window] == query_first[:, base : base + tile]
            bias[0, number] = jnp.where(same, 0.0, far_below)
        for side in range(2):
            begin_row = 0 if side == 0 else max(rows - REACH, 0)
            begin = first_row - REACH if side == 0 else first_row + rows
            at = counted((crops, REACH), 1) + begin
            inside_t = (at >= start_c) & (at < start_c + volume_c)
            query_first = jnp.sum(jnp.where(inside_t, start_c + 1.0, 0.0), axis=0, keepdims=True)
            same = key_first[REACH + begin_row : 2 * REACH + begin_row] == query_first
            edge_bias[0, side] = jnp.where(same, 0.0, far_below)

    return body


def geometry_tables(crop_sides, rows):
    seqs, crops = crop_sides.shape
    sides = jnp.pad(crop_sides, ((0, 0), (0, CROP_ROWS - crops)))
    tile = min(rows, QUERY_TILE)
    return kernel_call(
        geometry_kernel(rows, CROP_ROWS),
        seqs,
        (sides[:, None, :], sides[:, :, None]),
        (),
        (
            ((seqs, rows, 32), jnp.int32),
            ((seqs, rows + 2 * EDGE, CROP_ROWS), low_type),
            ((seqs, CROP_ROWS, rows), low_type),
            ((seqs, CROP_ROWS, 128), wide),
            ((seqs, rows // tile, tile + 2 * REACH, tile), wide),
            ((seqs, 2, REACH, REACH), wide),
        ),
        (),
        [],
        0,
    )


def row_of(vector, lanes=slice(None)):
    return vector[lanes].reshape(1, -1)


def normed_rows(values):
    centered = values - jnp.mean(values, axis=-1, keepdims=True)
    variance = jnp.mean(centered * centered, axis=-1, keepdims=True)
    scale = lax.rsqrt(variance + norm_eps)
    return (centered * scale, scale)


def norm_pull(grad, normed, scale, gain):
    inner = grad * gain
    first = jnp.mean(inner, axis=-1, keepdims=True)
    second = jnp.mean(inner * normed, axis=-1, keepdims=True)
    return scale * (inner - first - normed * second)


def error_function(value):
    bounded = jnp.clip(value, -3.832506856900711, 3.832506856900711)
    square = bounded * bounded
    top = 0.00022905065861350646
    for term in (0.0034082910107109506, 0.050955695062380861, 0.18520832239976145, 1.128379143519084):
        top = top * square + term
    bottom = -1.1791602954361697e-7
    for term in (
        0.000023547966471313185, 0.0010179625278914885, 0.014070470171167667,
        0.11098505178285362, 0.49746925110067538, 1.0,
    ):
        bottom = bottom * square + term
    return bounded * top / bottom


def gelu_parts(value):
    cumulative = 0.5 + 0.5 * error_function(value * math.sqrt(0.5))
    density = jnp.exp(-0.5 * value * value) * (1.0 / math.sqrt(2.0 * math.pi))
    return (value * cumulative, cumulative + value * density)


def head_lanes(block, half):
    lane = lax.broadcasted_iota(jnp.int32, block.shape, 1)
    chosen = lane < HEAD_DIM if half == 0 else lane >= HEAD_DIM
    return jnp.where(chosen, block, jnp.zeros_like(block))


def turned(block):
    return jnp.transpose(block.astype(wide))


def forward_kernel(rows, model_width, hidden, seqs, near_given):
    tile = min(rows, QUERY_TILE)
    window = tile + 2 * REACH
    chunk = 768
    scale = 1.0 / math.sqrt(HEAD_DIM)

    def body(*refs):
        tokens, bias = refs[:2]
        if near_given:
            left, right = refs[2:4]
            refs = refs[2:]
        (
            ln1_gain, ln1_bias, qkv_weight, qv_bias, out_bias, ln2_gain, ln2_bias,
            fc1_bias, fc2_bias, all_tokens, skip, out_away, fc1_away, fc2_away, deconv_away,
            normed_out, queries, keys, values, attended, log_totals, resid_out, second_out,
            act_out, slope_out, resid_low, upsampled, up_left, up_right, skip_left, skip_right,
            near_ref, turned_ref, skip_send, skip_recv, near_left, near_right, near_send, near_recv,
            out_weight, fc1_weight, fc2_weight, deconv_weight, weight_sem, *edge_refs,
        ) = refs[2:]
        step = pl.program_id(0)
        pay = Payload(seqs, up_left, up_right, *edge_refs)
        skip_edge = Edge(
            skip.at[:, :EDGE],
            skip.at[:, rows - EDGE :],
            skip_left,
            skip_right,
            skip_send,
            skip_recv,
        )

        def token_edge(number):
            return Edge(
                all_tokens.at[number, :REACH],
                all_tokens.at[number, rows - REACH :],
                near_left.at[number],
                near_right.at[number],
                near_send.at[number],
                near_recv.at[number],
            )

        weight_copies = [
            pltpu.make_async_copy(source, target, weight_sem.at[number])
            for number, (source, target) in enumerate(
                (
                    (out_away, out_weight),
                    (fc1_away, fc1_weight),
                    (fc2_away, fc2_weight),
                    (deconv_away, deconv_weight),
                )
            )
        ]

        def weights_ready(*numbers):
            @pl.when(step == 0)
            def _():
                for number in numbers:
                    weight_copies[number].wait()

        @pl.when(step == 0)
        def _():
            for copy in weight_copies:
                copy.start()

        pay.enter()

        @pl.when(step == 0)
        def _():
            met()
            if near_given:
                skip_edge.start()
            else:
                token_edge(0).start()
                for field, there in zip((near_left, near_right), tok_sides()):

                    @pl.when(jnp.logical_not(there))
                    def _():
                        field[...] = jnp.zeros_like(field)

            for field, there in zip((skip_left, skip_right), tok_sides()):

                @pl.when(jnp.logical_not(there))
                def _():
                    copies = [
                        pltpu.make_async_copy(pay.zero_ref, field.at[n], pay.zero_sem.at[n])
                        for n in range(seqs)
                    ]
                    for copy in copies:
                        copy.start()
                    for copy in copies:
                        copy.wait()

        def put_normed(values, begin):
            normed = normed_rows(values.astype(wide))[0] * row_of(ln1_gain) + row_of(ln1_bias)
            near_ref[begin : begin + values.shape[0], :] = normed.astype(low_type)

        def project(at):
            for number, target in enumerate((queries, keys, values)):
                lanes = sub_lanes(number, model_width)
                found = dot(near_ref[at, :], qkv_weight[:, lanes])
                if number != 1:
                    found = found + qv_bias[number // 2 : number // 2 + 1, :]
                target[0, at, :] = found.astype(low_type)

        own_rows = slice(REACH, REACH + rows)
        put_normed(tokens[0], REACH)
        normed_out[0] = near_ref[own_rows, :]
        project(own_rows)
        if near_given:
            put_normed(left[0], 0)
            put_normed(right[0], REACH + rows)
        else:
            token_edge(step).land()

            @pl.when(step < seqs - 1)
            def _():
                token_edge(step + 1).start()

            @pl.when(step == seqs - 1)
            def _():
                skip_edge.start()

            put_normed(near_left[step], 0)
            put_normed(near_right[step], REACH + rows)
        project(slice(0, REACH))
        project(slice(REACH + rows, 2 * REACH + rows))
        for pair in range(model_width // 128):
            lanes = sub_lanes(pair, 128)
            turned_ref[lanes, :] = turned(values[0, :, lanes]).astype(low_type)
        for number in range(rows // tile):
            base = number * tile
            at = slice(base, base + tile)
            near = slice(base, base + window)
            for pair in range(model_width // 128):
                lanes = sub_lanes(pair, 128)
                query = queries[0, REACH + base : REACH + base + tile, lanes] * scale
                key = keys[0, near, lanes]
                halves = []
                for half in range(2):
                    head = 2 * pair + half
                    scores = dot_t(key, head_lanes(query, half)) + bias[0, number]
                    top = jnp.max(scores, axis=0, keepdims=True)
                    weights = jnp.exp(scores - top)
                    total = jnp.sum(weights, axis=0, keepdims=True)
                    log_totals[0, head : head + 1, at] = top + jnp.log(total)
                    probs = (weights * (1.0 / total)).astype(low_type)
                    value = turned_ref[head * HEAD_DIM : (head + 1) * HEAD_DIM, near]
                    halves.append(dot(value, probs))
                both = jnp.concatenate(halves, axis=0)
                attended[0, at, lanes] = jnp.transpose(both).astype(low_type)
        weights_ready(0)
        resid = tokens[0].astype(wide) + dot(attended[0], out_weight[...]) + row_of(out_bias)
        resid_out[0] = resid
        second = normed_rows(resid)[0] * row_of(ln2_gain) + row_of(ln2_bias)
        second_out[0] = second.astype(low_type)
        weights_ready(1, 2, 3)
        total = resid + row_of(fc2_bias)
        for number in range(hidden // chunk):
            lanes = sub_lanes(number, chunk)
            pre = dot(second_out[0], fc1_weight[:, lanes]) + row_of(fc1_bias, lanes)
            act, slope = gelu_parts(pre)
            act_out[0, :, lanes] = act.astype(low_type)
            slope_out[0, :, lanes] = slope.astype(low_type)
            total = total + dot(act_out[0, :, lanes], fc2_weight[lanes, :])
        resid_low[0] = total.astype(low_type)
        upsampled[0] = dot(resid_low[0], deconv_weight[...]).astype(low_type)
        pay.low[0] = upsampled[0, :EDGE, :]
        pay.high[0] = upsampled[0, rows - EDGE :, :]
        pay.send(True)

        @pl.when(step == seqs - 1)
        def _():
            skip_edge.land()
            skip_edge.sent()
            if not near_given:
                for number in range(seqs):
                    token_edge(number).sent()

    return body


def hidden_back_kernel(rows, model_width, hidden):
    chunk = 768

    def body(
        up_grad, slope, resid, attended, log_totals,
        deconv_weight, fc2_weight, fc1_weight, out_weight, ln2_gain,
        branch_out, pre_out, resid_grad, mixed_out, pulled_out, stats,
        fc2_sum, fc1_sum, out_sum, gain_sum, shift_sum,
    ):
        @pl.when(pl.program_id(0) == 0)
        def _():
            for ref in (fc2_sum, fc1_sum, out_sum, gain_sum, shift_sum):
                ref[...] = jnp.zeros_like(ref)

        def column_sum(field):
            return jnp.sum(field, axis=0, keepdims=True)

        incoming = dot_t(up_grad[0], deconv_weight[...])
        branch = incoming.astype(low_type)
        branch_out[0] = branch
        fc2_sum[...] += column_sum(branch.astype(wide))
        total = None
        for number in range(hidden // chunk):
            lanes = sub_lanes(number, chunk)
            act_grad = dot_t(branch_out[0], fc2_weight[lanes, :])
            pre = (act_grad * slope[0, :, lanes].astype(wide)).astype(low_type)
            pre_out[0, :, lanes] = pre
            fc1_sum[:, lanes] += column_sum(pre.astype(wide))
            term = dot_t(pre_out[0, :, lanes], fc1_weight[:, lanes])
            total = term if total is None else total + term
        normed, norm_scale = normed_rows(resid[0])
        gain_sum[...] += column_sum(total * normed)
        shift_sum[...] += column_sum(total)
        mixed = incoming + norm_pull(total, normed, norm_scale, row_of(ln2_gain))
        resid_grad[0] = mixed
        mixed = mixed.astype(low_type)
        mixed_out[0] = mixed
        out_sum[...] += column_sum(mixed.astype(wide))
        pulled = dot_t(mixed_out[0], out_weight[...]).astype(low_type)
        pulled_out[0] = pulled
        product = pulled.astype(wide) * attended[0].astype(wide)
        lane = lax.broadcasted_iota(jnp.int32, (16, model_width), 1)
        begin = lax.broadcasted_iota(jnp.int32, (16, model_width), 0) * HEAD_DIM
        chosen = (lane >= begin) & (lane < begin + HEAD_DIM)
        chosen = jnp.where(chosen, 1.0, 0.0).astype(low_type)
        inner = None
        for term in three_terms(product):
            part = dot_t(chosen, term)
            inner = part if inner is None else inner + part
        for pair in range(model_width // 128):
            heads = slice(2 * pair, 2 * pair + 2)
            unused = jnp.zeros((4, rows), wide)
            stats[0, pair] = jnp.concatenate([log_totals[0, heads], inner[heads], unused], axis=0)

    return body


def attention_back_kernel(rows, model_width):
    tile = min(rows, QUERY_TILE)
    window = tile + 2 * REACH
    scale = 1.0 / math.sqrt(HEAD_DIM)

    def body(
        queries, keys, values, pulls, stats, bias,
        query_grad, key_own, value_own, low_pay, high_pay, near_key, near_value, turned_ref,
    ):
        for pair in range(model_width // 128):
            lanes = sub_lanes(pair, 128)
            turned_ref[lanes, :] = turned(keys[0, :, lanes]).astype(low_type)
        near_key[...] = jnp.zeros_like(near_key)
        near_value[...] = jnp.zeros_like(near_value)
        for number in range(rows // tile):
            base = number * tile
            at = slice(base, base + tile)
            near = slice(base, base + window)
            for pair in range(model_width // 128):
                lanes = sub_lanes(pair, 128)
                query = queries[0, REACH + base : REACH + base + tile, lanes] * scale
                key = keys[0, near, lanes]
                value = values[0, near, lanes]
                halves = []
                for half in range(2):
                    head = 2 * pair + half
                    probs, score_grad, one_query, one_pull = head_unit(
                        key, value, query, pulls[0, at, lanes], bias[0, number],
                        stats[0, pair, half : half + 1, at], stats[0, pair, 2 + half : 3 + half, at],
                        half,
                    )
                    near_key[near, lanes] += dot(score_grad, one_query)
                    near_value[near, lanes] += dot(probs, one_pull)
                    key_turned = turned_ref[head * HEAD_DIM : (head + 1) * HEAD_DIM, near]
                    halves.append(dot(key_turned, score_grad) * scale)
                both = jnp.concatenate(halves, axis=0)
                query_grad[0, at, lanes] = jnp.transpose(both).astype(low_type)
        for field, own_out, begin in (
            (near_key, key_own, 0),
            (near_value, value_own, model_width),
        ):
            lanes = slice(begin, begin + model_width)
            own_out[0] = field[REACH : REACH + rows, :]
            low_pay[0, :, lanes] = field[:REACH, :].astype(low_type)
            high_pay[0, :, lanes] = field[REACH + rows :, :].astype(low_type)

    return body


def token_kernel(rows, model_width):
    def body(
        tokens, resid_grad, query_grad, key_own, value_own, qkv_weight, ln1_gain,
        grad_out, token_grad, bias_sum, gain_sum, shift_sum,
    ):
        @pl.when(pl.program_id(0) == 0)
        def _():
            for ref in (bias_sum, gain_sum, shift_sum):
                ref[...] = jnp.zeros_like(ref)

        grad_out[0, :, :model_width] = query_grad[0]
        for number, own in enumerate((key_own, value_own)):
            to = sub_lanes(number + 1, model_width)
            grad_out[0, :, to] = own[0].astype(low_type)
        bias_sum[...] += jnp.sum(grad_out[0].astype(wide), axis=0, keepdims=True)
        total = dot_t(grad_out[0], qkv_weight[...])
        normed, norm_scale = normed_rows(tokens[0].astype(wide))
        gain_sum[...] += jnp.sum(total * normed, axis=0, keepdims=True)
        shift_sum[...] += jnp.sum(total, axis=0, keepdims=True)
        token_grad[0] = resid_grad[0] + norm_pull(total, normed, norm_scale, row_of(ln1_gain))

    return body


def near_rows(field):
    rows = field.shape[1]
    lefts, rights = ([], [])
    distance, missing = (1, REACH)
    while missing > 0:
        take = min(rows, missing)
        lefts.insert(0, passed_along(field[:, rows - take :], "tok", distance))
        rights.append(passed_along(field[:, :take], "tok", -distance))
        distance, missing = (distance + 1, missing - take)
    if len(lefts) == 1:
        return (lefts[0], rights[0])
    return (jnp.concatenate(lefts, axis=1), jnp.concatenate(rights, axis=1))


def returned_rows(own, low_pay, high_pay):
    rows = own.shape[1]
    distance, missing = (1, REACH)
    while missing > 0:
        take = min(rows, missing)
        low_piece = low_pay[:, missing - take : missing]
        begin = REACH - missing
        high_piece = high_pay[:, begin : begin + take]
        own = own.at[:, rows - take :].add(passed_along(low_piece, "tok", -distance).astype(wide))
        own = own.at[:, :take].add(passed_along(high_piece, "tok", distance).astype(wide))
        distance, missing = (distance + 1, missing - take)
    return own


def head_unit(key, value, query, pulled, bias, log_total, inner, half):
    one_query = head_lanes(query, half)
    one_pull = head_lanes(pulled, half)
    scores = dot_t(key, one_query) + bias
    probs = jnp.exp(scores - log_total)
    probs_grad = dot_t(value, one_pull)
    score_grad = (probs * (probs_grad - inner)).astype(low_type)
    return (probs.astype(low_type), score_grad, one_query, one_pull)


def piece_list(shapes):
    pieces = []
    for index, (rows, lanes) in enumerate(shapes):
        if lanes % 256 != 0:
            parts = 2 if rows % 64 == 0 else 1
            for part in range(parts):
                pieces.append((index, part * rows // parts, rows // parts, 0, lanes, 0))
            continue
        take = 768 if lanes % 768 == 0 else lanes
        step = 48 if rows % 48 == 0 else rows
        for begin in range(0, rows, step):
            for lane in range(0, lanes, take):
                pieces.append((index, begin, step, lane, take, 1))
    return pieces


def half_slice(piece, half):
    _, _, rows, _, lanes, axis = piece
    if isinstance(half, int) and axis == 0:
        return (slice(half * (rows // 2), (half + 1) * (rows // 2)), slice(None))
    if isinstance(half, int):
        return (slice(None), slice(half * (lanes // 2), (half + 1) * (lanes // 2)))
    if axis == 0:
        return (pl.ds(pl.multiple_of(half * (rows // 2), 16), rows // 2), slice(None))
    return (slice(None), pl.ds(pl.multiple_of(half * (lanes // 2), 128), lanes // 2))


def half_shape(piece):
    _, _, rows, _, lanes, axis = piece
    return (rows // 2, lanes) if axis == 0 else (rows, lanes // 2)


def closing_kernel(rows, model_width, seqs, shapes, bits):
    early = piece_list(shapes[:-1])
    last = len(shapes) - 1
    late = [p for p in piece_list(shapes[last:])]
    late = [(last,) + p[1:] for p in late]
    pieces = early + late
    count = len(pieces)
    mesh_id = pl.DeviceIdType.MESH
    tile = min(rows, QUERY_TILE)
    window = tile + 2 * REACH
    scale = 1.0 / math.sqrt(HEAD_DIM)
    pairs = model_width // 128
    phases = bits + 2
    vector_phases = bits + 1
    slots = AHEAD + 2

    def body(*refs):
        given = refs[: len(shapes) - 1]
        (
            queries, keys, values, pulls, pulls_left, pulls_right, stats, stats_left, stats_right,
            bias, edge_bias, normed_low, tokens, resid_grad, qkv_weight, ln1_gain, early_vectors,
        ) = refs[len(shapes) - 1 : len(shapes) + 16]
        rest = refs[len(shapes) + 16 :]
        results = rest[: len(shapes)]
        token_grad, vector_out = rest[len(shapes) : len(shapes) + 2]
        rest = rest[len(shapes) + 2 :]
        (
            near, key_turned, key_total, value_total, grads, normed_turned, late_grad, kept,
            vectors, vectors_landed, near_sem, local_sem, core_send, core_recv, send_sem, recv_sem,
            vector_send, vector_recv,
        ) = rest[:18]
        landed = [rest[18 + i * phases : 18 + (i + 1) * phases] for i in range(count)]
        tok = lax.axis_index("tok")
        seq = lax.axis_index("seq")
        core = tok % 2

        def tok_bit(bit):
            return (tok // (1 << bit)) % 2

        def tok_step(bit):
            return (1 << bit) * (1 - 2 * tok_bit(bit))

        def kept_bit(phase):
            first = seq if phase == 1 else tok_bit(phase - 1)
            second = tok_bit(phase) if phase < bits else seq
            return (1 - core) * first + core * second

        def partner(phase):
            if phase == 0:
                return (seq, tok + tok_step(0))
            if phase > bits:
                return (1 - seq, tok)
            first = 0 if phase == 1 else tok_step(phase - 1)
            second = tok_step(phase) if phase < bits else 0
            across = 0
            if phase == 1:
                across = 1 - core
            if phase == bits:
                across = core
            return (
                seq + across * (1 - 2 * seq),
                tok + (1 - core) * first + core * second,
            )

        def vector_partner(phase):
            if phase < bits:
                return (seq, tok + tok_step(phase))
            return (1 - seq, tok)

        barrier = pltpu.get_barrier_semaphore()
        for phase in range(vector_phases):
            pl.semaphore_signal(
                barrier, inc=1, device_id=vector_partner(phase), device_id_type=mesh_id
            )
        pl.semaphore_wait(barrier, vector_phases)

        def source(number, core_bit):
            index, begin, take, lane, lanes, _ = pieces[number]
            at = (slice(None),) * (bits - 1) + (core_bit,)
            if index == last:
                return late_grad.at[(number - len(early),) + at]
            return given[index].at[at + (pl.ds(begin, take), pl.ds(lane, lanes))]

        def core_copy(number, half, receiver):
            index, begin, take, lane, lanes, axis = pieces[number]
            at = (slice(None),) * (bits - 1) + (1 - core,)
            if axis == 0:
                part = (pl.ds(begin + half * (take // 2), take // 2), pl.ds(lane, lanes))
            else:
                part = (pl.ds(begin, take), pl.ds(lane + half * (lanes // 2), lanes // 2))
            if index == last:
                view = late_grad.at[
                    (number - len(early),)
                    + at
                    + (slice(None), pl.ds(half * (lanes // 2), lanes // 2))
                ]
            else:
                view = given[index].at[at + part]
            if receiver == 0:
                to = landed[number][0].at[(slice(None),) * (bits - 1) + (half,)]
            else:
                to = landed[number][0].at[half]
            return pltpu.make_async_remote_copy(
                src_ref=view,
                dst_ref=to,
                send_sem=core_send.at[number, half],
                recv_sem=core_recv.at[number, half],
                device_id=partner(0),
                device_id_type=mesh_id,
            )

        def local_copy(number):
            slot = number % slots
            _, _, take, _, lanes, _ = pieces[number]
            to = kept.at[slot] if (take, lanes) == (48, 768) else wide_kept[number]
            return pltpu.make_async_copy(source(number, core), to, local_sem.at[number])

        wide_kept = {}
        extra = iter(rest[18 + count * phases :])
        for number, piece in enumerate(early):
            if (piece[2], piece[4]) != (48, 768):
                wide_kept[number] = next(extra)

        def remote_copy(number, phase):
            if phase > bits:
                view = landed[number][bits]
            else:
                view = landed[number][phase - 1].at[
                    (slice(None),) * (bits - phase) + (1 - kept_bit(phase),)
                ]
            return pltpu.make_async_remote_copy(
                src_ref=view,
                dst_ref=landed[number][phase],
                send_sem=send_sem.at[number, phase - 1],
                recv_sem=recv_sem.at[number, phase - 1],
                device_id=partner(phase),
                device_id_type=mesh_id,
            )

        def begin(number):
            for half in range(2):
                for mine in range(2):

                    @pl.when(core == mine)
                    def _():
                        core_copy(number, half, 1 - mine).start()

            if number < len(early):
                local_copy(number).start()

        def bits_of(flat, length):
            return tuple((flat // (1 << bit)) % 2 for bit in reversed(range(length)))

        def finish(number, phase):
            piece = pieces[number]
            index, first, take, lane, lanes, axis = piece
            if phase == 0:
                for half in range(2):
                    for mine in range(2):

                        @pl.when(core == mine)
                        def _():
                            core_copy(number, half, mine).wait_recv()

                if number < len(early):
                    local_copy(number).wait()
                    _, _, t, _, l, _ = piece
                    own = kept.at[number % slots] if (t, l) == (48, 768) else wide_kept[number]
                blocks = 1 << (bits - 1)

                def step(block, carry):
                    at = bits_of(block, bits - 1)
                    for half in range(2):
                        flat = (1 - core) * (2 * block + half) + core * (blocks * half + block)
                        to = bits_of(flat, bits)
                        part = half_slice(piece, half)
                        if number < len(early):
                            mine = own[at + part]
                        else:
                            mine = late_grad[(number - len(early),) + at + (core,) + part]
                        landed[number][0][to] = landed[number][0][to] + mine
                    return carry

                lax.fori_loop(0, blocks, step, 0)
                remote_copy(number, 1).start()
                return
            remote_copy(number, phase).wait_recv()
            got = landed[number][phase]
            if phase <= bits:
                before = landed[number][phase - 1]

                def step(block, carry):
                    at = bits_of(block, bits - phase)
                    got[at] = got[at] + before[at + (kept_bit(phase),)]
                    return carry

                if phase < bits:
                    lax.fori_loop(0, 1 << (bits - phase), step, 0)
                else:
                    got[...] = got[...] + before[kept_bit(phase)]
                remote_copy(number, phase + 1).start()
                return
            height, span = half_shape(piece)
            for half, value in ((seq, landed[number][bits]), (1 - seq, got)):
                if axis == 0:
                    at = (pl.ds(pl.multiple_of(first + half * height, 8), height), pl.ds(lane, span))
                else:
                    at = (pl.ds(first, take), pl.ds(pl.multiple_of(lane + half * span, 128), span))
                results[index][at] = value[...].astype(wide)

        def near_copies(number):
            slot = number % 2
            return [
                pltpu.make_async_copy(field.at[number], near.at[slot, i], near_sem.at[slot, i])
                for i, field in enumerate((queries, keys, values))
            ]

        def own_segment(number, base):
            slot = number % 2
            own = slice(REACH + base, REACH + base + tile)
            near_rows_at = slice(base, base + window)
            inside = slice(REACH - base, REACH - base + rows)

            def step(pair, carry):
                lanes = pl.ds(pl.multiple_of(pair * 128, 128), 128)
                query = near[slot, 0, own, lanes] * scale
                key = near[slot, 1, near_rows_at, lanes]
                value = near[slot, 2, near_rows_at, lanes]
                pulled = pulls[number, base : base + tile, lanes]
                key_term, value_term, halves = (None, None, [])
                for half in range(2):
                    head = 2 * pair + half
                    log_total = stats[number, pair, half : half + 1, base : base + tile]
                    inner = stats[number, pair, 2 + half : 3 + half, base : base + tile]
                    probs, score_grad, one_query, one_pull = head_unit(
                        key, value, query, pulled, bias[number, base // tile], log_total, inner, half
                    )
                    here = dot(score_grad[inside], one_query)
                    key_term = here if key_term is None else key_term + here
                    here = dot(probs[inside], one_pull)
                    value_term = here if value_term is None else value_term + here
                    feature = pl.ds(pl.multiple_of(head * HEAD_DIM, HEAD_DIM), HEAD_DIM)
                    halves.append(dot(key_turned[feature, near_rows_at], score_grad) * scale)
                if base == 0:
                    key_total[:, lanes] = key_term
                    value_total[:, lanes] = value_term
                else:
                    key_total[:, lanes] += key_term
                    value_total[:, lanes] += value_term
                both = jnp.transpose(jnp.concatenate(halves, axis=0)).astype(low_type)
                grads[number * rows + base : number * rows + base + tile, lanes] = both
                return carry

            lax.fori_loop(0, pairs, step, 0)

        def edge_segment(number, side):
            slot = number % 2
            from_rows = slice(0, REACH) if side == 0 else slice(REACH + rows, 2 * REACH + rows)
            begin_row = 0 if side == 0 else rows - REACH
            at = slice(begin_row, begin_row + REACH)
            key_rows = slice(REACH + begin_row, 2 * REACH + begin_row)
            pull_ref, stat_ref = ((pulls_left, stats_left), (pulls_right, stats_right))[side]

            def step(pair, carry):
                lanes = pl.ds(pl.multiple_of(pair * 128, 128), 128)
                query = near[slot, 0, from_rows, lanes] * scale
                key = near[slot, 1, key_rows, lanes]
                value = near[slot, 2, key_rows, lanes]
                pulled = pull_ref[number, :, lanes]
                key_term, value_term = (None, None)
                for half in range(2):
                    log_total = stat_ref[number, pair, half : half + 1, :]
                    inner = stat_ref[number, pair, 2 + half : 3 + half, :]
                    probs, score_grad, one_query, one_pull = head_unit(
                        key, value, query, pulled, edge_bias[number, side], log_total, inner, half
                    )
                    here = dot(score_grad, one_query)
                    key_term = here if key_term is None else key_term + here
                    here = dot(probs, one_pull)
                    value_term = here if value_term is None else value_term + here
                key_total[at, lanes] += key_term
                value_total[at, lanes] += value_term
                return carry

            lax.fori_loop(0, pairs, step, 0)

        def open_sequence(number):
            for copy in near_copies(number):
                copy.wait()
            if number + 1 < seqs:
                for copy in near_copies(number + 1):
                    copy.start()

            def step(pair, carry):
                lanes = pl.ds(pl.multiple_of(pair * 128, 128), 128)
                block = turned(near[number % 2, 1, :, lanes])
                key_turned[lanes, :] = block.astype(low_type)
                return carry

            lax.fori_loop(0, pairs, step, 0)

        def close_sequence(number):
            at = slice(number * rows, (number + 1) * rows)
            grads[at, model_width : 2 * model_width] = key_total[...].astype(low_type)
            grads[at, 2 * model_width :] = value_total[...].astype(low_type)

        def late_product(part):
            lanes = sub_lanes(part, model_width)
            product = dot(normed_turned[...], grads[:, lanes]).astype(low_type)
            shard_rows = model_width >> bits
            for shard in range(1 << bits):
                at = tuple((shard >> bit) & 1 for bit in reversed(range(bits)))
                late_grad[(part,) + at] = product[shard * shard_rows : (shard + 1) * shard_rows]

        def token_segment(number):
            at = slice(number * rows, (number + 1) * rows)
            total = dot_t(grads[at, :], qkv_weight[...])
            normed, norm_scale = normed_rows(tokens[number].astype(wide))
            vectors[0, 0:1, :] += jnp.sum(total * normed, axis=0, keepdims=True)
            vectors[0, 1:2, :] += jnp.sum(total, axis=0, keepdims=True)
            for row, part in ((2, 0), (3, 2)):
                field = grads[at, sub_lanes(part, model_width)].astype(wide)
                vectors[0, row : row + 1, :] += jnp.sum(field, axis=0, keepdims=True)
            pull = norm_pull(total, normed, norm_scale, row_of(ln1_gain))
            token_grad[number] = resid_grad[number] + pull

        def vector_copy(phase):
            return pltpu.make_async_remote_copy(
                src_ref=vectors.at[phase],
                dst_ref=vectors_landed.at[phase],
                send_sem=vector_send.at[phase],
                recv_sem=vector_recv.at[phase],
                device_id=vector_partner(phase),
                device_id_type=mesh_id,
            )

        segments = []
        for number in range(seqs):
            parts = [partial(own_segment, number, base) for base in range(0, rows, tile)]
            parts += [partial(edge_segment, number, side) for side in range(2)]

            def opened(first, number=number):
                open_sequence(number)
                first()

            def closed(final, number=number):
                final()
                close_sequence(number)

            parts[0] = partial(opened, parts[0])
            parts[-1] = partial(closed, parts[-1])
            segments += parts

        vectors[0, 0:8, :] = jnp.zeros((8, model_width), wide)
        vectors[0, 8:16, :] = early_vectors[...]
        for copy in near_copies(0):
            copy.start()
        begin_at = {number: max(number - AHEAD, 0) for number in range(len(early))}
        land_at = {number: number + 1 for number in range(len(early))}
        first_segment = 1
        compute_steps = max(len(segments) + first_segment, len(early) - 1)
        for part in range(len(late)):
            begin_at[len(early) + part] = compute_steps + part
            land_at[len(early) + part] = max(compute_steps, len(early)) + part + 1
        lags = [0, 2] + [phase + 1 for phase in range(2, phases)]
        token_step = compute_steps + len(late) - 1
        final_step = max(
            max(land_at.values()) + lags[-1] + 1, token_step + seqs + vector_phases
        )
        for step in range(final_step):
            for number in range(count):
                if begin_at[number] == step:
                    part = number - len(early)
                    if part >= 0:
                        late_product(part)
                    begin(number)
            if step == 0:
                for line in range(seqs):
                    for column in range(pairs):
                        block = turned(normed_low[line, :, sub_lanes(column, 128)])
                        at = (sub_lanes(column, 128), slice(line * rows, (line + 1) * rows))
                        normed_turned[at] = block.astype(low_type)
            for number in reversed(range(count)):
                if step - land_at[number] in lags:
                    finish(number, lags.index(step - land_at[number]))
            if 0 <= step - first_segment < len(segments):
                segments[step - first_segment]()
            after = step - token_step
            if 0 <= after < seqs:
                token_segment(after)
            if after == seqs - 1:
                vector_copy(0).start()
            phase = after - seqs
            if 0 <= phase < vector_phases:
                vector_copy(phase).wait_recv()
                if phase + 1 < vector_phases:
                    vectors[phase + 1] = vectors[phase] + vectors_landed[phase]
                    vector_copy(phase + 1).start()
                else:
                    vector_out[...] = vectors[phase] + vectors_landed[phase]
        for number in range(count):
            for half in range(2):
                core_copy(number, half, 0).wait_send()
            for phase in range(1, phases):
                remote_copy(number, phase).wait_send()
        for phase in range(vector_phases):
            vector_copy(phase).wait_send()

    scratch = [
        pltpu.VMEM((2, 3, rows + 2 * REACH, model_width), low_type),
        pltpu.VMEM((model_width, rows + 2 * REACH), low_type),
        pltpu.VMEM((rows, model_width), wide),
        pltpu.VMEM((rows, model_width), wide),
        pltpu.VMEM((seqs * rows, 3 * model_width), low_type),
        pltpu.VMEM((model_width, seqs * rows), low_type),
        pltpu.VMEM((len(late),) + (2,) * bits + (48, 768), low_type),
        pltpu.VMEM((slots,) + (2,) * (bits - 1) + (48, 768), low_type),
        pltpu.VMEM((vector_phases, 16, model_width), wide),
        pltpu.VMEM((vector_phases, 16, model_width), wide),
        pltpu.SemaphoreType.DMA((2, 3)),
        pltpu.SemaphoreType.DMA((count,)),
        pltpu.SemaphoreType.DMA((count, 2)),
        pltpu.SemaphoreType.DMA((count, 2)),
        pltpu.SemaphoreType.DMA((count, phases - 1)),
        pltpu.SemaphoreType.DMA((count, phases - 1)),
        pltpu.SemaphoreType.DMA((vector_phases,)),
        pltpu.SemaphoreType.DMA((vector_phases,)),
    ]
    for piece in pieces:
        block = half_shape(piece)
        scratch += [pltpu.VMEM((2,) * (bits - phase) + block, low_type) for phase in range(bits + 1)]
        scratch.append(pltpu.VMEM(block, low_type))
    for piece in early:
        if (piece[2], piece[4]) != (48, 768):
            scratch.append(pltpu.VMEM((2,) * (bits - 1) + (piece[2], piece[4]), low_type))
    return (body, scratch)


def closing(grads, fields, qkv_shape):
    shards = lax.axis_size("tok")
    bits = bit_count(shards)
    queries, tokens = (fields[0], fields[12])
    seqs, rows, model_width = tokens.shape
    shapes = [g.shape[1:] for g in grads] + [(qkv_shape[0] // shards, qkv_shape[1])]
    body, scratch = closing_kernel(rows, model_width, seqs, shapes, bits)
    given = [g.reshape((2,) * bits + g.shape[1:]) for g in grads]
    held = pl.BlockSpec(memory_space=pltpu.VMEM)
    away = pl.BlockSpec(memory_space=pl.ANY)
    inputs = given + list(fields)
    in_specs = [away] * (len(given) + 3) + [held] * (len(fields) - 3)
    out_shape = [jax.ShapeDtypeStruct(s, wide) for s in shapes]
    out_shape.append(jax.ShapeDtypeStruct(tokens.shape, wide))
    out_shape.append(jax.ShapeDtypeStruct((16, model_width), wide))
    return pl.pallas_call(
        body,
        in_specs=in_specs,
        out_specs=[held] * len(out_shape),
        out_shape=out_shape,
        scratch_shapes=scratch,
        compiler_params=pltpu.CompilerParams(
            vmem_limit_bytes=CLOSING_LIMIT, collective_id=1, has_side_effects=True
        ),
        cost_estimate=pl.CostEstimate(
            flops=40 * 10**9, bytes_accessed=60 * 10**6, transcendentals=0
        ),
    )(*inputs)


def local(
    tokens,
    skip_features,
    crop_sides,
    ln1_gain,
    ln1_bias,
    qkv_weight,
    qv_bias,
    out_weight,
    out_bias,
    ln2_gain,
    ln2_bias,
    fc1_weight,
    fc1_bias,
    fc2_weight,
    fc2_bias,
    deconv_weight,
    conv1_weight,
    conv2_weight,
    conv3_weight,
    cotangent,
):
    seq_count, row_count, model_width = tokens.shape
    channels = conv2_weight.shape[2]
    hidden = fc1_weight.shape[1]
    reaches = (key_reach + row_count - 1) // row_count
    reach_rows = row_count + 2 * REACH
    near_given = row_count < REACH
    near = near_rows(tokens) if near_given else ()
    near_block = (seq_count, 16 if near_given else REACH, model_width)
    skip = skip_features.reshape(seq_count, row_count, 8 * channels)
    edge_block = ((seq_count, EDGE, 8 * channels), low_type)
    place, owner, crop_t, inverse, bias, edge_bias = geometry_tables(crop_sides, row_count)

    def block(lanes, kind, rows=row_count):
        return ((seq_count, rows, lanes), kind)

    matrix_flops = 2 * seq_count * row_count * model_width
    (
        normed_low, queries, keys, values, attended, log_totals, resid_one, normed_two,
        act_low, slope_low, resid_low, upsampled, *edges,
    ) = kernel_call(
        forward_kernel(row_count, model_width, hidden, seq_count, near_given),
        seq_count,
        (tokens, bias) + tuple(near),
        (
            ln1_gain, ln1_bias, qkv_weight, qv_bias, out_bias, ln2_gain, ln2_bias, fc1_bias, fc2_bias,
        ),
        (
            block(model_width, low_type),
            block(model_width, low_type, reach_rows),
            block(model_width, low_type, reach_rows),
            block(model_width, low_type, reach_rows),
            block(model_width, low_type),
            block(row_count, wide, 16),
            block(model_width, wide),
            block(model_width, low_type),
            block(hidden, low_type),
            block(hidden, low_type),
            block(model_width, low_type),
            block(8 * channels, low_type),
        ),
        (),
        [
            pltpu.VMEM((reach_rows, model_width), low_type),
            pltpu.VMEM((model_width, reach_rows), low_type),
            pltpu.SemaphoreType.DMA((2,)),
            pltpu.SemaphoreType.DMA((2,)),
            pltpu.VMEM(near_block, low_type),
            pltpu.VMEM(near_block, low_type),
            pltpu.SemaphoreType.DMA((seq_count, 2)),
            pltpu.SemaphoreType.DMA((seq_count, 2)),
            pltpu.VMEM(out_weight.shape, low_type),
            pltpu.VMEM(fc1_weight.shape, low_type),
            pltpu.VMEM(fc2_weight.shape, low_type),
            pltpu.VMEM(deconv_weight.shape, low_type),
            pltpu.SemaphoreType.DMA((4,)),
        ]
        + edge_scratch(seq_count, EDGE, 8 * channels),
        matrix_flops * (8 * model_width + 2 * hidden + 8 * channels),
        away=(tokens, skip, out_weight, fc1_weight, fc2_weight, deconv_weight),
        landing=(edge_block,) * 4,
        collective=2,
    )
    section_out, up_grad, skip_grad, conv1_grad, conv2_grad, conv3_grad = conv_section(
        upsampled,
        skip,
        edges,
        cotangent.reshape(seq_count, row_count, 8 * channels),
        (conv1_weight, conv2_weight, conv3_weight),
        (place, owner, crop_t, inverse),
        reaches,
    )
    section_out = section_out.reshape(seq_count, row_count, 8, channels)
    skip_grad = skip_grad.reshape(seq_count, row_count, 8, channels)
    (
        branch_low, pre_low, resid_grad, mixed_low, pulled, stats,
        fc2_bias_grad, fc1_bias_grad, out_bias_grad, ln2_gain_grad, ln2_bias_grad,
    ) = kernel_call(
        hidden_back_kernel(row_count, model_width, hidden),
        seq_count,
        (up_grad, slope_low, resid_one, attended, log_totals),
        (deconv_weight, fc2_weight, fc1_weight, out_weight, ln2_gain),
        (
            block(model_width, low_type),
            block(hidden, low_type),
            block(model_width, wide),
            block(model_width, low_type),
            block(model_width, low_type),
            ((seq_count, model_width // 128, 8, row_count), wide),
        ),
        (
            ((1, model_width), wide),
            ((1, hidden), wide),
            ((1, model_width), wide),
            ((1, model_width), wide),
            ((1, model_width), wide),
        ),
        [],
        matrix_flops * (model_width + 2 * hidden + 8 * channels),
    )

    def weight_product(left, right):
        return jnp.einsum(
            "rd,re->de",
            left.reshape(-1, left.shape[-1]),
            right.reshape(-1, right.shape[-1]),
            preferred_element_type=wide,
        )

    deconv_grad = weight_product(resid_low, up_grad)
    fc2_grad = weight_product(act_low, branch_low)
    fc1_grad = weight_product(normed_two, pre_low)
    out_grad = weight_product(attended, mixed_low)
    conv3_turned = jnp.moveaxis(conv3_grad.reshape(1, 2, channels, channels), 2, 3)
    conv_grads = (conv1_grad, conv2_grad, conv3_turned)
    matrices = (deconv_grad, fc2_grad, fc1_grad, out_grad)
    shards = lax.axis_size("tok")
    if row_count >= REACH and lax.axis_size("seq") == 2 and model_width // shards == 48:
        pulls = exchanged(pulled[:, :REACH], pulled[:, row_count - REACH :])
        near_stats = exchanged(stats[..., :REACH], stats[..., row_count - REACH :])
        early = (
            out_bias_grad, ln2_gain_grad, ln2_bias_grad, fc2_bias_grad,
            fc1_bias_grad.reshape(-1, model_width),
        )
        parts = [conv_rows(g).astype(low_type) for g in conv_grads]
        spare = -sum(p.shape[1] for p in parts) % 64
        packed = jnp.concatenate(parts + [jnp.zeros((shards, spare, 128), low_type)], axis=1)
        results = closing(
            [packed] + [sharded_rows(m) for m in matrices],
            (
                queries, keys, values, pulled, pulls[0], pulls[1], stats, near_stats[0],
                near_stats[1], bias, edge_bias, normed_low, tokens, resid_grad, qkv_weight,
                ln1_gain, jnp.concatenate(early, axis=0),
            ),
            qkv_weight.shape,
        )
        conv_shares = []
        cursor = 0
        for part, grad in zip(parts, conv_grads):
            rows_here = results[0][cursor : cursor + part.shape[1]]
            conv_shares.append(conv_share(rows_here, grad.shape[0], grad.shape[1]))
            cursor += part.shape[1]
        shares = results[1:6]
        token_grad, lines = results[6:8]
        span = model_width // shards
        own = lax.dynamic_slice_in_dim(lines[:12], lax.axis_index("tok") * span, span, 1)
        long_span = hidden // shards
        long_line = lines[12:16].reshape(hidden)
        long_own = lax.dynamic_slice_in_dim(
            long_line, lax.axis_index("tok") * long_span, long_span, 0
        )
        vectors = (own[0], own[1], own[2], own[3], own[8], own[9], own[10], long_own, own[11])
    else:
        query_grad, key_own, value_own, low_pay, high_pay = kernel_call(
            attention_back_kernel(row_count, model_width),
            seq_count,
            (queries, keys, values, pulled, stats, bias),
            (),
            (
                block(model_width, low_type),
                block(model_width, wide),
                block(model_width, wide),
                block(2 * model_width, low_type, REACH),
                block(2 * model_width, low_type, REACH),
            ),
            (),
            [
                pltpu.VMEM((reach_rows, model_width), wide),
                pltpu.VMEM((reach_rows, model_width), wide),
                pltpu.VMEM((model_width, reach_rows), low_type),
            ],
            matrix_flops * 12 * model_width,
        )
        both = jnp.concatenate([key_own, value_own], axis=-1)
        both = returned_rows(both, low_pay, high_pay)
        qkv_grad_low, token_grad, column_sums, ln1_gain_grad, ln1_bias_grad = kernel_call(
            token_kernel(row_count, model_width),
            seq_count,
            (tokens, resid_grad, query_grad, both[:, :, :model_width], both[:, :, model_width:]),
            (qkv_weight, ln1_gain),
            (block(3 * model_width, low_type), block(model_width, wide)),
            (
                ((1, 3 * model_width), wide),
                ((1, model_width), wide),
                ((1, model_width), wide),
            ),
            [],
            matrix_flops * 3 * model_width,
        )
        qkv_grad = weight_product(normed_low, qkv_grad_low)
        conv_shares, shares, vectors = reduced_all(
            conv_grads,
            matrices + (qkv_grad,),
            (
                ln1_gain_grad, ln1_bias_grad, column_sums[:, :model_width],
                column_sums[:, 2 * model_width :], out_bias_grad, ln2_gain_grad, ln2_bias_grad,
                fc1_bias_grad, fc2_bias_grad,
            ),
        )
    return (
        section_out,
        token_grad,
        skip_grad,
        vectors[0],
        vectors[1],
        shares[4],
        jnp.stack([vectors[2], vectors[3]]),
        shares[3],
        vectors[4],
        vectors[5],
        vectors[6],
        shares[2],
        vectors[7],
        shares[1],
        vectors[8],
        shares[0],
        conv_shares[0],
        conv_shares[1],
        conv_shares[2][0],
    )


def solution(mesh):
    in_specs = (
        P("seq", "tok", None),
        P("seq", "tok", None, None),
        P("seq", None),
        P(),
        P(),
        P(),
        P(),
        P(),
        P(),
        P(),
        P(),
        P(),
        P(),
        P(),
        P(),
        P(),
        P(),
        P(),
        P(),
        P("seq", "tok", None, None),
    )
    out_specs = (
        P("seq", "tok", None, None),
        P("seq", "tok", None),
        P("seq", "tok", None, None),
        P("tok"),
        P("tok"),
        P("tok", None),
        P(None, "tok"),
        P("tok", None),
        P("tok"),
        P("tok"),
        P("tok"),
        P("tok", None),
        P("tok"),
        P("tok", None),
        P("tok"),
        P("tok", None),
        P(None, None, "tok"),
        P(None, None, "tok"),
        P(None, "tok"),
    )
    return jax.shard_map(local, mesh=mesh, in_specs=in_specs, out_specs=out_specs, check_vma=False)
```

```python
from functools import partial
import math

import jax
import jax.numpy as jnp
import numpy as np
from jax import lax
from jax.experimental import pallas as pl
from jax.experimental.pallas import tpu as pltpu
from jax.sharding import PartitionSpec as P

HEADS = 12
HEAD_DIM = 64


side_small = 4
side_big = 6
halo_rows = 43
key_reach = 215
norm_eps = 1e-05
far_below = -1e30
highest = lax.Precision.HIGHEST
in_part = {-1: (1, 2), 0: (0, 2), 1: (0, 1)}
out_part = {-1: (0, 1), 0: (0, 2), 1: (1, 2)}


def passed_along(block, axis, distance):
    devices = range(lax.axis_size(axis))
    route = [(i - distance, i) for i in devices if i - distance in devices]
    return lax.ppermute(block, axis, route)


def all_offsets():
    step_values = (-1, 0, 1)
    return [
        (step_x, step_y, step_z)
        for step_x in step_values
        for step_y in step_values
        for step_z in step_values
    ]


EDGE = 48
WINDOW = 256
TILE = 128
CROP_ROWS = 48
SUBS = 8
VMEM_LIMIT = 60 * 1024 * 1024
lowest_step = {-1: -43, 0: -7, 1: 11}
low_type = jnp.bfloat16
wide = jnp.float32


def dot(left, right):
    return jnp.dot(left, right, preferred_element_type=wide)


def three_terms(field):
    first = field.astype(low_type)
    rest = field - first.astype(wide)
    second = rest.astype(low_type)
    third = (rest - second.astype(wide)).astype(low_type)
    return (first, second, third)


def exact_dot(chosen, field):
    first, second, third = three_terms(field)
    return dot(chosen, first) + dot(chosen, second) + dot(chosen, third)


def sub_lanes(number, width):
    return slice(number * width, (number + 1) * width)


def all_taps():
    return [(x, y, z) for x in range(3) for y in range(3) for z in range(3)]


def forward_band(weight, band_ref):
    inner, outer = weight.shape[1:]
    band_ref[...] = jnp.zeros_like(band_ref)
    for tap_x, tap_y, tap_z in all_taps():
        for side in range(2):
            rows = sub_lanes(tap_y * 4 + tap_z + side, inner)
            lanes = sub_lanes(side, outer)
            band_ref[tap_x, rows, lanes] = weight[tap_x * 9 + tap_y * 3 + tap_z]


def backward_band(weight, band_ref):
    inner, outer = weight.shape[1:]
    band_ref[...] = jnp.zeros_like(band_ref)
    for tap_x, tap_y, tap_z in all_taps():
        for side in range(2):
            rows = sub_lanes(side, inner)
            lanes = sub_lanes(tap_y * 4 + tap_z + side, outer)
            band_ref[tap_x, rows, lanes] = weight[26 - (tap_x * 9 + tap_y * 3 + tap_z)]


def once(fill, *refs):
    @pl.when(pl.program_id(0) == 0)
    def _():
        fill(*refs)


def window_positions(step):
    return {-1: ((0, 1),), 0: ((1, 0), (2, 1)), 1: ((3, 0),)}[step]


def fill_windows(x_ref, place_ref, p_ref, rows, width):
    tile = min(rows, TILE)
    for base in range(0, rows, tile):
        own = slice(base, base + tile)
        for number, (step_x, step_y, step_z) in enumerate(all_offsets()):
            low = (EDGE + base + lowest_step[step_x]) // 16 * 16
            centre = (step_x, step_y, step_z) == (0, 0, 0)
            if not centre:
                lane = lax.broadcasted_iota(jnp.int32, (tile, WINDOW), 1) + low
                chosen = jnp.where(lane == place_ref[0, own, number : number + 1], 1.0, 0.0)
                chosen = chosen.astype(low_type)
            for x_to, x_from in window_positions(step_x):
                for y_to, y_from in window_positions(step_y):
                    z_to, z_from = window_positions(step_z)[0]
                    count = (2 if step_z == 0 else 1) * width
                    to = ((x_to * 4 + y_to) * 4 + z_to) * width
                    source = (x_from * 4 + y_from * 2 + z_from) * width
                    if centre:
                        got = x_ref[EDGE + base : EDGE + base + tile, source : source + count]
                    else:
                        got = dot(chosen, x_ref[low : low + WINDOW, source : source + count])
                    p_ref[own, to : to + count] = got.astype(low_type)


def window_conv(p_ref, band_ref, pair, width, product):
    first, second = pair
    total = None
    for tap in range(3):
        begin = ((first + tap) * 4 + second) * 4 * width
        term = product(p_ref[:, begin : begin + 12 * width], band_ref[tap])
        total = term if total is None else total + term
    return total


def all_pairs():
    return [(first, second) for first in range(2) for second in range(2)]


def add_grads(left_ref, p_ref, total_ref, width, channels):
    for tap_x in range(3):
        for tap_y in range(3):
            term = None
            for number, (first, second) in enumerate(all_pairs()):
                begin = ((first + tap_x) * 4 + second + tap_y) * 4 * channels
                left = left_ref[number * 2 * width : (number + 1) * 2 * width, :]
                part = dot(left, p_ref[:, begin : begin + 4 * channels])
                term = part if term is None else term + part
            total_ref[tap_x * 3 + tap_y] += term


def fold_grads(total_ref, grad_ref, width, channels):
    for tap_x in range(3):
        for tap_y in range(3):
            for tap_z in range(3):
                number = tap_x * 3 + tap_y
                here = total_ref[number, :width, sub_lanes(tap_z, channels)]
                there = total_ref[number, width:, sub_lanes(tap_z + 1, channels)]
                tap = 26 - (number * 3 + tap_z)
                for half in range(width // channels):
                    rows = slice(half * channels, (half + 1) * channels)
                    grad_ref[tap, half] = jnp.transpose(here[rows] + there[rows])


def fold_packed(total_ref, grad_ref, width, channels, shards, side_ref=None):
    blocks = []
    for tap in range(27):
        number, tap_z = divmod(26 - tap, 3)
        here = total_ref[number, :width, sub_lanes(tap_z, channels)]
        there = total_ref[number, width:, sub_lanes(tap_z + 1, channels)]
        both = here + there
        for half in range(width // channels):
            blocks.append(jnp.transpose(both[half * channels : (half + 1) * channels]))
    if side_ref is not None:
        for half in range(width // channels):
            blocks.append(jnp.transpose(side_ref[half * channels : (half + 1) * channels, :]))
    if len(blocks) % 2 == 1:
        blocks.append(jnp.zeros_like(blocks[0]))
    for pair in range(len(blocks) // 2):
        split = [b.reshape(shards, -1, channels) for b in blocks[2 * pair : 2 * pair + 2]]
        joined = jnp.concatenate(split, axis=1).astype(low_type)
        grad_ref[:, 16 * pair : 16 * pair + 16, :] = joined


def kernel_call(
    body, seqs, inputs, shared, outputs, summed, scratch, flops, away=(), landing=(), collective=None
):
    def row_spec(shape):
        return pl.BlockSpec((1,) + tuple(shape[1:]), lambda i: (i,) + (0,) * (len(shape) - 1))

    def whole_spec(shape):
        return pl.BlockSpec(
            tuple(shape), lambda i: (0,) * len(shape), pipeline_mode=pl.Buffered(1)
        )

    far_spec = pl.BlockSpec(memory_space=pl.ANY)
    moved = sum(math.prod(a.shape) * a.dtype.itemsize for a in list(inputs) + list(shared))
    moved += sum(math.prod(s) * jnp.dtype(t).itemsize for s, t in list(outputs) + list(summed))
    results = list(outputs) + list(summed) + list(landing)
    return pl.pallas_call(
        body,
        grid=(seqs,),
        in_specs=[row_spec(a.shape) for a in inputs]
        + [whole_spec(a.shape) for a in shared]
        + [far_spec] * len(away),
        out_specs=[row_spec(s) for s, _ in outputs]
        + [whole_spec(s) for s, _ in summed]
        + [far_spec] * len(landing),
        out_shape=[jax.ShapeDtypeStruct(s, t) for s, t in results],
        scratch_shapes=scratch,
        compiler_params=pltpu.CompilerParams(
            vmem_limit_bytes=VMEM_LIMIT,
            collective_id=collective,
            has_side_effects=collective is not None,
        ),
        cost_estimate=pl.CostEstimate(flops=flops, bytes_accessed=moved, transcendentals=0),
    )(*inputs, *shared, *away)


def tok_sides():
    tok, count = (lax.axis_index("tok"), lax.axis_size("tok"))
    return (tok > 0, tok < count - 1)


def greet():
    seq, tok, count = (lax.axis_index("seq"), lax.axis_index("tok"), lax.axis_size("tok"))
    barrier = pltpu.get_barrier_semaphore()
    for there, shift in zip(tok_sides(), (count - 1, 1)):

        @pl.when(there)
        def _():
            pl.semaphore_signal(
                barrier,
                inc=1,
                device_id=(seq, lax.rem(tok + shift, count)),
                device_id_type=pl.DeviceIdType.MESH,
            )


def met():
    tok, count = (lax.axis_index("tok"), lax.axis_size("tok"))
    peers = jnp.minimum(tok, 1) + jnp.minimum(count - 1 - tok, 1)
    pl.semaphore_wait(pltpu.get_barrier_semaphore(), peers)


class Edge:
    def __init__(self, low, high, left, right, send_sem, recv_sem):
        self.sources = (low, high)
        self.targets = (right, left)
        self.send_sem = send_sem
        self.recv_sem = recv_sem

    def copy(self, way):
        seq, tok, count = (lax.axis_index("seq"), lax.axis_index("tok"), lax.axis_size("tok"))
        shift = count - 1 if way == 0 else 1
        return pltpu.make_async_remote_copy(
            src_ref=self.sources[way],
            dst_ref=self.targets[way],
            send_sem=self.send_sem.at[way],
            recv_sem=self.recv_sem.at[way],
            device_id=(seq, lax.rem(tok + shift, count)),
            device_id_type=pl.DeviceIdType.MESH,
        )

    def start(self):
        for way, there in enumerate(tok_sides()):

            @pl.when(there)
            def _():
                self.copy(way).start()

    def land(self):
        for way, there in enumerate(tok_sides()):

            @pl.when(there)
            def _():
                self.copy(1 - way).wait_recv()

    def sent(self):
        for way, there in enumerate(tok_sides()):

            @pl.when(there)
            def _():
                self.copy(way).wait_send()


def edge_scratch(seqs, rows, lanes):
    return [
        pltpu.VMEM((seqs, rows, lanes), low_type),
        pltpu.VMEM((seqs, rows, lanes), low_type),
        pltpu.VMEM((rows, lanes), low_type),
        pltpu.SemaphoreType.DMA((seqs, 2)),
        pltpu.SemaphoreType.DMA((seqs, 2)),
        pltpu.SemaphoreType.DMA((seqs,)),
    ]


class Payload:
    def __init__(self, seqs, left, right, low_pay, high_pay, zero_ref, send_sem, recv_sem, zero_sem):
        self.seqs = seqs
        self.refs = (left, right, low_pay, high_pay, send_sem, recv_sem)
        self.zero_ref = zero_ref
        self.zero_sem = zero_sem
        self.step = pl.program_id(0)
        self.low = low_pay.at[pl.ds(self.step, 1)]
        self.high = high_pay.at[pl.ds(self.step, 1)]

    def edge(self, number):
        left, right, low, high, send_sem, recv_sem = (ref.at[number] for ref in self.refs)
        return Edge(low, high, left, right, send_sem, recv_sem)

    def enter(self):
        @pl.when(self.step == 0)
        def _():
            greet()
            self.zero_ref[...] = jnp.zeros_like(self.zero_ref)
            for field, there in zip(self.refs[:2], tok_sides()):

                @pl.when(jnp.logical_not(there))
                def _():
                    copies = [
                        pltpu.make_async_copy(self.zero_ref, field.at[n], self.zero_sem.at[n])
                        for n in range(self.seqs)
                    ]
                    for copy in copies:
                        copy.start()
                    for copy in copies:
                        copy.wait()

    def send(self, greeted=False):
        if not greeted:

            @pl.when(self.step == 0)
            def _():
                met()

        self.edge(self.step).start()

        @pl.when(self.step == self.seqs - 1)
        def _():
            for number in range(self.seqs):
                self.edge(number).land()
            for number in range(self.seqs):
                self.edge(number).sent()


def conv_scratch(rows, width, band_shape):
    return [
        pltpu.VMEM((rows + 192, SUBS * width), low_type),
        pltpu.VMEM((rows, 64 * width), low_type),
        pltpu.VMEM((3,) + band_shape, low_type),
    ]


def conv_flops(seqs, rows, inner, outer):
    return 2 * seqs * rows * (36 * 4 * inner * 2 * outer + 56 * WINDOW * inner)


def put_edges(low_pay, high_pay, number, field, channels, rows):
    lanes = sub_lanes(number, channels)
    low_pay[0, :, lanes] = field[:EDGE].astype(low_type)
    high_pay[0, :, lanes] = field[rows - EDGE :].astype(low_type)


def put_sums(sums_ref, low_pay, high_pay, number, value, channels):
    lanes = sub_lanes(number, channels)
    sums_ref[0, :, lanes] = value
    pay_lanes = sub_lanes(SUBS + number, channels)
    low_pay[0, :, pay_lanes] = value.astype(low_type)
    high_pay[0, :, pay_lanes] = value.astype(low_type)


def taken_sums(sums_ref, left_pay, right_pay, number, channels):
    lanes = sub_lanes(number, channels)
    pay_lanes = sub_lanes(SUBS + number, channels)
    total = sums_ref[0, :, lanes] + left_pay[0, :, pay_lanes].astype(wide)
    return total + right_pay[0, :, pay_lanes].astype(wide)


def mean_and_scale(total, square, inverse):
    mean = total * inverse
    variance = jnp.maximum(square * inverse - mean * mean, 0.0)
    return (mean, lax.rsqrt(variance + norm_eps))


def silu_parts(value):
    gate = 1.0 / (1.0 + jnp.exp(-value))
    return (value * gate, gate * (1.0 + value * (1.0 - gate)))


def first_conv_kernel(rows, channels, seqs):
    width = 2 * channels

    def body(
        up, up_left, up_right, skip, skip_left, skip_right, place, crop_t, weight, side,
        first_out, side_out, sums, to_left, to_right, x_ref, p_ref, band_ref, *edge_refs,
    ):
        pay = Payload(seqs, to_left, to_right, *edge_refs)
        pay.enter()
        low_pay, high_pay = (pay.low, pay.high)
        once(forward_band, weight, band_ref)
        for number in range(SUBS):
            for half, (own, left, right) in enumerate(
                ((up, up_left, up_right), (skip, skip_left, skip_right))
            ):
                to = sub_lanes(2 * number + half, channels)
                lanes = sub_lanes(number, channels)
                x_ref[:EDGE, to] = left[0, :, lanes]
                x_ref[EDGE : EDGE + rows, to] = own[0, :, lanes]
                x_ref[EDGE + rows : 2 * EDGE + rows, to] = right[0, :, lanes]
        x_ref[2 * EDGE + rows :, :] = jnp.zeros((96, SUBS * width), low_type)
        fill_windows(x_ref, place, p_ref, rows, width)
        total = [jnp.zeros((rows, channels), wide) for _ in range(4)]
        for index, pair in enumerate(all_pairs()):
            result = window_conv(p_ref, band_ref, pair, width, dot)
            first_out[0, :, sub_lanes(index, width)] = result
            for half in range(2):
                number = 2 * index + half
                value = result[:, sub_lanes(half, channels)]
                put_edges(low_pay, high_pay, number, value, channels, rows)
                flat = dot(x_ref[EDGE : EDGE + rows, sub_lanes(number, width)], side[...])
                side_out[0, :, sub_lanes(number, channels)] = flat
                terms = (value, value * value, flat, flat * flat)
                total = [have + term for have, term in zip(total, terms)]
        for number in range(4):
            value = exact_dot(crop_t[0], total[number])
            put_sums(sums, low_pay, high_pay, number, value, channels)
        pay.send()

    return body


def second_conv_kernel(rows, channels, seqs):
    def body(
        first, left_pay, right_pay, own_sums, inverse, owner, place, crop_t, weight,
        second_out, stats, sums, to_left, to_right, x_ref, p_ref, band_ref, *edge_refs,
    ):
        pay = Payload(seqs, to_left, to_right, *edge_refs)
        pay.enter()
        low_pay, high_pay = (pay.low, pay.high)
        once(forward_band, weight, band_ref)
        taken = [taken_sums(own_sums, left_pay, right_pay, n, channels) for n in range(4)]
        mean, scale = mean_and_scale(taken[0], taken[1], inverse[0])
        side_mean, side_scale = mean_and_scale(taken[2], taken[3], inverse[0])
        for number, value in enumerate((mean, scale, side_mean, side_scale)):
            stats[0, :, sub_lanes(number, channels)] = value
        mean_rows = exact_dot(owner[0], mean)
        scale_rows = exact_dot(owner[0], scale)
        parts = (
            (left_pay, slice(0, EDGE)),
            (first, slice(EDGE, EDGE + rows)),
            (right_pay, slice(EDGE + rows, 2 * EDGE + rows)),
        )
        for number in range(SUBS):
            lanes = sub_lanes(number, channels)
            for field, place_rows in parts:
                normed = field[0, :, lanes].astype(wide) - mean_rows[place_rows]
                normed = normed * scale_rows[place_rows]
                x_ref[place_rows, lanes] = silu_parts(normed)[0].astype(low_type)
        x_ref[2 * EDGE + rows :, :] = jnp.zeros((96, SUBS * channels), low_type)
        fill_windows(x_ref, place, p_ref, rows, channels)
        total = [jnp.zeros((rows, channels), wide) for _ in range(2)]
        for index, pair in enumerate(all_pairs()):
            result = window_conv(p_ref, band_ref, pair, channels, dot)
            second_out[0, :, sub_lanes(index, 2 * channels)] = result
            for half in range(2):
                value = result[:, sub_lanes(half, channels)]
                put_edges(low_pay, high_pay, 2 * index + half, value, channels, rows)
                total = [total[0] + value, total[1] + value * value]
        for number in range(2):
            value = exact_dot(crop_t[0], total[number])
            put_sums(sums, low_pay, high_pay, number, value, channels)
        pay.send()

    return body


def output_kernel(rows, channels, seqs):
    def body(
        second, side_field, cotangent, stats, left_pay, right_pay, own_sums, inverse, owner, crop_t,
        section, grad_out, second_stats, sums, to_left, to_right, *edge_refs,
    ):
        pay = Payload(seqs, to_left, to_right, *edge_refs)
        pay.enter()
        low_pay, high_pay = (pay.low, pay.high)
        taken = [taken_sums(own_sums, left_pay, right_pay, n, channels) for n in range(2)]
        mean, scale = mean_and_scale(taken[0], taken[1], inverse[0])
        second_stats[0, :, sub_lanes(0, channels)] = mean
        second_stats[0, :, sub_lanes(1, channels)] = scale
        own = owner[0, EDGE : EDGE + rows, :]
        mean_rows = exact_dot(own, mean)
        scale_rows = exact_dot(own, scale)
        side_mean = exact_dot(own, stats[0, :, sub_lanes(2, channels)])
        side_scale = exact_dot(own, stats[0, :, sub_lanes(3, channels)])
        total = [jnp.zeros((rows, channels), wide) for _ in range(3)]
        for number in range(SUBS):
            lanes = sub_lanes(number, channels)
            normed = (second[0, :, lanes] - mean_rows) * scale_rows
            side = (side_field[0, :, lanes] - side_mean) * side_scale
            value, slope = silu_parts(normed + side)
            section[0, :, lanes] = value.astype(low_type)
            grad = cotangent[0, :, lanes].astype(wide) * slope
            grad_out[0, :, lanes] = grad
            put_edges(low_pay, high_pay, number, grad, channels, rows)
            terms = (grad, grad * normed, grad * side)
            total = [have + term for have, term in zip(total, terms)]
        for number in range(3):
            value = exact_dot(crop_t[0], total[number])
            put_sums(sums, low_pay, high_pay, number, value, channels)
        pay.send()

    return body


def second_back_kernel(rows, channels, seqs, shards):
    def body(
        grad, grad_left, grad_right, own_sums, second, second_left, second_right, side_field, first,
        stats, second_stats, inverse, owner, place, crop_t, weight,
        first_grad, side_grad, sums, weight_grad, to_left, to_right,
        x_ref, p_ref, band_ref, left_ref, total_ref, *edge_refs,
    ):
        pay = Payload(seqs, to_left, to_right, *edge_refs)
        pay.enter()
        low_pay, high_pay = (pay.low, pay.high)
        once(backward_band, weight, band_ref)
        means = [
            taken_sums(own_sums, grad_left, grad_right, n, channels) * inverse[0] for n in range(3)
        ]
        mean_rows = exact_dot(owner[0], second_stats[0, :, sub_lanes(0, channels)])
        scale_rows = exact_dot(owner[0], second_stats[0, :, sub_lanes(1, channels)])
        lead_rows = exact_dot(owner[0], means[0])
        slope_rows = exact_dot(owner[0], means[1])
        parts = (
            (grad_left, second_left, slice(0, EDGE)),
            (grad, second, slice(EDGE, EDGE + rows)),
            (grad_right, second_right, slice(EDGE + rows, 2 * EDGE + rows)),
        )
        own = slice(EDGE, EDGE + rows)
        side_mean = exact_dot(owner[0, own, :], stats[0, :, sub_lanes(2, channels)])
        side_scale = exact_dot(owner[0, own, :], stats[0, :, sub_lanes(3, channels)])
        side_slope = exact_dot(owner[0, own, :], means[2])
        first_mean = exact_dot(owner[0, own, :], stats[0, :, sub_lanes(0, channels)])
        first_scale = exact_dot(owner[0, own, :], stats[0, :, sub_lanes(1, channels)])
        for number in range(SUBS):
            lanes = sub_lanes(number, channels)
            for grad_from, field, at in parts:
                normed = (field[0, :, lanes].astype(wide) - mean_rows[at]) * scale_rows[at]
                pulled = grad_from[0, :, lanes].astype(wide) - lead_rows[at]
                pulled = scale_rows[at] * (pulled - normed * slope_rows[at])
                x_ref[at, lanes] = pulled.astype(low_type)
            side = (side_field[0, :, lanes] - side_mean) * side_scale
            pulled = side_scale * (grad[0, :, lanes] - lead_rows[own] - side * side_slope)
            side_grad[0, :, lanes] = pulled.astype(low_type)
            normed = (first[0, :, lanes] - first_mean) * first_scale
            hidden = silu_parts(normed)[0]
            left_ref[lanes, :] = jnp.transpose(hidden).astype(low_type)
        x_ref[2 * EDGE + rows :, :] = jnp.zeros((96, SUBS * channels), low_type)
        fill_windows(x_ref, place, p_ref, rows, channels)
        total = [jnp.zeros((rows, channels), wide) for _ in range(2)]
        for index, pair in enumerate(all_pairs()):
            result = window_conv(p_ref, band_ref, pair, channels, dot_t)
            for half in range(2):
                number = 2 * index + half
                lanes = sub_lanes(number, channels)
                normed = (first[0, :, lanes] - first_mean) * first_scale
                value = result[:, sub_lanes(half, channels)] * silu_parts(normed)[1]
                first_grad[0, :, lanes] = value
                put_edges(low_pay, high_pay, number, value, channels, rows)
                total = [total[0] + value, total[1] + value * normed]
        for number in range(2):
            value = exact_dot(crop_t[0], total[number])
            put_sums(sums, low_pay, high_pay, number, value, channels)
        pay.send()

        @pl.when(pl.program_id(0) == 0)
        def _():
            total_ref[...] = jnp.zeros_like(total_ref)

        add_grads(left_ref, p_ref, total_ref, channels, channels)

        @pl.when(pl.program_id(0) == seqs - 1)
        def _():
            if shards * 8 == channels:
                fold_packed(total_ref, weight_grad, channels, channels, shards)
            else:
                fold_grads(total_ref, weight_grad, channels, channels)

    return body


def first_back_kernel(rows, channels, seqs, shards):
    width = 2 * channels

    def body(
        grad, grad_left, grad_right, own_sums, first, first_left, first_right, stats, inverse, owner,
        place, side_grad, up, skip, weight, side_weight,
        up_grad, skip_grad, weight_grad, side_weight_grad,
        x_ref, p_ref, band_ref, left_ref, total_ref,
    ):
        once(backward_band, weight, band_ref)
        means = [
            taken_sums(own_sums, grad_left, grad_right, n, channels) * inverse[0] for n in range(2)
        ]
        mean_rows = exact_dot(owner[0], stats[0, :, sub_lanes(0, channels)])
        scale_rows = exact_dot(owner[0], stats[0, :, sub_lanes(1, channels)])
        lead_rows = exact_dot(owner[0], means[0])
        slope_rows = exact_dot(owner[0], means[1])
        parts = (
            (grad_left, first_left, slice(0, EDGE)),
            (grad, first, slice(EDGE, EDGE + rows)),
            (grad_right, first_right, slice(EDGE + rows, 2 * EDGE + rows)),
        )
        for number in range(SUBS):
            lanes = sub_lanes(number, channels)
            for grad_from, field, at in parts:
                normed = (field[0, :, lanes].astype(wide) - mean_rows[at]) * scale_rows[at]
                pulled = grad_from[0, :, lanes].astype(wide) - lead_rows[at]
                pulled = scale_rows[at] * (pulled - normed * slope_rows[at])
                x_ref[at, lanes] = pulled.astype(low_type)
            for half, field in enumerate((up, skip)):
                turned = jnp.transpose(field[0, :, lanes].astype(wide)).astype(low_type)
                left_ref[sub_lanes(2 * number + half, channels), :] = turned
        x_ref[2 * EDGE + rows :, :] = jnp.zeros((96, SUBS * channels), low_type)
        fill_windows(x_ref, place, p_ref, rows, channels)
        for index, pair in enumerate(all_pairs()):
            result = window_conv(p_ref, band_ref, pair, channels, dot_t)
            for half in range(2):
                number = 2 * index + half
                lanes = sub_lanes(number, channels)
                value = result[:, sub_lanes(half, width)]
                value = value + dot_t(side_grad[0, :, lanes], side_weight[...])
                up_grad[0, :, lanes] = value[:, :channels].astype(low_type)
                skip_grad[0, :, lanes] = value[:, channels:]

        @pl.when(pl.program_id(0) == 0)
        def _():
            total_ref[...] = jnp.zeros_like(total_ref)
            side_weight_grad[...] = jnp.zeros_like(side_weight_grad)

        for number in range(SUBS):
            side_weight_grad[...] += dot(
                left_ref[sub_lanes(number, width), :], side_grad[0, :, sub_lanes(number, channels)]
            )
        add_grads(left_ref, p_ref, total_ref, width, channels)

        @pl.when(pl.program_id(0) == seqs - 1)
        def _():
            if shards * 8 == channels:
                fold_packed(total_ref, weight_grad, width, channels, shards, side_weight_grad)
            else:
                fold_grads(total_ref, weight_grad, width, channels)

    return body


def exchanged(low_pay, high_pay):
    return (passed_along(high_pay, "tok", 1), passed_along(low_pay, "tok", -1))


def with_far(sums, reaches):
    total = sums
    for distance in range(2, reaches + 1):
        for shift_by in (distance, -distance):
            total = total + passed_along(sums.astype(low_type), "tok", shift_by).astype(wide)
    return total


def conv_section(upsampled, skip, edges, cotangent, weights, geometry_in, reaches):
    conv1_weight, conv2_weight, conv3_weight = weights
    seqs, rows, lanes = upsampled.shape
    channels = lanes // SUBS
    width = 2 * channels
    place, owner, crop_t, inverse = geometry_in
    field = ((seqs, rows, lanes), wide)
    low_field = ((seqs, rows, lanes), low_type)

    def pay(count):
        return ((seqs, EDGE, (SUBS + count) * channels), low_type)

    def pay_scratch(count):
        return edge_scratch(seqs, EDGE, (SUBS + count) * channels)

    def table(count):
        return ((seqs, CROP_ROWS, count * channels), wide)

    up_left, up_right, skip_left, skip_right = edges
    shards = lax.axis_size("tok")
    fits = shards * 8 == channels

    def packed_out(blocks):
        return ((shards, (blocks + 1) // 2 * 16, channels), low_type)

    first, side_field, sums, first_left, first_right = kernel_call(
        first_conv_kernel(rows, channels, seqs),
        seqs,
        (upsampled, up_left, up_right, skip, skip_left, skip_right, place, crop_t),
        (conv1_weight, conv3_weight),
        (field, field, table(4)),
        (),
        conv_scratch(rows, width, (12 * width, 2 * channels)) + pay_scratch(4),
        conv_flops(seqs, rows, width, channels),
        landing=(pay(4), pay(4)),
        collective=3,
    )
    second, stats, sums, second_left, second_right = kernel_call(
        second_conv_kernel(rows, channels, seqs),
        seqs,
        (first, first_left, first_right, with_far(sums, reaches), inverse, owner, place, crop_t),
        (conv2_weight,),
        (field, table(4), table(2)),
        (),
        conv_scratch(rows, channels, (12 * channels, 2 * channels)) + pay_scratch(2),
        conv_flops(seqs, rows, channels, channels),
        landing=(pay(2), pay(2)),
        collective=4,
    )
    section_out, grad, second_stats, sums, grad_left, grad_right = kernel_call(
        output_kernel(rows, channels, seqs),
        seqs,
        (
            second, side_field, cotangent, stats, second_left, second_right,
            with_far(sums, reaches), inverse, owner, crop_t,
        ),
        (),
        (low_field, field, table(2), table(3)),
        (),
        pay_scratch(3),
        seqs * rows * lanes * 20,
        landing=(pay(3), pay(3)),
        collective=5,
    )
    first_grad, side_grad, sums, conv2_grad, back_left, back_right = kernel_call(
        second_back_kernel(rows, channels, seqs, shards),
        seqs,
        (
            grad, grad_left, grad_right, with_far(sums, reaches), second, second_left, second_right,
            side_field, first, stats, second_stats, inverse, owner, place, crop_t,
        ),
        (conv2_weight,),
        (field, low_field, table(2)),
        (packed_out(27) if fits else ((27, 1, channels, channels), wide),),
        conv_scratch(rows, channels, (2 * channels, 12 * channels))
        + [
            pltpu.VMEM((SUBS * channels, rows), low_type),
            pltpu.VMEM((9, 2 * channels, 4 * channels), wide),
        ]
        + pay_scratch(2),
        2 * conv_flops(seqs, rows, channels, channels),
        landing=(pay(2), pay(2)),
        collective=6,
    )
    up_grad, skip_grad, conv1_grad, conv3_grad = kernel_call(
        first_back_kernel(rows, channels, seqs, shards),
        seqs,
        (
            first_grad, back_left, back_right, with_far(sums, reaches), first, first_left,
            first_right, stats, inverse, owner, place, side_grad, upsampled, skip,
        ),
        (conv1_weight, conv3_weight),
        (low_field, field),
        (
            packed_out(56) if fits else ((27, 2, channels, channels), wide),
            ((width, channels), wide),
        ),
        conv_scratch(rows, channels, (2 * width, 12 * channels))
        + [
            pltpu.VMEM((SUBS * width, rows), low_type),
            pltpu.VMEM((9, 2 * width, 4 * channels), wide),
        ],
        2 * conv_flops(seqs, rows, channels, width),
    )
    return (section_out, up_grad, skip_grad, conv1_grad, conv2_grad, conv3_grad)


PIECE_BYTES = 2400 * 1024


def bit_count(size):
    return size.bit_length() - 1


def pieces_of(shapes):
    pieces = []
    for index, (shards, rows, lanes) in enumerate(shapes):
        parts = max(1, round(shards * rows * lanes * 2 / PIECE_BYTES))
        while rows % (16 * parts) != 0 and parts > 1:
            parts -= 1
        take = rows // parts
        pieces.extend((index, part * take, take, lanes) for part in range(parts))
    return pieces


def all_of(count):
    return (slice(None),) * count


def reduce_kernel(pieces, arrays, tok_bits, seq_bits):
    phases = tok_bits + seq_bits
    mesh_id = pl.DeviceIdType.MESH

    def body(*refs):
        given = refs[:arrays]
        results = refs[arrays : 2 * arrays]
        count = len(pieces)
        rest = refs[2 * arrays :]
        kept = rest[:count]
        landed = [rest[count + i * phases : count + (i + 1) * phases] for i in range(count)]
        local_sem, send_sem, recv_sem = rest[count + count * phases :]
        tok = lax.axis_index("tok")
        seq = lax.axis_index("seq")

        def bit_of(phase):
            if phase < tok_bits:
                return (tok // (1 << phase)) % 2
            return (seq // (1 << (phase - tok_bits))) % 2

        def partner(phase):
            bit = bit_of(phase)
            if phase < tok_bits:
                return (seq, tok + (1 << phase) * (1 - 2 * bit))
            return (seq + (1 << (phase - tok_bits)) * (1 - 2 * bit), tok)

        barrier = pltpu.get_barrier_semaphore()
        for phase in range(phases):
            pl.semaphore_signal(barrier, inc=1, device_id=partner(phase), device_id_type=mesh_id)
        pl.semaphore_wait(barrier, phases)

        def local_copy(piece):
            index, begin, take, _ = pieces[piece]
            view = given[index].at[all_of(tok_bits - 1) + (bit_of(0), pl.ds(begin, take))]
            return pltpu.make_async_copy(view, kept[piece], local_sem.at[piece])

        def remote_copy(piece, phase):
            index, begin, take, _ = pieces[piece]
            if phase == 0:
                view = given[index].at[all_of(tok_bits - 1) + (1 - bit_of(0), pl.ds(begin, take))]
            elif phase < tok_bits:
                view = landed[piece][phase - 1].at[all_of(tok_bits - 1 - phase) + (1 - bit_of(phase),)]
            else:
                view = landed[piece][phase - 1]
            return pltpu.make_async_remote_copy(
                src_ref=view,
                dst_ref=landed[piece][phase],
                send_sem=send_sem.at[piece, phase],
                recv_sem=recv_sem.at[piece, phase],
                device_id=partner(phase),
                device_id_type=mesh_id,
            )

        def begin(piece):
            remote_copy(piece, 0).start()
            local_copy(piece).start()

        def finish(piece, phase):
            index, first, take, _ = pieces[piece]
            remote_copy(piece, phase).wait_recv()
            got = landed[piece][phase]
            if phase == 0:
                local_copy(piece).wait()

            if phase < tok_bits:
                kept_bits = tok_bits - 1 - phase

                def step(block, carry):
                    at = tuple((block // (1 << bit)) % 2 for bit in reversed(range(kept_bits)))
                    if phase == 0:
                        mine = kept[piece][at]
                    else:
                        mine = landed[piece][phase - 1][at + (bit_of(phase),)]
                    got[at] = got[at] + mine
                    return carry

                lax.fori_loop(0, 1 << kept_bits, step, 0)
            elif phase + 1 < phases:
                got[...] = got[...] + landed[piece][phase - 1][...]
            if phase + 1 < phases:
                remote_copy(piece, phase + 1).start()
            else:
                total = got[...].astype(wide) + landed[piece][phase - 1][...].astype(wide)
                results[index][pl.ds(first, take), :] = total

        begin(0)
        for step in range(count + phases - 1):
            if step + 1 < count:
                begin(step + 1)
            for phase in range(phases):
                if 0 <= step - phase < count:
                    finish(step - phase, phase)
        for piece in range(count):
            for phase in range(phases):
                remote_copy(piece, phase).wait_send()

    return body


def reduced(grads):
    shards = lax.axis_size("tok")
    tok_bits = bit_count(shards)
    seq_bits = bit_count(lax.axis_size("seq"))
    shapes = [g.shape for g in grads]
    pieces = pieces_of(shapes)
    scratch = [
        pltpu.VMEM((2,) * (tok_bits - 1) + (take, lanes), low_type) for _, _, take, lanes in pieces
    ]
    for _, _, take, lanes in pieces:
        for phase in range(tok_bits - 1):
            bits = tok_bits - 1 - phase
            scratch.append(pltpu.VMEM((2,) * bits + (take, lanes), low_type))
        scratch += [pltpu.VMEM((take, lanes), low_type) for _ in range(1 + seq_bits)]
    count, phases = len(pieces), tok_bits + seq_bits
    scratch += [
        pltpu.SemaphoreType.DMA((count,)),
        pltpu.SemaphoreType.DMA((count, phases)),
        pltpu.SemaphoreType.DMA((count, phases)),
    ]
    total = sum(math.prod(s) for s in shapes)
    return pl.pallas_call(
        reduce_kernel(pieces, len(grads), tok_bits, seq_bits),
        in_specs=[pl.BlockSpec(memory_space=pl.ANY)] * len(grads),
        out_specs=[pl.BlockSpec(memory_space=pltpu.VMEM)] * len(grads),
        out_shape=[jax.ShapeDtypeStruct(s[1:], wide) for s in shapes],
        scratch_shapes=scratch,
        compiler_params=pltpu.CompilerParams(
            vmem_limit_bytes=VMEM_LIMIT, collective_id=0, has_side_effects=True
        ),
        cost_estimate=pl.CostEstimate(flops=total, bytes_accessed=4 * total, transcendentals=0),
    )(*[g.reshape((2,) * tok_bits + g.shape[1:]) for g in grads])


def sharded_rows(grad):
    shards = lax.axis_size("tok")
    rows = grad.shape[0] // shards
    grad = grad.astype(low_type)
    if rows % 16 == 0:
        return grad.reshape(shards, rows, grad.shape[1])
    return grad.reshape(shards, rows * grad.shape[1] // 128, 128)


def conv_rows(turned):
    shards = lax.axis_size("tok")
    taps, halves, channels, lanes = turned.shape
    split = turned.reshape(taps, halves, shards, channels // shards, lanes)
    return jnp.moveaxis(split, 2, 0).reshape(shards, -1, lanes)


def conv_share(rows, taps, halves):
    split = rows.reshape(taps, halves, -1, rows.shape[-1])
    return jnp.moveaxis(split, 2, 3).reshape(taps, halves * rows.shape[-1], -1)


def reduced_all(conv_grads, matrices, vectors):
    shards = lax.axis_size("tok")
    parts = [conv_rows(g) for g in conv_grads]
    flat = jnp.concatenate([v.reshape(shards, -1) for v in vectors], axis=1)
    used = flat.shape[1]
    taken = sum(p.shape[1] for p in parts)
    rows = -(-used // 128)
    rows += -(rows + taken) % 16
    flat = jnp.pad(flat, ((0, 0), (0, rows * 128 - used))).reshape(shards, rows, 128)
    packed = jnp.concatenate([p.astype(low_type) for p in parts] + [flat.astype(low_type)], axis=1)
    results = reduced([packed] + [sharded_rows(m) for m in matrices])
    shares = []
    cursor = 0
    for part, grad in zip(parts, conv_grads):
        rows_here = results[0][cursor : cursor + part.shape[1]]
        shares.append(conv_share(rows_here, grad.shape[0], grad.shape[1]))
        cursor += part.shape[1]
    flat = results[0][cursor:].reshape(-1)
    cursor = 0
    pieces = []
    for vector in vectors:
        size = vector.size // shards
        pieces.append(flat[cursor : cursor + size])
        cursor += size
    whole = [r.reshape(-1, m.shape[1]) for r, m in zip(results[1:], matrices)]
    return (shares, whole, pieces)


REACH = 224
QUERY_TILE = 128
CLOSING_LIMIT = 63 * 1024 * 1024


def dot_t(left, right):
    return lax.dot_general(
        left, right, (((1,), (1,)), ((), ())), preferred_element_type=wide
    )


def counted(shape, axis):
    return lax.broadcasted_iota(jnp.int32, shape, axis).astype(wide)


def geometry_kernel(rows, crops):
    reach_rows = rows + 2 * REACH
    tile = min(rows, QUERY_TILE)
    window = tile + 2 * REACH

    def body(side_row, side_column, place, owner, crop_t, inverse, bias, edge_bias):
        first_row = (lax.axis_index("tok") * rows).astype(wide)
        sides_r = side_row[0].astype(wide)
        sides_c = side_column[0].astype(wide)
        volume_r = sides_r * sides_r * sides_r
        volume_c = sides_c * sides_c * sides_c
        shape = (crops, crops)
        start_r = jnp.sum(
            jnp.where(counted(shape, 0) < counted(shape, 1), volume_c, 0.0), axis=0, keepdims=True
        )
        start_c = jnp.sum(
            jnp.where(counted(shape, 1) < counted(shape, 0), volume_r, 0.0), axis=1, keepdims=True
        )

        def inside_of(length, begin):
            at = counted((length, crops), 0) + begin
            return ((at >= start_r) & (at < start_r + volume_r), at)

        wide_inside, _ = inside_of(rows + 2 * EDGE, first_row - EDGE)
        owner[0] = jnp.where(wide_inside, 1.0, 0.0).astype(low_type)
        inside, _ = inside_of(rows, first_row)
        side = jnp.sum(jnp.where(inside, sides_r, 0.0), axis=1, keepdims=True)
        first = jnp.sum(jnp.where(inside, start_r, 0.0), axis=1, keepdims=True)
        own = counted((rows, 1), 0)
        offset = own + first_row - first
        safe = jnp.maximum(side, 1.0)
        row_pos = jnp.floor((offset + 0.5) / (safe * safe))
        offset = offset - row_pos * safe * safe
        column = jnp.floor((offset + 0.5) / safe)
        depth_pos = offset - column * safe
        lane = counted((1, 32), 1)
        step_x = jnp.floor((lane + 0.5) / 9.0)
        step_y = jnp.floor((lane - 9.0 * step_x + 0.5) / 3.0)
        step_z = lane - 9.0 * step_x - 3.0 * step_y - 1.0
        step_x, step_y = (step_x - 1.0, step_y - 1.0)
        valid = None
        for at, step in ((row_pos, step_x), (column, step_y), (depth_pos, step_z)):
            moved = at + step
            here = (moved >= 0.0) & (moved < side)
            valid = here if valid is None else valid & here
        target = own + EDGE + (step_x * safe + step_y) * safe + step_z
        place[0] = jnp.where(valid, target, -1.0).astype(jnp.int32)
        at = counted((crops, rows), 1) + first_row
        inside_t = (at >= start_c) & (at < start_c + volume_c)
        crop_t[0] = jnp.where(inside_t, 1.0, 0.0).astype(low_type)
        inverse[0] = jnp.broadcast_to(1.0 / jnp.maximum(8.0 * volume_c, 1.0), (crops, 128))
        key_inside, _ = inside_of(reach_rows, first_row - REACH)
        key_first = jnp.sum(jnp.where(key_inside, start_r + 1.0, 0.0), axis=1, keepdims=True)
        query_first = jnp.sum(jnp.where(inside_t, start_c + 1.0, 0.0), axis=0, keepdims=True)
        for number in range(rows // tile):
            base = number * tile
            same = key_first[base : base + window] == query_first[:, base : base + tile]
            bias[0, number] = jnp.where(same, 0.0, far_below)
        for side in range(2):
            begin_row = 0 if side == 0 else max(rows - REACH, 0)
            begin = first_row - REACH if side == 0 else first_row + rows
            at = counted((crops, REACH), 1) + begin
            inside_t = (at >= start_c) & (at < start_c + volume_c)
            query_first = jnp.sum(jnp.where(inside_t, start_c + 1.0, 0.0), axis=0, keepdims=True)
            same = key_first[REACH + begin_row : 2 * REACH + begin_row] == query_first
            edge_bias[0, side] = jnp.where(same, 0.0, far_below)

    return body


def geometry_tables(crop_sides, rows):
    seqs, crops = crop_sides.shape
    sides = jnp.pad(crop_sides, ((0, 0), (0, CROP_ROWS - crops)))
    tile = min(rows, QUERY_TILE)
    return kernel_call(
        geometry_kernel(rows, CROP_ROWS),
        seqs,
        (sides[:, None, :], sides[:, :, None]),
        (),
        (
            ((seqs, rows, 32), jnp.int32),
            ((seqs, rows + 2 * EDGE, CROP_ROWS), low_type),
            ((seqs, CROP_ROWS, rows), low_type),
            ((seqs, CROP_ROWS, 128), wide),
            ((seqs, rows // tile, tile + 2 * REACH, tile), wide),
            ((seqs, 2, REACH, REACH), wide),
        ),
        (),
        [],
        0,
    )


def row_of(vector, lanes=slice(None)):
    return vector[lanes].reshape(1, -1)


def normed_rows(values):
    centered = values - jnp.mean(values, axis=-1, keepdims=True)
    variance = jnp.mean(centered * centered, axis=-1, keepdims=True)
    scale = lax.rsqrt(variance + norm_eps)
    return (centered * scale, scale)


def norm_pull(grad, normed, scale, gain):
    inner = grad * gain
    first = jnp.mean(inner, axis=-1, keepdims=True)
    second = jnp.mean(inner * normed, axis=-1, keepdims=True)
    return scale * (inner - first - normed * second)


def gelu_parts(value):
    size = jnp.abs(value) * math.sqrt(0.5)
    ratio = 1.0 / (1.0 + 0.3275911 * size)
    series = 1.061405429
    for term in (-1.453152027, 1.421413741, -0.284496736, 0.254829592):
        series = series * ratio + term
    decay = jnp.exp(-size * size)
    beyond = 0.5 * series * ratio * decay
    cumulative = jnp.where(value >= 0.0, 1.0 - beyond, beyond)
    return (value * cumulative, cumulative + value * decay * (1.0 / math.sqrt(2.0 * math.pi)))


def head_lanes(block, half):
    lane = lax.broadcasted_iota(jnp.int32, block.shape, 1)
    chosen = lane < HEAD_DIM if half == 0 else lane >= HEAD_DIM
    return jnp.where(chosen, block, jnp.zeros_like(block))


def turned(block):
    return jnp.transpose(block.astype(wide))


def forward_kernel(rows, model_width, hidden, seqs, near_given):
    tile = min(rows, QUERY_TILE)
    window = tile + 2 * REACH
    chunk = 768
    scale = 1.0 / math.sqrt(HEAD_DIM)

    def body(*refs):
        tokens, bias = refs[:2]
        if near_given:
            left, right = refs[2:4]
            refs = refs[2:]
        (
            ln1_gain, ln1_bias, qkv_weight, qv_bias, out_bias, ln2_gain, ln2_bias,
            fc1_bias, fc2_bias, all_tokens, skip, out_away, fc1_away, fc2_away, deconv_away,
            normed_out, queries, keys, values, attended, log_totals, resid_out, second_out,
            act_out, slope_out, resid_low, upsampled, up_left, up_right, skip_left, skip_right,
            near_ref, turned_ref, skip_send, skip_recv, near_left, near_right, near_send, near_recv,
            out_weight, fc1_weight, fc2_weight, deconv_weight, weight_sem, *edge_refs,
        ) = refs[2:]
        step = pl.program_id(0)
        pay = Payload(seqs, up_left, up_right, *edge_refs)
        skip_edge = Edge(
            skip.at[:, :EDGE],
            skip.at[:, rows - EDGE :],
            skip_left,
            skip_right,
            skip_send,
            skip_recv,
        )

        def token_edge(number):
            return Edge(
                all_tokens.at[number, :REACH],
                all_tokens.at[number, rows - REACH :],
                near_left.at[number],
                near_right.at[number],
                near_send.at[number],
                near_recv.at[number],
            )

        weight_copies = [
            pltpu.make_async_copy(source, target, weight_sem.at[number])
            for number, (source, target) in enumerate(
                (
                    (out_away, out_weight),
                    (fc1_away, fc1_weight),
                    (fc2_away, fc2_weight),
                    (deconv_away, deconv_weight),
                )
            )
        ]

        def weights_ready(*numbers):
            @pl.when(step == 0)
            def _():
                for number in numbers:
                    weight_copies[number].wait()

        @pl.when(step == 0)
        def _():
            for copy in weight_copies:
                copy.start()

        pay.enter()

        @pl.when(step == 0)
        def _():
            met()
            if near_given:
                skip_edge.start()
            else:
                token_edge(0).start()
                for field, there in zip((near_left, near_right), tok_sides()):

                    @pl.when(jnp.logical_not(there))
                    def _():
                        field[...] = jnp.zeros_like(field)

            for field, there in zip((skip_left, skip_right), tok_sides()):

                @pl.when(jnp.logical_not(there))
                def _():
                    copies = [
                        pltpu.make_async_copy(pay.zero_ref, field.at[n], pay.zero_sem.at[n])
                        for n in range(seqs)
                    ]
                    for copy in copies:
                        copy.start()
                    for copy in copies:
                        copy.wait()

        def put_normed(values, begin):
            normed = normed_rows(values.astype(wide))[0] * row_of(ln1_gain) + row_of(ln1_bias)
            near_ref[begin : begin + values.shape[0], :] = normed.astype(low_type)

        def project(at):
            for number, target in enumerate((queries, keys, values)):
                lanes = sub_lanes(number, model_width)
                found = dot(near_ref[at, :], qkv_weight[:, lanes])
                if number != 1:
                    found = found + qv_bias[number // 2 : number // 2 + 1, :]
                target[0, at, :] = found.astype(low_type)

        own_rows = slice(REACH, REACH + rows)
        put_normed(tokens[0], REACH)
        normed_out[0] = near_ref[own_rows, :]
        project(own_rows)
        if near_given:
            put_normed(left[0], 0)
            put_normed(right[0], REACH + rows)
        else:
            token_edge(step).land()

            @pl.when(step < seqs - 1)
            def _():
                token_edge(step + 1).start()

            @pl.when(step == seqs - 1)
            def _():
                skip_edge.start()

            put_normed(near_left[step], 0)
            put_normed(near_right[step], REACH + rows)
        project(slice(0, REACH))
        project(slice(REACH + rows, 2 * REACH + rows))
        for pair in range(model_width // 128):
            lanes = sub_lanes(pair, 128)
            turned_ref[lanes, :] = turned(values[0, :, lanes]).astype(low_type)
        for number in range(rows // tile):
            base = number * tile
            at = slice(base, base + tile)
            near = slice(base, base + window)
            for pair in range(model_width // 128):
                lanes = sub_lanes(pair, 128)
                query = queries[0, REACH + base : REACH + base + tile, lanes] * scale
                key = keys[0, near, lanes]
                halves = []
                for half in range(2):
                    head = 2 * pair + half
                    scores = dot_t(key, head_lanes(query, half)) + bias[0, number]
                    top = jnp.max(scores, axis=0, keepdims=True)
                    weights = jnp.exp(scores - top)
                    total = jnp.sum(weights, axis=0, keepdims=True)
                    log_totals[0, head : head + 1, at] = top + jnp.log(total)
                    probs = (weights * (1.0 / total)).astype(low_type)
                    value = turned_ref[head * HEAD_DIM : (head + 1) * HEAD_DIM, near]
                    halves.append(dot(value, probs))
                both = jnp.concatenate(halves, axis=0)
                attended[0, at, lanes] = jnp.transpose(both).astype(low_type)
        weights_ready(0)
        resid = tokens[0].astype(wide) + dot(attended[0], out_weight[...]) + row_of(out_bias)
        resid_out[0] = resid
        second = normed_rows(resid)[0] * row_of(ln2_gain) + row_of(ln2_bias)
        second_out[0] = second.astype(low_type)
        weights_ready(1, 2, 3)
        total = resid + row_of(fc2_bias)
        for number in range(hidden // chunk):
            lanes = sub_lanes(number, chunk)
            pre = dot(second_out[0], fc1_weight[:, lanes]) + row_of(fc1_bias, lanes)
            act, slope = gelu_parts(pre)
            act_out[0, :, lanes] = act.astype(low_type)
            slope_out[0, :, lanes] = slope.astype(low_type)
            total = total + dot(act_out[0, :, lanes], fc2_weight[lanes, :])
        resid_low[0] = total.astype(low_type)
        upsampled[0] = dot(resid_low[0], deconv_weight[...]).astype(low_type)
        pay.low[0] = upsampled[0, :EDGE, :]
        pay.high[0] = upsampled[0, rows - EDGE :, :]
        pay.send(True)

        @pl.when(step == seqs - 1)
        def _():
            skip_edge.land()
            skip_edge.sent()
            if not near_given:
                for number in range(seqs):
                    token_edge(number).sent()

    return body


def hidden_back_kernel(rows, model_width, hidden, seqs, linked):
    chunk = 768

    def body(
        up_grad, slope, resid, attended, log_totals,
        deconv_weight, fc2_weight, fc1_weight, out_weight, ln2_gain,
        branch_out, pre_out, resid_grad, mixed_out, pulled_out, stats,
        fc2_sum, fc1_sum, out_sum, gain_sum, shift_sum, *edge_refs,
    ):
        step = pl.program_id(0)
        if linked:
            (
                pulls_left, pulls_right, stats_left, stats_right, pull_keep, stat_keep,
                zero_pull, zero_stat, pull_send, pull_recv, stat_send, stat_recv, zero_sem,
            ) = edge_refs

        def edges(number):
            pull = Edge(
                pull_keep.at[number, :REACH],
                pull_keep.at[number, rows - REACH :],
                pulls_left.at[number],
                pulls_right.at[number],
                pull_send.at[number],
                pull_recv.at[number],
            )
            stat = Edge(
                stat_keep.at[number],
                stat_keep.at[number],
                stats_left.at[number],
                stats_right.at[number],
                stat_send.at[number],
                stat_recv.at[number],
            )
            return (pull, stat)

        if linked:

            @pl.when(step == 0)
            def _():
                greet()
                zero_pull[...] = jnp.zeros_like(zero_pull)
                zero_stat[...] = jnp.zeros_like(zero_stat)
                fields = ((pulls_left, stats_left), (pulls_right, stats_right))
                for (pull, stat), there in zip(fields, tok_sides()):

                    @pl.when(jnp.logical_not(there))
                    def _():
                        copies = []
                        for n in range(seqs):
                            copies += [
                                pltpu.make_async_copy(zero_pull, pull.at[n], zero_sem.at[0, n]),
                                pltpu.make_async_copy(zero_stat, stat.at[n], zero_sem.at[1, n]),
                            ]
                        for copy in copies:
                            copy.start()
                        for copy in copies:
                            copy.wait()

        @pl.when(pl.program_id(0) == 0)
        def _():
            for ref in (fc2_sum, fc1_sum, out_sum, gain_sum, shift_sum):
                ref[...] = jnp.zeros_like(ref)

        def column_sum(field):
            return jnp.sum(field, axis=0, keepdims=True)

        incoming = dot_t(up_grad[0], deconv_weight[...])
        branch = incoming.astype(low_type)
        branch_out[0] = branch
        fc2_sum[...] += column_sum(branch.astype(wide))
        total = None
        for number in range(hidden // chunk):
            lanes = sub_lanes(number, chunk)
            act_grad = dot_t(branch_out[0], fc2_weight[lanes, :])
            pre = (act_grad * slope[0, :, lanes].astype(wide)).astype(low_type)
            pre_out[0, :, lanes] = pre
            fc1_sum[:, lanes] += column_sum(pre.astype(wide))
            term = dot_t(pre_out[0, :, lanes], fc1_weight[:, lanes])
            total = term if total is None else total + term
        normed, norm_scale = normed_rows(resid[0])
        gain_sum[...] += column_sum(total * normed)
        shift_sum[...] += column_sum(total)
        mixed = incoming + norm_pull(total, normed, norm_scale, row_of(ln2_gain))
        resid_grad[0] = mixed
        mixed = mixed.astype(low_type)
        mixed_out[0] = mixed
        out_sum[...] += column_sum(mixed.astype(wide))
        pulled = dot_t(mixed_out[0], out_weight[...]).astype(low_type)
        pulled_out[0] = pulled
        product = pulled.astype(wide) * attended[0].astype(wide)
        lane = lax.broadcasted_iota(jnp.int32, (16, model_width), 1)
        begin = lax.broadcasted_iota(jnp.int32, (16, model_width), 0) * HEAD_DIM
        chosen = (lane >= begin) & (lane < begin + HEAD_DIM)
        chosen = jnp.where(chosen, 1.0, 0.0).astype(low_type)
        inner = None
        for term in three_terms(product):
            part = dot_t(chosen, term)
            inner = part if inner is None else inner + part
        for pair in range(model_width // 128):
            heads = slice(2 * pair, 2 * pair + 2)
            unused = jnp.zeros((4, rows), wide)
            stats[0, pair] = jnp.concatenate([log_totals[0, heads], inner[heads], unused], axis=0)
        if linked:
            pull_keep[step] = pulled
            stat_keep[step] = stats[0]

            @pl.when(step == 0)
            def _():
                met()

            for edge in edges(step):
                edge.start()

            @pl.when(step == seqs - 1)
            def _():
                for number in range(seqs):
                    for edge in edges(number):
                        edge.land()
                for number in range(seqs):
                    for edge in edges(number):
                        edge.sent()

    return body


def attention_back_kernel(rows, model_width):
    tile = min(rows, QUERY_TILE)
    window = tile + 2 * REACH
    scale = 1.0 / math.sqrt(HEAD_DIM)

    def body(
        queries, keys, values, pulls, stats, bias,
        query_grad, key_own, value_own, low_pay, high_pay, near_key, near_value, turned_ref,
    ):
        for pair in range(model_width // 128):
            lanes = sub_lanes(pair, 128)
            turned_ref[lanes, :] = turned(keys[0, :, lanes]).astype(low_type)
        near_key[...] = jnp.zeros_like(near_key)
        near_value[...] = jnp.zeros_like(near_value)
        for number in range(rows // tile):
            base = number * tile
            at = slice(base, base + tile)
            near = slice(base, base + window)
            for pair in range(model_width // 128):
                lanes = sub_lanes(pair, 128)
                query = queries[0, REACH + base : REACH + base + tile, lanes] * scale
                key = keys[0, near, lanes]
                value = values[0, near, lanes]
                halves = []
                for half in range(2):
                    head = 2 * pair + half
                    probs, score_grad, one_query, one_pull = head_unit(
                        key, value, query, pulls[0, at, lanes], bias[0, number],
                        stats[0, pair, half : half + 1, at], stats[0, pair, 2 + half : 3 + half, at],
                        half,
                    )
                    near_key[near, lanes] += dot(score_grad, one_query)
                    near_value[near, lanes] += dot(probs, one_pull)
                    key_turned = turned_ref[head * HEAD_DIM : (head + 1) * HEAD_DIM, near]
                    halves.append(dot(key_turned, score_grad) * scale)
                both = jnp.concatenate(halves, axis=0)
                query_grad[0, at, lanes] = jnp.transpose(both).astype(low_type)
        for field, own_out, begin in (
            (near_key, key_own, 0),
            (near_value, value_own, model_width),
        ):
            lanes = slice(begin, begin + model_width)
            own_out[0] = field[REACH : REACH + rows, :]
            low_pay[0, :, lanes] = field[:REACH, :].astype(low_type)
            high_pay[0, :, lanes] = field[REACH + rows :, :].astype(low_type)

    return body


def token_kernel(rows, model_width):
    def body(
        tokens, resid_grad, query_grad, key_own, value_own, qkv_weight, ln1_gain,
        grad_out, token_grad, bias_sum, gain_sum, shift_sum,
    ):
        @pl.when(pl.program_id(0) == 0)
        def _():
            for ref in (bias_sum, gain_sum, shift_sum):
                ref[...] = jnp.zeros_like(ref)

        grad_out[0, :, :model_width] = query_grad[0]
        for number, own in enumerate((key_own, value_own)):
            to = sub_lanes(number + 1, model_width)
            grad_out[0, :, to] = own[0].astype(low_type)
        bias_sum[...] += jnp.sum(grad_out[0].astype(wide), axis=0, keepdims=True)
        total = dot_t(grad_out[0], qkv_weight[...])
        normed, norm_scale = normed_rows(tokens[0].astype(wide))
        gain_sum[...] += jnp.sum(total * normed, axis=0, keepdims=True)
        shift_sum[...] += jnp.sum(total, axis=0, keepdims=True)
        token_grad[0] = resid_grad[0] + norm_pull(total, normed, norm_scale, row_of(ln1_gain))

    return body


def near_rows(field):
    rows = field.shape[1]
    lefts, rights = ([], [])
    distance, missing = (1, REACH)
    while missing > 0:
        take = min(rows, missing)
        lefts.insert(0, passed_along(field[:, rows - take :], "tok", distance))
        rights.append(passed_along(field[:, :take], "tok", -distance))
        distance, missing = (distance + 1, missing - take)
    if len(lefts) == 1:
        return (lefts[0], rights[0])
    return (jnp.concatenate(lefts, axis=1), jnp.concatenate(rights, axis=1))


def returned_rows(own, low_pay, high_pay):
    rows = own.shape[1]
    distance, missing = (1, REACH)
    while missing > 0:
        take = min(rows, missing)
        low_piece = low_pay[:, missing - take : missing]
        begin = REACH - missing
        high_piece = high_pay[:, begin : begin + take]
        own = own.at[:, rows - take :].add(passed_along(low_piece, "tok", -distance).astype(wide))
        own = own.at[:, :take].add(passed_along(high_piece, "tok", distance).astype(wide))
        distance, missing = (distance + 1, missing - take)
    return own


def head_unit(key, value, query, pulled, bias, log_total, inner, half):
    one_query = head_lanes(query, half)
    one_pull = head_lanes(pulled, half)
    scores = dot_t(key, one_query) + bias
    probs = jnp.exp(scores - log_total)
    probs_grad = dot_t(value, one_pull)
    score_grad = (probs * (probs_grad - inner)).astype(low_type)
    return (probs.astype(low_type), score_grad, one_query, one_pull)


def half_slice(piece, half):
    _, _, rows, _, lanes, axis = piece
    if isinstance(half, int) and axis == 0:
        return (slice(half * (rows // 2), (half + 1) * (rows // 2)), slice(None))
    if isinstance(half, int):
        return (slice(None), slice(half * (lanes // 2), (half + 1) * (lanes // 2)))
    if axis == 0:
        return (pl.ds(pl.multiple_of(half * (rows // 2), 16), rows // 2), slice(None))
    return (slice(None), pl.ds(pl.multiple_of(half * (lanes // 2), 128), lanes // 2))


def half_shape(piece):
    _, _, rows, _, lanes, axis = piece
    return (rows // 2, lanes) if axis == 0 else (rows, lanes // 2)


def closing_pieces(shapes):
    first, second, deconv, fc2, fc1, out, qkv = shapes
    pieces = [(1, 0, second[0], 0, second[1], 0)]
    pieces += [(0, part * first[0] // 2, first[0] // 2, 0, first[1], 0) for part in range(2)]
    pieces += [(2, 0, 48, lane, 512, 1) for lane in range(0, deconv[1], 512)]
    pieces += [(3, row, 48, 0, 768, 1) for row in range(0, fc2[0], 48)]
    pieces += [(4, 0, 48, lane, 768, 1) for lane in range(0, fc1[1], 768)]
    pieces += [(5, 0, 48, 0, 768, 1)]
    pieces += [(6, 0, 48, lane, 768, 1) for lane in range(0, qkv[1], 768)]
    return pieces


def closing_kernel(rows, model_width, hidden, seqs, shapes, bits, held_count):
    pieces = closing_pieces(shapes)
    count = len(pieces)
    stored = 3
    slots = 3
    mesh_id = pl.DeviceIdType.MESH
    tile = min(rows, QUERY_TILE)
    window = tile + 2 * REACH
    reach_rows = rows + 2 * REACH
    scale = 1.0 / math.sqrt(HEAD_DIM)
    pairs = model_width // 128
    phases = bits + 2
    vector_phases = bits + 1
    lines = seqs * rows
    spare_row = hidden
    own_scratch = 24
    span = 256
    items = seqs * (model_width // span)

    def body(*refs):
        packed = refs[:2]
        windows = refs[2:5]
        sources = refs[5:13]
        away = refs[13 : 13 + held_count]
        ln1_gain, early_vectors = refs[13 + held_count : 15 + held_count]
        rest = refs[15 + held_count :]
        results = rest[: len(shapes)]
        token_grad, vector_out = rest[len(shapes) : len(shapes) + 2]
        rest = rest[len(shapes) + 2 :]
        held = rest[:held_count]
        (
            pulls, pulls_left, pulls_right, stats, stats_left, stats_right, bias, edge_bias,
            normed_low, tokens, qkv_weight,
        ) = held
        rest = rest[held_count:]
        (
            arena, near, key_turned, key_total, value_total, grads, normed_turned, products,
            kept_first, kept_second, kept_third, vectors, vectors_landed, near_sem, held_sem, fetch_sem,
            local_sem, core_send, core_recv, send_sem, recv_sem, vector_send, vector_recv, spare,
        ) = rest[:own_scratch]
        del spare
        kept = (kept_first, kept_second, kept_third)
        landed = [
            rest[own_scratch + i * phases : own_scratch + (i + 1) * phases] for i in range(count)
        ]
        tok = lax.axis_index("tok")
        seq = lax.axis_index("seq")
        core = tok % 2

        def tok_bit(bit):
            return (tok // (1 << bit)) % 2

        def tok_step(bit):
            return (1 << bit) * (1 - 2 * tok_bit(bit))

        def kept_bit(phase):
            first = seq if phase == 1 else tok_bit(phase - 1)
            second = tok_bit(phase) if phase < bits else seq
            return (1 - core) * first + core * second

        def partner(phase):
            if phase == 0:
                return (seq, tok + tok_step(0))
            if phase > bits:
                return (1 - seq, tok)
            first = 0 if phase == 1 else tok_step(phase - 1)
            second = tok_step(phase) if phase < bits else 0
            across = 0
            if phase == 1:
                across = 1 - core
            if phase == bits:
                across = core
            return (
                seq + across * (1 - 2 * seq),
                tok + (1 - core) * first + core * second,
            )

        def vector_partner(phase):
            if phase < bits:
                return (seq, tok + tok_step(phase))
            return (1 - seq, tok)

        barrier = pltpu.get_barrier_semaphore()
        for phase in range(vector_phases):
            pl.semaphore_signal(
                barrier, inc=1, device_id=vector_partner(phase), device_id_type=mesh_id
            )

        def held_copies():
            return [
                pltpu.make_async_copy(source, target, held_sem.at[number])
                for number, (source, target) in enumerate(zip(away, held))
            ]

        def core_copy(number, half, receiver):
            index, begin, take, lane, lanes, axis = pieces[number]
            at = (slice(None),) * (bits - 1) + (1 - core,)
            if axis == 0:
                part = (pl.ds(begin + half * (take // 2), take // 2), slice(None))
                view = packed[index].at[at + part]
            else:
                slot = (number - stored) % slots
                part = (slice(None), pl.ds(half * (lanes // 2), lanes // 2))
                view = products.at[(slot,) + at + part]
            if receiver == 0:
                to = landed[number][0].at[(slice(None),) * (bits - 1) + (half,)]
            else:
                to = landed[number][0].at[half]
            return pltpu.make_async_remote_copy(
                src_ref=view,
                dst_ref=to,
                send_sem=core_send.at[number, half],
                recv_sem=core_recv.at[number, half],
                device_id=partner(0),
                device_id_type=mesh_id,
            )

        def local_copy(number):
            index, begin, take, _, _, _ = pieces[number]
            at = (slice(None),) * (bits - 1) + (core, pl.ds(begin, take))
            return pltpu.make_async_copy(packed[index].at[at], kept[number], local_sem.at[number])

        def remote_copy(number, phase):
            if phase > bits:
                view = landed[number][bits]
            else:
                view = landed[number][phase - 1].at[
                    (slice(None),) * (bits - phase) + (1 - kept_bit(phase),)
                ]
            return pltpu.make_async_remote_copy(
                src_ref=view,
                dst_ref=landed[number][phase],
                send_sem=send_sem.at[number, phase - 1],
                recv_sem=recv_sem.at[number, phase - 1],
                device_id=partner(phase),
                device_id_type=mesh_id,
            )

        def begin(number):
            for half in range(2):
                for mine in range(2):

                    @pl.when(core == mine)
                    def _():
                        core_copy(number, half, 1 - mine).start()

            if number < stored:
                local_copy(number).start()

        def bits_of(flat, length):
            return tuple((flat // (1 << bit)) % 2 for bit in reversed(range(length)))

        def finish(number, phase):
            piece = pieces[number]
            index, first, take, lane, lanes, axis = piece
            if phase == 0:
                for half in range(2):
                    for mine in range(2):

                        @pl.when(core == mine)
                        def _():
                            core_copy(number, half, mine).wait_recv()

                if number < stored:
                    local_copy(number).wait()
                blocks = 1 << (bits - 1)

                def step(block, carry):
                    at = bits_of(block, bits - 1)
                    for half in range(2):
                        flat = (1 - core) * (2 * block + half) + core * (blocks * half + block)
                        to = bits_of(flat, bits)
                        part = half_slice(piece, half)
                        if number < stored:
                            mine = kept[number][at + part]
                        else:
                            mine = products[((number - stored) % slots,) + at + (core,) + part]
                        landed[number][0][to] = landed[number][0][to] + mine
                    return carry

                lax.fori_loop(0, blocks, step, 0)
                return
            remote_copy(number, phase).wait_recv()
            got = landed[number][phase]
            if phase <= bits:
                before = landed[number][phase - 1]

                def step(block, carry):
                    at = bits_of(block, bits - phase)
                    got[at] = got[at] + before[at + (kept_bit(phase),)]
                    return carry

                if phase < bits:
                    lax.fori_loop(0, 1 << (bits - phase), step, 0)
                else:
                    got[...] = got[...] + before[kept_bit(phase)]
                remote_copy(number, phase + 1).start()
                return
            height, length = half_shape(piece)
            for half, value in ((seq, landed[number][bits]), (1 - seq, got)):
                if axis == 0:
                    at = (pl.ds(pl.multiple_of(first + half * height, 8), height), slice(None))
                else:
                    at = (pl.ds(first, take), pl.ds(pl.multiple_of(lane + half * length, 128), length))
                results[index][at] = value[...].astype(wide)

        def near_copies(item):
            group, number = divmod(item, seqs)
            return [
                pltpu.make_async_copy(
                    source.at[number, :, pl.ds(group * span, span)],
                    near.at[item % 2, field],
                    near_sem.at[item % 2, field],
                )
                for field, source in enumerate(windows)
            ]

        def pair_places(group, pair):
            lanes = pl.ds(pl.multiple_of(pair * 128, 128), 128)
            whole = pl.ds(pl.multiple_of(group * span + pair * 128, 128), 128)
            return (lanes, whole, group * (span // 128) + pair)

        def own_segment(item, base):
            group, number = divmod(item, seqs)
            slot = item % 2
            own = slice(REACH + base, REACH + base + tile)
            near_rows_at = slice(base, base + window)
            inside = slice(REACH - base, REACH - base + rows)

            def step(pair, carry):
                lanes, whole, heads = pair_places(group, pair)
                query = near[slot, 0, own, lanes] * scale
                key = near[slot, 1, near_rows_at, lanes]
                value = near[slot, 2, near_rows_at, lanes]
                pulled = pulls[number, base : base + tile, whole]
                key_term, value_term, halves = (None, None, [])
                for half in range(2):
                    log_total = stats[number, heads, half : half + 1, base : base + tile]
                    inner = stats[number, heads, 2 + half : 3 + half, base : base + tile]
                    probs, score_grad, one_query, one_pull = head_unit(
                        key, value, query, pulled, bias[number, base // tile], log_total, inner, half
                    )
                    here = dot(score_grad[inside], one_query)
                    key_term = here if key_term is None else key_term + here
                    here = dot(probs[inside], one_pull)
                    value_term = here if value_term is None else value_term + here
                    begin_row = pair * 128 + half * HEAD_DIM
                    feature = pl.ds(pl.multiple_of(begin_row, HEAD_DIM), HEAD_DIM)
                    halves.append(dot(key_turned[feature, near_rows_at], score_grad) * scale)
                if base == 0:
                    key_total[:, lanes] = key_term
                    value_total[:, lanes] = value_term
                else:
                    key_total[:, lanes] += key_term
                    value_total[:, lanes] += value_term
                both = jnp.transpose(jnp.concatenate(halves, axis=0)).astype(low_type)
                grads[number * rows + base : number * rows + base + tile, whole] = both
                return carry

            lax.fori_loop(0, span // 128, step, 0)

        def edge_segment(item, side):
            group, number = divmod(item, seqs)
            slot = item % 2
            from_rows = slice(0, REACH) if side == 0 else slice(REACH + rows, reach_rows)
            begin_row = 0 if side == 0 else rows - REACH
            at = slice(begin_row, begin_row + REACH)
            key_rows = slice(REACH + begin_row, 2 * REACH + begin_row)
            columns = slice(rows - REACH, rows) if side == 0 else slice(0, REACH)
            pull_ref, stat_ref = ((pulls_left, stats_left), (pulls_right, stats_right))[side]

            def step(pair, carry):
                lanes, whole, heads = pair_places(group, pair)
                query = near[slot, 0, from_rows, lanes] * scale
                key = near[slot, 1, key_rows, lanes]
                value = near[slot, 2, key_rows, lanes]
                pulled = pull_ref[number, :, whole]
                key_term, value_term = (None, None)
                for half in range(2):
                    log_total = stat_ref[number, heads, half : half + 1, :][:, columns]
                    inner = stat_ref[number, heads, 2 + half : 3 + half, :][:, columns]
                    probs, score_grad, one_query, one_pull = head_unit(
                        key, value, query, pulled, edge_bias[number, side], log_total, inner, half
                    )
                    here = dot(score_grad, one_query)
                    key_term = here if key_term is None else key_term + here
                    here = dot(probs, one_pull)
                    value_term = here if value_term is None else value_term + here
                key_total[at, lanes] += key_term
                value_total[at, lanes] += value_term
                return carry

            lax.fori_loop(0, span // 128, step, 0)

        def open_item(item):
            for copy in near_copies(item):
                copy.wait()
            if item + 1 < items:
                for copy in near_copies(item + 1):
                    copy.start()
            for block in range(span // 128):
                lanes = sub_lanes(block, 128)
                key_turned[lanes, :] = turned(near[item % 2, 1, :, lanes]).astype(low_type)

        def close_item(item):
            group, number = divmod(item, seqs)
            at = slice(number * rows, (number + 1) * rows)
            for part, total in ((1, key_total), (2, value_total)):
                lanes = pl.ds(part * model_width + group * span, span)
                grads[at, lanes] = total[...].astype(low_type)

        def group_grads(group):
            parts = [
                grads[:, part * model_width + group * span : part * model_width + (group + 1) * span]
                for part in range(3)
            ]
            return jnp.concatenate(parts, axis=1)

        def product(number, left_rows, right):
            lanes = pieces[number][4]
            slot = (number - stored) % slots
            shard_rows = model_width >> bits
            group = (1 << bits) // 2

            def step(part, carry):
                begin_row = pl.multiple_of(part * group * shard_rows, 16)
                found = dot(left_rows(begin_row, group * shard_rows), right()).astype(low_type)
                for shard in range(group):
                    at = bits_of(part * group + shard, bits)
                    block = found[shard * shard_rows : (shard + 1) * shard_rows]
                    products[(slot,) + at + (slice(None), slice(0, lanes))] = block
                return carry

            lax.fori_loop(0, 2, step, 0)

        def token_segment(number):
            at = slice(number * rows, (number + 1) * rows)
            total = dot_t(grads[at, :], qkv_weight[...])
            normed, norm_scale = normed_rows(tokens[number].astype(wide))
            vectors[0, 0:1, :] += jnp.sum(total * normed, axis=0, keepdims=True)
            vectors[0, 1:2, :] += jnp.sum(total, axis=0, keepdims=True)
            for row, part in ((2, 0), (3, 2)):
                field = grads[at, sub_lanes(part, model_width)].astype(wide)
                vectors[0, row : row + 1, :] += jnp.sum(field, axis=0, keepdims=True)
            pull = norm_pull(total, normed, norm_scale, row_of(ln1_gain))
            token_grad[number] = pull

        def vector_copy(phase):
            return pltpu.make_async_remote_copy(
                src_ref=vectors.at[phase],
                dst_ref=vectors_landed.at[phase],
                send_sem=vector_send.at[phase],
                recv_sem=vector_recv.at[phase],
                device_id=vector_partner(phase),
                device_id_type=mesh_id,
            )

        def finish_vector(phase):
            vector_copy(phase).wait_recv()
            if phase + 1 < vector_phases:
                vectors[phase + 1] = vectors[phase] + vectors_landed[phase]
                vector_copy(phase + 1).start()
            else:
                vector_out[...] = vectors[phase] + vectors_landed[phase]

        resid_low, up_grad, act, branch, normed_two, pre, attended, mixed = sources
        fetches = [(resid_low, 0, model_width)]
        fetches += [(up_grad, lane, 512) for lane in range(0, up_grad.shape[1], 512)]
        fetches += [(act, lane, model_width) for lane in range(0, hidden, model_width)]
        fetches += [(branch, 0, model_width), (normed_two, 0, model_width)]
        fetches += [(pre, lane, model_width) for lane in range(0, hidden, model_width)]
        fetches += [(attended, 0, model_width), (mixed, 0, model_width)]

        def fetch(number):
            source, lane, lanes = fetches[number]
            to = pl.ds((number % 3) * model_width, lanes)
            return pltpu.make_async_copy(
                source.at[:, pl.ds(lane, lanes)], grads.at[:, to], fetch_sem.at[number]
            )

        def fetched(number):
            lanes = fetches[number][2]
            begin_lane = (number % 3) * model_width
            return lambda: grads[:, begin_lane : begin_lane + lanes]

        def turn_fetched(number, chunk=None):
            begin_lane = (number % 3) * model_width

            def step(block, carry):
                lanes = pl.ds(pl.multiple_of(begin_lane + block * 128, 128), 128)
                found = turned(grads[:, lanes]).astype(low_type)
                if chunk is None:
                    at = pl.ds(pl.multiple_of(spare_row + block * 128, 128), 128)
                    arena[at, :] = found
                else:
                    shard_rows = hidden >> bits
                    for granule in range(8):
                        feature = chunk * model_width + block * 128 + granule * 16
                        shard, inner = (feature // shard_rows, feature % shard_rows)
                        to = (inner // 48) * model_width + shard * 48 + inner % 48
                        at = pl.ds(pl.multiple_of(to, 16), 16)
                        arena[at, :] = found[granule * 16 : (granule + 1) * 16]
                return carry

            lax.fori_loop(0, pairs, step, 0)

        def arena_rows(base):
            return lambda begin_row, take: arena[pl.ds(pl.multiple_of(base + begin_row, 16), take), :]

        def turned_rows(begin_row, take):
            return normed_turned[pl.ds(begin_row, take), :]

        state = {"now": 0.0, "link": 0.0, "flying": 0}
        events = []
        waiting = []
        sent = set()
        sizes = [p[2] * p[4] / (48.0 * 768.0) for p in pieces]

        def one_event():
            events.sort()
            ready, number, phase = events.pop(0)
            state["now"] = max(state["now"], ready)
            if number == count:
                finish_vector(phase)
                if phase + 1 < vector_phases:
                    events.append((state["now"] + 2.5, number, phase + 1))
                return
            finish(number, phase)
            if phase == 0:
                waiting.append(number)
            elif phase + 1 < phases:
                cost = (6.0, 5.0, 4.0, 3.0, 2.0)[min(phase - 1, 4)]
                events.append((state["now"] + 2.5 + cost * sizes[number], number, phase + 1))
            if phase == 1:
                state["flying"] -= 1
            while waiting and state["flying"] < 4:
                chosen = waiting.pop(0)
                remote_copy(chosen, 1).start()
                state["flying"] += 1
                start = max(state["now"], state["link"])
                state["link"] = start + 4.0 * sizes[chosen]
                events.append((state["link"] + 1.0, chosen, 1))

        def pump(spent):
            state["now"] += spent
            while events and min(events)[0] <= state["now"]:
                one_event()

        def open_piece(number):
            begin(number)
            events.append((state["now"] + 2.5 + 2.0 * sizes[number], number, 0))

        def make_product(number, left_rows, right):
            before = number - slots
            if before >= stored:
                while any(e[1] == before and e[2] == 0 for e in events):
                    one_event()
                for half in range(2):
                    core_copy(before, half, 0).wait_send()
                    sent.add((before, half))
            product(number, left_rows, right)
            open_piece(number)
            pump(1.2)

        vectors[0, 0:8, :] = jnp.zeros((8, model_width), wide)
        vectors[0, 8:16, :] = early_vectors[...]
        for number in range(3):
            fetch(number).start()
        pl.semaphore_wait(barrier, vector_phases)
        for number in range(stored):
            open_piece(number)
        for copy in held_copies():
            copy.start()
        cursor = 0
        piece = stored

        def used():
            if cursor + 3 < len(fetches):
                fetch(cursor + 3).start()
            return cursor + 1

        def turn_next(chunk=None):
            fetch(cursor).wait()
            turn_fetched(cursor, chunk)
            pump(1.0)

        def product_next(number, left_rows):
            fetch(cursor).wait()
            make_product(number, left_rows, fetched(cursor))

        turn_next()
        cursor = used()
        for _ in range(up_grad.shape[1] // 512):
            product_next(piece, arena_rows(spare_row))
            cursor, piece = (used(), piece + 1)
        for chunk in range(hidden // model_width):
            turn_next(chunk)
            cursor = used()
        fetch(cursor).wait()
        for part in range(hidden // model_width):
            make_product(piece, arena_rows(part * model_width), fetched(cursor))
            piece += 1
        cursor = used()
        turn_next()
        cursor = used()
        for _ in range(hidden // model_width):
            product_next(piece, arena_rows(spare_row))
            cursor, piece = (used(), piece + 1)
        turn_next()
        cursor = used()
        product_next(piece, arena_rows(spare_row))
        cursor, piece = (used(), piece + 1)
        for copy in near_copies(0):
            copy.start()
        for copy in held_copies():
            copy.wait()
        for line in range(seqs):

            def turn_normed(column, carry):
                lanes = pl.ds(pl.multiple_of(column * 128, 128), 128)
                block = turned(normed_low[line, :, lanes]).astype(low_type)
                normed_turned[lanes, line * rows : (line + 1) * rows] = block
                return carry

            lax.fori_loop(0, pairs, turn_normed, 0)
        pump(1.5)
        for item in range(items):
            open_item(item)
            for base in range(0, rows, tile):
                own_segment(item, base)
                pump(1.8)
            for side in range(2):
                edge_segment(item, side)
                pump(1.3)
            close_item(item)
            if item % seqs == seqs - 1:
                make_product(piece, turned_rows, partial(group_grads, item // seqs))
                piece += 1
        for number in range(seqs):
            token_segment(number)
            pump(3.0)
        vector_copy(0).start()
        events.append((state["now"] + 2.5, count, 0))
        while events:
            one_event()
        for number in range(count):
            for half in range(2):
                if (number, half) not in sent:
                    core_copy(number, half, 0).wait_send()
            for phase in range(1, phases):
                remote_copy(number, phase).wait_send()
        for phase in range(vector_phases):
            vector_copy(phase).wait_send()

    fetch_count = 7 + 2 * (hidden // model_width) - 2 + shapes[2][1] // 512
    scratch = [
        pltpu.VMEM((hidden + model_width, model_width), low_type),
        pltpu.VMEM((2, 3, reach_rows, span), low_type),
        pltpu.VMEM((span, reach_rows), low_type),
        pltpu.VMEM((rows, span), wide),
        pltpu.VMEM((rows, span), wide),
        pltpu.VMEM((lines, 3 * model_width), low_type),
        pltpu.VMEM((model_width, lines), low_type),
        pltpu.VMEM((slots,) + (2,) * bits + (48, 768), low_type),
        pltpu.VMEM((2,) * (bits - 1) + (pieces[0][2], pieces[0][4]), low_type),
        pltpu.VMEM((2,) * (bits - 1) + (pieces[1][2], pieces[1][4]), low_type),
        pltpu.VMEM((2,) * (bits - 1) + (pieces[2][2], pieces[2][4]), low_type),
        pltpu.VMEM((vector_phases, 16, model_width), wide),
        pltpu.VMEM((vector_phases, 16, model_width), wide),
        pltpu.SemaphoreType.DMA((2, 3)),
        pltpu.SemaphoreType.DMA((held_count,)),
        pltpu.SemaphoreType.DMA((fetch_count,)),
        pltpu.SemaphoreType.DMA((stored,)),
        pltpu.SemaphoreType.DMA((count, 2)),
        pltpu.SemaphoreType.DMA((count, 2)),
        pltpu.SemaphoreType.DMA((count, phases - 1)),
        pltpu.SemaphoreType.DMA((count, phases - 1)),
        pltpu.SemaphoreType.DMA((vector_phases,)),
        pltpu.SemaphoreType.DMA((vector_phases,)),
        pltpu.SemaphoreType.DMA((1,)),
    ]
    for piece in pieces:
        block = half_shape(piece)
        scratch += [pltpu.VMEM((2,) * (bits - phase) + block, low_type) for phase in range(bits + 1)]
        scratch.append(pltpu.VMEM(block, low_type))
    return (body, scratch)


def closing(packed, windows, sources, held, small):
    shards = lax.axis_size("tok")
    bits = bit_count(shards)
    tokens, qkv_weight = (held[9], held[10])
    seqs, rows, model_width = tokens.shape
    hidden = sources[2].shape[1]
    shapes = [
        packed[0].shape[1:],
        packed[1].shape[1:],
        (model_width // shards, sources[1].shape[1]),
        (hidden // shards, model_width),
        (model_width // shards, hidden),
        (model_width // shards, model_width),
        (model_width // shards, qkv_weight.shape[1]),
    ]
    body, scratch = closing_kernel(
        rows, model_width, hidden, seqs, shapes, bits, len(held)
    )
    inside = pl.BlockSpec(memory_space=pltpu.VMEM)
    far = pl.BlockSpec(memory_space=pl.ANY)
    out_shape = [jax.ShapeDtypeStruct(s, wide) for s in shapes]
    out_shape.append(jax.ShapeDtypeStruct(tokens.shape, wide))
    out_shape.append(jax.ShapeDtypeStruct((16, model_width), wide))
    away = [p.reshape((2,) * bits + p.shape[1:]) for p in packed]
    away += list(windows) + list(sources) + list(held)
    return pl.pallas_call(
        body,
        in_specs=[far] * len(away) + [inside] * len(small),
        out_specs=[inside] * len(out_shape),
        out_shape=out_shape,
        scratch_shapes=[pltpu.VMEM(f.shape, f.dtype) for f in held] + scratch,
        compiler_params=pltpu.CompilerParams(
            vmem_limit_bytes=CLOSING_LIMIT, collective_id=1, has_side_effects=True
        ),
        cost_estimate=pl.CostEstimate(
            flops=50 * 10**9, bytes_accessed=60 * 10**6, transcendentals=0
        ),
    )(*away, *small)


def local(
    tokens,
    skip_features,
    crop_sides,
    ln1_gain,
    ln1_bias,
    qkv_weight,
    qv_bias,
    out_weight,
    out_bias,
    ln2_gain,
    ln2_bias,
    fc1_weight,
    fc1_bias,
    fc2_weight,
    fc2_bias,
    deconv_weight,
    conv1_weight,
    conv2_weight,
    conv3_weight,
    cotangent,
):
    seq_count, row_count, model_width = tokens.shape
    channels = conv2_weight.shape[2]
    hidden = fc1_weight.shape[1]
    reaches = (key_reach + row_count - 1) // row_count
    reach_rows = row_count + 2 * REACH
    near_given = row_count < REACH
    near = near_rows(tokens) if near_given else ()
    near_block = (seq_count, 16 if near_given else REACH, model_width)
    skip = skip_features.reshape(seq_count, row_count, 8 * channels)
    edge_block = ((seq_count, EDGE, 8 * channels), low_type)
    place, owner, crop_t, inverse, bias, edge_bias = geometry_tables(crop_sides, row_count)

    def block(lanes, kind, rows=row_count):
        return ((seq_count, rows, lanes), kind)

    matrix_flops = 2 * seq_count * row_count * model_width
    (
        normed_low, queries, keys, values, attended, log_totals, resid_one, normed_two,
        act_low, slope_low, resid_low, upsampled, *edges,
    ) = kernel_call(
        forward_kernel(row_count, model_width, hidden, seq_count, near_given),
        seq_count,
        (tokens, bias) + tuple(near),
        (
            ln1_gain, ln1_bias, qkv_weight, qv_bias, out_bias, ln2_gain, ln2_bias, fc1_bias, fc2_bias,
        ),
        (
            block(model_width, low_type),
            block(model_width, low_type, reach_rows),
            block(model_width, low_type, reach_rows),
            block(model_width, low_type, reach_rows),
            block(model_width, low_type),
            block(row_count, wide, 16),
            block(model_width, wide),
            block(model_width, low_type),
            block(hidden, low_type),
            block(hidden, low_type),
            block(model_width, low_type),
            block(8 * channels, low_type),
        ),
        (),
        [
            pltpu.VMEM((reach_rows, model_width), low_type),
            pltpu.VMEM((model_width, reach_rows), low_type),
            pltpu.SemaphoreType.DMA((2,)),
            pltpu.SemaphoreType.DMA((2,)),
            pltpu.VMEM(near_block, low_type),
            pltpu.VMEM(near_block, low_type),
            pltpu.SemaphoreType.DMA((seq_count, 2)),
            pltpu.SemaphoreType.DMA((seq_count, 2)),
            pltpu.VMEM(out_weight.shape, low_type),
            pltpu.VMEM(fc1_weight.shape, low_type),
            pltpu.VMEM(fc2_weight.shape, low_type),
            pltpu.VMEM(deconv_weight.shape, low_type),
            pltpu.SemaphoreType.DMA((4,)),
        ]
        + edge_scratch(seq_count, EDGE, 8 * channels),
        matrix_flops * (8 * model_width + 2 * hidden + 8 * channels),
        away=(tokens, skip, out_weight, fc1_weight, fc2_weight, deconv_weight),
        landing=(edge_block,) * 4,
        collective=2,
    )
    section_out, up_grad, skip_grad, conv1_grad, conv2_grad, conv3_grad = conv_section(
        upsampled,
        skip,
        edges,
        cotangent.reshape(seq_count, row_count, 8 * channels),
        (conv1_weight, conv2_weight, conv3_weight),
        (place, owner, crop_t, inverse),
        reaches,
    )
    section_out = section_out.reshape(seq_count, row_count, 8, channels)
    skip_grad = skip_grad.reshape(seq_count, row_count, 8, channels)
    shards = lax.axis_size("tok")
    linked = (
        row_count >= REACH
        and lax.axis_size("seq") == 2
        and model_width // shards == 48
        and shards * 8 == channels
    )
    pairs = model_width // 128
    pull_block = ((seq_count, REACH, model_width), low_type)
    stat_block = ((seq_count, pairs, 8, row_count), wide)
    (
        branch_low, pre_low, resid_grad, mixed_low, pulled, stats,
        fc2_bias_grad, fc1_bias_grad, out_bias_grad, ln2_gain_grad, ln2_bias_grad, *near_back,
    ) = kernel_call(
        hidden_back_kernel(row_count, model_width, hidden, seq_count, linked),
        seq_count,
        (up_grad, slope_low, resid_one, attended, log_totals),
        (deconv_weight, fc2_weight, fc1_weight, out_weight, ln2_gain),
        (
            block(model_width, low_type),
            block(hidden, low_type),
            block(model_width, wide),
            block(model_width, low_type),
            block(model_width, low_type),
            stat_block,
        ),
        (
            ((1, model_width), wide),
            ((1, hidden), wide),
            ((1, model_width), wide),
            ((1, model_width), wide),
            ((1, model_width), wide),
        ),
        [
            pltpu.VMEM((seq_count, row_count, model_width), low_type),
            pltpu.VMEM(*stat_block),
            pltpu.VMEM((REACH, model_width), low_type),
            pltpu.VMEM(stat_block[0][1:], wide),
            pltpu.SemaphoreType.DMA((seq_count, 2)),
            pltpu.SemaphoreType.DMA((seq_count, 2)),
            pltpu.SemaphoreType.DMA((seq_count, 2)),
            pltpu.SemaphoreType.DMA((seq_count, 2)),
            pltpu.SemaphoreType.DMA((2, seq_count)),
        ]
        if linked
        else [],
        matrix_flops * (model_width + 2 * hidden + 8 * channels),
        landing=(pull_block, pull_block, stat_block, stat_block) if linked else (),
        collective=7 if linked else None,
    )

    def weight_product(left, right):
        return jnp.einsum(
            "rd,re->de",
            left.reshape(-1, left.shape[-1]),
            right.reshape(-1, right.shape[-1]),
            preferred_element_type=wide,
        )

    if linked:
        early = (
            out_bias_grad, ln2_gain_grad, ln2_bias_grad, fc2_bias_grad,
            fc1_bias_grad.reshape(-1, model_width),
        )
        def lines_of(field):
            return field.reshape(-1, field.shape[-1])

        results = closing(
            (conv1_grad, conv2_grad),
            (queries, keys, values),
            [
                lines_of(field)
                for field in (
                    resid_low, up_grad, act_low, branch_low, normed_two, pre_low, attended, mixed_low
                )
            ],
            (
                pulled, near_back[0], near_back[1], stats, near_back[2], near_back[3], bias,
                edge_bias, normed_low, tokens, qkv_weight,
            ),
            (ln1_gain, jnp.concatenate(early, axis=0)),
        )
        conv_shares = (
            conv_share(results[0][:432], 27, 2),
            conv_share(results[1][:216], 27, 1),
            conv_share(results[0][432:448], 1, 2),
        )
        split = results[6].reshape(-1, 3, 3, model_width // 3)
        shares = list(results[2:6]) + [split.swapaxes(1, 2).reshape(results[6].shape)]
        token_grad = resid_grad + results[7]
        lines = results[8]
        span = model_width // shards
        own = lax.dynamic_slice_in_dim(lines[:12], lax.axis_index("tok") * span, span, 1)
        long_span = hidden // shards
        long_line = lines[12:16].reshape(hidden)
        long_own = lax.dynamic_slice_in_dim(
            long_line, lax.axis_index("tok") * long_span, long_span, 0
        )
        vectors = (own[0], own[1], own[2], own[3], own[8], own[9], own[10], long_own, own[11])
    else:
        query_grad, key_own, value_own, low_pay, high_pay = kernel_call(
            attention_back_kernel(row_count, model_width),
            seq_count,
            (queries, keys, values, pulled, stats, bias),
            (),
            (
                block(model_width, low_type),
                block(model_width, wide),
                block(model_width, wide),
                block(2 * model_width, low_type, REACH),
                block(2 * model_width, low_type, REACH),
            ),
            (),
            [
                pltpu.VMEM((reach_rows, model_width), wide),
                pltpu.VMEM((reach_rows, model_width), wide),
                pltpu.VMEM((model_width, reach_rows), low_type),
            ],
            matrix_flops * 12 * model_width,
        )
        both = jnp.concatenate([key_own, value_own], axis=-1)
        both = returned_rows(both, low_pay, high_pay)
        qkv_grad_low, token_grad, column_sums, ln1_gain_grad, ln1_bias_grad = kernel_call(
            token_kernel(row_count, model_width),
            seq_count,
            (tokens, resid_grad, query_grad, both[:, :, :model_width], both[:, :, model_width:]),
            (qkv_weight, ln1_gain),
            (block(3 * model_width, low_type), block(model_width, wide)),
            (
                ((1, 3 * model_width), wide),
                ((1, model_width), wide),
                ((1, model_width), wide),
            ),
            [],
            matrix_flops * 3 * model_width,
        )
        matrices = (
            weight_product(resid_low, up_grad),
            weight_product(act_low, branch_low),
            weight_product(normed_two, pre_low),
            weight_product(attended, mixed_low),
            weight_product(normed_low, qkv_grad_low),
        )
        conv3_turned = jnp.moveaxis(conv3_grad.reshape(1, 2, channels, channels), 2, 3)
        conv_grads = (conv1_grad, conv2_grad, conv3_turned)
        conv_shares, shares, vectors = reduced_all(
            conv_grads,
            matrices,
            (
                ln1_gain_grad, ln1_bias_grad, column_sums[:, :model_width],
                column_sums[:, 2 * model_width :], out_bias_grad, ln2_gain_grad, ln2_bias_grad,
                fc1_bias_grad, fc2_bias_grad,
            ),
        )
    return (
        section_out,
        token_grad,
        skip_grad,
        vectors[0],
        vectors[1],
        shares[4],
        jnp.stack([vectors[2], vectors[3]]),
        shares[3],
        vectors[4],
        vectors[5],
        vectors[6],
        shares[2],
        vectors[7],
        shares[1],
        vectors[8],
        shares[0],
        conv_shares[0],
        conv_shares[1],
        conv_shares[2][0],
    )


def solution(mesh):
    in_specs = (
        P("seq", "tok", None),
        P("seq", "tok", None, None),
        P("seq", None),
        P(),
        P(),
        P(),
        P(),
        P(),
        P(),
        P(),
        P(),
        P(),
        P(),
        P(),
        P(),
        P(),
        P(),
        P(),
        P(),
        P("seq", "tok", None, None),
    )
    out_specs = (
        P("seq", "tok", None, None),
        P("seq", "tok", None),
        P("seq", "tok", None, None),
        P("tok"),
        P("tok"),
        P("tok", None),
        P(None, "tok"),
        P("tok", None),
        P("tok"),
        P("tok"),
        P("tok"),
        P("tok", None),
        P("tok"),
        P("tok", None),
        P("tok"),
        P("tok", None),
        P(None, None, "tok"),
        P(None, None, "tok"),
        P(None, "tok"),
    )
    return jax.shard_map(local, mesh=mesh, in_specs=in_specs, out_specs=out_specs, check_vma=False)
```

```python
from functools import partial
import math

import jax
import jax.numpy as jnp
import numpy as np
from jax import lax
from jax.experimental import pallas as pl
from jax.experimental.pallas import tpu as pltpu
from jax.sharding import PartitionSpec as P

HEADS = 12
HEAD_DIM = 64


side_small = 4
side_big = 6
halo_rows = 43
key_reach = 215
norm_eps = 1e-05
far_below = -1e30
highest = lax.Precision.HIGHEST
in_part = {-1: (1, 2), 0: (0, 2), 1: (0, 1)}
out_part = {-1: (0, 1), 0: (0, 2), 1: (1, 2)}


def passed_along(block, axis, distance):
    devices = range(lax.axis_size(axis))
    route = [(i - distance, i) for i in devices if i - distance in devices]
    return lax.ppermute(block, axis, route)


def all_offsets():
    step_values = (-1, 0, 1)
    return [
        (step_x, step_y, step_z)
        for step_x in step_values
        for step_y in step_values
        for step_z in step_values
    ]


EDGE = 48
WINDOW = 256
TILE = 128
CROP_ROWS = 48
SUBS = 8
VMEM_LIMIT = 60 * 1024 * 1024
lowest_step = {-1: -43, 0: -7, 1: 11}
low_type = jnp.bfloat16
wide = jnp.float32


def dot(left, right):
    return jnp.dot(left, right, preferred_element_type=wide)


def three_terms(field):
    first = field.astype(low_type)
    rest = field - first.astype(wide)
    second = rest.astype(low_type)
    third = (rest - second.astype(wide)).astype(low_type)
    return (first, second, third)


def exact_dot(chosen, field):
    first, second, third = three_terms(field)
    return dot(chosen, first) + dot(chosen, second) + dot(chosen, third)


def sub_lanes(number, width):
    return slice(number * width, (number + 1) * width)


def all_taps():
    return [(x, y, z) for x in range(3) for y in range(3) for z in range(3)]


def forward_band(weight, band_ref):
    inner, outer = weight.shape[1:]
    band_ref[...] = jnp.zeros_like(band_ref)
    for tap_x, tap_y, tap_z in all_taps():
        for side in range(2):
            rows = sub_lanes(tap_y * 4 + tap_z + side, inner)
            lanes = sub_lanes(side, outer)
            band_ref[tap_x, rows, lanes] = weight[tap_x * 9 + tap_y * 3 + tap_z]


def backward_band(weight, band_ref):
    inner, outer = weight.shape[1:]
    band_ref[...] = jnp.zeros_like(band_ref)
    for tap_x, tap_y, tap_z in all_taps():
        for side in range(2):
            rows = sub_lanes(side, inner)
            lanes = sub_lanes(tap_y * 4 + tap_z + side, outer)
            band_ref[tap_x, rows, lanes] = weight[26 - (tap_x * 9 + tap_y * 3 + tap_z)]


def once(fill, *refs):
    @pl.when(pl.program_id(0) == 0)
    def _():
        fill(*refs)


def window_positions(step):
    return {-1: ((0, 1),), 0: ((1, 0), (2, 1)), 1: ((3, 0),)}[step]


def fill_windows(x_ref, place_ref, p_ref, rows, width):
    tile = min(rows, TILE)
    for base in range(0, rows, tile):
        own = slice(base, base + tile)
        for number, (step_x, step_y, step_z) in enumerate(all_offsets()):
            low = (EDGE + base + lowest_step[step_x]) // 16 * 16
            centre = (step_x, step_y, step_z) == (0, 0, 0)
            if not centre:
                lane = lax.broadcasted_iota(jnp.int32, (tile, WINDOW), 1) + low
                chosen = jnp.where(lane == place_ref[0, own, number : number + 1], 1.0, 0.0)
                chosen = chosen.astype(low_type)
            for x_to, x_from in window_positions(step_x):
                for y_to, y_from in window_positions(step_y):
                    z_to, z_from = window_positions(step_z)[0]
                    count = (2 if step_z == 0 else 1) * width
                    to = ((x_to * 4 + y_to) * 4 + z_to) * width
                    source = (x_from * 4 + y_from * 2 + z_from) * width
                    if centre:
                        got = x_ref[EDGE + base : EDGE + base + tile, source : source + count]
                    else:
                        got = dot(chosen, x_ref[low : low + WINDOW, source : source + count])
                    p_ref[own, to : to + count] = got.astype(low_type)


def window_conv(p_ref, band_ref, pair, width, product):
    first, second = pair
    total = None
    for tap in range(3):
        begin = ((first + tap) * 4 + second) * 4 * width
        term = product(p_ref[:, begin : begin + 12 * width], band_ref[tap])
        total = term if total is None else total + term
    return total


def all_pairs():
    return [(first, second) for first in range(2) for second in range(2)]


def add_grads(left_ref, p_ref, total_ref, width, channels):
    for tap_x in range(3):
        for tap_y in range(3):
            term = None
            for number, (first, second) in enumerate(all_pairs()):
                begin = ((first + tap_x) * 4 + second + tap_y) * 4 * channels
                left = left_ref[number * 2 * width : (number + 1) * 2 * width, :]
                part = dot(left, p_ref[:, begin : begin + 4 * channels])
                term = part if term is None else term + part
            total_ref[tap_x * 3 + tap_y] += term


def fold_grads(total_ref, grad_ref, width, channels):
    for tap_x in range(3):
        for tap_y in range(3):
            for tap_z in range(3):
                number = tap_x * 3 + tap_y
                here = total_ref[number, :width, sub_lanes(tap_z, channels)]
                there = total_ref[number, width:, sub_lanes(tap_z + 1, channels)]
                tap = 26 - (number * 3 + tap_z)
                for half in range(width // channels):
                    rows = slice(half * channels, (half + 1) * channels)
                    grad_ref[tap, half] = jnp.transpose(here[rows] + there[rows])


def fold_packed(total_ref, grad_ref, width, channels, shards, side_ref=None):
    blocks = []
    for tap in range(27):
        number, tap_z = divmod(26 - tap, 3)
        here = total_ref[number, :width, sub_lanes(tap_z, channels)]
        there = total_ref[number, width:, sub_lanes(tap_z + 1, channels)]
        both = here + there
        for half in range(width // channels):
            blocks.append(jnp.transpose(both[half * channels : (half + 1) * channels]))
    if side_ref is not None:
        for half in range(width // channels):
            blocks.append(jnp.transpose(side_ref[half * channels : (half + 1) * channels, :]))
    if len(blocks) % 2 == 1:
        blocks.append(jnp.zeros_like(blocks[0]))
    for pair in range(len(blocks) // 2):
        split = [b.reshape(shards, -1, channels) for b in blocks[2 * pair : 2 * pair + 2]]
        joined = jnp.concatenate(split, axis=1).astype(low_type)
        grad_ref[:, 16 * pair : 16 * pair + 16, :] = joined


def kernel_call(
    body, seqs, inputs, shared, outputs, summed, scratch, flops, away=(), landing=(), collective=None
):
    def row_spec(shape):
        return pl.BlockSpec((1,) + tuple(shape[1:]), lambda i: (i,) + (0,) * (len(shape) - 1))

    def whole_spec(shape):
        return pl.BlockSpec(
            tuple(shape), lambda i: (0,) * len(shape), pipeline_mode=pl.Buffered(1)
        )

    far_spec = pl.BlockSpec(memory_space=pl.ANY)
    moved = sum(math.prod(a.shape) * a.dtype.itemsize for a in list(inputs) + list(shared))
    moved += sum(math.prod(s) * jnp.dtype(t).itemsize for s, t in list(outputs) + list(summed))
    results = list(outputs) + list(summed) + list(landing)
    return pl.pallas_call(
        body,
        grid=(seqs,),
        in_specs=[row_spec(a.shape) for a in inputs]
        + [whole_spec(a.shape) for a in shared]
        + [far_spec] * len(away),
        out_specs=[row_spec(s) for s, _ in outputs]
        + [whole_spec(s) for s, _ in summed]
        + [far_spec] * len(landing),
        out_shape=[jax.ShapeDtypeStruct(s, t) for s, t in results],
        scratch_shapes=scratch,
        compiler_params=pltpu.CompilerParams(
            vmem_limit_bytes=VMEM_LIMIT,
            collective_id=collective,
            has_side_effects=collective is not None,
        ),
        cost_estimate=pl.CostEstimate(flops=flops, bytes_accessed=moved, transcendentals=0),
    )(*inputs, *shared, *away)


def tok_sides():
    tok, count = (lax.axis_index("tok"), lax.axis_size("tok"))
    return (tok > 0, tok < count - 1)


def greet():
    seq, tok, count = (lax.axis_index("seq"), lax.axis_index("tok"), lax.axis_size("tok"))
    barrier = pltpu.get_barrier_semaphore()
    for there, shift in zip(tok_sides(), (count - 1, 1)):

        @pl.when(there)
        def _():
            pl.semaphore_signal(
                barrier,
                inc=1,
                device_id=(seq, lax.rem(tok + shift, count)),
                device_id_type=pl.DeviceIdType.MESH,
            )


def met():
    tok, count = (lax.axis_index("tok"), lax.axis_size("tok"))
    peers = jnp.minimum(tok, 1) + jnp.minimum(count - 1 - tok, 1)
    pl.semaphore_wait(pltpu.get_barrier_semaphore(), peers)


class Edge:
    def __init__(self, low, high, left, right, send_sem, recv_sem):
        self.sources = (low, high)
        self.targets = (right, left)
        self.send_sem = send_sem
        self.recv_sem = recv_sem

    def copy(self, way):
        seq, tok, count = (lax.axis_index("seq"), lax.axis_index("tok"), lax.axis_size("tok"))
        shift = count - 1 if way == 0 else 1
        return pltpu.make_async_remote_copy(
            src_ref=self.sources[way],
            dst_ref=self.targets[way],
            send_sem=self.send_sem.at[way],
            recv_sem=self.recv_sem.at[way],
            device_id=(seq, lax.rem(tok + shift, count)),
            device_id_type=pl.DeviceIdType.MESH,
        )

    def start(self):
        for way, there in enumerate(tok_sides()):

            @pl.when(there)
            def _():
                self.copy(way).start()

    def land(self):
        for way, there in enumerate(tok_sides()):

            @pl.when(there)
            def _():
                self.copy(1 - way).wait_recv()

    def sent(self):
        for way, there in enumerate(tok_sides()):

            @pl.when(there)
            def _():
                self.copy(way).wait_send()


def edge_scratch(seqs, rows, lanes):
    return [
        pltpu.VMEM((seqs, rows, lanes), low_type),
        pltpu.VMEM((seqs, rows, lanes), low_type),
        pltpu.VMEM((rows, lanes), low_type),
        pltpu.SemaphoreType.DMA((seqs, 2)),
        pltpu.SemaphoreType.DMA((seqs, 2)),
        pltpu.SemaphoreType.DMA((seqs,)),
    ]


class Payload:
    def __init__(self, seqs, left, right, low_pay, high_pay, zero_ref, send_sem, recv_sem, zero_sem):
        self.seqs = seqs
        self.refs = (left, right, low_pay, high_pay, send_sem, recv_sem)
        self.zero_ref = zero_ref
        self.zero_sem = zero_sem
        self.step = pl.program_id(0)
        self.low = low_pay.at[pl.ds(self.step, 1)]
        self.high = high_pay.at[pl.ds(self.step, 1)]

    def edge(self, number):
        left, right, low, high, send_sem, recv_sem = (ref.at[number] for ref in self.refs)
        return Edge(low, high, left, right, send_sem, recv_sem)

    def enter(self):
        @pl.when(self.step == 0)
        def _():
            greet()
            self.zero_ref[...] = jnp.zeros_like(self.zero_ref)
            for field, there in zip(self.refs[:2], tok_sides()):

                @pl.when(jnp.logical_not(there))
                def _():
                    copies = [
                        pltpu.make_async_copy(self.zero_ref, field.at[n], self.zero_sem.at[n])
                        for n in range(self.seqs)
                    ]
                    for copy in copies:
                        copy.start()
                    for copy in copies:
                        copy.wait()

    def send(self, greeted=False, later=False):
        if not greeted:

            @pl.when(self.step == 0)
            def _():
                met()

        self.edge(self.step).start()
        if not later:
            self.close()

    def close(self):
        @pl.when(self.step == self.seqs - 1)
        def _():
            for number in range(self.seqs):
                self.edge(number).land()
            for number in range(self.seqs):
                self.edge(number).sent()


def conv_scratch(rows, width, band_shape):
    return [
        pltpu.VMEM((rows + 192, SUBS * width), low_type),
        pltpu.VMEM((rows, 64 * width), low_type),
        pltpu.VMEM((3,) + band_shape, low_type),
    ]


def conv_flops(seqs, rows, inner, outer):
    return 2 * seqs * rows * (36 * 4 * inner * 2 * outer + 56 * WINDOW * inner)


def put_edges(low_pay, high_pay, number, field, channels, rows):
    lanes = sub_lanes(number, channels)
    low_pay[0, :, lanes] = field[:EDGE].astype(low_type)
    high_pay[0, :, lanes] = field[rows - EDGE :].astype(low_type)


def put_sums(sums_ref, low_pay, high_pay, number, value, channels):
    lanes = sub_lanes(number, channels)
    sums_ref[0, :, lanes] = value
    pay_lanes = sub_lanes(SUBS + number, channels)
    low_pay[0, :, pay_lanes] = value.astype(low_type)
    high_pay[0, :, pay_lanes] = value.astype(low_type)


def taken_sums(sums_ref, left_pay, right_pay, number, channels):
    lanes = sub_lanes(number, channels)
    pay_lanes = sub_lanes(SUBS + number, channels)
    total = sums_ref[0, :, lanes] + left_pay[0, :, pay_lanes].astype(wide)
    return total + right_pay[0, :, pay_lanes].astype(wide)


def mean_and_scale(total, square, inverse):
    mean = total * inverse
    variance = jnp.maximum(square * inverse - mean * mean, 0.0)
    return (mean, lax.rsqrt(variance + norm_eps))


def silu_parts(value):
    gate = 1.0 / (1.0 + jnp.exp(-value))
    return (value * gate, gate * (1.0 + value * (1.0 - gate)))


def first_conv_kernel(rows, channels, seqs):
    width = 2 * channels

    def body(
        up, up_left, up_right, skip, skip_left, skip_right, place, crop_t, weight, side,
        first_out, side_out, sums, to_left, to_right, x_ref, p_ref, band_ref, *edge_refs,
    ):
        pay = Payload(seqs, to_left, to_right, *edge_refs)
        pay.enter()
        low_pay, high_pay = (pay.low, pay.high)
        once(forward_band, weight, band_ref)
        for number in range(SUBS):
            for half, (own, left, right) in enumerate(
                ((up, up_left, up_right), (skip, skip_left, skip_right))
            ):
                to = sub_lanes(2 * number + half, channels)
                lanes = sub_lanes(number, channels)
                x_ref[:EDGE, to] = left[0, :, lanes]
                x_ref[EDGE : EDGE + rows, to] = own[0, :, lanes]
                x_ref[EDGE + rows : 2 * EDGE + rows, to] = right[0, :, lanes]
        x_ref[2 * EDGE + rows :, :] = jnp.zeros((96, SUBS * width), low_type)
        fill_windows(x_ref, place, p_ref, rows, width)
        total = [jnp.zeros((rows, channels), wide) for _ in range(4)]
        for index, pair in enumerate(all_pairs()):
            result = window_conv(p_ref, band_ref, pair, width, dot)
            first_out[0, :, sub_lanes(index, width)] = result
            for half in range(2):
                number = 2 * index + half
                value = result[:, sub_lanes(half, channels)]
                put_edges(low_pay, high_pay, number, value, channels, rows)
                flat = dot(x_ref[EDGE : EDGE + rows, sub_lanes(number, width)], side[...])
                side_out[0, :, sub_lanes(number, channels)] = flat
                terms = (value, value * value, flat, flat * flat)
                total = [have + term for have, term in zip(total, terms)]
        for number in range(4):
            value = exact_dot(crop_t[0], total[number])
            put_sums(sums, low_pay, high_pay, number, value, channels)
        pay.send()

    return body


def second_conv_kernel(rows, channels, seqs):
    def body(
        first, left_pay, right_pay, own_sums, inverse, owner, place, crop_t, weight,
        second_out, stats, sums, to_left, to_right, x_ref, p_ref, band_ref, *edge_refs,
    ):
        pay = Payload(seqs, to_left, to_right, *edge_refs)
        pay.enter()
        low_pay, high_pay = (pay.low, pay.high)
        once(forward_band, weight, band_ref)
        taken = [taken_sums(own_sums, left_pay, right_pay, n, channels) for n in range(4)]
        mean, scale = mean_and_scale(taken[0], taken[1], inverse[0])
        side_mean, side_scale = mean_and_scale(taken[2], taken[3], inverse[0])
        for number, value in enumerate((mean, scale, side_mean, side_scale)):
            stats[0, :, sub_lanes(number, channels)] = value
        mean_rows = exact_dot(owner[0], mean)
        scale_rows = exact_dot(owner[0], scale)
        parts = (
            (left_pay, slice(0, EDGE)),
            (first, slice(EDGE, EDGE + rows)),
            (right_pay, slice(EDGE + rows, 2 * EDGE + rows)),
        )
        for number in range(SUBS):
            lanes = sub_lanes(number, channels)
            for field, place_rows in parts:
                normed = field[0, :, lanes].astype(wide) - mean_rows[place_rows]
                normed = normed * scale_rows[place_rows]
                x_ref[place_rows, lanes] = silu_parts(normed)[0].astype(low_type)
        x_ref[2 * EDGE + rows :, :] = jnp.zeros((96, SUBS * channels), low_type)
        fill_windows(x_ref, place, p_ref, rows, channels)
        total = [jnp.zeros((rows, channels), wide) for _ in range(2)]
        for index, pair in enumerate(all_pairs()):
            result = window_conv(p_ref, band_ref, pair, channels, dot)
            second_out[0, :, sub_lanes(index, 2 * channels)] = result
            for half in range(2):
                value = result[:, sub_lanes(half, channels)]
                put_edges(low_pay, high_pay, 2 * index + half, value, channels, rows)
                total = [total[0] + value, total[1] + value * value]
        for number in range(2):
            value = exact_dot(crop_t[0], total[number])
            put_sums(sums, low_pay, high_pay, number, value, channels)
        pay.send()

    return body


def output_kernel(rows, channels, seqs):
    def body(
        second, side_field, cotangent, stats, left_pay, right_pay, own_sums, inverse, owner, crop_t,
        section, grad_out, second_stats, sums, to_left, to_right, *edge_refs,
    ):
        pay = Payload(seqs, to_left, to_right, *edge_refs)
        pay.enter()
        low_pay, high_pay = (pay.low, pay.high)
        taken = [taken_sums(own_sums, left_pay, right_pay, n, channels) for n in range(2)]
        mean, scale = mean_and_scale(taken[0], taken[1], inverse[0])
        second_stats[0, :, sub_lanes(0, channels)] = mean
        second_stats[0, :, sub_lanes(1, channels)] = scale
        own = owner[0, EDGE : EDGE + rows, :]
        mean_rows = exact_dot(own, mean)
        scale_rows = exact_dot(own, scale)
        side_mean = exact_dot(own, stats[0, :, sub_lanes(2, channels)])
        side_scale = exact_dot(own, stats[0, :, sub_lanes(3, channels)])
        total = [jnp.zeros((rows, channels), wide) for _ in range(3)]
        for number in range(SUBS):
            lanes = sub_lanes(number, channels)
            normed = (second[0, :, lanes] - mean_rows) * scale_rows
            side = (side_field[0, :, lanes] - side_mean) * side_scale
            value, slope = silu_parts(normed + side)
            section[0, :, lanes] = value.astype(low_type)
            grad = cotangent[0, :, lanes].astype(wide) * slope
            grad_out[0, :, lanes] = grad
            put_edges(low_pay, high_pay, number, grad, channels, rows)
            terms = (grad, grad * normed, grad * side)
            total = [have + term for have, term in zip(total, terms)]
        for number in range(3):
            value = exact_dot(crop_t[0], total[number])
            put_sums(sums, low_pay, high_pay, number, value, channels)
        pay.send()

    return body


def second_back_kernel(rows, channels, seqs, shards):
    def body(
        grad, grad_left, grad_right, own_sums, second, second_left, second_right, side_field, first,
        stats, second_stats, inverse, owner, place, crop_t, weight,
        first_grad, side_grad, sums, weight_grad, to_left, to_right,
        x_ref, p_ref, band_ref, left_ref, total_ref, *edge_refs,
    ):
        pay = Payload(seqs, to_left, to_right, *edge_refs)
        pay.enter()
        low_pay, high_pay = (pay.low, pay.high)
        once(backward_band, weight, band_ref)
        means = [
            taken_sums(own_sums, grad_left, grad_right, n, channels) * inverse[0] for n in range(3)
        ]
        mean_rows = exact_dot(owner[0], second_stats[0, :, sub_lanes(0, channels)])
        scale_rows = exact_dot(owner[0], second_stats[0, :, sub_lanes(1, channels)])
        lead_rows = exact_dot(owner[0], means[0])
        slope_rows = exact_dot(owner[0], means[1])
        parts = (
            (grad_left, second_left, slice(0, EDGE)),
            (grad, second, slice(EDGE, EDGE + rows)),
            (grad_right, second_right, slice(EDGE + rows, 2 * EDGE + rows)),
        )
        own = slice(EDGE, EDGE + rows)
        side_mean = exact_dot(owner[0, own, :], stats[0, :, sub_lanes(2, channels)])
        side_scale = exact_dot(owner[0, own, :], stats[0, :, sub_lanes(3, channels)])
        side_slope = exact_dot(owner[0, own, :], means[2])
        first_mean = exact_dot(owner[0, own, :], stats[0, :, sub_lanes(0, channels)])
        first_scale = exact_dot(owner[0, own, :], stats[0, :, sub_lanes(1, channels)])
        for number in range(SUBS):
            lanes = sub_lanes(number, channels)
            for grad_from, field, at in parts:
                normed = (field[0, :, lanes].astype(wide) - mean_rows[at]) * scale_rows[at]
                pulled = grad_from[0, :, lanes].astype(wide) - lead_rows[at]
                pulled = scale_rows[at] * (pulled - normed * slope_rows[at])
                x_ref[at, lanes] = pulled.astype(low_type)
            side = (side_field[0, :, lanes] - side_mean) * side_scale
            pulled = side_scale * (grad[0, :, lanes] - lead_rows[own] - side * side_slope)
            side_grad[0, :, lanes] = pulled.astype(low_type)
            normed = (first[0, :, lanes] - first_mean) * first_scale
            hidden = silu_parts(normed)[0]
            left_ref[lanes, :] = jnp.transpose(hidden).astype(low_type)
        x_ref[2 * EDGE + rows :, :] = jnp.zeros((96, SUBS * channels), low_type)
        fill_windows(x_ref, place, p_ref, rows, channels)
        total = [jnp.zeros((rows, channels), wide) for _ in range(2)]
        for index, pair in enumerate(all_pairs()):
            result = window_conv(p_ref, band_ref, pair, channels, dot_t)
            for half in range(2):
                number = 2 * index + half
                lanes = sub_lanes(number, channels)
                normed = (first[0, :, lanes] - first_mean) * first_scale
                value = result[:, sub_lanes(half, channels)] * silu_parts(normed)[1]
                first_grad[0, :, lanes] = value
                put_edges(low_pay, high_pay, number, value, channels, rows)
                total = [total[0] + value, total[1] + value * normed]
        for number in range(2):
            value = exact_dot(crop_t[0], total[number])
            put_sums(sums, low_pay, high_pay, number, value, channels)
        pay.send(later=True)

        @pl.when(pl.program_id(0) == 0)
        def _():
            total_ref[...] = jnp.zeros_like(total_ref)

        add_grads(left_ref, p_ref, total_ref, channels, channels)

        @pl.when(pl.program_id(0) == seqs - 1)
        def _():
            if shards * 8 == channels:
                fold_packed(total_ref, weight_grad, channels, channels, shards)
            else:
                fold_grads(total_ref, weight_grad, channels, channels)

        pay.close()

    return body


def first_back_kernel(rows, channels, seqs, shards):
    width = 2 * channels

    def body(
        grad, grad_left, grad_right, own_sums, first, first_left, first_right, stats, inverse, owner,
        place, side_grad, up, skip, weight, side_weight,
        up_grad, skip_grad, weight_grad, side_weight_grad,
        x_ref, p_ref, band_ref, left_ref, total_ref,
    ):
        once(backward_band, weight, band_ref)
        means = [
            taken_sums(own_sums, grad_left, grad_right, n, channels) * inverse[0] for n in range(2)
        ]
        mean_rows = exact_dot(owner[0], stats[0, :, sub_lanes(0, channels)])
        scale_rows = exact_dot(owner[0], stats[0, :, sub_lanes(1, channels)])
        lead_rows = exact_dot(owner[0], means[0])
        slope_rows = exact_dot(owner[0], means[1])
        parts = (
            (grad_left, first_left, slice(0, EDGE)),
            (grad, first, slice(EDGE, EDGE + rows)),
            (grad_right, first_right, slice(EDGE + rows, 2 * EDGE + rows)),
        )
        for number in range(SUBS):
            lanes = sub_lanes(number, channels)
            for grad_from, field, at in parts:
                normed = (field[0, :, lanes].astype(wide) - mean_rows[at]) * scale_rows[at]
                pulled = grad_from[0, :, lanes].astype(wide) - lead_rows[at]
                pulled = scale_rows[at] * (pulled - normed * slope_rows[at])
                x_ref[at, lanes] = pulled.astype(low_type)
            for half, field in enumerate((up, skip)):
                turned = jnp.transpose(field[0, :, lanes].astype(wide)).astype(low_type)
                left_ref[sub_lanes(2 * number + half, channels), :] = turned
        x_ref[2 * EDGE + rows :, :] = jnp.zeros((96, SUBS * channels), low_type)
        fill_windows(x_ref, place, p_ref, rows, channels)
        for index, pair in enumerate(all_pairs()):
            result = window_conv(p_ref, band_ref, pair, channels, dot_t)
            for half in range(2):
                number = 2 * index + half
                lanes = sub_lanes(number, channels)
                value = result[:, sub_lanes(half, width)]
                value = value + dot_t(side_grad[0, :, lanes], side_weight[...])
                up_grad[0, :, lanes] = value[:, :channels].astype(low_type)
                skip_grad[0, :, lanes] = value[:, channels:]

        @pl.when(pl.program_id(0) == 0)
        def _():
            total_ref[...] = jnp.zeros_like(total_ref)
            side_weight_grad[...] = jnp.zeros_like(side_weight_grad)

        for number in range(SUBS):
            side_weight_grad[...] += dot(
                left_ref[sub_lanes(number, width), :], side_grad[0, :, sub_lanes(number, channels)]
            )
        add_grads(left_ref, p_ref, total_ref, width, channels)

        @pl.when(pl.program_id(0) == seqs - 1)
        def _():
            if shards * 8 == channels:
                fold_packed(total_ref, weight_grad, width, channels, shards, side_weight_grad)
            else:
                fold_grads(total_ref, weight_grad, width, channels)

    return body


def exchanged(low_pay, high_pay):
    return (passed_along(high_pay, "tok", 1), passed_along(low_pay, "tok", -1))


def with_far(sums, reaches):
    total = sums
    for distance in range(2, reaches + 1):
        for shift_by in (distance, -distance):
            total = total + passed_along(sums.astype(low_type), "tok", shift_by).astype(wide)
    return total


def conv_section(upsampled, skip, edges, cotangent, weights, geometry_in, reaches):
    conv1_weight, conv2_weight, conv3_weight = weights
    seqs, rows, lanes = upsampled.shape
    channels = lanes // SUBS
    width = 2 * channels
    place, owner, crop_t, inverse = geometry_in
    field = ((seqs, rows, lanes), wide)
    low_field = ((seqs, rows, lanes), low_type)

    def pay(count):
        return ((seqs, EDGE, (SUBS + count) * channels), low_type)

    def pay_scratch(count):
        return edge_scratch(seqs, EDGE, (SUBS + count) * channels)

    def table(count):
        return ((seqs, CROP_ROWS, count * channels), wide)

    up_left, up_right, skip_left, skip_right = edges
    shards = lax.axis_size("tok")
    fits = shards * 8 == channels

    def packed_out(blocks):
        return ((shards, (blocks + 1) // 2 * 16, channels), low_type)

    first, side_field, sums, first_left, first_right = kernel_call(
        first_conv_kernel(rows, channels, seqs),
        seqs,
        (upsampled, up_left, up_right, skip, skip_left, skip_right, place, crop_t),
        (conv1_weight, conv3_weight),
        (field, field, table(4)),
        (),
        conv_scratch(rows, width, (12 * width, 2 * channels)) + pay_scratch(4),
        conv_flops(seqs, rows, width, channels),
        landing=(pay(4), pay(4)),
        collective=3,
    )
    second, stats, sums, second_left, second_right = kernel_call(
        second_conv_kernel(rows, channels, seqs),
        seqs,
        (first, first_left, first_right, with_far(sums, reaches), inverse, owner, place, crop_t),
        (conv2_weight,),
        (field, table(4), table(2)),
        (),
        conv_scratch(rows, channels, (12 * channels, 2 * channels)) + pay_scratch(2),
        conv_flops(seqs, rows, channels, channels),
        landing=(pay(2), pay(2)),
        collective=4,
    )
    section_out, grad, second_stats, sums, grad_left, grad_right = kernel_call(
        output_kernel(rows, channels, seqs),
        seqs,
        (
            second, side_field, cotangent, stats, second_left, second_right,
            with_far(sums, reaches), inverse, owner, crop_t,
        ),
        (),
        (low_field, field, table(2), table(3)),
        (),
        pay_scratch(3),
        seqs * rows * lanes * 20,
        landing=(pay(3), pay(3)),
        collective=5,
    )
    first_grad, side_grad, sums, conv2_grad, back_left, back_right = kernel_call(
        second_back_kernel(rows, channels, seqs, shards),
        seqs,
        (
            grad, grad_left, grad_right, with_far(sums, reaches), second, second_left, second_right,
            side_field, first, stats, second_stats, inverse, owner, place, crop_t,
        ),
        (conv2_weight,),
        (field, low_field, table(2)),
        (packed_out(27) if fits else ((27, 1, channels, channels), wide),),
        conv_scratch(rows, channels, (2 * channels, 12 * channels))
        + [
            pltpu.VMEM((SUBS * channels, rows), low_type),
            pltpu.VMEM((9, 2 * channels, 4 * channels), wide),
        ]
        + pay_scratch(2),
        2 * conv_flops(seqs, rows, channels, channels),
        landing=(pay(2), pay(2)),
        collective=6,
    )
    up_grad, skip_grad, conv1_grad, conv3_grad = kernel_call(
        first_back_kernel(rows, channels, seqs, shards),
        seqs,
        (
            first_grad, back_left, back_right, with_far(sums, reaches), first, first_left,
            first_right, stats, inverse, owner, place, side_grad, upsampled, skip,
        ),
        (conv1_weight, conv3_weight),
        (low_field, field),
        (
            packed_out(56) if fits else ((27, 2, channels, channels), wide),
            ((width, channels), wide),
        ),
        conv_scratch(rows, channels, (2 * width, 12 * channels))
        + [
            pltpu.VMEM((SUBS * width, rows), low_type),
            pltpu.VMEM((9, 2 * width, 4 * channels), wide),
        ],
        2 * conv_flops(seqs, rows, channels, width),
    )
    return (section_out, up_grad, skip_grad, conv1_grad, conv2_grad, conv3_grad)


PIECE_BYTES = 2400 * 1024


def bit_count(size):
    return size.bit_length() - 1


def pieces_of(shapes):
    pieces = []
    for index, (shards, rows, lanes) in enumerate(shapes):
        parts = max(1, round(shards * rows * lanes * 2 / PIECE_BYTES))
        while rows % (16 * parts) != 0 and parts > 1:
            parts -= 1
        take = rows // parts
        pieces.extend((index, part * take, take, lanes) for part in range(parts))
    return pieces


def all_of(count):
    return (slice(None),) * count


def reduce_kernel(pieces, arrays, tok_bits, seq_bits):
    phases = tok_bits + seq_bits
    mesh_id = pl.DeviceIdType.MESH

    def body(*refs):
        given = refs[:arrays]
        results = refs[arrays : 2 * arrays]
        count = len(pieces)
        rest = refs[2 * arrays :]
        kept = rest[:count]
        landed = [rest[count + i * phases : count + (i + 1) * phases] for i in range(count)]
        local_sem, send_sem, recv_sem = rest[count + count * phases :]
        tok = lax.axis_index("tok")
        seq = lax.axis_index("seq")

        def bit_of(phase):
            if phase < tok_bits:
                return (tok // (1 << phase)) % 2
            return (seq // (1 << (phase - tok_bits))) % 2

        def partner(phase):
            bit = bit_of(phase)
            if phase < tok_bits:
                return (seq, tok + (1 << phase) * (1 - 2 * bit))
            return (seq + (1 << (phase - tok_bits)) * (1 - 2 * bit), tok)

        barrier = pltpu.get_barrier_semaphore()
        for phase in range(phases):
            pl.semaphore_signal(barrier, inc=1, device_id=partner(phase), device_id_type=mesh_id)
        pl.semaphore_wait(barrier, phases)

        def local_copy(piece):
            index, begin, take, _ = pieces[piece]
            view = given[index].at[all_of(tok_bits - 1) + (bit_of(0), pl.ds(begin, take))]
            return pltpu.make_async_copy(view, kept[piece], local_sem.at[piece])

        def remote_copy(piece, phase):
            index, begin, take, _ = pieces[piece]
            if phase == 0:
                view = given[index].at[all_of(tok_bits - 1) + (1 - bit_of(0), pl.ds(begin, take))]
            elif phase < tok_bits:
                view = landed[piece][phase - 1].at[all_of(tok_bits - 1 - phase) + (1 - bit_of(phase),)]
            else:
                view = landed[piece][phase - 1]
            return pltpu.make_async_remote_copy(
                src_ref=view,
                dst_ref=landed[piece][phase],
                send_sem=send_sem.at[piece, phase],
                recv_sem=recv_sem.at[piece, phase],
                device_id=partner(phase),
                device_id_type=mesh_id,
            )

        def begin(piece):
            remote_copy(piece, 0).start()
            local_copy(piece).start()

        def finish(piece, phase):
            index, first, take, _ = pieces[piece]
            remote_copy(piece, phase).wait_recv()
            got = landed[piece][phase]
            if phase == 0:
                local_copy(piece).wait()

            if phase < tok_bits:
                kept_bits = tok_bits - 1 - phase

                def step(block, carry):
                    at = tuple((block // (1 << bit)) % 2 for bit in reversed(range(kept_bits)))
                    if phase == 0:
                        mine = kept[piece][at]
                    else:
                        mine = landed[piece][phase - 1][at + (bit_of(phase),)]
                    got[at] = got[at] + mine
                    return carry

                lax.fori_loop(0, 1 << kept_bits, step, 0)
            elif phase + 1 < phases:
                got[...] = got[...] + landed[piece][phase - 1][...]
            if phase + 1 < phases:
                remote_copy(piece, phase + 1).start()
            else:
                total = got[...].astype(wide) + landed[piece][phase - 1][...].astype(wide)
                results[index][pl.ds(first, take), :] = total

        begin(0)
        for step in range(count + phases - 1):
            if step + 1 < count:
                begin(step + 1)
            for phase in range(phases):
                if 0 <= step - phase < count:
                    finish(step - phase, phase)
        for piece in range(count):
            for phase in range(phases):
                remote_copy(piece, phase).wait_send()

    return body


def reduced(grads):
    shards = lax.axis_size("tok")
    tok_bits = bit_count(shards)
    seq_bits = bit_count(lax.axis_size("seq"))
    shapes = [g.shape for g in grads]
    pieces = pieces_of(shapes)
    scratch = [
        pltpu.VMEM((2,) * (tok_bits - 1) + (take, lanes), low_type) for _, _, take, lanes in pieces
    ]
    for _, _, take, lanes in pieces:
        for phase in range(tok_bits - 1):
            bits = tok_bits - 1 - phase
            scratch.append(pltpu.VMEM((2,) * bits + (take, lanes), low_type))
        scratch += [pltpu.VMEM((take, lanes), low_type) for _ in range(1 + seq_bits)]
    count, phases = len(pieces), tok_bits + seq_bits
    scratch += [
        pltpu.SemaphoreType.DMA((count,)),
        pltpu.SemaphoreType.DMA((count, phases)),
        pltpu.SemaphoreType.DMA((count, phases)),
    ]
    total = sum(math.prod(s) for s in shapes)
    return pl.pallas_call(
        reduce_kernel(pieces, len(grads), tok_bits, seq_bits),
        in_specs=[pl.BlockSpec(memory_space=pl.ANY)] * len(grads),
        out_specs=[pl.BlockSpec(memory_space=pltpu.VMEM)] * len(grads),
        out_shape=[jax.ShapeDtypeStruct(s[1:], wide) for s in shapes],
        scratch_shapes=scratch,
        compiler_params=pltpu.CompilerParams(
            vmem_limit_bytes=VMEM_LIMIT, collective_id=0, has_side_effects=True
        ),
        cost_estimate=pl.CostEstimate(flops=total, bytes_accessed=4 * total, transcendentals=0),
    )(*[g.reshape((2,) * tok_bits + g.shape[1:]) for g in grads])


def sharded_rows(grad):
    shards = lax.axis_size("tok")
    rows = grad.shape[0] // shards
    grad = grad.astype(low_type)
    if rows % 16 == 0:
        return grad.reshape(shards, rows, grad.shape[1])
    return grad.reshape(shards, rows * grad.shape[1] // 128, 128)


def conv_rows(turned):
    shards = lax.axis_size("tok")
    taps, halves, channels, lanes = turned.shape
    split = turned.reshape(taps, halves, shards, channels // shards, lanes)
    return jnp.moveaxis(split, 2, 0).reshape(shards, -1, lanes)


def conv_share(rows, taps, halves):
    split = rows.reshape(taps, halves, -1, rows.shape[-1])
    return jnp.moveaxis(split, 2, 3).reshape(taps, halves * rows.shape[-1], -1)


def reduced_all(conv_grads, matrices, vectors):
    shards = lax.axis_size("tok")
    parts = [conv_rows(g) for g in conv_grads]
    flat = jnp.concatenate([v.reshape(shards, -1) for v in vectors], axis=1)
    used = flat.shape[1]
    taken = sum(p.shape[1] for p in parts)
    rows = -(-used // 128)
    rows += -(rows + taken) % 16
    flat = jnp.pad(flat, ((0, 0), (0, rows * 128 - used))).reshape(shards, rows, 128)
    packed = jnp.concatenate([p.astype(low_type) for p in parts] + [flat.astype(low_type)], axis=1)
    results = reduced([packed] + [sharded_rows(m) for m in matrices])
    shares = []
    cursor = 0
    for part, grad in zip(parts, conv_grads):
        rows_here = results[0][cursor : cursor + part.shape[1]]
        shares.append(conv_share(rows_here, grad.shape[0], grad.shape[1]))
        cursor += part.shape[1]
    flat = results[0][cursor:].reshape(-1)
    cursor = 0
    pieces = []
    for vector in vectors:
        size = vector.size // shards
        pieces.append(flat[cursor : cursor + size])
        cursor += size
    whole = [r.reshape(-1, m.shape[1]) for r, m in zip(results[1:], matrices)]
    return (shares, whole, pieces)


REACH = 224
QUERY_TILE = 128
CLOSING_LIMIT = 63 * 1024 * 1024


def dot_t(left, right):
    return lax.dot_general(
        left, right, (((1,), (1,)), ((), ())), preferred_element_type=wide
    )


def counted(shape, axis):
    return lax.broadcasted_iota(jnp.int32, shape, axis).astype(wide)


def geometry_kernel(rows, crops):
    reach_rows = rows + 2 * REACH
    tile = min(rows, QUERY_TILE)
    window = tile + 2 * REACH

    def body(side_row, side_column, place, owner, crop_t, inverse, bias, edge_bias):
        first_row = (lax.axis_index("tok") * rows).astype(wide)
        sides_r = side_row[0].astype(wide)
        sides_c = side_column[0].astype(wide)
        volume_r = sides_r * sides_r * sides_r
        volume_c = sides_c * sides_c * sides_c
        shape = (crops, crops)
        start_r = jnp.sum(
            jnp.where(counted(shape, 0) < counted(shape, 1), volume_c, 0.0), axis=0, keepdims=True
        )
        start_c = jnp.sum(
            jnp.where(counted(shape, 1) < counted(shape, 0), volume_r, 0.0), axis=1, keepdims=True
        )

        def inside_of(length, begin):
            at = counted((length, crops), 0) + begin
            return ((at >= start_r) & (at < start_r + volume_r), at)

        wide_inside, _ = inside_of(rows + 2 * EDGE, first_row - EDGE)
        owner[0] = jnp.where(wide_inside, 1.0, 0.0).astype(low_type)
        inside, _ = inside_of(rows, first_row)
        side = jnp.sum(jnp.where(inside, sides_r, 0.0), axis=1, keepdims=True)
        first = jnp.sum(jnp.where(inside, start_r, 0.0), axis=1, keepdims=True)
        own = counted((rows, 1), 0)
        offset = own + first_row - first
        safe = jnp.maximum(side, 1.0)
        row_pos = jnp.floor((offset + 0.5) / (safe * safe))
        offset = offset - row_pos * safe * safe
        column = jnp.floor((offset + 0.5) / safe)
        depth_pos = offset - column * safe
        lane = counted((1, 32), 1)
        step_x = jnp.floor((lane + 0.5) / 9.0)
        step_y = jnp.floor((lane - 9.0 * step_x + 0.5) / 3.0)
        step_z = lane - 9.0 * step_x - 3.0 * step_y - 1.0
        step_x, step_y = (step_x - 1.0, step_y - 1.0)
        valid = None
        for at, step in ((row_pos, step_x), (column, step_y), (depth_pos, step_z)):
            moved = at + step
            here = (moved >= 0.0) & (moved < side)
            valid = here if valid is None else valid & here
        target = own + EDGE + (step_x * safe + step_y) * safe + step_z
        place[0] = jnp.where(valid, target, -1.0).astype(jnp.int32)
        at = counted((crops, rows), 1) + first_row
        inside_t = (at >= start_c) & (at < start_c + volume_c)
        crop_t[0] = jnp.where(inside_t, 1.0, 0.0).astype(low_type)
        inverse[0] = jnp.broadcast_to(1.0 / jnp.maximum(8.0 * volume_c, 1.0), (crops, 128))
        key_inside, _ = inside_of(reach_rows, first_row - REACH)
        key_first = jnp.sum(jnp.where(key_inside, start_r + 1.0, 0.0), axis=1, keepdims=True)
        query_first = jnp.sum(jnp.where(inside_t, start_c + 1.0, 0.0), axis=0, keepdims=True)
        for number in range(rows // tile):
            base = number * tile
            same = key_first[base : base + window] == query_first[:, base : base + tile]
            bias[0, number] = jnp.where(same, 0.0, far_below)
        for side in range(2):
            begin_row = 0 if side == 0 else max(rows - REACH, 0)
            begin = first_row - REACH if side == 0 else first_row + rows
            at = counted((crops, REACH), 1) + begin
            inside_t = (at >= start_c) & (at < start_c + volume_c)
            query_first = jnp.sum(jnp.where(inside_t, start_c + 1.0, 0.0), axis=0, keepdims=True)
            same = key_first[REACH + begin_row : 2 * REACH + begin_row] == query_first
            edge_bias[0, side] = jnp.where(same, 0.0, far_below)

    return body


def geometry_tables(crop_sides, rows):
    seqs, crops = crop_sides.shape
    sides = jnp.pad(crop_sides, ((0, 0), (0, CROP_ROWS - crops)))
    tile = min(rows, QUERY_TILE)
    return kernel_call(
        geometry_kernel(rows, CROP_ROWS),
        seqs,
        (sides[:, None, :], sides[:, :, None]),
        (),
        (
            ((seqs, rows, 32), jnp.int32),
            ((seqs, rows + 2 * EDGE, CROP_ROWS), low_type),
            ((seqs, CROP_ROWS, rows), low_type),
            ((seqs, CROP_ROWS, 128), wide),
            ((seqs, rows // tile, tile + 2 * REACH, tile), wide),
            ((seqs, 2, REACH, REACH), wide),
        ),
        (),
        [],
        0,
    )


def row_of(vector, lanes=slice(None)):
    return vector[lanes].reshape(1, -1)


def normed_rows(values):
    centered = values - jnp.mean(values, axis=-1, keepdims=True)
    variance = jnp.mean(centered * centered, axis=-1, keepdims=True)
    scale = lax.rsqrt(variance + norm_eps)
    return (centered * scale, scale)


def norm_pull(grad, normed, scale, gain):
    inner = grad * gain
    first = jnp.mean(inner, axis=-1, keepdims=True)
    second = jnp.mean(inner * normed, axis=-1, keepdims=True)
    return scale * (inner - first - normed * second)


def gelu_parts(value):
    size = jnp.abs(value) * math.sqrt(0.5)
    ratio = 1.0 / (1.0 + 0.3275911 * size)
    series = 1.061405429
    for term in (-1.453152027, 1.421413741, -0.284496736, 0.254829592):
        series = series * ratio + term
    decay = jnp.exp(-size * size)
    beyond = 0.5 * series * ratio * decay
    cumulative = jnp.where(value >= 0.0, 1.0 - beyond, beyond)
    return (value * cumulative, cumulative + value * decay * (1.0 / math.sqrt(2.0 * math.pi)))


def head_lanes(block, half):
    lane = lax.broadcasted_iota(jnp.int32, block.shape, 1)
    chosen = lane < HEAD_DIM if half == 0 else lane >= HEAD_DIM
    return jnp.where(chosen, block, jnp.zeros_like(block))


def turned(block):
    return jnp.transpose(block.astype(wide))


def forward_kernel(rows, model_width, hidden, seqs, near_given):
    tile = min(rows, QUERY_TILE)
    window = tile + 2 * REACH
    chunk = 768
    scale = 1.0 / math.sqrt(HEAD_DIM)

    def body(*refs):
        tokens, bias = refs[:2]
        if near_given:
            left, right = refs[2:4]
            refs = refs[2:]
        (
            ln1_gain, ln1_bias, qkv_weight, qv_bias, out_bias, ln2_gain, ln2_bias,
            fc1_bias, fc2_bias, all_tokens, skip, out_away, fc1_away, fc2_away, deconv_away,
            normed_out, queries, keys, values, attended, log_totals, resid_out, second_out,
            act_out, slope_out, resid_low, upsampled, up_left, up_right, skip_left, skip_right,
            near_ref, turned_ref, skip_send, skip_recv, near_left, near_right, near_send, near_recv,
            out_weight, fc1_weight, fc2_weight, deconv_weight, weight_sem, *edge_refs,
        ) = refs[2:]
        step = pl.program_id(0)
        pay = Payload(seqs, up_left, up_right, *edge_refs)
        skip_edge = Edge(
            skip.at[:, :EDGE],
            skip.at[:, rows - EDGE :],
            skip_left,
            skip_right,
            skip_send,
            skip_recv,
        )

        def token_edge(number):
            return Edge(
                all_tokens.at[number, :REACH],
                all_tokens.at[number, rows - REACH :],
                near_left.at[number],
                near_right.at[number],
                near_send.at[number],
                near_recv.at[number],
            )

        weight_copies = [
            pltpu.make_async_copy(source, target, weight_sem.at[number])
            for number, (source, target) in enumerate(
                (
                    (out_away, out_weight),
                    (fc1_away, fc1_weight),
                    (fc2_away, fc2_weight),
                    (deconv_away, deconv_weight),
                )
            )
        ]

        def weights_ready(*numbers):
            @pl.when(step == 0)
            def _():
                for number in numbers:
                    weight_copies[number].wait()

        @pl.when(step == 0)
        def _():
            for copy in weight_copies:
                copy.start()

        pay.enter()

        @pl.when(step == 0)
        def _():
            met()
            if near_given:
                skip_edge.start()
            else:
                token_edge(0).start()
                for field, there in zip((near_left, near_right), tok_sides()):

                    @pl.when(jnp.logical_not(there))
                    def _():
                        field[...] = jnp.zeros_like(field)

            for field, there in zip((skip_left, skip_right), tok_sides()):

                @pl.when(jnp.logical_not(there))
                def _():
                    copies = [
                        pltpu.make_async_copy(pay.zero_ref, field.at[n], pay.zero_sem.at[n])
                        for n in range(seqs)
                    ]
                    for copy in copies:
                        copy.start()
                    for copy in copies:
                        copy.wait()

        def put_normed(values, begin):
            normed = normed_rows(values.astype(wide))[0] * row_of(ln1_gain) + row_of(ln1_bias)
            near_ref[begin : begin + values.shape[0], :] = normed.astype(low_type)

        def project(at):
            for number, target in enumerate((queries, keys, values)):
                lanes = sub_lanes(number, model_width)
                found = dot(near_ref[at, :], qkv_weight[:, lanes])
                if number != 1:
                    found = found + qv_bias[number // 2 : number // 2 + 1, :]
                target[0, at, :] = found.astype(low_type)

        own_rows = slice(REACH, REACH + rows)
        put_normed(tokens[0], REACH)
        normed_out[0] = near_ref[own_rows, :]
        project(own_rows)
        if near_given:
            put_normed(left[0], 0)
            put_normed(right[0], REACH + rows)
        else:
            token_edge(step).land()

            @pl.when(step < seqs - 1)
            def _():
                token_edge(step + 1).start()

            @pl.when(step == seqs - 1)
            def _():
                skip_edge.start()

            put_normed(near_left[step], 0)
            put_normed(near_right[step], REACH + rows)
        project(slice(0, REACH))
        project(slice(REACH + rows, 2 * REACH + rows))
        for pair in range(model_width // 128):
            lanes = sub_lanes(pair, 128)
            turned_ref[lanes, :] = turned(values[0, :, lanes]).astype(low_type)
        for number in range(rows // tile):
            base = number * tile
            at = slice(base, base + tile)
            near = slice(base, base + window)
            for pair in range(model_width // 128):
                lanes = sub_lanes(pair, 128)
                query = queries[0, REACH + base : REACH + base + tile, lanes] * scale
                key = keys[0, near, lanes]
                halves = []
                for half in range(2):
                    head = 2 * pair + half
                    scores = dot_t(key, head_lanes(query, half)) + bias[0, number]
                    top = jnp.max(scores, axis=0, keepdims=True)
                    weights = jnp.exp(scores - top)
                    total = jnp.sum(weights, axis=0, keepdims=True)
                    log_totals[0, head : head + 1, at] = top + jnp.log(total)
                    probs = (weights * (1.0 / total)).astype(low_type)
                    value = turned_ref[head * HEAD_DIM : (head + 1) * HEAD_DIM, near]
                    halves.append(dot(value, probs))
                both = jnp.concatenate(halves, axis=0)
                attended[0, at, lanes] = jnp.transpose(both).astype(low_type)
        weights_ready(0)
        resid = tokens[0].astype(wide) + dot(attended[0], out_weight[...]) + row_of(out_bias)
        resid_out[0] = resid
        second = normed_rows(resid)[0] * row_of(ln2_gain) + row_of(ln2_bias)
        second_out[0] = second.astype(low_type)
        weights_ready(1, 2, 3)
        total = resid + row_of(fc2_bias)
        for number in range(hidden // chunk):
            lanes = sub_lanes(number, chunk)
            pre = dot(second_out[0], fc1_weight[:, lanes]) + row_of(fc1_bias, lanes)
            act, slope = gelu_parts(pre)
            act_out[0, :, lanes] = act.astype(low_type)
            slope_out[0, :, lanes] = slope.astype(low_type)
            total = total + dot(act_out[0, :, lanes], fc2_weight[lanes, :])
        resid_low[0] = total.astype(low_type)
        upsampled[0] = dot(resid_low[0], deconv_weight[...]).astype(low_type)
        pay.low[0] = upsampled[0, :EDGE, :]
        pay.high[0] = upsampled[0, rows - EDGE :, :]
        pay.send(True)

        @pl.when(step == seqs - 1)
        def _():
            skip_edge.land()
            skip_edge.sent()
            if not near_given:
                for number in range(seqs):
                    token_edge(number).sent()

    return body


def hidden_back_kernel(rows, model_width, hidden, seqs, linked):
    chunk = 768

    def body(
        up_grad, slope, resid, attended, log_totals,
        deconv_weight, fc2_weight, fc1_weight, out_weight, ln2_gain,
        branch_out, pre_out, resid_grad, mixed_out, pulled_out, stats,
        fc2_sum, fc1_sum, out_sum, gain_sum, shift_sum, *edge_refs,
    ):
        step = pl.program_id(0)
        if linked:
            (
                pulls_left, pulls_right, stats_left, stats_right, pull_keep, stat_keep,
                zero_pull, zero_stat, pull_send, pull_recv, stat_send, stat_recv, zero_sem,
            ) = edge_refs

        def edges(number):
            pull = Edge(
                pull_keep.at[number, :REACH],
                pull_keep.at[number, rows - REACH :],
                pulls_left.at[number],
                pulls_right.at[number],
                pull_send.at[number],
                pull_recv.at[number],
            )
            stat = Edge(
                stat_keep.at[number],
                stat_keep.at[number],
                stats_left.at[number],
                stats_right.at[number],
                stat_send.at[number],
                stat_recv.at[number],
            )
            return (pull, stat)

        if linked:

            @pl.when(step == 0)
            def _():
                greet()
                zero_pull[...] = jnp.zeros_like(zero_pull)
                zero_stat[...] = jnp.zeros_like(zero_stat)
                fields = ((pulls_left, stats_left), (pulls_right, stats_right))
                for (pull, stat), there in zip(fields, tok_sides()):

                    @pl.when(jnp.logical_not(there))
                    def _():
                        copies = []
                        for n in range(seqs):
                            copies += [
                                pltpu.make_async_copy(zero_pull, pull.at[n], zero_sem.at[0, n]),
                                pltpu.make_async_copy(zero_stat, stat.at[n], zero_sem.at[1, n]),
                            ]
                        for copy in copies:
                            copy.start()
                        for copy in copies:
                            copy.wait()

        @pl.when(pl.program_id(0) == 0)
        def _():
            for ref in (fc2_sum, fc1_sum, out_sum, gain_sum, shift_sum):
                ref[...] = jnp.zeros_like(ref)

        def column_sum(field):
            return jnp.sum(field, axis=0, keepdims=True)

        incoming = dot_t(up_grad[0], deconv_weight[...])
        branch = incoming.astype(low_type)
        branch_out[0] = branch
        fc2_sum[...] += column_sum(branch.astype(wide))
        total = None
        for number in range(hidden // chunk):
            lanes = sub_lanes(number, chunk)
            act_grad = dot_t(branch_out[0], fc2_weight[lanes, :])
            pre = (act_grad * slope[0, :, lanes].astype(wide)).astype(low_type)
            pre_out[0, :, lanes] = pre
            fc1_sum[:, lanes] += column_sum(pre.astype(wide))
            term = dot_t(pre_out[0, :, lanes], fc1_weight[:, lanes])
            total = term if total is None else total + term
        normed, norm_scale = normed_rows(resid[0])
        gain_sum[...] += column_sum(total * normed)
        shift_sum[...] += column_sum(total)
        mixed = incoming + norm_pull(total, normed, norm_scale, row_of(ln2_gain))
        resid_grad[0] = mixed
        mixed = mixed.astype(low_type)
        mixed_out[0] = mixed
        out_sum[...] += column_sum(mixed.astype(wide))
        pulled = dot_t(mixed_out[0], out_weight[...]).astype(low_type)
        pulled_out[0] = pulled
        product = pulled.astype(wide) * attended[0].astype(wide)
        lane = lax.broadcasted_iota(jnp.int32, (16, model_width), 1)
        begin = lax.broadcasted_iota(jnp.int32, (16, model_width), 0) * HEAD_DIM
        chosen = (lane >= begin) & (lane < begin + HEAD_DIM)
        chosen = jnp.where(chosen, 1.0, 0.0).astype(low_type)
        inner = None
        for term in three_terms(product):
            part = dot_t(chosen, term)
            inner = part if inner is None else inner + part
        for pair in range(model_width // 128):
            heads = slice(2 * pair, 2 * pair + 2)
            unused = jnp.zeros((4, rows), wide)
            stats[0, pair] = jnp.concatenate([log_totals[0, heads], inner[heads], unused], axis=0)
        if linked:
            pull_keep[step] = pulled
            stat_keep[step] = stats[0]

            @pl.when(step == 0)
            def _():
                met()

            for edge in edges(step):
                edge.start()

            @pl.when(step == seqs - 1)
            def _():
                for number in range(seqs):
                    for edge in edges(number):
                        edge.land()
                for number in range(seqs):
                    for edge in edges(number):
                        edge.sent()

    return body


def attention_back_kernel(rows, model_width):
    tile = min(rows, QUERY_TILE)
    window = tile + 2 * REACH
    scale = 1.0 / math.sqrt(HEAD_DIM)

    def body(
        queries, keys, values, pulls, stats, bias,
        query_grad, key_own, value_own, low_pay, high_pay, near_key, near_value, turned_ref,
    ):
        for pair in range(model_width // 128):
            lanes = sub_lanes(pair, 128)
            turned_ref[lanes, :] = turned(keys[0, :, lanes]).astype(low_type)
        near_key[...] = jnp.zeros_like(near_key)
        near_value[...] = jnp.zeros_like(near_value)
        for number in range(rows // tile):
            base = number * tile
            at = slice(base, base + tile)
            near = slice(base, base + window)
            for pair in range(model_width // 128):
                lanes = sub_lanes(pair, 128)
                query = queries[0, REACH + base : REACH + base + tile, lanes] * scale
                key = keys[0, near, lanes]
                value = values[0, near, lanes]
                halves = []
                for half in range(2):
                    head = 2 * pair + half
                    probs, score_grad, one_query, one_pull = head_unit(
                        key, value, query, pulls[0, at, lanes], bias[0, number],
                        stats[0, pair, half : half + 1, at], stats[0, pair, 2 + half : 3 + half, at],
                        half,
                    )
                    near_key[near, lanes] += dot(score_grad, one_query)
                    near_value[near, lanes] += dot(probs, one_pull)
                    key_turned = turned_ref[head * HEAD_DIM : (head + 1) * HEAD_DIM, near]
                    halves.append(dot(key_turned, score_grad) * scale)
                both = jnp.concatenate(halves, axis=0)
                query_grad[0, at, lanes] = jnp.transpose(both).astype(low_type)
        for field, own_out, begin in (
            (near_key, key_own, 0),
            (near_value, value_own, model_width),
        ):
            lanes = slice(begin, begin + model_width)
            own_out[0] = field[REACH : REACH + rows, :]
            low_pay[0, :, lanes] = field[:REACH, :].astype(low_type)
            high_pay[0, :, lanes] = field[REACH + rows :, :].astype(low_type)

    return body


def token_kernel(rows, model_width):
    def body(
        tokens, resid_grad, query_grad, key_own, value_own, qkv_weight, ln1_gain,
        grad_out, token_grad, bias_sum, gain_sum, shift_sum,
    ):
        @pl.when(pl.program_id(0) == 0)
        def _():
            for ref in (bias_sum, gain_sum, shift_sum):
                ref[...] = jnp.zeros_like(ref)

        grad_out[0, :, :model_width] = query_grad[0]
        for number, own in enumerate((key_own, value_own)):
            to = sub_lanes(number + 1, model_width)
            grad_out[0, :, to] = own[0].astype(low_type)
        bias_sum[...] += jnp.sum(grad_out[0].astype(wide), axis=0, keepdims=True)
        total = dot_t(grad_out[0], qkv_weight[...])
        normed, norm_scale = normed_rows(tokens[0].astype(wide))
        gain_sum[...] += jnp.sum(total * normed, axis=0, keepdims=True)
        shift_sum[...] += jnp.sum(total, axis=0, keepdims=True)
        token_grad[0] = resid_grad[0] + norm_pull(total, normed, norm_scale, row_of(ln1_gain))

    return body


def near_rows(field):
    rows = field.shape[1]
    lefts, rights = ([], [])
    distance, missing = (1, REACH)
    while missing > 0:
        take = min(rows, missing)
        lefts.insert(0, passed_along(field[:, rows - take :], "tok", distance))
        rights.append(passed_along(field[:, :take], "tok", -distance))
        distance, missing = (distance + 1, missing - take)
    if len(lefts) == 1:
        return (lefts[0], rights[0])
    return (jnp.concatenate(lefts, axis=1), jnp.concatenate(rights, axis=1))


def returned_rows(own, low_pay, high_pay):
    rows = own.shape[1]
    distance, missing = (1, REACH)
    while missing > 0:
        take = min(rows, missing)
        low_piece = low_pay[:, missing - take : missing]
        begin = REACH - missing
        high_piece = high_pay[:, begin : begin + take]
        own = own.at[:, rows - take :].add(passed_along(low_piece, "tok", -distance).astype(wide))
        own = own.at[:, :take].add(passed_along(high_piece, "tok", distance).astype(wide))
        distance, missing = (distance + 1, missing - take)
    return own


def head_unit(key, value, query, pulled, bias, log_total, inner, half):
    one_query = head_lanes(query, half)
    one_pull = head_lanes(pulled, half)
    scores = dot_t(key, one_query) + bias
    probs = jnp.exp(scores - log_total)
    probs_grad = dot_t(value, one_pull)
    score_grad = (probs * (probs_grad - inner)).astype(low_type)
    return (probs.astype(low_type), score_grad, one_query, one_pull)


def half_slice(piece, half):
    _, _, rows, _, lanes, axis = piece
    if isinstance(half, int) and axis == 0:
        return (slice(half * (rows // 2), (half + 1) * (rows // 2)), slice(None))
    if isinstance(half, int):
        return (slice(None), slice(half * (lanes // 2), (half + 1) * (lanes // 2)))
    if axis == 0:
        return (pl.ds(pl.multiple_of(half * (rows // 2), 16), rows // 2), slice(None))
    return (slice(None), pl.ds(pl.multiple_of(half * (lanes // 2), 128), lanes // 2))


def half_shape(piece):
    _, _, rows, _, lanes, axis = piece
    return (rows // 2, lanes) if axis == 0 else (rows, lanes // 2)


def closing_pieces(shapes):
    first, second, deconv, fc2, fc1, out, qkv = shapes
    pieces = [(1, 0, second[0], 0, second[1], 0)]
    pieces += [(0, part * first[0] // 2, first[0] // 2, 0, first[1], 0) for part in range(2)]
    pieces += [(2, 0, 48, lane, 512, 1) for lane in range(0, deconv[1], 512)]
    pieces += [(3, row, 48, 0, 768, 1) for row in range(0, fc2[0], 48)]
    pieces += [(4, 0, 48, lane, 768, 1) for lane in range(0, fc1[1], 768)]
    pieces += [(5, 0, 48, 0, 768, 1)]
    pieces += [(6, 0, 48, lane, 768, 1) for lane in range(0, qkv[1], 768)]
    return pieces


def closing_kernel(rows, model_width, hidden, seqs, shapes, bits, held_count):
    pieces = closing_pieces(shapes)
    count = len(pieces)
    stored = 3
    slots = 3
    mesh_id = pl.DeviceIdType.MESH
    tile = min(rows, QUERY_TILE)
    window = tile + 2 * REACH
    reach_rows = rows + 2 * REACH
    scale = 1.0 / math.sqrt(HEAD_DIM)
    pairs = model_width // 128
    phases = bits + 2
    vector_phases = bits + 1
    first_order = (0, 2, 1) + tuple(range(3, bits))
    lines = seqs * rows
    spare_row = hidden
    own_scratch = 24
    span = 256
    items = seqs * (model_width // span)

    def body(*refs):
        packed = refs[:2]
        windows = refs[2:5]
        sources = refs[5:13]
        away = refs[13 : 13 + held_count]
        ln1_gain, early_vectors = refs[13 + held_count : 15 + held_count]
        rest = refs[15 + held_count :]
        results = rest[: len(shapes)]
        token_grad, vector_out = rest[len(shapes) : len(shapes) + 2]
        rest = rest[len(shapes) + 2 :]
        held = rest[:held_count]
        (
            pulls, pulls_left, pulls_right, stats, stats_left, stats_right, bias, edge_bias,
            normed_low, tokens, qkv_weight,
        ) = held
        rest = rest[held_count:]
        (
            arena, near, key_turned, key_total, value_total, grads, normed_turned, products,
            kept_first, kept_second, kept_third, vectors, vectors_landed, near_sem, held_sem, fetch_sem,
            local_sem, core_send, core_recv, send_sem, recv_sem, vector_send, vector_recv, spare,
        ) = rest[:own_scratch]
        del spare
        kept = (kept_first, kept_second, kept_third)
        landed = [
            rest[own_scratch + i * phases : own_scratch + (i + 1) * phases] for i in range(count)
        ]
        tok = lax.axis_index("tok")
        seq = lax.axis_index("seq")
        core = tok % 2

        def tok_bit(bit):
            return (tok // (1 << bit)) % 2

        def tok_step(bit):
            return (1 << bit) * (1 - 2 * tok_bit(bit))

        def kept_bit(phase):
            first = seq if phase == 1 else tok_bit(first_order[phase - 1])
            second = tok_bit(phase) if phase < bits else seq
            return (1 - core) * first + core * second

        def partner(phase):
            if phase == 0:
                return (seq, tok + tok_step(0))
            if phase > bits:
                return (1 - seq, tok)
            first = 0 if phase == 1 else tok_step(first_order[phase - 1])
            second = tok_step(phase) if phase < bits else 0
            across = 0
            if phase == 1:
                across = 1 - core
            if phase == bits:
                across = core
            return (
                seq + across * (1 - 2 * seq),
                tok + (1 - core) * first + core * second,
            )

        def vector_partner(phase):
            if phase < bits:
                return (seq, tok + tok_step(phase))
            return (1 - seq, tok)

        barrier = pltpu.get_barrier_semaphore()
        for phase in range(vector_phases):
            pl.semaphore_signal(
                barrier, inc=1, device_id=vector_partner(phase), device_id_type=mesh_id
            )

        def held_copies():
            return [
                pltpu.make_async_copy(source, target, held_sem.at[number])
                for number, (source, target) in enumerate(zip(away, held))
            ]

        def core_copy(number, half, receiver):
            index, begin, take, lane, lanes, axis = pieces[number]
            at = (slice(None),) * (bits - 1) + (1 - core,)
            if axis == 0:
                part = (pl.ds(begin + half * (take // 2), take // 2), slice(None))
                view = packed[index].at[at + part]
            else:
                slot = (number - stored) % slots
                part = (slice(None), pl.ds(half * (lanes // 2), lanes // 2))
                view = products.at[(slot,) + at + part]
            if receiver == 0:
                to = landed[number][0].at[(slice(None),) * (bits - 1) + (half,)]
            else:
                to = landed[number][0].at[half]
            return pltpu.make_async_remote_copy(
                src_ref=view,
                dst_ref=to,
                send_sem=core_send.at[number, half],
                recv_sem=core_recv.at[number, half],
                device_id=partner(0),
                device_id_type=mesh_id,
            )

        def local_copy(number):
            index, begin, take, _, _, _ = pieces[number]
            at = (slice(None),) * (bits - 1) + (core, pl.ds(begin, take))
            return pltpu.make_async_copy(packed[index].at[at], kept[number], local_sem.at[number])

        def remote_copy(number, phase, mine=1):
            if phase > bits:
                view = landed[number][bits]
            elif phase == 2 and mine == 0:
                at = (slice(None),) * (bits - 3) + (1 - kept_bit(phase),)
                view = landed[number][1].at[at]
            else:
                view = landed[number][phase - 1].at[
                    (slice(None),) * (bits - phase) + (1 - kept_bit(phase),)
                ]
            return pltpu.make_async_remote_copy(
                src_ref=view,
                dst_ref=landed[number][phase],
                send_sem=send_sem.at[number, phase - 1],
                recv_sem=recv_sem.at[number, phase - 1],
                device_id=partner(phase),
                device_id_type=mesh_id,
            )

        def begin(number):
            for half in range(2):
                for mine in range(2):

                    @pl.when(core == mine)
                    def _():
                        core_copy(number, half, 1 - mine).start()

            if number < stored:
                local_copy(number).start()

        def start_copy(number, phase):
            if phase != 2:
                remote_copy(number, phase).start()
                return
            for mine in range(2):

                @pl.when(core == mine)
                def _():
                    remote_copy(number, phase, mine).start()

        def bits_of(flat, length):
            return tuple((flat // (1 << bit)) % 2 for bit in reversed(range(length)))

        def finish(number, phase):
            piece = pieces[number]
            index, first, take, lane, lanes, axis = piece
            if phase == 0:
                for half in range(2):
                    for mine in range(2):

                        @pl.when(core == mine)
                        def _():
                            core_copy(number, half, mine).wait_recv()

                if number < stored:
                    local_copy(number).wait()
                blocks = 1 << (bits - 1)

                def step(block, carry):
                    at = bits_of(block, bits - 1)
                    for half in range(2):
                        flat = (1 - core) * (2 * block + half) + core * (blocks * half + block)
                        to = bits_of(flat, bits)
                        part = half_slice(piece, half)
                        if number < stored:
                            mine = kept[number][at + part]
                        else:
                            mine = products[((number - stored) % slots,) + at + (core,) + part]
                        landed[number][0][to] = landed[number][0][to] + mine
                    return carry

                lax.fori_loop(0, blocks, step, 0)
                return
            remote_copy(number, phase).wait_recv()
            got = landed[number][phase]
            if phase <= bits:
                before = landed[number][phase - 1]

                def step(block, carry):
                    at = bits_of(block, bits - phase)
                    keep = kept_bit(phase)
                    from_at = at + (keep,)
                    if phase == 2:
                        from_at = at[:-1] + (
                            (1 - core) * keep + core * at[-1],
                            (1 - core) * at[-1] + core * keep,
                        )
                    got[at] = got[at] + before[from_at]
                    return carry

                if phase < bits:
                    lax.fori_loop(0, 1 << (bits - phase), step, 0)
                else:
                    got[...] = got[...] + before[kept_bit(phase)]
                start_copy(number, phase + 1)
                return
            height, length = half_shape(piece)
            for half, value in ((seq, landed[number][bits]), (1 - seq, got)):
                if axis == 0:
                    at = (pl.ds(pl.multiple_of(first + half * height, 8), height), slice(None))
                else:
                    at = (pl.ds(first, take), pl.ds(pl.multiple_of(lane + half * length, 128), length))
                results[index][at] = value[...].astype(wide)

        def near_copies(item):
            group, number = divmod(item, seqs)
            return [
                pltpu.make_async_copy(
                    source.at[number, :, pl.ds(group * span, span)],
                    near.at[item % 2, field],
                    near_sem.at[item % 2, field],
                )
                for field, source in enumerate(windows)
            ]

        def pair_places(group, pair):
            lanes = pl.ds(pl.multiple_of(pair * 128, 128), 128)
            whole = pl.ds(pl.multiple_of(group * span + pair * 128, 128), 128)
            return (lanes, whole, group * (span // 128) + pair)

        def own_segment(item, base):
            group, number = divmod(item, seqs)
            slot = item % 2
            own = slice(REACH + base, REACH + base + tile)
            near_rows_at = slice(base, base + window)
            inside = slice(REACH - base, REACH - base + rows)

            def step(pair, carry):
                lanes, whole, heads = pair_places(group, pair)
                query = near[slot, 0, own, lanes] * scale
                key = near[slot, 1, near_rows_at, lanes]
                value = near[slot, 2, near_rows_at, lanes]
                pulled = pulls[number, base : base + tile, whole]
                key_term, value_term, halves = (None, None, [])
                for half in range(2):
                    log_total = stats[number, heads, half : half + 1, base : base + tile]
                    inner = stats[number, heads, 2 + half : 3 + half, base : base + tile]
                    probs, score_grad, one_query, one_pull = head_unit(
                        key, value, query, pulled, bias[number, base // tile], log_total, inner, half
                    )
                    here = dot(score_grad[inside], one_query)
                    key_term = here if key_term is None else key_term + here
                    here = dot(probs[inside], one_pull)
                    value_term = here if value_term is None else value_term + here
                    begin_row = pair * 128 + half * HEAD_DIM
                    feature = pl.ds(pl.multiple_of(begin_row, HEAD_DIM), HEAD_DIM)
                    halves.append(dot(key_turned[feature, near_rows_at], score_grad) * scale)
                if base == 0:
                    key_total[:, lanes] = key_term
                    value_total[:, lanes] = value_term
                else:
                    key_total[:, lanes] += key_term
                    value_total[:, lanes] += value_term
                both = jnp.transpose(jnp.concatenate(halves, axis=0)).astype(low_type)
                grads[number * rows + base : number * rows + base + tile, whole] = both
                return carry

            lax.fori_loop(0, span // 128, step, 0)

        def edge_segment(item, side):
            group, number = divmod(item, seqs)
            slot = item % 2
            from_rows = slice(0, REACH) if side == 0 else slice(REACH + rows, reach_rows)
            begin_row = 0 if side == 0 else rows - REACH
            at = slice(begin_row, begin_row + REACH)
            key_rows = slice(REACH + begin_row, 2 * REACH + begin_row)
            columns = slice(rows - REACH, rows) if side == 0 else slice(0, REACH)
            pull_ref, stat_ref = ((pulls_left, stats_left), (pulls_right, stats_right))[side]

            def step(pair, carry):
                lanes, whole, heads = pair_places(group, pair)
                query = near[slot, 0, from_rows, lanes] * scale
                key = near[slot, 1, key_rows, lanes]
                value = near[slot, 2, key_rows, lanes]
                pulled = pull_ref[number, :, whole]
                key_term, value_term = (None, None)
                for half in range(2):
                    log_total = stat_ref[number, heads, half : half + 1, :][:, columns]
                    inner = stat_ref[number, heads, 2 + half : 3 + half, :][:, columns]
                    probs, score_grad, one_query, one_pull = head_unit(
                        key, value, query, pulled, edge_bias[number, side], log_total, inner, half
                    )
                    here = dot(score_grad, one_query)
                    key_term = here if key_term is None else key_term + here
                    here = dot(probs, one_pull)
                    value_term = here if value_term is None else value_term + here
                key_total[at, lanes] += key_term
                value_total[at, lanes] += value_term
                return carry

            lax.fori_loop(0, span // 128, step, 0)

        def open_item(item):
            for copy in near_copies(item):
                copy.wait()
            if item + 1 < items:
                for copy in near_copies(item + 1):
                    copy.start()
            for block in range(span // 128):
                lanes = sub_lanes(block, 128)
                key_turned[lanes, :] = turned(near[item % 2, 1, :, lanes]).astype(low_type)

        def close_item(item):
            group, number = divmod(item, seqs)
            at = slice(number * rows, (number + 1) * rows)
            for part, total in ((1, key_total), (2, value_total)):
                lanes = pl.ds(part * model_width + group * span, span)
                grads[at, lanes] = total[...].astype(low_type)

        def group_grads(group):
            parts = [
                grads[:, part * model_width + group * span : part * model_width + (group + 1) * span]
                for part in range(3)
            ]
            return jnp.concatenate(parts, axis=1)

        def product(number, left_rows, right):
            lanes = pieces[number][4]
            slot = (number - stored) % slots
            shard_rows = model_width >> bits
            group = (1 << bits) // 2

            def step(part, carry):
                begin_row = pl.multiple_of(part * group * shard_rows, 16)
                found = dot(left_rows(begin_row, group * shard_rows), right()).astype(low_type)
                for shard in range(group):
                    at = bits_of(part * group + shard, bits)
                    block = found[shard * shard_rows : (shard + 1) * shard_rows]
                    products[(slot,) + at + (slice(None), slice(0, lanes))] = block
                return carry

            lax.fori_loop(0, 2, step, 0)

        def token_segment(number):
            at = slice(number * rows, (number + 1) * rows)
            total = dot_t(grads[at, :], qkv_weight[...])
            normed, norm_scale = normed_rows(tokens[number].astype(wide))
            vectors[0, 0:1, :] += jnp.sum(total * normed, axis=0, keepdims=True)
            vectors[0, 1:2, :] += jnp.sum(total, axis=0, keepdims=True)
            for row, part in ((2, 0), (3, 2)):
                field = grads[at, sub_lanes(part, model_width)].astype(wide)
                vectors[0, row : row + 1, :] += jnp.sum(field, axis=0, keepdims=True)
            pull = norm_pull(total, normed, norm_scale, row_of(ln1_gain))
            token_grad[number] = pull

        def vector_copy(phase):
            return pltpu.make_async_remote_copy(
                src_ref=vectors.at[phase],
                dst_ref=vectors_landed.at[phase],
                send_sem=vector_send.at[phase],
                recv_sem=vector_recv.at[phase],
                device_id=vector_partner(phase),
                device_id_type=mesh_id,
            )

        def finish_vector(phase):
            vector_copy(phase).wait_recv()
            if phase + 1 < vector_phases:
                vectors[phase + 1] = vectors[phase] + vectors_landed[phase]
                vector_copy(phase + 1).start()
            else:
                vector_out[...] = vectors[phase] + vectors_landed[phase]

        resid_low, up_grad, act, branch, normed_two, pre, attended, mixed = sources
        fetches = [(resid_low, 0, model_width)]
        fetches += [(up_grad, lane, 512) for lane in range(0, up_grad.shape[1], 512)]
        fetches += [(act, lane, model_width) for lane in range(0, hidden, model_width)]
        fetches += [(branch, 0, model_width), (normed_two, 0, model_width)]
        fetches += [(pre, lane, model_width) for lane in range(0, hidden, model_width)]
        fetches += [(attended, 0, model_width), (mixed, 0, model_width)]

        def fetch(number):
            source, lane, lanes = fetches[number]
            to = pl.ds((number % 3) * model_width, lanes)
            return pltpu.make_async_copy(
                source.at[:, pl.ds(lane, lanes)], grads.at[:, to], fetch_sem.at[number]
            )

        def fetched(number):
            lanes = fetches[number][2]
            begin_lane = (number % 3) * model_width
            return lambda: grads[:, begin_lane : begin_lane + lanes]

        def turn_fetched(number, chunk=None):
            begin_lane = (number % 3) * model_width

            def step(block, carry):
                lanes = pl.ds(pl.multiple_of(begin_lane + block * 128, 128), 128)
                found = turned(grads[:, lanes]).astype(low_type)
                if chunk is None:
                    at = pl.ds(pl.multiple_of(spare_row + block * 128, 128), 128)
                    arena[at, :] = found
                else:
                    shard_rows = hidden >> bits
                    for granule in range(8):
                        feature = chunk * model_width + block * 128 + granule * 16
                        shard, inner = (feature // shard_rows, feature % shard_rows)
                        to = (inner // 48) * model_width + shard * 48 + inner % 48
                        at = pl.ds(pl.multiple_of(to, 16), 16)
                        arena[at, :] = found[granule * 16 : (granule + 1) * 16]
                return carry

            lax.fori_loop(0, pairs, step, 0)

        def arena_rows(base):
            return lambda begin_row, take: arena[pl.ds(pl.multiple_of(base + begin_row, 16), take), :]

        def turned_rows(begin_row, take):
            return normed_turned[pl.ds(begin_row, take), :]

        state = {"now": 0.0, "link": 0.0, "flying": 0}
        events = []
        waiting = []
        sent = set()
        sizes = [p[2] * p[4] / (48.0 * 768.0) for p in pieces]

        def one_event():
            events.sort()
            ready, number, phase = events.pop(0)
            state["now"] = max(state["now"], ready)
            if number == count:
                finish_vector(phase)
                if phase + 1 < vector_phases:
                    events.append((state["now"] + 2.5, number, phase + 1))
                return
            finish(number, phase)
            if phase == 0:
                waiting.append(number)
            elif phase + 1 < phases:
                cost = (6.0, 5.0, 4.0, 3.0, 2.0)[min(phase - 1, 4)]
                events.append((state["now"] + 2.5 + cost * sizes[number], number, phase + 1))
            if phase == 1:
                state["flying"] -= 1
            while waiting and state["flying"] < 4:
                chosen = waiting.pop(0)
                start_copy(chosen, 1)
                state["flying"] += 1
                start = max(state["now"], state["link"])
                state["link"] = start + 4.0 * sizes[chosen]
                events.append((state["link"] + 1.0, chosen, 1))

        def pump(spent):
            state["now"] += spent
            while events and min(events)[0] <= state["now"]:
                one_event()

        def open_piece(number):
            begin(number)
            events.append((state["now"] + 2.5 + 2.0 * sizes[number], number, 0))

        def make_product(number, left_rows, right):
            before = number - slots
            if before >= stored:
                while any(e[1] == before and e[2] == 0 for e in events):
                    one_event()
                for half in range(2):
                    core_copy(before, half, 0).wait_send()
                    sent.add((before, half))
            product(number, left_rows, right)
            open_piece(number)
            pump(1.2)

        vectors[0, 0:8, :] = jnp.zeros((8, model_width), wide)
        vectors[0, 8:16, :] = early_vectors[...]
        for number in range(3):
            fetch(number).start()
        pl.semaphore_wait(barrier, vector_phases)
        for number in range(stored):
            open_piece(number)
        for copy in held_copies():
            copy.start()
        cursor = 0
        piece = stored

        def used():
            if cursor + 3 < len(fetches):
                fetch(cursor + 3).start()
            return cursor + 1

        def turn_next(chunk=None):
            fetch(cursor).wait()
            turn_fetched(cursor, chunk)
            pump(1.0)

        def product_next(number, left_rows):
            fetch(cursor).wait()
            make_product(number, left_rows, fetched(cursor))

        turn_next()
        cursor = used()
        for _ in range(up_grad.shape[1] // 512):
            product_next(piece, arena_rows(spare_row))
            cursor, piece = (used(), piece + 1)
        for chunk in range(hidden // model_width):
            turn_next(chunk)
            cursor = used()
        fetch(cursor).wait()
        for part in range(hidden // model_width):
            make_product(piece, arena_rows(part * model_width), fetched(cursor))
            piece += 1
        cursor = used()
        turn_next()
        cursor = used()
        for _ in range(hidden // model_width):
            product_next(piece, arena_rows(spare_row))
            cursor, piece = (used(), piece + 1)
        turn_next()
        cursor = used()
        product_next(piece, arena_rows(spare_row))
        cursor, piece = (used(), piece + 1)
        for copy in near_copies(0):
            copy.start()
        for copy in held_copies():
            copy.wait()
        for line in range(seqs):

            def turn_normed(column, carry):
                lanes = pl.ds(pl.multiple_of(column * 128, 128), 128)
                block = turned(normed_low[line, :, lanes]).astype(low_type)
                normed_turned[lanes, line * rows : (line + 1) * rows] = block
                return carry

            lax.fori_loop(0, pairs, turn_normed, 0)
        pump(1.5)
        for item in range(items):
            open_item(item)
            for base in range(0, rows, tile):
                own_segment(item, base)
                pump(1.8)
            for side in range(2):
                edge_segment(item, side)
                pump(1.3)
            close_item(item)
            if item % seqs == seqs - 1:
                make_product(piece, turned_rows, partial(group_grads, item // seqs))
                piece += 1
        for number in range(seqs):
            token_segment(number)
            pump(3.0)
        vector_copy(0).start()
        events.append((state["now"] + 2.5, count, 0))
        while events:
            one_event()
        for number in range(count):
            for half in range(2):
                if (number, half) not in sent:
                    core_copy(number, half, 0).wait_send()
            for phase in range(1, phases):
                remote_copy(number, phase).wait_send()
        for phase in range(vector_phases):
            vector_copy(phase).wait_send()

    fetch_count = 7 + 2 * (hidden // model_width) - 2 + shapes[2][1] // 512
    scratch = [
        pltpu.VMEM((hidden + model_width, model_width), low_type),
        pltpu.VMEM((2, 3, reach_rows, span), low_type),
        pltpu.VMEM((span, reach_rows), low_type),
        pltpu.VMEM((rows, span), wide),
        pltpu.VMEM((rows, span), wide),
        pltpu.VMEM((lines, 3 * model_width), low_type),
        pltpu.VMEM((model_width, lines), low_type),
        pltpu.VMEM((slots,) + (2,) * bits + (48, 768), low_type),
        pltpu.VMEM((2,) * (bits - 1) + (pieces[0][2], pieces[0][4]), low_type),
        pltpu.VMEM((2,) * (bits - 1) + (pieces[1][2], pieces[1][4]), low_type),
        pltpu.VMEM((2,) * (bits - 1) + (pieces[2][2], pieces[2][4]), low_type),
        pltpu.VMEM((vector_phases, 16, model_width), wide),
        pltpu.VMEM((vector_phases, 16, model_width), wide),
        pltpu.SemaphoreType.DMA((2, 3)),
        pltpu.SemaphoreType.DMA((held_count,)),
        pltpu.SemaphoreType.DMA((fetch_count,)),
        pltpu.SemaphoreType.DMA((stored,)),
        pltpu.SemaphoreType.DMA((count, 2)),
        pltpu.SemaphoreType.DMA((count, 2)),
        pltpu.SemaphoreType.DMA((count, phases - 1)),
        pltpu.SemaphoreType.DMA((count, phases - 1)),
        pltpu.SemaphoreType.DMA((vector_phases,)),
        pltpu.SemaphoreType.DMA((vector_phases,)),
        pltpu.SemaphoreType.DMA((1,)),
    ]
    for piece in pieces:
        block = half_shape(piece)
        scratch += [pltpu.VMEM((2,) * (bits - phase) + block, low_type) for phase in range(bits + 1)]
        scratch.append(pltpu.VMEM(block, low_type))
    return (body, scratch)


def closing(packed, windows, sources, held, small):
    shards = lax.axis_size("tok")
    bits = bit_count(shards)
    tokens, qkv_weight = (held[9], held[10])
    seqs, rows, model_width = tokens.shape
    hidden = sources[2].shape[1]
    shapes = [
        packed[0].shape[1:],
        packed[1].shape[1:],
        (model_width // shards, sources[1].shape[1]),
        (hidden // shards, model_width),
        (model_width // shards, hidden),
        (model_width // shards, model_width),
        (model_width // shards, qkv_weight.shape[1]),
    ]
    body, scratch = closing_kernel(
        rows, model_width, hidden, seqs, shapes, bits, len(held)
    )
    inside = pl.BlockSpec(memory_space=pltpu.VMEM)
    far = pl.BlockSpec(memory_space=pl.ANY)
    out_shape = [jax.ShapeDtypeStruct(s, wide) for s in shapes]
    out_shape.append(jax.ShapeDtypeStruct(tokens.shape, wide))
    out_shape.append(jax.ShapeDtypeStruct((16, model_width), wide))
    away = [p.reshape((2,) * bits + p.shape[1:]) for p in packed]
    away += list(windows) + list(sources) + list(held)
    return pl.pallas_call(
        body,
        in_specs=[far] * len(away) + [inside] * len(small),
        out_specs=[inside] * len(out_shape),
        out_shape=out_shape,
        scratch_shapes=[pltpu.VMEM(f.shape, f.dtype) for f in held] + scratch,
        compiler_params=pltpu.CompilerParams(
            vmem_limit_bytes=CLOSING_LIMIT, collective_id=1, has_side_effects=True
        ),
        cost_estimate=pl.CostEstimate(
            flops=50 * 10**9, bytes_accessed=60 * 10**6, transcendentals=0
        ),
    )(*away, *small)


def local(
    tokens,
    skip_features,
    crop_sides,
    ln1_gain,
    ln1_bias,
    qkv_weight,
    qv_bias,
    out_weight,
    out_bias,
    ln2_gain,
    ln2_bias,
    fc1_weight,
    fc1_bias,
    fc2_weight,
    fc2_bias,
    deconv_weight,
    conv1_weight,
    conv2_weight,
    conv3_weight,
    cotangent,
):
    seq_count, row_count, model_width = tokens.shape
    channels = conv2_weight.shape[2]
    hidden = fc1_weight.shape[1]
    reaches = (key_reach + row_count - 1) // row_count
    reach_rows = row_count + 2 * REACH
    near_given = row_count < REACH
    near = near_rows(tokens) if near_given else ()
    near_block = (seq_count, 16 if near_given else REACH, model_width)
    skip = skip_features.reshape(seq_count, row_count, 8 * channels)
    edge_block = ((seq_count, EDGE, 8 * channels), low_type)
    place, owner, crop_t, inverse, bias, edge_bias = geometry_tables(crop_sides, row_count)

    def block(lanes, kind, rows=row_count):
        return ((seq_count, rows, lanes), kind)

    matrix_flops = 2 * seq_count * row_count * model_width
    (
        normed_low, queries, keys, values, attended, log_totals, resid_one, normed_two,
        act_low, slope_low, resid_low, upsampled, *edges,
    ) = kernel_call(
        forward_kernel(row_count, model_width, hidden, seq_count, near_given),
        seq_count,
        (tokens, bias) + tuple(near),
        (
            ln1_gain, ln1_bias, qkv_weight, qv_bias, out_bias, ln2_gain, ln2_bias, fc1_bias, fc2_bias,
        ),
        (
            block(model_width, low_type),
            block(model_width, low_type, reach_rows),
            block(model_width, low_type, reach_rows),
            block(model_width, low_type, reach_rows),
            block(model_width, low_type),
            block(row_count, wide, 16),
            block(model_width, wide),
            block(model_width, low_type),
            block(hidden, low_type),
            block(hidden, low_type),
            block(model_width, low_type),
            block(8 * channels, low_type),
        ),
        (),
        [
            pltpu.VMEM((reach_rows, model_width), low_type),
            pltpu.VMEM((model_width, reach_rows), low_type),
            pltpu.SemaphoreType.DMA((2,)),
            pltpu.SemaphoreType.DMA((2,)),
            pltpu.VMEM(near_block, low_type),
            pltpu.VMEM(near_block, low_type),
            pltpu.SemaphoreType.DMA((seq_count, 2)),
            pltpu.SemaphoreType.DMA((seq_count, 2)),
            pltpu.VMEM(out_weight.shape, low_type),
            pltpu.VMEM(fc1_weight.shape, low_type),
            pltpu.VMEM(fc2_weight.shape, low_type),
            pltpu.VMEM(deconv_weight.shape, low_type),
            pltpu.SemaphoreType.DMA((4,)),
        ]
        + edge_scratch(seq_count, EDGE, 8 * channels),
        matrix_flops * (8 * model_width + 2 * hidden + 8 * channels),
        away=(tokens, skip, out_weight, fc1_weight, fc2_weight, deconv_weight),
        landing=(edge_block,) * 4,
        collective=2,
    )
    section_out, up_grad, skip_grad, conv1_grad, conv2_grad, conv3_grad = conv_section(
        upsampled,
        skip,
        edges,
        cotangent.reshape(seq_count, row_count, 8 * channels),
        (conv1_weight, conv2_weight, conv3_weight),
        (place, owner, crop_t, inverse),
        reaches,
    )
    section_out = section_out.reshape(seq_count, row_count, 8, channels)
    skip_grad = skip_grad.reshape(seq_count, row_count, 8, channels)
    shards = lax.axis_size("tok")
    linked = (
        row_count >= REACH
        and lax.axis_size("seq") == 2
        and model_width // shards == 48
        and shards * 8 == channels
    )
    pairs = model_width // 128
    pull_block = ((seq_count, REACH, model_width), low_type)
    stat_block = ((seq_count, pairs, 8, row_count), wide)
    (
        branch_low, pre_low, resid_grad, mixed_low, pulled, stats,
        fc2_bias_grad, fc1_bias_grad, out_bias_grad, ln2_gain_grad, ln2_bias_grad, *near_back,
    ) = kernel_call(
        hidden_back_kernel(row_count, model_width, hidden, seq_count, linked),
        seq_count,
        (up_grad, slope_low, resid_one, attended, log_totals),
        (deconv_weight, fc2_weight, fc1_weight, out_weight, ln2_gain),
        (
            block(model_width, low_type),
            block(hidden, low_type),
            block(model_width, wide),
            block(model_width, low_type),
            block(model_width, low_type),
            stat_block,
        ),
        (
            ((1, model_width), wide),
            ((1, hidden), wide),
            ((1, model_width), wide),
            ((1, model_width), wide),
            ((1, model_width), wide),
        ),
        [
            pltpu.VMEM((seq_count, row_count, model_width), low_type),
            pltpu.VMEM(*stat_block),
            pltpu.VMEM((REACH, model_width), low_type),
            pltpu.VMEM(stat_block[0][1:], wide),
            pltpu.SemaphoreType.DMA((seq_count, 2)),
            pltpu.SemaphoreType.DMA((seq_count, 2)),
            pltpu.SemaphoreType.DMA((seq_count, 2)),
            pltpu.SemaphoreType.DMA((seq_count, 2)),
            pltpu.SemaphoreType.DMA((2, seq_count)),
        ]
        if linked
        else [],
        matrix_flops * (model_width + 2 * hidden + 8 * channels),
        landing=(pull_block, pull_block, stat_block, stat_block) if linked else (),
        collective=7 if linked else None,
    )

    def weight_product(left, right):
        return jnp.einsum(
            "rd,re->de",
            left.reshape(-1, left.shape[-1]),
            right.reshape(-1, right.shape[-1]),
            preferred_element_type=wide,
        )

    if linked:
        early = (
            out_bias_grad, ln2_gain_grad, ln2_bias_grad, fc2_bias_grad,
            fc1_bias_grad.reshape(-1, model_width),
        )
        def lines_of(field):
            return field.reshape(-1, field.shape[-1])

        results = closing(
            (conv1_grad, conv2_grad),
            (queries, keys, values),
            [
                lines_of(field)
                for field in (
                    resid_low, up_grad, act_low, branch_low, normed_two, pre_low, attended, mixed_low
                )
            ],
            (
                pulled, near_back[0], near_back[1], stats, near_back[2], near_back[3], bias,
                edge_bias, normed_low, tokens, qkv_weight,
            ),
            (ln1_gain, jnp.concatenate(early, axis=0)),
        )
        conv_shares = (
            conv_share(results[0][:432], 27, 2),
            conv_share(results[1][:216], 27, 1),
            conv_share(results[0][432:448], 1, 2),
        )
        split = results[6].reshape(-1, 3, 3, model_width // 3)
        shares = list(results[2:6]) + [split.swapaxes(1, 2).reshape(results[6].shape)]
        token_grad = resid_grad + results[7]
        lines = results[8]
        span = model_width // shards
        own = lax.dynamic_slice_in_dim(lines[:12], lax.axis_index("tok") * span, span, 1)
        long_span = hidden // shards
        long_line = lines[12:16].reshape(hidden)
        long_own = lax.dynamic_slice_in_dim(
            long_line, lax.axis_index("tok") * long_span, long_span, 0
        )
        vectors = (own[0], own[1], own[2], own[3], own[8], own[9], own[10], long_own, own[11])
    else:
        query_grad, key_own, value_own, low_pay, high_pay = kernel_call(
            attention_back_kernel(row_count, model_width),
            seq_count,
            (queries, keys, values, pulled, stats, bias),
            (),
            (
                block(model_width, low_type),
                block(model_width, wide),
                block(model_width, wide),
                block(2 * model_width, low_type, REACH),
                block(2 * model_width, low_type, REACH),
            ),
            (),
            [
                pltpu.VMEM((reach_rows, model_width), wide),
                pltpu.VMEM((reach_rows, model_width), wide),
                pltpu.VMEM((model_width, reach_rows), low_type),
            ],
            matrix_flops * 12 * model_width,
        )
        both = jnp.concatenate([key_own, value_own], axis=-1)
        both = returned_rows(both, low_pay, high_pay)
        qkv_grad_low, token_grad, column_sums, ln1_gain_grad, ln1_bias_grad = kernel_call(
            token_kernel(row_count, model_width),
            seq_count,
            (tokens, resid_grad, query_grad, both[:, :, :model_width], both[:, :, model_width:]),
            (qkv_weight, ln1_gain),
            (block(3 * model_width, low_type), block(model_width, wide)),
            (
                ((1, 3 * model_width), wide),
                ((1, model_width), wide),
                ((1, model_width), wide),
            ),
            [],
            matrix_flops * 3 * model_width,
        )
        matrices = (
            weight_product(resid_low, up_grad),
            weight_product(act_low, branch_low),
            weight_product(normed_two, pre_low),
            weight_product(attended, mixed_low),
            weight_product(normed_low, qkv_grad_low),
        )
        conv3_turned = jnp.moveaxis(conv3_grad.reshape(1, 2, channels, channels), 2, 3)
        conv_grads = (conv1_grad, conv2_grad, conv3_turned)
        conv_shares, shares, vectors = reduced_all(
            conv_grads,
            matrices,
            (
                ln1_gain_grad, ln1_bias_grad, column_sums[:, :model_width],
                column_sums[:, 2 * model_width :], out_bias_grad, ln2_gain_grad, ln2_bias_grad,
                fc1_bias_grad, fc2_bias_grad,
            ),
        )
    return (
        section_out,
        token_grad,
        skip_grad,
        vectors[0],
        vectors[1],
        shares[4],
        jnp.stack([vectors[2], vectors[3]]),
        shares[3],
        vectors[4],
        vectors[5],
        vectors[6],
        shares[2],
        vectors[7],
        shares[1],
        vectors[8],
        shares[0],
        conv_shares[0],
        conv_shares[1],
        conv_shares[2][0],
    )


def solution(mesh):
    in_specs = (
        P("seq", "tok", None),
        P("seq", "tok", None, None),
        P("seq", None),
        P(),
        P(),
        P(),
        P(),
        P(),
        P(),
        P(),
        P(),
        P(),
        P(),
        P(),
        P(),
        P(),
        P(),
        P(),
        P(),
        P("seq", "tok", None, None),
    )
    out_specs = (
        P("seq", "tok", None, None),
        P("seq", "tok", None),
        P("seq", "tok", None, None),
        P("tok"),
        P("tok"),
        P("tok", None),
        P(None, "tok"),
        P("tok", None),
        P("tok"),
        P("tok"),
        P("tok"),
        P("tok", None),
        P("tok"),
        P("tok", None),
        P("tok"),
        P("tok", None),
        P(None, None, "tok"),
        P(None, None, "tok"),
        P(None, "tok"),
    )
    return jax.shard_map(local, mesh=mesh, in_specs=in_specs, out_specs=out_specs, check_vma=False)
```

```python
from functools import partial
import math

import jax
import jax.numpy as jnp
import numpy as np
from jax import lax
from jax.experimental import pallas as pl
from jax.experimental.pallas import tpu as pltpu
from jax.sharding import PartitionSpec as P

HEADS = 12
HEAD_DIM = 64


side_small = 4
side_big = 6
halo_rows = 43
key_reach = 215
norm_eps = 1e-05
far_below = -1e30
highest = lax.Precision.HIGHEST
in_part = {-1: (1, 2), 0: (0, 2), 1: (0, 1)}
out_part = {-1: (0, 1), 0: (0, 2), 1: (1, 2)}


def passed_along(block, axis, distance):
    devices = range(lax.axis_size(axis))
    route = [(i - distance, i) for i in devices if i - distance in devices]
    return lax.ppermute(block, axis, route)


def all_offsets():
    step_values = (-1, 0, 1)
    return [
        (step_x, step_y, step_z)
        for step_x in step_values
        for step_y in step_values
        for step_z in step_values
    ]


EDGE = 48
WINDOW = 256
TILE = 128
CROP_ROWS = 48
SUBS = 8
VMEM_LIMIT = 60 * 1024 * 1024
lowest_step = {-1: -43, 0: -7, 1: 11}
low_type = jnp.bfloat16
wide = jnp.float32


def dot(left, right):
    return jnp.dot(left, right, preferred_element_type=wide)


def three_terms(field):
    first = field.astype(low_type)
    rest = field - first.astype(wide)
    second = rest.astype(low_type)
    third = (rest - second.astype(wide)).astype(low_type)
    return (first, second, third)


def exact_dot(chosen, field):
    first, second, third = three_terms(field)
    return dot(chosen, first) + dot(chosen, second) + dot(chosen, third)


def sub_lanes(number, width):
    return slice(number * width, (number + 1) * width)


def all_taps():
    return [(x, y, z) for x in range(3) for y in range(3) for z in range(3)]


def forward_band(weight, band_ref):
    inner, outer = weight.shape[1:]
    band_ref[...] = jnp.zeros_like(band_ref)
    for tap_x, tap_y, tap_z in all_taps():
        for side in range(2):
            rows = sub_lanes(tap_y * 4 + tap_z + side, inner)
            lanes = sub_lanes(side, outer)
            band_ref[tap_x, rows, lanes] = weight[tap_x * 9 + tap_y * 3 + tap_z]


def backward_band(weight, band_ref):
    inner, outer = weight.shape[1:]
    band_ref[...] = jnp.zeros_like(band_ref)
    for tap_x, tap_y, tap_z in all_taps():
        for side in range(2):
            rows = sub_lanes(side, inner)
            lanes = sub_lanes(tap_y * 4 + tap_z + side, outer)
            band_ref[tap_x, rows, lanes] = weight[26 - (tap_x * 9 + tap_y * 3 + tap_z)]


def once(fill, *refs):
    @pl.when(pl.program_id(0) == 0)
    def _():
        fill(*refs)


def window_positions(step):
    return {-1: ((0, 1),), 0: ((1, 0), (2, 1)), 1: ((3, 0),)}[step]


def fill_windows(x_ref, place_ref, p_ref, rows, width):
    tile = min(rows, TILE)
    for base in range(0, rows, tile):
        own = slice(base, base + tile)
        for number, (step_x, step_y, step_z) in enumerate(all_offsets()):
            low = (EDGE + base + lowest_step[step_x]) // 16 * 16
            centre = (step_x, step_y, step_z) == (0, 0, 0)
            if not centre:
                lane = lax.broadcasted_iota(jnp.int32, (tile, WINDOW), 1) + low
                chosen = jnp.where(lane == place_ref[0, own, number : number + 1], 1.0, 0.0)
                chosen = chosen.astype(low_type)
            for x_to, x_from in window_positions(step_x):
                for y_to, y_from in window_positions(step_y):
                    z_to, z_from = window_positions(step_z)[0]
                    count = (2 if step_z == 0 else 1) * width
                    to = ((x_to * 4 + y_to) * 4 + z_to) * width
                    source = (x_from * 4 + y_from * 2 + z_from) * width
                    if centre:
                        got = x_ref[EDGE + base : EDGE + base + tile, source : source + count]
                    else:
                        got = dot(chosen, x_ref[low : low + WINDOW, source : source + count])
                    p_ref[own, to : to + count] = got.astype(low_type)


def window_conv(p_ref, band_ref, pair, width, product):
    first, second = pair
    total = None
    for tap in range(3):
        begin = ((first + tap) * 4 + second) * 4 * width
        term = product(p_ref[:, begin : begin + 12 * width], band_ref[tap])
        total = term if total is None else total + term
    return total


def all_pairs():
    return [(first, second) for first in range(2) for second in range(2)]


def add_grads(left_ref, p_ref, total_ref, width, channels):
    for tap_x in range(3):
        for tap_y in range(3):
            term = None
            for number, (first, second) in enumerate(all_pairs()):
                begin = ((first + tap_x) * 4 + second + tap_y) * 4 * channels
                left = left_ref[number * 2 * width : (number + 1) * 2 * width, :]
                part = dot(left, p_ref[:, begin : begin + 4 * channels])
                term = part if term is None else term + part
            total_ref[tap_x * 3 + tap_y] += term


def fold_grads(total_ref, grad_ref, width, channels):
    for tap_x in range(3):
        for tap_y in range(3):
            for tap_z in range(3):
                number = tap_x * 3 + tap_y
                here = total_ref[number, :width, sub_lanes(tap_z, channels)]
                there = total_ref[number, width:, sub_lanes(tap_z + 1, channels)]
                tap = 26 - (number * 3 + tap_z)
                for half in range(width // channels):
                    rows = slice(half * channels, (half + 1) * channels)
                    grad_ref[tap, half] = jnp.transpose(here[rows] + there[rows])


def fold_packed(total_ref, grad_ref, width, channels, shards, side_ref=None):
    blocks = []
    for tap in range(27):
        number, tap_z = divmod(26 - tap, 3)
        here = total_ref[number, :width, sub_lanes(tap_z, channels)]
        there = total_ref[number, width:, sub_lanes(tap_z + 1, channels)]
        both = here + there
        for half in range(width // channels):
            blocks.append(jnp.transpose(both[half * channels : (half + 1) * channels]))
    if side_ref is not None:
        for half in range(width // channels):
            blocks.append(jnp.transpose(side_ref[half * channels : (half + 1) * channels, :]))
    if len(blocks) % 2 == 1:
        blocks.append(jnp.zeros_like(blocks[0]))
    for pair in range(len(blocks) // 2):
        split = [b.reshape(shards, -1, channels) for b in blocks[2 * pair : 2 * pair + 2]]
        joined = jnp.concatenate(split, axis=1).astype(low_type)
        grad_ref[:, 16 * pair : 16 * pair + 16, :] = joined


def kernel_call(
    body, seqs, inputs, shared, outputs, summed, scratch, flops, away=(), landing=(), collective=None
):
    def row_spec(shape):
        return pl.BlockSpec((1,) + tuple(shape[1:]), lambda i: (i,) + (0,) * (len(shape) - 1))

    def whole_spec(shape):
        return pl.BlockSpec(
            tuple(shape), lambda i: (0,) * len(shape), pipeline_mode=pl.Buffered(1)
        )

    far_spec = pl.BlockSpec(memory_space=pl.ANY)
    moved = sum(math.prod(a.shape) * a.dtype.itemsize for a in list(inputs) + list(shared))
    moved += sum(math.prod(s) * jnp.dtype(t).itemsize for s, t in list(outputs) + list(summed))
    results = list(outputs) + list(summed) + list(landing)
    return pl.pallas_call(
        body,
        grid=(seqs,),
        in_specs=[row_spec(a.shape) for a in inputs]
        + [whole_spec(a.shape) for a in shared]
        + [far_spec] * len(away),
        out_specs=[row_spec(s) for s, _ in outputs]
        + [whole_spec(s) for s, _ in summed]
        + [far_spec] * len(landing),
        out_shape=[jax.ShapeDtypeStruct(s, t) for s, t in results],
        scratch_shapes=scratch,
        compiler_params=pltpu.CompilerParams(
            vmem_limit_bytes=VMEM_LIMIT,
            collective_id=collective,
            has_side_effects=collective is not None,
        ),
        cost_estimate=pl.CostEstimate(flops=flops, bytes_accessed=moved, transcendentals=0),
    )(*inputs, *shared, *away)


def tok_sides():
    tok, count = (lax.axis_index("tok"), lax.axis_size("tok"))
    return (tok > 0, tok < count - 1)


def greet():
    seq, tok, count = (lax.axis_index("seq"), lax.axis_index("tok"), lax.axis_size("tok"))
    barrier = pltpu.get_barrier_semaphore()
    for there, shift in zip(tok_sides(), (count - 1, 1)):

        @pl.when(there)
        def _():
            pl.semaphore_signal(
                barrier,
                inc=1,
                device_id=(seq, lax.rem(tok + shift, count)),
                device_id_type=pl.DeviceIdType.MESH,
            )


def met():
    tok, count = (lax.axis_index("tok"), lax.axis_size("tok"))
    peers = jnp.minimum(tok, 1) + jnp.minimum(count - 1 - tok, 1)
    pl.semaphore_wait(pltpu.get_barrier_semaphore(), peers)


class Edge:
    def __init__(self, low, high, left, right, send_sem, recv_sem):
        self.sources = (low, high)
        self.targets = (right, left)
        self.send_sem = send_sem
        self.recv_sem = recv_sem

    def copy(self, way):
        seq, tok, count = (lax.axis_index("seq"), lax.axis_index("tok"), lax.axis_size("tok"))
        shift = count - 1 if way == 0 else 1
        return pltpu.make_async_remote_copy(
            src_ref=self.sources[way],
            dst_ref=self.targets[way],
            send_sem=self.send_sem.at[way],
            recv_sem=self.recv_sem.at[way],
            device_id=(seq, lax.rem(tok + shift, count)),
            device_id_type=pl.DeviceIdType.MESH,
        )

    def start(self):
        for way, there in enumerate(tok_sides()):

            @pl.when(there)
            def _():
                self.copy(way).start()

    def land(self):
        for way, there in enumerate(tok_sides()):

            @pl.when(there)
            def _():
                self.copy(1 - way).wait_recv()

    def sent(self):
        for way, there in enumerate(tok_sides()):

            @pl.when(there)
            def _():
                self.copy(way).wait_send()


def edge_scratch(seqs, rows, lanes):
    return [
        pltpu.VMEM((seqs, rows, lanes), low_type),
        pltpu.VMEM((seqs, rows, lanes), low_type),
        pltpu.VMEM((rows, lanes), low_type),
        pltpu.SemaphoreType.DMA((seqs, 2)),
        pltpu.SemaphoreType.DMA((seqs, 2)),
        pltpu.SemaphoreType.DMA((seqs,)),
    ]


class Payload:
    def __init__(self, seqs, left, right, low_pay, high_pay, zero_ref, send_sem, recv_sem, zero_sem):
        self.seqs = seqs
        self.refs = (left, right, low_pay, high_pay, send_sem, recv_sem)
        self.zero_ref = zero_ref
        self.zero_sem = zero_sem
        self.step = pl.program_id(0)
        self.low = low_pay.at[pl.ds(self.step, 1)]
        self.high = high_pay.at[pl.ds(self.step, 1)]

    def edge(self, number):
        left, right, low, high, send_sem, recv_sem = (ref.at[number] for ref in self.refs)
        return Edge(low, high, left, right, send_sem, recv_sem)

    def enter(self):
        @pl.when(self.step == 0)
        def _():
            greet()
            self.zero_ref[...] = jnp.zeros_like(self.zero_ref)
            for field, there in zip(self.refs[:2], tok_sides()):

                @pl.when(jnp.logical_not(there))
                def _():
                    copies = [
                        pltpu.make_async_copy(self.zero_ref, field.at[n], self.zero_sem.at[n])
                        for n in range(self.seqs)
                    ]
                    for copy in copies:
                        copy.start()
                    for copy in copies:
                        copy.wait()

    def send(self, greeted=False, later=False):
        if not greeted:

            @pl.when(self.step == 0)
            def _():
                met()

        self.edge(self.step).start()
        if not later:
            self.close()

    def close(self):
        @pl.when(self.step == self.seqs - 1)
        def _():
            for number in range(self.seqs):
                self.edge(number).land()
            for number in range(self.seqs):
                self.edge(number).sent()


def conv_scratch(rows, width, band_shape):
    return [
        pltpu.VMEM((rows + 192, SUBS * width), low_type),
        pltpu.VMEM((rows, 64 * width), low_type),
        pltpu.VMEM((3,) + band_shape, low_type),
    ]


def conv_flops(seqs, rows, inner, outer):
    return 2 * seqs * rows * (36 * 4 * inner * 2 * outer + 56 * WINDOW * inner)


def put_edges(low_pay, high_pay, number, field, channels, rows):
    lanes = sub_lanes(number, channels)
    low_pay[0, :, lanes] = field[:EDGE].astype(low_type)
    high_pay[0, :, lanes] = field[rows - EDGE :].astype(low_type)


def put_sums(sums_ref, low_pay, high_pay, number, value, channels):
    lanes = sub_lanes(number, channels)
    sums_ref[0, :, lanes] = value
    pay_lanes = sub_lanes(SUBS + number, channels)
    low_pay[0, :, pay_lanes] = value.astype(low_type)
    high_pay[0, :, pay_lanes] = value.astype(low_type)


def taken_sums(sums_ref, left_pay, right_pay, number, channels):
    lanes = sub_lanes(number, channels)
    pay_lanes = sub_lanes(SUBS + number, channels)
    total = sums_ref[0, :, lanes] + left_pay[0, :, pay_lanes].astype(wide)
    return total + right_pay[0, :, pay_lanes].astype(wide)


def mean_and_scale(total, square, inverse):
    mean = total * inverse
    variance = jnp.maximum(square * inverse - mean * mean, 0.0)
    return (mean, lax.rsqrt(variance + norm_eps))


def silu_parts(value):
    gate = 1.0 / (1.0 + jnp.exp(-value))
    return (value * gate, gate * (1.0 + value * (1.0 - gate)))


def first_conv_kernel(rows, channels, seqs):
    width = 2 * channels

    def body(
        up, up_left, up_right, skip, skip_left, skip_right, place, crop_t, weight, side,
        first_out, side_out, sums, to_left, to_right, x_ref, p_ref, band_ref, *edge_refs,
    ):
        pay = Payload(seqs, to_left, to_right, *edge_refs)
        pay.enter()
        low_pay, high_pay = (pay.low, pay.high)
        once(forward_band, weight, band_ref)
        for number in range(SUBS):
            for half, (own, left, right) in enumerate(
                ((up, up_left, up_right), (skip, skip_left, skip_right))
            ):
                to = sub_lanes(2 * number + half, channels)
                lanes = sub_lanes(number, channels)
                x_ref[:EDGE, to] = left[0, :, lanes]
                x_ref[EDGE : EDGE + rows, to] = own[0, :, lanes]
                x_ref[EDGE + rows : 2 * EDGE + rows, to] = right[0, :, lanes]
        x_ref[2 * EDGE + rows :, :] = jnp.zeros((96, SUBS * width), low_type)
        fill_windows(x_ref, place, p_ref, rows, width)
        total = [jnp.zeros((rows, channels), wide) for _ in range(4)]
        for index, pair in enumerate(all_pairs()):
            result = window_conv(p_ref, band_ref, pair, width, dot)
            first_out[0, :, sub_lanes(index, width)] = result
            for half in range(2):
                number = 2 * index + half
                value = result[:, sub_lanes(half, channels)]
                put_edges(low_pay, high_pay, number, value, channels, rows)
                flat = dot(x_ref[EDGE : EDGE + rows, sub_lanes(number, width)], side[...])
                side_out[0, :, sub_lanes(number, channels)] = flat
                terms = (value, value * value, flat, flat * flat)
                total = [have + term for have, term in zip(total, terms)]
        for number in range(4):
            value = exact_dot(crop_t[0], total[number])
            put_sums(sums, low_pay, high_pay, number, value, channels)
        pay.send()

    return body


def second_conv_kernel(rows, channels, seqs):
    def body(
        first, left_pay, right_pay, own_sums, inverse, owner, place, crop_t, weight,
        second_out, stats, sums, to_left, to_right, x_ref, p_ref, band_ref, *edge_refs,
    ):
        pay = Payload(seqs, to_left, to_right, *edge_refs)
        pay.enter()
        low_pay, high_pay = (pay.low, pay.high)
        once(forward_band, weight, band_ref)
        taken = [taken_sums(own_sums, left_pay, right_pay, n, channels) for n in range(4)]
        mean, scale = mean_and_scale(taken[0], taken[1], inverse[0])
        side_mean, side_scale = mean_and_scale(taken[2], taken[3], inverse[0])
        for number, value in enumerate((mean, scale, side_mean, side_scale)):
            stats[0, :, sub_lanes(number, channels)] = value
        mean_rows = exact_dot(owner[0], mean)
        scale_rows = exact_dot(owner[0], scale)
        parts = (
            (left_pay, slice(0, EDGE)),
            (first, slice(EDGE, EDGE + rows)),
            (right_pay, slice(EDGE + rows, 2 * EDGE + rows)),
        )
        for number in range(SUBS):
            lanes = sub_lanes(number, channels)
            for field, place_rows in parts:
                normed = field[0, :, lanes].astype(wide) - mean_rows[place_rows]
                normed = normed * scale_rows[place_rows]
                x_ref[place_rows, lanes] = silu_parts(normed)[0].astype(low_type)
        x_ref[2 * EDGE + rows :, :] = jnp.zeros((96, SUBS * channels), low_type)
        fill_windows(x_ref, place, p_ref, rows, channels)
        total = [jnp.zeros((rows, channels), wide) for _ in range(2)]
        for index, pair in enumerate(all_pairs()):
            result = window_conv(p_ref, band_ref, pair, channels, dot)
            second_out[0, :, sub_lanes(index, 2 * channels)] = result
            for half in range(2):
                value = result[:, sub_lanes(half, channels)]
                put_edges(low_pay, high_pay, 2 * index + half, value, channels, rows)
                total = [total[0] + value, total[1] + value * value]
        for number in range(2):
            value = exact_dot(crop_t[0], total[number])
            put_sums(sums, low_pay, high_pay, number, value, channels)
        pay.send()

    return body


def output_kernel(rows, channels, seqs):
    def body(
        second, side_field, cotangent, stats, left_pay, right_pay, own_sums, inverse, owner, crop_t,
        section, grad_out, second_stats, sums, to_left, to_right, *edge_refs,
    ):
        pay = Payload(seqs, to_left, to_right, *edge_refs)
        pay.enter()
        low_pay, high_pay = (pay.low, pay.high)
        taken = [taken_sums(own_sums, left_pay, right_pay, n, channels) for n in range(2)]
        mean, scale = mean_and_scale(taken[0], taken[1], inverse[0])
        second_stats[0, :, sub_lanes(0, channels)] = mean
        second_stats[0, :, sub_lanes(1, channels)] = scale
        own = owner[0, EDGE : EDGE + rows, :]
        mean_rows = exact_dot(own, mean)
        scale_rows = exact_dot(own, scale)
        side_mean = exact_dot(own, stats[0, :, sub_lanes(2, channels)])
        side_scale = exact_dot(own, stats[0, :, sub_lanes(3, channels)])
        total = [jnp.zeros((rows, channels), wide) for _ in range(3)]
        for number in range(SUBS):
            lanes = sub_lanes(number, channels)
            normed = (second[0, :, lanes] - mean_rows) * scale_rows
            side = (side_field[0, :, lanes] - side_mean) * side_scale
            value, slope = silu_parts(normed + side)
            section[0, :, lanes] = value.astype(low_type)
            grad = cotangent[0, :, lanes].astype(wide) * slope
            grad_out[0, :, lanes] = grad
            put_edges(low_pay, high_pay, number, grad, channels, rows)
            terms = (grad, grad * normed, grad * side)
            total = [have + term for have, term in zip(total, terms)]
        for number in range(3):
            value = exact_dot(crop_t[0], total[number])
            put_sums(sums, low_pay, high_pay, number, value, channels)
        pay.send()

    return body


def second_back_kernel(rows, channels, seqs, shards):
    def body(
        grad, grad_left, grad_right, own_sums, second, second_left, second_right, side_field, first,
        stats, second_stats, inverse, owner, place, crop_t, weight,
        first_grad, side_grad, sums, weight_grad, to_left, to_right,
        x_ref, p_ref, band_ref, left_ref, total_ref, *edge_refs,
    ):
        pay = Payload(seqs, to_left, to_right, *edge_refs)
        pay.enter()
        low_pay, high_pay = (pay.low, pay.high)
        once(backward_band, weight, band_ref)
        means = [
            taken_sums(own_sums, grad_left, grad_right, n, channels) * inverse[0] for n in range(3)
        ]
        mean_rows = exact_dot(owner[0], second_stats[0, :, sub_lanes(0, channels)])
        scale_rows = exact_dot(owner[0], second_stats[0, :, sub_lanes(1, channels)])
        lead_rows = exact_dot(owner[0], means[0])
        slope_rows = exact_dot(owner[0], means[1])
        parts = (
            (grad_left, second_left, slice(0, EDGE)),
            (grad, second, slice(EDGE, EDGE + rows)),
            (grad_right, second_right, slice(EDGE + rows, 2 * EDGE + rows)),
        )
        own = slice(EDGE, EDGE + rows)
        side_mean = exact_dot(owner[0, own, :], stats[0, :, sub_lanes(2, channels)])
        side_scale = exact_dot(owner[0, own, :], stats[0, :, sub_lanes(3, channels)])
        side_slope = exact_dot(owner[0, own, :], means[2])
        first_mean = exact_dot(owner[0, own, :], stats[0, :, sub_lanes(0, channels)])
        first_scale = exact_dot(owner[0, own, :], stats[0, :, sub_lanes(1, channels)])
        for number in range(SUBS):
            lanes = sub_lanes(number, channels)
            for grad_from, field, at in parts:
                normed = (field[0, :, lanes].astype(wide) - mean_rows[at]) * scale_rows[at]
                pulled = grad_from[0, :, lanes].astype(wide) - lead_rows[at]
                pulled = scale_rows[at] * (pulled - normed * slope_rows[at])
                x_ref[at, lanes] = pulled.astype(low_type)
            side = (side_field[0, :, lanes] - side_mean) * side_scale
            pulled = side_scale * (grad[0, :, lanes] - lead_rows[own] - side * side_slope)
            side_grad[0, :, lanes] = pulled.astype(low_type)
            normed = (first[0, :, lanes] - first_mean) * first_scale
            hidden = silu_parts(normed)[0]
            left_ref[lanes, :] = jnp.transpose(hidden).astype(low_type)
        x_ref[2 * EDGE + rows :, :] = jnp.zeros((96, SUBS * channels), low_type)
        fill_windows(x_ref, place, p_ref, rows, channels)
        total = [jnp.zeros((rows, channels), wide) for _ in range(2)]
        for index, pair in enumerate(all_pairs()):
            result = window_conv(p_ref, band_ref, pair, channels, dot_t)
            for half in range(2):
                number = 2 * index + half
                lanes = sub_lanes(number, channels)
                normed = (first[0, :, lanes] - first_mean) * first_scale
                value = result[:, sub_lanes(half, channels)] * silu_parts(normed)[1]
                first_grad[0, :, lanes] = value
                put_edges(low_pay, high_pay, number, value, channels, rows)
                total = [total[0] + value, total[1] + value * normed]
        for number in range(2):
            value = exact_dot(crop_t[0], total[number])
            put_sums(sums, low_pay, high_pay, number, value, channels)
        pay.send(later=True)

        @pl.when(pl.program_id(0) == 0)
        def _():
            total_ref[...] = jnp.zeros_like(total_ref)

        add_grads(left_ref, p_ref, total_ref, channels, channels)

        @pl.when(pl.program_id(0) == seqs - 1)
        def _():
            if shards * 8 == channels:
                fold_packed(total_ref, weight_grad, channels, channels, shards)
            else:
                fold_grads(total_ref, weight_grad, channels, channels)

        pay.close()

    return body


def first_back_kernel(rows, channels, seqs, shards):
    width = 2 * channels

    def body(
        grad, grad_left, grad_right, own_sums, first, first_left, first_right, stats, inverse, owner,
        place, side_grad, up, skip, weight, side_weight,
        up_grad, skip_grad, weight_grad, side_weight_grad,
        x_ref, p_ref, band_ref, left_ref, total_ref,
    ):
        once(backward_band, weight, band_ref)
        means = [
            taken_sums(own_sums, grad_left, grad_right, n, channels) * inverse[0] for n in range(2)
        ]
        mean_rows = exact_dot(owner[0], stats[0, :, sub_lanes(0, channels)])
        scale_rows = exact_dot(owner[0], stats[0, :, sub_lanes(1, channels)])
        lead_rows = exact_dot(owner[0], means[0])
        slope_rows = exact_dot(owner[0], means[1])
        parts = (
            (grad_left, first_left, slice(0, EDGE)),
            (grad, first, slice(EDGE, EDGE + rows)),
            (grad_right, first_right, slice(EDGE + rows, 2 * EDGE + rows)),
        )
        for number in range(SUBS):
            lanes = sub_lanes(number, channels)
            for grad_from, field, at in parts:
                normed = (field[0, :, lanes].astype(wide) - mean_rows[at]) * scale_rows[at]
                pulled = grad_from[0, :, lanes].astype(wide) - lead_rows[at]
                pulled = scale_rows[at] * (pulled - normed * slope_rows[at])
                x_ref[at, lanes] = pulled.astype(low_type)
            for half, field in enumerate((up, skip)):
                turned = jnp.transpose(field[0, :, lanes].astype(wide)).astype(low_type)
                left_ref[sub_lanes(2 * number + half, channels), :] = turned
        x_ref[2 * EDGE + rows :, :] = jnp.zeros((96, SUBS * channels), low_type)
        fill_windows(x_ref, place, p_ref, rows, channels)
        for index, pair in enumerate(all_pairs()):
            result = window_conv(p_ref, band_ref, pair, channels, dot_t)
            for half in range(2):
                number = 2 * index + half
                lanes = sub_lanes(number, channels)
                value = result[:, sub_lanes(half, width)]
                value = value + dot_t(side_grad[0, :, lanes], side_weight[...])
                up_grad[0, :, lanes] = value[:, :channels].astype(low_type)
                skip_grad[0, :, lanes] = value[:, channels:]

        @pl.when(pl.program_id(0) == 0)
        def _():
            total_ref[...] = jnp.zeros_like(total_ref)
            side_weight_grad[...] = jnp.zeros_like(side_weight_grad)

        for number in range(SUBS):
            side_weight_grad[...] += dot(
                left_ref[sub_lanes(number, width), :], side_grad[0, :, sub_lanes(number, channels)]
            )
        add_grads(left_ref, p_ref, total_ref, width, channels)

        @pl.when(pl.program_id(0) == seqs - 1)
        def _():
            if shards * 8 == channels:
                fold_packed(total_ref, weight_grad, width, channels, shards, side_weight_grad)
            else:
                fold_grads(total_ref, weight_grad, width, channels)

    return body


def exchanged(low_pay, high_pay):
    return (passed_along(high_pay, "tok", 1), passed_along(low_pay, "tok", -1))


def with_far(sums, reaches):
    total = sums
    for distance in range(2, reaches + 1):
        for shift_by in (distance, -distance):
            total = total + passed_along(sums.astype(low_type), "tok", shift_by).astype(wide)
    return total


def conv_section(upsampled, skip, edges, cotangent, weights, geometry_in, reaches):
    conv1_weight, conv2_weight, conv3_weight = weights
    seqs, rows, lanes = upsampled.shape
    channels = lanes // SUBS
    width = 2 * channels
    place, owner, crop_t, inverse = geometry_in
    field = ((seqs, rows, lanes), wide)
    low_field = ((seqs, rows, lanes), low_type)

    def pay(count):
        return ((seqs, EDGE, (SUBS + count) * channels), low_type)

    def pay_scratch(count):
        return edge_scratch(seqs, EDGE, (SUBS + count) * channels)

    def table(count):
        return ((seqs, CROP_ROWS, count * channels), wide)

    up_left, up_right, skip_left, skip_right = edges
    shards = lax.axis_size("tok")
    fits = shards * 8 == channels

    def packed_out(blocks):
        return ((shards, (blocks + 1) // 2 * 16, channels), low_type)

    first, side_field, sums, first_left, first_right = kernel_call(
        first_conv_kernel(rows, channels, seqs),
        seqs,
        (upsampled, up_left, up_right, skip, skip_left, skip_right, place, crop_t),
        (conv1_weight, conv3_weight),
        (field, field, table(4)),
        (),
        conv_scratch(rows, width, (12 * width, 2 * channels)) + pay_scratch(4),
        conv_flops(seqs, rows, width, channels),
        landing=(pay(4), pay(4)),
        collective=3,
    )
    second, stats, sums, second_left, second_right = kernel_call(
        second_conv_kernel(rows, channels, seqs),
        seqs,
        (first, first_left, first_right, with_far(sums, reaches), inverse, owner, place, crop_t),
        (conv2_weight,),
        (field, table(4), table(2)),
        (),
        conv_scratch(rows, channels, (12 * channels, 2 * channels)) + pay_scratch(2),
        conv_flops(seqs, rows, channels, channels),
        landing=(pay(2), pay(2)),
        collective=4,
    )
    section_out, grad, second_stats, sums, grad_left, grad_right = kernel_call(
        output_kernel(rows, channels, seqs),
        seqs,
        (
            second, side_field, cotangent, stats, second_left, second_right,
            with_far(sums, reaches), inverse, owner, crop_t,
        ),
        (),
        (low_field, field, table(2), table(3)),
        (),
        pay_scratch(3),
        seqs * rows * lanes * 20,
        landing=(pay(3), pay(3)),
        collective=5,
    )
    first_grad, side_grad, sums, conv2_grad, back_left, back_right = kernel_call(
        second_back_kernel(rows, channels, seqs, shards),
        seqs,
        (
            grad, grad_left, grad_right, with_far(sums, reaches), second, second_left, second_right,
            side_field, first, stats, second_stats, inverse, owner, place, crop_t,
        ),
        (conv2_weight,),
        (field, low_field, table(2)),
        (packed_out(27) if fits else ((27, 1, channels, channels), wide),),
        conv_scratch(rows, channels, (2 * channels, 12 * channels))
        + [
            pltpu.VMEM((SUBS * channels, rows), low_type),
            pltpu.VMEM((9, 2 * channels, 4 * channels), wide),
        ]
        + pay_scratch(2),
        2 * conv_flops(seqs, rows, channels, channels),
        landing=(pay(2), pay(2)),
        collective=6,
    )
    up_grad, skip_grad, conv1_grad, conv3_grad = kernel_call(
        first_back_kernel(rows, channels, seqs, shards),
        seqs,
        (
            first_grad, back_left, back_right, with_far(sums, reaches), first, first_left,
            first_right, stats, inverse, owner, place, side_grad, upsampled, skip,
        ),
        (conv1_weight, conv3_weight),
        (low_field, field),
        (
            packed_out(56) if fits else ((27, 2, channels, channels), wide),
            ((width, channels), wide),
        ),
        conv_scratch(rows, channels, (2 * width, 12 * channels))
        + [
            pltpu.VMEM((SUBS * width, rows), low_type),
            pltpu.VMEM((9, 2 * width, 4 * channels), wide),
        ],
        2 * conv_flops(seqs, rows, channels, width),
    )
    return (section_out, up_grad, skip_grad, conv1_grad, conv2_grad, conv3_grad)


PIECE_BYTES = 2400 * 1024


def bit_count(size):
    return size.bit_length() - 1


def pieces_of(shapes):
    pieces = []
    for index, (shards, rows, lanes) in enumerate(shapes):
        parts = max(1, round(shards * rows * lanes * 2 / PIECE_BYTES))
        while rows % (16 * parts) != 0 and parts > 1:
            parts -= 1
        take = rows // parts
        pieces.extend((index, part * take, take, lanes) for part in range(parts))
    return pieces


def all_of(count):
    return (slice(None),) * count


def reduce_kernel(pieces, arrays, tok_bits, seq_bits):
    phases = tok_bits + seq_bits
    mesh_id = pl.DeviceIdType.MESH

    def body(*refs):
        given = refs[:arrays]
        results = refs[arrays : 2 * arrays]
        count = len(pieces)
        rest = refs[2 * arrays :]
        kept = rest[:count]
        landed = [rest[count + i * phases : count + (i + 1) * phases] for i in range(count)]
        local_sem, send_sem, recv_sem = rest[count + count * phases :]
        tok = lax.axis_index("tok")
        seq = lax.axis_index("seq")

        def bit_of(phase):
            if phase < tok_bits:
                return (tok // (1 << phase)) % 2
            return (seq // (1 << (phase - tok_bits))) % 2

        def partner(phase):
            bit = bit_of(phase)
            if phase < tok_bits:
                return (seq, tok + (1 << phase) * (1 - 2 * bit))
            return (seq + (1 << (phase - tok_bits)) * (1 - 2 * bit), tok)

        barrier = pltpu.get_barrier_semaphore()
        for phase in range(phases):
            pl.semaphore_signal(barrier, inc=1, device_id=partner(phase), device_id_type=mesh_id)
        pl.semaphore_wait(barrier, phases)

        def local_copy(piece):
            index, begin, take, _ = pieces[piece]
            view = given[index].at[all_of(tok_bits - 1) + (bit_of(0), pl.ds(begin, take))]
            return pltpu.make_async_copy(view, kept[piece], local_sem.at[piece])

        def remote_copy(piece, phase):
            index, begin, take, _ = pieces[piece]
            if phase == 0:
                view = given[index].at[all_of(tok_bits - 1) + (1 - bit_of(0), pl.ds(begin, take))]
            elif phase < tok_bits:
                view = landed[piece][phase - 1].at[all_of(tok_bits - 1 - phase) + (1 - bit_of(phase),)]
            else:
                view = landed[piece][phase - 1]
            return pltpu.make_async_remote_copy(
                src_ref=view,
                dst_ref=landed[piece][phase],
                send_sem=send_sem.at[piece, phase],
                recv_sem=recv_sem.at[piece, phase],
                device_id=partner(phase),
                device_id_type=mesh_id,
            )

        def begin(piece):
            remote_copy(piece, 0).start()
            local_copy(piece).start()

        def finish(piece, phase):
            index, first, take, _ = pieces[piece]
            remote_copy(piece, phase).wait_recv()
            got = landed[piece][phase]
            if phase == 0:
                local_copy(piece).wait()

            if phase < tok_bits:
                kept_bits = tok_bits - 1 - phase

                def step(block, carry):
                    at = tuple((block // (1 << bit)) % 2 for bit in reversed(range(kept_bits)))
                    if phase == 0:
                        mine = kept[piece][at]
                    else:
                        mine = landed[piece][phase - 1][at + (bit_of(phase),)]
                    got[at] = got[at] + mine
                    return carry

                lax.fori_loop(0, 1 << kept_bits, step, 0)
            elif phase + 1 < phases:
                got[...] = got[...] + landed[piece][phase - 1][...]
            if phase + 1 < phases:
                remote_copy(piece, phase + 1).start()
            else:
                total = got[...].astype(wide) + landed[piece][phase - 1][...].astype(wide)
                results[index][pl.ds(first, take), :] = total

        begin(0)
        for step in range(count + phases - 1):
            if step + 1 < count:
                begin(step + 1)
            for phase in range(phases):
                if 0 <= step - phase < count:
                    finish(step - phase, phase)
        for piece in range(count):
            for phase in range(phases):
                remote_copy(piece, phase).wait_send()

    return body


def reduced(grads):
    shards = lax.axis_size("tok")
    tok_bits = bit_count(shards)
    seq_bits = bit_count(lax.axis_size("seq"))
    shapes = [g.shape for g in grads]
    pieces = pieces_of(shapes)
    scratch = [
        pltpu.VMEM((2,) * (tok_bits - 1) + (take, lanes), low_type) for _, _, take, lanes in pieces
    ]
    for _, _, take, lanes in pieces:
        for phase in range(tok_bits - 1):
            bits = tok_bits - 1 - phase
            scratch.append(pltpu.VMEM((2,) * bits + (take, lanes), low_type))
        scratch += [pltpu.VMEM((take, lanes), low_type) for _ in range(1 + seq_bits)]
    count, phases = len(pieces), tok_bits + seq_bits
    scratch += [
        pltpu.SemaphoreType.DMA((count,)),
        pltpu.SemaphoreType.DMA((count, phases)),
        pltpu.SemaphoreType.DMA((count, phases)),
    ]
    total = sum(math.prod(s) for s in shapes)
    return pl.pallas_call(
        reduce_kernel(pieces, len(grads), tok_bits, seq_bits),
        in_specs=[pl.BlockSpec(memory_space=pl.ANY)] * len(grads),
        out_specs=[pl.BlockSpec(memory_space=pltpu.VMEM)] * len(grads),
        out_shape=[jax.ShapeDtypeStruct(s[1:], wide) for s in shapes],
        scratch_shapes=scratch,
        compiler_params=pltpu.CompilerParams(
            vmem_limit_bytes=VMEM_LIMIT, collective_id=0, has_side_effects=True
        ),
        cost_estimate=pl.CostEstimate(flops=total, bytes_accessed=4 * total, transcendentals=0),
    )(*[g.reshape((2,) * tok_bits + g.shape[1:]) for g in grads])


def sharded_rows(grad):
    shards = lax.axis_size("tok")
    rows = grad.shape[0] // shards
    grad = grad.astype(low_type)
    if rows % 16 == 0:
        return grad.reshape(shards, rows, grad.shape[1])
    return grad.reshape(shards, rows * grad.shape[1] // 128, 128)


def conv_rows(turned):
    shards = lax.axis_size("tok")
    taps, halves, channels, lanes = turned.shape
    split = turned.reshape(taps, halves, shards, channels // shards, lanes)
    return jnp.moveaxis(split, 2, 0).reshape(shards, -1, lanes)


def conv_share(rows, taps, halves):
    split = rows.reshape(taps, halves, -1, rows.shape[-1])
    return jnp.moveaxis(split, 2, 3).reshape(taps, halves * rows.shape[-1], -1)


def reduced_all(conv_grads, matrices, vectors):
    shards = lax.axis_size("tok")
    parts = [conv_rows(g) for g in conv_grads]
    flat = jnp.concatenate([v.reshape(shards, -1) for v in vectors], axis=1)
    used = flat.shape[1]
    taken = sum(p.shape[1] for p in parts)
    rows = -(-used // 128)
    rows += -(rows + taken) % 16
    flat = jnp.pad(flat, ((0, 0), (0, rows * 128 - used))).reshape(shards, rows, 128)
    packed = jnp.concatenate([p.astype(low_type) for p in parts] + [flat.astype(low_type)], axis=1)
    results = reduced([packed] + [sharded_rows(m) for m in matrices])
    shares = []
    cursor = 0
    for part, grad in zip(parts, conv_grads):
        rows_here = results[0][cursor : cursor + part.shape[1]]
        shares.append(conv_share(rows_here, grad.shape[0], grad.shape[1]))
        cursor += part.shape[1]
    flat = results[0][cursor:].reshape(-1)
    cursor = 0
    pieces = []
    for vector in vectors:
        size = vector.size // shards
        pieces.append(flat[cursor : cursor + size])
        cursor += size
    whole = [r.reshape(-1, m.shape[1]) for r, m in zip(results[1:], matrices)]
    return (shares, whole, pieces)


REACH = 224
QUERY_TILE = 128
CLOSING_LIMIT = 63 * 1024 * 1024


def dot_t(left, right):
    return lax.dot_general(
        left, right, (((1,), (1,)), ((), ())), preferred_element_type=wide
    )


def counted(shape, axis):
    return lax.broadcasted_iota(jnp.int32, shape, axis).astype(wide)


def geometry_kernel(rows, crops):
    reach_rows = rows + 2 * REACH
    tile = min(rows, QUERY_TILE)
    window = tile + 2 * REACH

    def body(side_row, side_column, place, owner, crop_t, inverse, bias, edge_bias):
        first_row = (lax.axis_index("tok") * rows).astype(wide)
        sides_r = side_row[0].astype(wide)
        sides_c = side_column[0].astype(wide)
        volume_r = sides_r * sides_r * sides_r
        volume_c = sides_c * sides_c * sides_c
        shape = (crops, crops)
        start_r = jnp.sum(
            jnp.where(counted(shape, 0) < counted(shape, 1), volume_c, 0.0), axis=0, keepdims=True
        )
        start_c = jnp.sum(
            jnp.where(counted(shape, 1) < counted(shape, 0), volume_r, 0.0), axis=1, keepdims=True
        )

        def inside_of(length, begin):
            at = counted((length, crops), 0) + begin
            return ((at >= start_r) & (at < start_r + volume_r), at)

        wide_inside, _ = inside_of(rows + 2 * EDGE, first_row - EDGE)
        owner[0] = jnp.where(wide_inside, 1.0, 0.0).astype(low_type)
        inside, _ = inside_of(rows, first_row)
        side = jnp.sum(jnp.where(inside, sides_r, 0.0), axis=1, keepdims=True)
        first = jnp.sum(jnp.where(inside, start_r, 0.0), axis=1, keepdims=True)
        own = counted((rows, 1), 0)
        offset = own + first_row - first
        safe = jnp.maximum(side, 1.0)
        row_pos = jnp.floor((offset + 0.5) / (safe * safe))
        offset = offset - row_pos * safe * safe
        column = jnp.floor((offset + 0.5) / safe)
        depth_pos = offset - column * safe
        lane = counted((1, 32), 1)
        step_x = jnp.floor((lane + 0.5) / 9.0)
        step_y = jnp.floor((lane - 9.0 * step_x + 0.5) / 3.0)
        step_z = lane - 9.0 * step_x - 3.0 * step_y - 1.0
        step_x, step_y = (step_x - 1.0, step_y - 1.0)
        valid = None
        for at, step in ((row_pos, step_x), (column, step_y), (depth_pos, step_z)):
            moved = at + step
            here = (moved >= 0.0) & (moved < side)
            valid = here if valid is None else valid & here
        target = own + EDGE + (step_x * safe + step_y) * safe + step_z
        place[0] = jnp.where(valid, target, -1.0).astype(jnp.int32)
        at = counted((crops, rows), 1) + first_row
        inside_t = (at >= start_c) & (at < start_c + volume_c)
        crop_t[0] = jnp.where(inside_t, 1.0, 0.0).astype(low_type)
        inverse[0] = jnp.broadcast_to(1.0 / jnp.maximum(8.0 * volume_c, 1.0), (crops, 128))
        key_inside, _ = inside_of(reach_rows, first_row - REACH)
        key_first = jnp.sum(jnp.where(key_inside, start_r + 1.0, 0.0), axis=1, keepdims=True)
        query_first = jnp.sum(jnp.where(inside_t, start_c + 1.0, 0.0), axis=0, keepdims=True)
        for number in range(rows // tile):
            base = number * tile
            same = key_first[base : base + window] == query_first[:, base : base + tile]
            bias[0, number] = jnp.where(same, 0.0, far_below)
        for side in range(2):
            begin_row = 0 if side == 0 else max(rows - REACH, 0)
            begin = first_row - REACH if side == 0 else first_row + rows
            at = counted((crops, REACH), 1) + begin
            inside_t = (at >= start_c) & (at < start_c + volume_c)
            query_first = jnp.sum(jnp.where(inside_t, start_c + 1.0, 0.0), axis=0, keepdims=True)
            same = key_first[REACH + begin_row : 2 * REACH + begin_row] == query_first
            edge_bias[0, side] = jnp.where(same, 0.0, far_below)

    return body


def geometry_tables(crop_sides, rows):
    seqs, crops = crop_sides.shape
    sides = jnp.pad(crop_sides, ((0, 0), (0, CROP_ROWS - crops)))
    tile = min(rows, QUERY_TILE)
    return kernel_call(
        geometry_kernel(rows, CROP_ROWS),
        seqs,
        (sides[:, None, :], sides[:, :, None]),
        (),
        (
            ((seqs, rows, 32), jnp.int32),
            ((seqs, rows + 2 * EDGE, CROP_ROWS), low_type),
            ((seqs, CROP_ROWS, rows), low_type),
            ((seqs, CROP_ROWS, 128), wide),
            ((seqs, rows // tile, tile + 2 * REACH, tile), wide),
            ((seqs, 2, REACH, REACH), wide),
        ),
        (),
        [],
        0,
    )


def row_of(vector, lanes=slice(None)):
    return vector[lanes].reshape(1, -1)


def normed_rows(values):
    centered = values - jnp.mean(values, axis=-1, keepdims=True)
    variance = jnp.mean(centered * centered, axis=-1, keepdims=True)
    scale = lax.rsqrt(variance + norm_eps)
    return (centered * scale, scale)


def norm_pull(grad, normed, scale, gain):
    inner = grad * gain
    first = jnp.mean(inner, axis=-1, keepdims=True)
    second = jnp.mean(inner * normed, axis=-1, keepdims=True)
    return scale * (inner - first - normed * second)


def gelu_parts(value):
    size = jnp.abs(value) * math.sqrt(0.5)
    ratio = 1.0 / (1.0 + 0.3275911 * size)
    series = 1.061405429
    for term in (-1.453152027, 1.421413741, -0.284496736, 0.254829592):
        series = series * ratio + term
    decay = jnp.exp(-size * size)
    beyond = 0.5 * series * ratio * decay
    cumulative = jnp.where(value >= 0.0, 1.0 - beyond, beyond)
    return (value * cumulative, cumulative + value * decay * (1.0 / math.sqrt(2.0 * math.pi)))


def head_lanes(block, half):
    lane = lax.broadcasted_iota(jnp.int32, block.shape, 1)
    chosen = lane < HEAD_DIM if half == 0 else lane >= HEAD_DIM
    return jnp.where(chosen, block, jnp.zeros_like(block))


def turned(block):
    return jnp.transpose(block.astype(wide))


def forward_kernel(rows, model_width, hidden, seqs, near_given):
    tile = min(rows, QUERY_TILE)
    window = tile + 2 * REACH
    chunk = 768
    scale = 1.0 / math.sqrt(HEAD_DIM)

    def body(*refs):
        tokens, bias = refs[:2]
        if near_given:
            left, right = refs[2:4]
            refs = refs[2:]
        (
            ln1_gain, ln1_bias, qkv_weight, qv_bias, out_bias, ln2_gain, ln2_bias,
            fc1_bias, fc2_bias, all_tokens, skip, out_away, fc1_away, fc2_away, deconv_away,
            normed_out, queries, keys, values, attended, log_totals, resid_out, second_out,
            act_out, slope_out, resid_low, upsampled, up_left, up_right, skip_left, skip_right,
            near_ref, turned_ref, skip_send, skip_recv, near_left, near_right, near_send, near_recv,
            out_weight, fc1_weight, fc2_weight, deconv_weight, weight_sem, *edge_refs,
        ) = refs[2:]
        step = pl.program_id(0)
        pay = Payload(seqs, up_left, up_right, *edge_refs)
        skip_edge = Edge(
            skip.at[:, :EDGE],
            skip.at[:, rows - EDGE :],
            skip_left,
            skip_right,
            skip_send,
            skip_recv,
        )

        def token_edge(number):
            return Edge(
                all_tokens.at[number, :REACH],
                all_tokens.at[number, rows - REACH :],
                near_left.at[number],
                near_right.at[number],
                near_send.at[number],
                near_recv.at[number],
            )

        weight_copies = [
            pltpu.make_async_copy(source, target, weight_sem.at[number])
            for number, (source, target) in enumerate(
                (
                    (out_away, out_weight),
                    (fc1_away, fc1_weight),
                    (fc2_away, fc2_weight),
                    (deconv_away, deconv_weight),
                )
            )
        ]

        def weights_ready(*numbers):
            @pl.when(step == 0)
            def _():
                for number in numbers:
                    weight_copies[number].wait()

        @pl.when(step == 0)
        def _():
            for copy in weight_copies:
                copy.start()

        pay.enter()

        @pl.when(step == 0)
        def _():
            met()
            if near_given:
                skip_edge.start()
            else:
                token_edge(0).start()
                for field, there in zip((near_left, near_right), tok_sides()):

                    @pl.when(jnp.logical_not(there))
                    def _():
                        field[...] = jnp.zeros_like(field)

            for field, there in zip((skip_left, skip_right), tok_sides()):

                @pl.when(jnp.logical_not(there))
                def _():
                    copies = [
                        pltpu.make_async_copy(pay.zero_ref, field.at[n], pay.zero_sem.at[n])
                        for n in range(seqs)
                    ]
                    for copy in copies:
                        copy.start()
                    for copy in copies:
                        copy.wait()

        def put_normed(values, begin):
            normed = normed_rows(values.astype(wide))[0] * row_of(ln1_gain) + row_of(ln1_bias)
            near_ref[begin : begin + values.shape[0], :] = normed.astype(low_type)

        def project(at):
            for number, target in enumerate((queries, keys, values)):
                lanes = sub_lanes(number, model_width)
                found = dot(near_ref[at, :], qkv_weight[:, lanes])
                if number != 1:
                    found = found + qv_bias[number // 2 : number // 2 + 1, :]
                target[0, at, :] = found.astype(low_type)

        own_rows = slice(REACH, REACH + rows)
        put_normed(tokens[0], REACH)
        normed_out[0] = near_ref[own_rows, :]
        project(own_rows)
        if near_given:
            put_normed(left[0], 0)
            put_normed(right[0], REACH + rows)
        else:
            token_edge(step).land()

            @pl.when(step < seqs - 1)
            def _():
                token_edge(step + 1).start()

            @pl.when(step == seqs - 1)
            def _():
                skip_edge.start()

            put_normed(near_left[step], 0)
            put_normed(near_right[step], REACH + rows)
        project(slice(0, REACH))
        project(slice(REACH + rows, 2 * REACH + rows))
        for pair in range(model_width // 128):
            lanes = sub_lanes(pair, 128)
            turned_ref[lanes, :] = turned(values[0, :, lanes]).astype(low_type)
        for number in range(rows // tile):
            base = number * tile
            at = slice(base, base + tile)
            near = slice(base, base + window)
            for pair in range(model_width // 128):
                lanes = sub_lanes(pair, 128)
                query = queries[0, REACH + base : REACH + base + tile, lanes] * scale
                key = keys[0, near, lanes]
                halves = []
                for half in range(2):
                    head = 2 * pair + half
                    scores = dot_t(key, head_lanes(query, half)) + bias[0, number]
                    top = jnp.max(scores, axis=0, keepdims=True)
                    weights = jnp.exp(scores - top)
                    total = jnp.sum(weights, axis=0, keepdims=True)
                    log_totals[0, head : head + 1, at] = top + jnp.log(total)
                    probs = (weights * (1.0 / total)).astype(low_type)
                    value = turned_ref[head * HEAD_DIM : (head + 1) * HEAD_DIM, near]
                    halves.append(dot(value, probs))
                both = jnp.concatenate(halves, axis=0)
                attended[0, at, lanes] = jnp.transpose(both).astype(low_type)
        weights_ready(0)
        resid = tokens[0].astype(wide) + dot(attended[0], out_weight[...]) + row_of(out_bias)
        resid_out[0] = resid
        second = normed_rows(resid)[0] * row_of(ln2_gain) + row_of(ln2_bias)
        second_out[0] = second.astype(low_type)
        weights_ready(1, 2, 3)
        total = resid + row_of(fc2_bias)
        for number in range(hidden // chunk):
            lanes = sub_lanes(number, chunk)
            pre = dot(second_out[0], fc1_weight[:, lanes]) + row_of(fc1_bias, lanes)
            act, slope = gelu_parts(pre)
            act_out[0, :, lanes] = act.astype(low_type)
            slope_out[0, :, lanes] = slope.astype(low_type)
            total = total + dot(act_out[0, :, lanes], fc2_weight[lanes, :])
        resid_low[0] = total.astype(low_type)
        upsampled[0] = dot(resid_low[0], deconv_weight[...]).astype(low_type)
        pay.low[0] = upsampled[0, :EDGE, :]
        pay.high[0] = upsampled[0, rows - EDGE :, :]
        pay.send(True)

        @pl.when(step == seqs - 1)
        def _():
            skip_edge.land()
            skip_edge.sent()
            if not near_given:
                for number in range(seqs):
                    token_edge(number).sent()

    return body


def hidden_back_kernel(rows, model_width, hidden, seqs, linked):
    chunk = 768

    def body(
        up_grad, slope, resid, attended, log_totals,
        deconv_weight, fc2_weight, fc1_weight, out_weight, ln2_gain,
        branch_out, pre_out, resid_grad, mixed_out, pulled_out, stats,
        fc2_sum, fc1_sum, out_sum, gain_sum, shift_sum, *edge_refs,
    ):
        step = pl.program_id(0)
        if linked:
            (
                pulls_left, pulls_right, stats_left, stats_right, pull_keep, stat_keep,
                zero_pull, zero_stat, pull_send, pull_recv, stat_send, stat_recv, zero_sem,
            ) = edge_refs

        def edges(number):
            pull = Edge(
                pull_keep.at[number, :REACH],
                pull_keep.at[number, rows - REACH :],
                pulls_left.at[number],
                pulls_right.at[number],
                pull_send.at[number],
                pull_recv.at[number],
            )
            stat = Edge(
                stat_keep.at[number],
                stat_keep.at[number],
                stats_left.at[number],
                stats_right.at[number],
                stat_send.at[number],
                stat_recv.at[number],
            )
            return (pull, stat)

        if linked:

            @pl.when(step == 0)
            def _():
                greet()
                zero_pull[...] = jnp.zeros_like(zero_pull)
                zero_stat[...] = jnp.zeros_like(zero_stat)
                fields = ((pulls_left, stats_left), (pulls_right, stats_right))
                for (pull, stat), there in zip(fields, tok_sides()):

                    @pl.when(jnp.logical_not(there))
                    def _():
                        copies = []
                        for n in range(seqs):
                            copies += [
                                pltpu.make_async_copy(zero_pull, pull.at[n], zero_sem.at[0, n]),
                                pltpu.make_async_copy(zero_stat, stat.at[n], zero_sem.at[1, n]),
                            ]
                        for copy in copies:
                            copy.start()
                        for copy in copies:
                            copy.wait()

        @pl.when(pl.program_id(0) == 0)
        def _():
            for ref in (fc2_sum, fc1_sum, out_sum, gain_sum, shift_sum):
                ref[...] = jnp.zeros_like(ref)

        def column_sum(field):
            return jnp.sum(field, axis=0, keepdims=True)

        incoming = dot_t(up_grad[0], deconv_weight[...])
        branch = incoming.astype(low_type)
        branch_out[0] = branch
        fc2_sum[...] += column_sum(branch.astype(wide))
        total = None
        for number in range(hidden // chunk):
            lanes = sub_lanes(number, chunk)
            act_grad = dot_t(branch_out[0], fc2_weight[lanes, :])
            pre = (act_grad * slope[0, :, lanes].astype(wide)).astype(low_type)
            pre_out[0, :, lanes] = pre
            fc1_sum[:, lanes] += column_sum(pre.astype(wide))
            term = dot_t(pre_out[0, :, lanes], fc1_weight[:, lanes])
            total = term if total is None else total + term
        normed, norm_scale = normed_rows(resid[0])
        gain_sum[...] += column_sum(total * normed)
        shift_sum[...] += column_sum(total)
        mixed = incoming + norm_pull(total, normed, norm_scale, row_of(ln2_gain))
        resid_grad[0] = mixed
        mixed = mixed.astype(low_type)
        mixed_out[0] = mixed
        out_sum[...] += column_sum(mixed.astype(wide))
        pulled = dot_t(mixed_out[0], out_weight[...]).astype(low_type)
        pulled_out[0] = pulled
        product = pulled.astype(wide) * attended[0].astype(wide)
        lane = lax.broadcasted_iota(jnp.int32, (16, model_width), 1)
        begin = lax.broadcasted_iota(jnp.int32, (16, model_width), 0) * HEAD_DIM
        chosen = (lane >= begin) & (lane < begin + HEAD_DIM)
        chosen = jnp.where(chosen, 1.0, 0.0).astype(low_type)
        inner = None
        for term in three_terms(product):
            part = dot_t(chosen, term)
            inner = part if inner is None else inner + part
        for pair in range(model_width // 128):
            heads = slice(2 * pair, 2 * pair + 2)
            unused = jnp.zeros((4, rows), wide)
            stats[0, pair] = jnp.concatenate([log_totals[0, heads], inner[heads], unused], axis=0)
        if linked:
            pull_keep[step] = pulled
            stat_keep[step] = stats[0]

            @pl.when(step == 0)
            def _():
                met()

            for edge in edges(step):
                edge.start()

            @pl.when(step == seqs - 1)
            def _():
                for number in range(seqs):
                    for edge in edges(number):
                        edge.land()
                for number in range(seqs):
                    for edge in edges(number):
                        edge.sent()

    return body


def attention_back_kernel(rows, model_width):
    tile = min(rows, QUERY_TILE)
    window = tile + 2 * REACH
    scale = 1.0 / math.sqrt(HEAD_DIM)

    def body(
        queries, keys, values, pulls, stats, bias,
        query_grad, key_own, value_own, low_pay, high_pay, near_key, near_value, turned_ref,
    ):
        for pair in range(model_width // 128):
            lanes = sub_lanes(pair, 128)
            turned_ref[lanes, :] = turned(keys[0, :, lanes]).astype(low_type)
        near_key[...] = jnp.zeros_like(near_key)
        near_value[...] = jnp.zeros_like(near_value)
        for number in range(rows // tile):
            base = number * tile
            at = slice(base, base + tile)
            near = slice(base, base + window)
            for pair in range(model_width // 128):
                lanes = sub_lanes(pair, 128)
                query = queries[0, REACH + base : REACH + base + tile, lanes] * scale
                key = keys[0, near, lanes]
                value = values[0, near, lanes]
                halves = []
                for half in range(2):
                    head = 2 * pair + half
                    probs, score_grad, one_query, one_pull = head_unit(
                        key, value, query, pulls[0, at, lanes], bias[0, number],
                        stats[0, pair, half : half + 1, at], stats[0, pair, 2 + half : 3 + half, at],
                        half,
                    )
                    near_key[near, lanes] += dot(score_grad, one_query)
                    near_value[near, lanes] += dot(probs, one_pull)
                    key_turned = turned_ref[head * HEAD_DIM : (head + 1) * HEAD_DIM, near]
                    halves.append(dot(key_turned, score_grad) * scale)
                both = jnp.concatenate(halves, axis=0)
                query_grad[0, at, lanes] = jnp.transpose(both).astype(low_type)
        for field, own_out, begin in (
            (near_key, key_own, 0),
            (near_value, value_own, model_width),
        ):
            lanes = slice(begin, begin + model_width)
            own_out[0] = field[REACH : REACH + rows, :]
            low_pay[0, :, lanes] = field[:REACH, :].astype(low_type)
            high_pay[0, :, lanes] = field[REACH + rows :, :].astype(low_type)

    return body


def token_kernel(rows, model_width):
    def body(
        tokens, resid_grad, query_grad, key_own, value_own, qkv_weight, ln1_gain,
        grad_out, token_grad, bias_sum, gain_sum, shift_sum,
    ):
        @pl.when(pl.program_id(0) == 0)
        def _():
            for ref in (bias_sum, gain_sum, shift_sum):
                ref[...] = jnp.zeros_like(ref)

        grad_out[0, :, :model_width] = query_grad[0]
        for number, own in enumerate((key_own, value_own)):
            to = sub_lanes(number + 1, model_width)
            grad_out[0, :, to] = own[0].astype(low_type)
        bias_sum[...] += jnp.sum(grad_out[0].astype(wide), axis=0, keepdims=True)
        total = dot_t(grad_out[0], qkv_weight[...])
        normed, norm_scale = normed_rows(tokens[0].astype(wide))
        gain_sum[...] += jnp.sum(total * normed, axis=0, keepdims=True)
        shift_sum[...] += jnp.sum(total, axis=0, keepdims=True)
        token_grad[0] = resid_grad[0] + norm_pull(total, normed, norm_scale, row_of(ln1_gain))

    return body


def near_rows(field):
    rows = field.shape[1]
    lefts, rights = ([], [])
    distance, missing = (1, REACH)
    while missing > 0:
        take = min(rows, missing)
        lefts.insert(0, passed_along(field[:, rows - take :], "tok", distance))
        rights.append(passed_along(field[:, :take], "tok", -distance))
        distance, missing = (distance + 1, missing - take)
    if len(lefts) == 1:
        return (lefts[0], rights[0])
    return (jnp.concatenate(lefts, axis=1), jnp.concatenate(rights, axis=1))


def returned_rows(own, low_pay, high_pay):
    rows = own.shape[1]
    distance, missing = (1, REACH)
    while missing > 0:
        take = min(rows, missing)
        low_piece = low_pay[:, missing - take : missing]
        begin = REACH - missing
        high_piece = high_pay[:, begin : begin + take]
        own = own.at[:, rows - take :].add(passed_along(low_piece, "tok", -distance).astype(wide))
        own = own.at[:, :take].add(passed_along(high_piece, "tok", distance).astype(wide))
        distance, missing = (distance + 1, missing - take)
    return own


def head_unit(key, value, query, pulled, bias, log_total, inner, half):
    one_query = head_lanes(query, half)
    one_pull = head_lanes(pulled, half)
    scores = dot_t(key, one_query) + bias
    probs = jnp.exp(scores - log_total)
    probs_grad = dot_t(value, one_pull)
    score_grad = (probs * (probs_grad - inner)).astype(low_type)
    return (probs.astype(low_type), score_grad, one_query, one_pull)


def half_slice(piece, half):
    _, _, rows, _, lanes, axis = piece
    if isinstance(half, int) and axis == 0:
        return (slice(half * (rows // 2), (half + 1) * (rows // 2)), slice(None))
    if isinstance(half, int):
        return (slice(None), slice(half * (lanes // 2), (half + 1) * (lanes // 2)))
    if axis == 0:
        return (pl.ds(pl.multiple_of(half * (rows // 2), 16), rows // 2), slice(None))
    return (slice(None), pl.ds(pl.multiple_of(half * (lanes // 2), 128), lanes // 2))


def half_shape(piece):
    _, _, rows, _, lanes, axis = piece
    return (rows // 2, lanes) if axis == 0 else (rows, lanes // 2)


def closing_pieces(shapes):
    first, second, deconv, fc2, fc1, out, qkv = shapes
    pieces = [(1, 0, second[0], 0, second[1], 0)]
    pieces += [(0, part * first[0] // 2, first[0] // 2, 0, first[1], 0) for part in range(2)]
    pieces += [(2, 0, 48, lane, 512, 1) for lane in range(0, deconv[1], 512)]
    pieces += [(3, row, 48, 0, 768, 1) for row in range(0, fc2[0], 48)]
    pieces += [(4, 0, 48, lane, 768, 1) for lane in range(0, fc1[1], 768)]
    pieces += [(5, 0, 48, 0, 768, 1)]
    pieces += [(6, 0, 48, lane, 768, 1) for lane in range(0, qkv[1], 768)]
    return pieces


def closing_kernel(rows, model_width, hidden, seqs, shapes, bits, held_count):
    pieces = closing_pieces(shapes)
    count = len(pieces)
    stored = 3
    slots = 3
    mesh_id = pl.DeviceIdType.MESH
    tile = min(rows, QUERY_TILE)
    window = tile + 2 * REACH
    reach_rows = rows + 2 * REACH
    scale = 1.0 / math.sqrt(HEAD_DIM)
    pairs = model_width // 128
    phases = bits + 2
    vector_phases = bits + 1
    first_order = (0, 2, 1) + tuple(range(3, bits))
    lines = seqs * rows
    spare_row = hidden
    own_scratch = 24
    span = 256
    items = seqs * (model_width // span)

    def body(*refs):
        packed = refs[:2]
        windows = refs[2:5]
        sources = refs[5:13]
        away = refs[13 : 13 + held_count]
        ln1_gain, *early_lines, long_line = refs[13 + held_count : 19 + held_count]
        rest = refs[19 + held_count :]
        results = rest[: len(shapes)]
        token_grad, vector_out = rest[len(shapes) : len(shapes) + 2]
        rest = rest[len(shapes) + 2 :]
        held = rest[:held_count]
        (
            pulls, pulls_left, pulls_right, stats, stats_left, stats_right, bias, edge_bias,
            normed_low, tokens, qkv_weight,
        ) = held
        rest = rest[held_count:]
        (
            arena, near, key_turned, key_total, value_total, grads, normed_turned, products,
            kept_first, kept_second, kept_third, vectors, vectors_landed, near_sem, held_sem, fetch_sem,
            local_sem, core_send, core_recv, send_sem, recv_sem, vector_send, vector_recv, spare,
        ) = rest[:own_scratch]
        del spare
        kept = (kept_first, kept_second, kept_third)
        landed = [
            rest[own_scratch + i * phases : own_scratch + (i + 1) * phases] for i in range(count)
        ]
        tok = lax.axis_index("tok")
        seq = lax.axis_index("seq")
        core = tok % 2

        def tok_bit(bit):
            return (tok // (1 << bit)) % 2

        def tok_step(bit):
            return (1 << bit) * (1 - 2 * tok_bit(bit))

        def kept_bit(phase):
            first = seq if phase == 1 else tok_bit(first_order[phase - 1])
            second = tok_bit(phase) if phase < bits else seq
            return (1 - core) * first + core * second

        def partner(phase):
            if phase == 0:
                return (seq, tok + tok_step(0))
            if phase > bits:
                return (1 - seq, tok)
            first = 0 if phase == 1 else tok_step(first_order[phase - 1])
            second = tok_step(phase) if phase < bits else 0
            across = 0
            if phase == 1:
                across = 1 - core
            if phase == bits:
                across = core
            return (
                seq + across * (1 - 2 * seq),
                tok + (1 - core) * first + core * second,
            )

        def vector_partner(phase):
            if phase < bits:
                return (seq, tok + tok_step(phase))
            return (1 - seq, tok)

        barrier = pltpu.get_barrier_semaphore()
        for phase in range(vector_phases):
            pl.semaphore_signal(
                barrier, inc=1, device_id=vector_partner(phase), device_id_type=mesh_id
            )

        def held_copies():
            return [
                pltpu.make_async_copy(source, target, held_sem.at[number])
                for number, (source, target) in enumerate(zip(away, held))
            ]

        def core_copy(number, half, receiver):
            index, begin, take, lane, lanes, axis = pieces[number]
            at = (slice(None),) * (bits - 1) + (1 - core,)
            if axis == 0:
                part = (pl.ds(begin + half * (take // 2), take // 2), slice(None))
                view = packed[index].at[at + part]
            else:
                slot = (number - stored) % slots
                part = (slice(None), pl.ds(half * (lanes // 2), lanes // 2))
                view = products.at[(slot,) + at + part]
            if receiver == 0:
                to = landed[number][0].at[(slice(None),) * (bits - 1) + (half,)]
            else:
                to = landed[number][0].at[half]
            return pltpu.make_async_remote_copy(
                src_ref=view,
                dst_ref=to,
                send_sem=core_send.at[number, half],
                recv_sem=core_recv.at[number, half],
                device_id=partner(0),
                device_id_type=mesh_id,
            )

        def local_copy(number):
            index, begin, take, _, _, _ = pieces[number]
            at = (slice(None),) * (bits - 1) + (core, pl.ds(begin, take))
            return pltpu.make_async_copy(packed[index].at[at], kept[number], local_sem.at[number])

        def remote_copy(number, phase, mine=1):
            if phase > bits:
                view = landed[number][bits]
            elif phase == 2 and mine == 0:
                at = (slice(None),) * (bits - 3) + (1 - kept_bit(phase),)
                view = landed[number][1].at[at]
            else:
                view = landed[number][phase - 1].at[
                    (slice(None),) * (bits - phase) + (1 - kept_bit(phase),)
                ]
            return pltpu.make_async_remote_copy(
                src_ref=view,
                dst_ref=landed[number][phase],
                send_sem=send_sem.at[number, phase - 1],
                recv_sem=recv_sem.at[number, phase - 1],
                device_id=partner(phase),
                device_id_type=mesh_id,
            )

        def begin(number):
            for half in range(2):
                for mine in range(2):

                    @pl.when(core == mine)
                    def _():
                        core_copy(number, half, 1 - mine).start()

            if number < stored:
                local_copy(number).start()

        def start_copy(number, phase):
            if phase != 2:
                remote_copy(number, phase).start()
                return
            for mine in range(2):

                @pl.when(core == mine)
                def _():
                    remote_copy(number, phase, mine).start()

        def bits_of(flat, length):
            return tuple((flat // (1 << bit)) % 2 for bit in reversed(range(length)))

        def finish(number, phase):
            piece = pieces[number]
            index, first, take, lane, lanes, axis = piece
            if phase == 0:
                for half in range(2):
                    for mine in range(2):

                        @pl.when(core == mine)
                        def _():
                            core_copy(number, half, mine).wait_recv()

                if number < stored:
                    local_copy(number).wait()
                blocks = 1 << (bits - 1)

                def step(block, carry):
                    at = bits_of(block, bits - 1)
                    for half in range(2):
                        flat = (1 - core) * (2 * block + half) + core * (blocks * half + block)
                        to = bits_of(flat, bits)
                        part = half_slice(piece, half)
                        if number < stored:
                            mine = kept[number][at + part]
                        else:
                            mine = products[((number - stored) % slots,) + at + (core,) + part]
                        landed[number][0][to] = landed[number][0][to] + mine
                    return carry

                lax.fori_loop(0, blocks, step, 0)
                return
            remote_copy(number, phase).wait_recv()
            got = landed[number][phase]
            if phase <= bits:
                before = landed[number][phase - 1]

                def step(block, carry):
                    at = bits_of(block, bits - phase)
                    keep = kept_bit(phase)
                    from_at = at + (keep,)
                    if phase == 2:
                        from_at = at[:-1] + (
                            (1 - core) * keep + core * at[-1],
                            (1 - core) * at[-1] + core * keep,
                        )
                    got[at] = got[at] + before[from_at]
                    return carry

                if phase < bits:
                    lax.fori_loop(0, 1 << (bits - phase), step, 0)
                else:
                    got[...] = got[...] + before[kept_bit(phase)]
                start_copy(number, phase + 1)
                return
            height, length = half_shape(piece)
            for half, value in ((seq, landed[number][bits]), (1 - seq, got)):
                if axis == 0:
                    at = (pl.ds(pl.multiple_of(first + half * height, 8), height), slice(None))
                else:
                    at = (pl.ds(first, take), pl.ds(pl.multiple_of(lane + half * length, 128), length))
                results[index][at] = value[...].astype(wide)

        def near_copies(item):
            group, number = divmod(item, seqs)
            return [
                pltpu.make_async_copy(
                    source.at[number, :, pl.ds(group * span, span)],
                    near.at[item % 2, field],
                    near_sem.at[item % 2, field],
                )
                for field, source in enumerate(windows)
            ]

        def pair_places(group, pair):
            lanes = pl.ds(pl.multiple_of(pair * 128, 128), 128)
            whole = pl.ds(pl.multiple_of(group * span + pair * 128, 128), 128)
            return (lanes, whole, group * (span // 128) + pair)

        def own_segment(item, base):
            group, number = divmod(item, seqs)
            slot = item % 2
            own = slice(REACH + base, REACH + base + tile)
            near_rows_at = slice(base, base + window)
            inside = slice(REACH - base, REACH - base + rows)

            def step(pair, carry):
                lanes, whole, heads = pair_places(group, pair)
                query = near[slot, 0, own, lanes] * scale
                key = near[slot, 1, near_rows_at, lanes]
                value = near[slot, 2, near_rows_at, lanes]
                pulled = pulls[number, base : base + tile, whole]
                key_term, value_term, halves = (None, None, [])
                for half in range(2):
                    log_total = stats[number, heads, half : half + 1, base : base + tile]
                    inner = stats[number, heads, 2 + half : 3 + half, base : base + tile]
                    probs, score_grad, one_query, one_pull = head_unit(
                        key, value, query, pulled, bias[number, base // tile], log_total, inner, half
                    )
                    here = dot(score_grad[inside], one_query)
                    key_term = here if key_term is None else key_term + here
                    here = dot(probs[inside], one_pull)
                    value_term = here if value_term is None else value_term + here
                    begin_row = pair * 128 + half * HEAD_DIM
                    feature = pl.ds(pl.multiple_of(begin_row, HEAD_DIM), HEAD_DIM)
                    halves.append(dot(key_turned[feature, near_rows_at], score_grad) * scale)
                if base == 0:
                    key_total[:, lanes] = key_term
                    value_total[:, lanes] = value_term
                else:
                    key_total[:, lanes] += key_term
                    value_total[:, lanes] += value_term
                both = jnp.transpose(jnp.concatenate(halves, axis=0)).astype(low_type)
                grads[number * rows + base : number * rows + base + tile, whole] = both
                return carry

            lax.fori_loop(0, span // 128, step, 0)

        def edge_segment(item, side):
            group, number = divmod(item, seqs)
            slot = item % 2
            from_rows = slice(0, REACH) if side == 0 else slice(REACH + rows, reach_rows)
            begin_row = 0 if side == 0 else rows - REACH
            at = slice(begin_row, begin_row + REACH)
            key_rows = slice(REACH + begin_row, 2 * REACH + begin_row)
            columns = slice(rows - REACH, rows) if side == 0 else slice(0, REACH)
            pull_ref, stat_ref = ((pulls_left, stats_left), (pulls_right, stats_right))[side]

            def step(pair, carry):
                lanes, whole, heads = pair_places(group, pair)
                query = near[slot, 0, from_rows, lanes] * scale
                key = near[slot, 1, key_rows, lanes]
                value = near[slot, 2, key_rows, lanes]
                pulled = pull_ref[number, :, whole]
                key_term, value_term = (None, None)
                for half in range(2):
                    log_total = stat_ref[number, heads, half : half + 1, :][:, columns]
                    inner = stat_ref[number, heads, 2 + half : 3 + half, :][:, columns]
                    probs, score_grad, one_query, one_pull = head_unit(
                        key, value, query, pulled, edge_bias[number, side], log_total, inner, half
                    )
                    here = dot(score_grad, one_query)
                    key_term = here if key_term is None else key_term + here
                    here = dot(probs, one_pull)
                    value_term = here if value_term is None else value_term + here
                key_total[at, lanes] += key_term
                value_total[at, lanes] += value_term
                return carry

            lax.fori_loop(0, span // 128, step, 0)

        def open_item(item):
            for copy in near_copies(item):
                copy.wait()
            if item + 1 < items:
                for copy in near_copies(item + 1):
                    copy.start()
            for block in range(span // 128):
                lanes = sub_lanes(block, 128)
                key_turned[lanes, :] = turned(near[item % 2, 1, :, lanes]).astype(low_type)

        def close_item(item):
            group, number = divmod(item, seqs)
            at = slice(number * rows, (number + 1) * rows)
            for part, total in ((1, key_total), (2, value_total)):
                lanes = pl.ds(part * model_width + group * span, span)
                grads[at, lanes] = total[...].astype(low_type)

        def group_grads(group):
            parts = [
                grads[:, part * model_width + group * span : part * model_width + (group + 1) * span]
                for part in range(3)
            ]
            return jnp.concatenate(parts, axis=1)

        def product(number, left_rows, right):
            lanes = pieces[number][4]
            slot = (number - stored) % slots
            shard_rows = model_width >> bits
            group = (1 << bits) // 2

            def step(part, carry):
                begin_row = pl.multiple_of(part * group * shard_rows, 16)
                found = dot(left_rows(begin_row, group * shard_rows), right()).astype(low_type)
                for shard in range(group):
                    at = bits_of(part * group + shard, bits)
                    block = found[shard * shard_rows : (shard + 1) * shard_rows]
                    products[(slot,) + at + (slice(None), slice(0, lanes))] = block
                return carry

            lax.fori_loop(0, 2, step, 0)

        def token_segment(number):
            at = slice(number * rows, (number + 1) * rows)
            total = dot_t(grads[at, :], qkv_weight[...])
            normed, norm_scale = normed_rows(tokens[number].astype(wide))
            vectors[0, 0:1, :] += jnp.sum(total * normed, axis=0, keepdims=True)
            vectors[0, 1:2, :] += jnp.sum(total, axis=0, keepdims=True)
            for row, part in ((2, 0), (3, 2)):
                field = grads[at, sub_lanes(part, model_width)].astype(wide)
                vectors[0, row : row + 1, :] += jnp.sum(field, axis=0, keepdims=True)
            pull = norm_pull(total, normed, norm_scale, row_of(ln1_gain))
            token_grad[number] = pull

        def vector_copy(phase):
            return pltpu.make_async_remote_copy(
                src_ref=vectors.at[phase],
                dst_ref=vectors_landed.at[phase],
                send_sem=vector_send.at[phase],
                recv_sem=vector_recv.at[phase],
                device_id=vector_partner(phase),
                device_id_type=mesh_id,
            )

        def finish_vector(phase):
            vector_copy(phase).wait_recv()
            if phase + 1 < vector_phases:
                vectors[phase + 1] = vectors[phase] + vectors_landed[phase]
                vector_copy(phase + 1).start()
            else:
                vector_out[...] = vectors[phase] + vectors_landed[phase]

        resid_low, up_grad, act, branch, normed_two, pre, attended, mixed = sources
        fetches = [(resid_low, 0, model_width)]
        fetches += [(up_grad, lane, 512) for lane in range(0, up_grad.shape[1], 512)]
        fetches += [(act, lane, model_width) for lane in range(0, hidden, model_width)]
        fetches += [(branch, 0, model_width), (normed_two, 0, model_width)]
        fetches += [(pre, lane, model_width) for lane in range(0, hidden, model_width)]
        fetches += [(attended, 0, model_width), (mixed, 0, model_width)]

        def fetch(number):
            source, lane, lanes = fetches[number]
            to = pl.ds((number % 3) * model_width, lanes)
            return pltpu.make_async_copy(
                source.at[:, pl.ds(lane, lanes)], grads.at[:, to], fetch_sem.at[number]
            )

        def fetched(number):
            lanes = fetches[number][2]
            begin_lane = (number % 3) * model_width
            return lambda: grads[:, begin_lane : begin_lane + lanes]

        def turn_fetched(number, chunk=None):
            begin_lane = (number % 3) * model_width

            def step(block, carry):
                lanes = pl.ds(pl.multiple_of(begin_lane + block * 128, 128), 128)
                found = turned(grads[:, lanes]).astype(low_type)
                if chunk is None:
                    at = pl.ds(pl.multiple_of(spare_row + block * 128, 128), 128)
                    arena[at, :] = found
                else:
                    shard_rows = hidden >> bits
                    for granule in range(8):
                        feature = chunk * model_width + block * 128 + granule * 16
                        shard, inner = (feature // shard_rows, feature % shard_rows)
                        to = (inner // 48) * model_width + shard * 48 + inner % 48
                        at = pl.ds(pl.multiple_of(to, 16), 16)
                        arena[at, :] = found[granule * 16 : (granule + 1) * 16]
                return carry

            lax.fori_loop(0, pairs, step, 0)

        def arena_rows(base):
            return lambda begin_row, take: arena[pl.ds(pl.multiple_of(base + begin_row, 16), take), :]

        def turned_rows(begin_row, take):
            return normed_turned[pl.ds(begin_row, take), :]

        state = {"now": 0.0, "link": 0.0, "flying": 0}
        events = []
        waiting = []
        sent = set()
        sizes = [p[2] * p[4] / (48.0 * 768.0) for p in pieces]

        def one_event():
            events.sort()
            ready, number, phase = events.pop(0)
            state["now"] = max(state["now"], ready)
            if number == count:
                finish_vector(phase)
                if phase + 1 < vector_phases:
                    events.append((state["now"] + 2.5, number, phase + 1))
                return
            finish(number, phase)
            if phase == 0:
                waiting.append(number)
            elif phase + 1 < phases:
                cost = (6.0, 5.0, 4.0, 3.0, 2.0)[min(phase - 1, 4)]
                events.append((state["now"] + 2.5 + cost * sizes[number], number, phase + 1))
            if phase == 1:
                state["flying"] -= 1
            while waiting and state["flying"] < 4:
                chosen = waiting.pop(0)
                start_copy(chosen, 1)
                state["flying"] += 1
                start = max(state["now"], state["link"])
                state["link"] = start + 4.0 * sizes[chosen]
                events.append((state["link"] + 1.0, chosen, 1))

        def pump(spent):
            state["now"] += spent
            while events and min(events)[0] <= state["now"]:
                one_event()

        def open_piece(number):
            begin(number)
            events.append((state["now"] + 2.5 + 2.0 * sizes[number], number, 0))

        def make_product(number, left_rows, right):
            before = number - slots
            if before >= stored:
                while any(e[1] == before and e[2] == 0 for e in events):
                    one_event()
                for half in range(2):
                    core_copy(before, half, 0).wait_send()
                    sent.add((before, half))
            product(number, left_rows, right)
            open_piece(number)
            pump(1.2)

        vectors[0, 0:8, :] = jnp.zeros((8, model_width), wide)
        for row, line in enumerate(early_lines):
            vectors[0, 8 + row : 9 + row, :] = line[...]
        for row in range(hidden // model_width):
            vectors[0, 12 + row : 13 + row, :] = long_line[:, sub_lanes(row, model_width)]
        for number in range(3):
            fetch(number).start()
        pl.semaphore_wait(barrier, vector_phases)
        for number in range(stored):
            open_piece(number)
        for copy in held_copies():
            copy.start()
        cursor = 0
        piece = stored

        def used():
            if cursor + 3 < len(fetches):
                fetch(cursor + 3).start()
            return cursor + 1

        def turn_next(chunk=None):
            fetch(cursor).wait()
            turn_fetched(cursor, chunk)
            pump(1.0)

        def product_next(number, left_rows):
            fetch(cursor).wait()
            make_product(number, left_rows, fetched(cursor))

        turn_next()
        cursor = used()
        for _ in range(up_grad.shape[1] // 512):
            product_next(piece, arena_rows(spare_row))
            cursor, piece = (used(), piece + 1)
        for chunk in range(hidden // model_width):
            turn_next(chunk)
            cursor = used()
        fetch(cursor).wait()
        for part in range(hidden // model_width):
            make_product(piece, arena_rows(part * model_width), fetched(cursor))
            piece += 1
        cursor = used()
        turn_next()
        cursor = used()
        for _ in range(hidden // model_width):
            product_next(piece, arena_rows(spare_row))
            cursor, piece = (used(), piece + 1)
        turn_next()
        cursor = used()
        product_next(piece, arena_rows(spare_row))
        cursor, piece = (used(), piece + 1)
        for copy in near_copies(0):
            copy.start()
        for copy in held_copies():
            copy.wait()
        for line in range(seqs):

            def turn_normed(column, carry):
                lanes = pl.ds(pl.multiple_of(column * 128, 128), 128)
                block = turned(normed_low[line, :, lanes]).astype(low_type)
                normed_turned[lanes, line * rows : (line + 1) * rows] = block
                return carry

            lax.fori_loop(0, pairs, turn_normed, 0)
        pump(1.5)
        for item in range(items):
            open_item(item)
            for base in range(0, rows, tile):
                own_segment(item, base)
                pump(1.8)
            for side in range(2):
                edge_segment(item, side)
                pump(1.3)
            close_item(item)
            if item % seqs == seqs - 1:
                make_product(piece, turned_rows, partial(group_grads, item // seqs))
                piece += 1
        for number in range(seqs):
            token_segment(number)
            pump(3.0)
        vector_copy(0).start()
        events.append((state["now"] + 2.5, count, 0))
        while events:
            one_event()
        for number in range(count):
            for half in range(2):
                if (number, half) not in sent:
                    core_copy(number, half, 0).wait_send()
            for phase in range(1, phases):
                remote_copy(number, phase).wait_send()
        for phase in range(vector_phases):
            vector_copy(phase).wait_send()

    fetch_count = 7 + 2 * (hidden // model_width) - 2 + shapes[2][1] // 512
    scratch = [
        pltpu.VMEM((hidden + model_width, model_width), low_type),
        pltpu.VMEM((2, 3, reach_rows, span), low_type),
        pltpu.VMEM((span, reach_rows), low_type),
        pltpu.VMEM((rows, span), wide),
        pltpu.VMEM((rows, span), wide),
        pltpu.VMEM((lines, 3 * model_width), low_type),
        pltpu.VMEM((model_width, lines), low_type),
        pltpu.VMEM((slots,) + (2,) * bits + (48, 768), low_type),
        pltpu.VMEM((2,) * (bits - 1) + (pieces[0][2], pieces[0][4]), low_type),
        pltpu.VMEM((2,) * (bits - 1) + (pieces[1][2], pieces[1][4]), low_type),
        pltpu.VMEM((2,) * (bits - 1) + (pieces[2][2], pieces[2][4]), low_type),
        pltpu.VMEM((vector_phases, 16, model_width), wide),
        pltpu.VMEM((vector_phases, 16, model_width), wide),
        pltpu.SemaphoreType.DMA((2, 3)),
        pltpu.SemaphoreType.DMA((held_count,)),
        pltpu.SemaphoreType.DMA((fetch_count,)),
        pltpu.SemaphoreType.DMA((stored,)),
        pltpu.SemaphoreType.DMA((count, 2)),
        pltpu.SemaphoreType.DMA((count, 2)),
        pltpu.SemaphoreType.DMA((count, phases - 1)),
        pltpu.SemaphoreType.DMA((count, phases - 1)),
        pltpu.SemaphoreType.DMA((vector_phases,)),
        pltpu.SemaphoreType.DMA((vector_phases,)),
        pltpu.SemaphoreType.DMA((1,)),
    ]
    for piece in pieces:
        block = half_shape(piece)
        scratch += [pltpu.VMEM((2,) * (bits - phase) + block, low_type) for phase in range(bits + 1)]
        scratch.append(pltpu.VMEM(block, low_type))
    return (body, scratch)


def closing(packed, windows, sources, held, small):
    shards = lax.axis_size("tok")
    bits = bit_count(shards)
    tokens, qkv_weight = (held[9], held[10])
    seqs, rows, model_width = tokens.shape
    hidden = sources[2].shape[1]
    shapes = [
        packed[0].shape[1:],
        packed[1].shape[1:],
        (model_width // shards, sources[1].shape[1]),
        (hidden // shards, model_width),
        (model_width // shards, hidden),
        (model_width // shards, model_width),
        (model_width // shards, qkv_weight.shape[1]),
    ]
    body, scratch = closing_kernel(
        rows, model_width, hidden, seqs, shapes, bits, len(held)
    )
    inside = pl.BlockSpec(memory_space=pltpu.VMEM)
    far = pl.BlockSpec(memory_space=pl.ANY)
    out_shape = [jax.ShapeDtypeStruct(s, wide) for s in shapes]
    out_shape.append(jax.ShapeDtypeStruct(tokens.shape, wide))
    out_shape.append(jax.ShapeDtypeStruct((16, model_width), wide))
    away = [p.reshape((2,) * bits + p.shape[1:]) for p in packed]
    away += list(windows) + list(sources) + list(held)
    return pl.pallas_call(
        body,
        in_specs=[far] * len(away) + [inside] * len(small),
        out_specs=[inside] * len(out_shape),
        out_shape=out_shape,
        scratch_shapes=[pltpu.VMEM(f.shape, f.dtype) for f in held] + scratch,
        compiler_params=pltpu.CompilerParams(
            vmem_limit_bytes=CLOSING_LIMIT, collective_id=1, has_side_effects=True
        ),
        cost_estimate=pl.CostEstimate(
            flops=50 * 10**9, bytes_accessed=60 * 10**6, transcendentals=0
        ),
    )(*away, *small)


def local(
    tokens,
    skip_features,
    crop_sides,
    ln1_gain,
    ln1_bias,
    qkv_weight,
    qv_bias,
    out_weight,
    out_bias,
    ln2_gain,
    ln2_bias,
    fc1_weight,
    fc1_bias,
    fc2_weight,
    fc2_bias,
    deconv_weight,
    conv1_weight,
    conv2_weight,
    conv3_weight,
    cotangent,
):
    seq_count, row_count, model_width = tokens.shape
    channels = conv2_weight.shape[2]
    hidden = fc1_weight.shape[1]
    reaches = (key_reach + row_count - 1) // row_count
    reach_rows = row_count + 2 * REACH
    near_given = row_count < REACH
    near = near_rows(tokens) if near_given else ()
    near_block = (seq_count, 16 if near_given else REACH, model_width)
    skip = skip_features.reshape(seq_count, row_count, 8 * channels)
    edge_block = ((seq_count, EDGE, 8 * channels), low_type)
    place, owner, crop_t, inverse, bias, edge_bias = geometry_tables(crop_sides, row_count)

    def block(lanes, kind, rows=row_count):
        return ((seq_count, rows, lanes), kind)

    matrix_flops = 2 * seq_count * row_count * model_width
    (
        normed_low, queries, keys, values, attended, log_totals, resid_one, normed_two,
        act_low, slope_low, resid_low, upsampled, *edges,
    ) = kernel_call(
        forward_kernel(row_count, model_width, hidden, seq_count, near_given),
        seq_count,
        (tokens, bias) + tuple(near),
        (
            ln1_gain, ln1_bias, qkv_weight, qv_bias, out_bias, ln2_gain, ln2_bias, fc1_bias, fc2_bias,
        ),
        (
            block(model_width, low_type),
            block(model_width, low_type, reach_rows),
            block(model_width, low_type, reach_rows),
            block(model_width, low_type, reach_rows),
            block(model_width, low_type),
            block(row_count, wide, 16),
            block(model_width, wide),
            block(model_width, low_type),
            block(hidden, low_type),
            block(hidden, low_type),
            block(model_width, low_type),
            block(8 * channels, low_type),
        ),
        (),
        [
            pltpu.VMEM((reach_rows, model_width), low_type),
            pltpu.VMEM((model_width, reach_rows), low_type),
            pltpu.SemaphoreType.DMA((2,)),
            pltpu.SemaphoreType.DMA((2,)),
            pltpu.VMEM(near_block, low_type),
            pltpu.VMEM(near_block, low_type),
            pltpu.SemaphoreType.DMA((seq_count, 2)),
            pltpu.SemaphoreType.DMA((seq_count, 2)),
            pltpu.VMEM(out_weight.shape, low_type),
            pltpu.VMEM(fc1_weight.shape, low_type),
            pltpu.VMEM(fc2_weight.shape, low_type),
            pltpu.VMEM(deconv_weight.shape, low_type),
            pltpu.SemaphoreType.DMA((4,)),
        ]
        + edge_scratch(seq_count, EDGE, 8 * channels),
        matrix_flops * (8 * model_width + 2 * hidden + 8 * channels),
        away=(tokens, skip, out_weight, fc1_weight, fc2_weight, deconv_weight),
        landing=(edge_block,) * 4,
        collective=2,
    )
    section_out, up_grad, skip_grad, conv1_grad, conv2_grad, conv3_grad = conv_section(
        upsampled,
        skip,
        edges,
        cotangent.reshape(seq_count, row_count, 8 * channels),
        (conv1_weight, conv2_weight, conv3_weight),
        (place, owner, crop_t, inverse),
        reaches,
    )
    section_out = section_out.reshape(seq_count, row_count, 8, channels)
    skip_grad = skip_grad.reshape(seq_count, row_count, 8, channels)
    shards = lax.axis_size("tok")
    linked = (
        row_count >= REACH
        and lax.axis_size("seq") == 2
        and model_width // shards == 48
        and shards * 8 == channels
    )
    pairs = model_width // 128
    pull_block = ((seq_count, REACH, model_width), low_type)
    stat_block = ((seq_count, pairs, 8, row_count), wide)
    (
        branch_low, pre_low, resid_grad, mixed_low, pulled, stats,
        fc2_bias_grad, fc1_bias_grad, out_bias_grad, ln2_gain_grad, ln2_bias_grad, *near_back,
    ) = kernel_call(
        hidden_back_kernel(row_count, model_width, hidden, seq_count, linked),
        seq_count,
        (up_grad, slope_low, resid_one, attended, log_totals),
        (deconv_weight, fc2_weight, fc1_weight, out_weight, ln2_gain),
        (
            block(model_width, low_type),
            block(hidden, low_type),
            block(model_width, wide),
            block(model_width, low_type),
            block(model_width, low_type),
            stat_block,
        ),
        (
            ((1, model_width), wide),
            ((1, hidden), wide),
            ((1, model_width), wide),
            ((1, model_width), wide),
            ((1, model_width), wide),
        ),
        [
            pltpu.VMEM((seq_count, row_count, model_width), low_type),
            pltpu.VMEM(*stat_block),
            pltpu.VMEM((REACH, model_width), low_type),
            pltpu.VMEM(stat_block[0][1:], wide),
            pltpu.SemaphoreType.DMA((seq_count, 2)),
            pltpu.SemaphoreType.DMA((seq_count, 2)),
            pltpu.SemaphoreType.DMA((seq_count, 2)),
            pltpu.SemaphoreType.DMA((seq_count, 2)),
            pltpu.SemaphoreType.DMA((2, seq_count)),
        ]
        if linked
        else [],
        matrix_flops * (model_width + 2 * hidden + 8 * channels),
        landing=(pull_block, pull_block, stat_block, stat_block) if linked else (),
        collective=7 if linked else None,
    )

    def weight_product(left, right):
        return jnp.einsum(
            "rd,re->de",
            left.reshape(-1, left.shape[-1]),
            right.reshape(-1, right.shape[-1]),
            preferred_element_type=wide,
        )

    if linked:
        def lines_of(field):
            return field.reshape(-1, field.shape[-1])

        results = closing(
            (conv1_grad, conv2_grad),
            (queries, keys, values),
            [
                lines_of(field)
                for field in (
                    resid_low, up_grad, act_low, branch_low, normed_two, pre_low, attended, mixed_low
                )
            ],
            (
                pulled, near_back[0], near_back[1], stats, near_back[2], near_back[3], bias,
                edge_bias, normed_low, tokens, qkv_weight,
            ),
            (
                ln1_gain, out_bias_grad, ln2_gain_grad, ln2_bias_grad, fc2_bias_grad, fc1_bias_grad,
            ),
        )
        conv_shares = (
            conv_share(results[0][:432], 27, 2),
            conv_share(results[1][:216], 27, 1),
            conv_share(results[0][432:448], 1, 2),
        )
        split = results[6].reshape(-1, 3, 3, model_width // 3)
        shares = list(results[2:6]) + [split.swapaxes(1, 2).reshape(results[6].shape)]
        token_grad = resid_grad + results[7]
        lines = results[8]
        span = model_width // shards
        own = lax.dynamic_slice_in_dim(lines[:12], lax.axis_index("tok") * span, span, 1)
        long_span = hidden // shards
        long_line = lines[12:16].reshape(hidden)
        long_own = lax.dynamic_slice_in_dim(
            long_line, lax.axis_index("tok") * long_span, long_span, 0
        )
        vectors = (own[0], own[1], own[2], own[3], own[8], own[9], own[10], long_own, own[11])
    else:
        query_grad, key_own, value_own, low_pay, high_pay = kernel_call(
            attention_back_kernel(row_count, model_width),
            seq_count,
            (queries, keys, values, pulled, stats, bias),
            (),
            (
                block(model_width, low_type),
                block(model_width, wide),
                block(model_width, wide),
                block(2 * model_width, low_type, REACH),
                block(2 * model_width, low_type, REACH),
            ),
            (),
            [
                pltpu.VMEM((reach_rows, model_width), wide),
                pltpu.VMEM((reach_rows, model_width), wide),
                pltpu.VMEM((model_width, reach_rows), low_type),
            ],
            matrix_flops * 12 * model_width,
        )
        both = jnp.concatenate([key_own, value_own], axis=-1)
        both = returned_rows(both, low_pay, high_pay)
        qkv_grad_low, token_grad, column_sums, ln1_gain_grad, ln1_bias_grad = kernel_call(
            token_kernel(row_count, model_width),
            seq_count,
            (tokens, resid_grad, query_grad, both[:, :, :model_width], both[:, :, model_width:]),
            (qkv_weight, ln1_gain),
            (block(3 * model_width, low_type), block(model_width, wide)),
            (
                ((1, 3 * model_width), wide),
                ((1, model_width), wide),
                ((1, model_width), wide),
            ),
            [],
            matrix_flops * 3 * model_width,
        )
        matrices = (
            weight_product(resid_low, up_grad),
            weight_product(act_low, branch_low),
            weight_product(normed_two, pre_low),
            weight_product(attended, mixed_low),
            weight_product(normed_low, qkv_grad_low),
        )
        conv3_turned = jnp.moveaxis(conv3_grad.reshape(1, 2, channels, channels), 2, 3)
        conv_grads = (conv1_grad, conv2_grad, conv3_turned)
        conv_shares, shares, vectors = reduced_all(
            conv_grads,
            matrices,
            (
                ln1_gain_grad, ln1_bias_grad, column_sums[:, :model_width],
                column_sums[:, 2 * model_width :], out_bias_grad, ln2_gain_grad, ln2_bias_grad,
                fc1_bias_grad, fc2_bias_grad,
            ),
        )
    return (
        section_out,
        token_grad,
        skip_grad,
        vectors[0],
        vectors[1],
        shares[4],
        jnp.stack([vectors[2], vectors[3]]),
        shares[3],
        vectors[4],
        vectors[5],
        vectors[6],
        shares[2],
        vectors[7],
        shares[1],
        vectors[8],
        shares[0],
        conv_shares[0],
        conv_shares[1],
        conv_shares[2][0],
    )


def solution(mesh):
    in_specs = (
        P("seq", "tok", None),
        P("seq", "tok", None, None),
        P("seq", None),
        P(),
        P(),
        P(),
        P(),
        P(),
        P(),
        P(),
        P(),
        P(),
        P(),
        P(),
        P(),
        P(),
        P(),
        P(),
        P(),
        P("seq", "tok", None, None),
    )
    out_specs = (
        P("seq", "tok", None, None),
        P("seq", "tok", None),
        P("seq", "tok", None, None),
        P("tok"),
        P("tok"),
        P("tok", None),
        P(None, "tok"),
        P("tok", None),
        P("tok"),
        P("tok"),
        P("tok"),
        P("tok", None),
        P("tok"),
        P("tok", None),
        P("tok"),
        P("tok", None),
        P(None, None, "tok"),
        P(None, None, "tok"),
        P(None, "tok"),
    )
    return jax.shard_map(local, mesh=mesh, in_specs=in_specs, out_specs=out_specs, check_vma=False)
```
